128 devices in a mesh: head: 4 (over x), blk: 32 (over y, z, core).
Axes of the slice: x: 4, y: 4, z: 4, core: 2. Of those that a mesh axis runs over, the one named last changes fastest.
Arguments:
- tokens: bfloat16 [16384, 1024], P(('blk', 'head')), may hold values from -6 to 6
- gain_one: bfloat16 [1024], P(('head', 'blk')), may hold values from 0.5 to 1.5
- w_query: bfloat16 [1024, 1024], P(('head', 'blk')), may hold values from -0.25 to 0.25
- w_key: bfloat16 [1024, 512], P(('head', 'blk')), may hold values from -0.25 to 0.25
- w_value: bfloat16 [1024, 512], P(('head', 'blk')), may hold values from -0.1875 to 0.1875
- w_out: bfloat16 [1024, 1024], P(('head', 'blk')), may hold values from -1 to 1
- gain_two: bfloat16 [1024], P(('head', 'blk')), may hold values from 0.5 to 1.5
- w_router: bfloat16 [1024, 32], P(('head', 'blk')), may hold values from -0.09375 to 0.09375
- w_gate: bfloat16 [32, 1024, 512], P('blk'), may hold values from -0.1875 to 0.1875
- w_up: bfloat16 [32, 1024, 512], P('blk'), may hold values from -0.1875 to 0.1875
- w_down: bfloat16 [32, 512, 1024], P('blk'), may hold values from -1 to 1
- dealt_order: int32 [16384], replicated, may hold values from 0 to 16383, as said below
- lengths: int32 [5], replicated, may hold values from 1024 to 8192, as said below
- routes: int32 [16384, 8], P(('blk', 'head')), may hold values from 0 to 31, all different within a row; in each aligned block of 128 rows (0 to 127, 128 to 255, ...) at most 36 rows name the same one
- cotangent: bfloat16 [16384, 1024], P(('blk', 'head')), may hold values from -6 to 6
Outputs:
- mixed: bfloat16 [16384, 1024], P(('blk', 'head'))
- grad_tokens: float32 [16384, 1024], P(('blk', 'head'))
- grad_gain_one: float32 [1024], P(('head', 'blk'))
- grad_query: float32 [1024, 1024], P(('head', 'blk'))
- grad_key: float32 [1024, 512], P(('head', 'blk'))
- grad_value: float32 [1024, 512], P(('head', 'blk'))
- grad_out: float32 [1024, 1024], P(('head', 'blk'))
- grad_gain_two: float32 [1024], P(('head', 'blk'))
- grad_router: float32 [1024, 32], P(('head', 'blk'))
- grad_gate: float32 [32, 1024, 512], P('blk', 'head')
- grad_up: float32 [32, 1024, 512], P('blk', 'head')
- grad_down: float32 [32, 512, 1024], P('blk', 'head')
The draws below stay inside these ranges and needn't reach their ends.
Inputs may be any that keep to these rules, and one draw needn't show every extreme that they name: `dealt_order`: A permutation. Cut the sequence order of the tokens into 64 runs of 256; each aligned block of 512 rows holds some run c < 32 in its first 256 rows and run 2 * 32 - 1 - c in the others, each in its own order; which c lies in which block varies. `lengths`: the sequences lie end to end and sum to 16384; the first or the last has 8192. `routes`: each row names 8 different experts; in the rows of one device (aligned blocks of 128) no expert is named more than 36 times.
All inputs are finite; a program needn't handle non-finite values.
Results may differ from the reference program's by a relative error of at most 0.028.
Values may be sent and summed in bfloat16 or wider, within the bound.
A program may use at most 192 MiB of HBM per device.

```python
import math
import jax
import jax.numpy as jnp
import numpy as np
from jax import lax

D = 1024
HEADS = 16
KV_HEADS = 8
HEAD_DIM = 64
EXPERTS = 32
TOP = 8
FF = 512
TOK_DEV = 128
MINLEN = 1024
GROUP = 512
RUN_ROWS = 256
TOKENS = 16384
KEYBLK = 2048
NSEQ = 5
CAP = 36


def draw_dealt_order(key, part):
    key = jax.random.fold_in(key, 7)
    block_total = TOKENS // GROUP
    pairing = jax.random.permutation(key, block_total).astype(jnp.int32)
    row_index = jnp.arange(TOKENS, dtype=jnp.int32)
    block_index = row_index // GROUP
    inner_index = row_index % GROUP
    first_run = pairing[block_index]
    run_index = jnp.where(inner_index < RUN_ROWS, first_run, 2 * block_total - 1 - first_run)
    return (run_index * RUN_ROWS + inner_index % RUN_ROWS).astype(jnp.int32)


def draw_lengths(key, part):
    key = jax.random.fold_in(key, 13)
    others = NSEQ - 1
    spare = TOKENS // 2 - others * MINLEN
    weight_key, side_key = jax.random.split(key)
    shares = jax.random.randint(weight_key, (others,), 1, 64).astype(jnp.int32)
    extra = (spare * shares // jnp.sum(shares)).astype(jnp.int32)
    extra = extra.at[0].add(spare - jnp.sum(extra))
    rest_lengths = (MINLEN + extra).astype(jnp.int32)
    whole = jnp.concatenate([jnp.full((1,), TOKENS // 2, jnp.int32), rest_lengths])
    side = jax.random.randint(side_key, (), 0, 2)
    return jnp.where(side == 1, jnp.roll(whole, -1), whole).astype(jnp.int32)


def level_of(stream_key, extent, cuts, low, high):
    gain = 1.0
    for dim, blocks in cuts:
        draws = jax.random.uniform(jax.random.fold_in(jax.random.fold_in(stream_key, 6), dim), (blocks,), jnp.float32, low / len(cuts), high / len(cuts))
        gain = gain * jnp.repeat(jnp.exp(draws), extent[dim] // blocks).reshape((-1,) + (1,) * (len(extent) - 1 - dim))
    return gain


def assign_block(own_key, own, number, rows, number_of, top, reach, lean):
    order = jax.random.permutation(own_key, number_of)
    heavy_load, ordinary = portions_of(number_of, rows * top, reach, lean, True), portions_of(number_of, rows * top, reach, lean, False)
    places = jnp.arange(number_of)

    def named(sizes, offset_by):
        used = int((sizes > 0).sum())
        fixed = max(1, used // 4)
        moved = fixed + (places - fixed + offset_by * (used - fixed)) % max(1, number_of - fixed)
        return jnp.zeros((number_of,), jnp.int32).at[order[jnp.where(places < fixed, places, moved)]].set(jnp.asarray(sizes, jnp.int32))

    sizes = jnp.where(number % 4 == 0, named(heavy_load, number // 4), named(ordinary, number - number // 4 - 1))
    mixed = jax.random.permutation(jax.random.fold_in(own, 3), number_of)
    source_of, sink = mixed[0:number_of // 2 * 2:2], mixed[1:number_of // 2 * 2:2]
    margin = jnp.minimum(sizes[source_of] - 1, reach - sizes[sink]) // 2
    margin = jnp.where((source_of == order[0]) | (sink == order[0]) | (sizes[sink] == 0), 0, jnp.maximum(margin, 0))
    moved = jax.random.randint(jax.random.fold_in(own, 4), (number_of // 2,), 0, 1 << 20) % (margin + 1)
    sizes = sizes.at[source_of].add(-moved).at[sink].add(moved)
    labels = jnp.searchsorted(jnp.cumsum(sizes), jnp.arange(rows * top), side="right").astype(jnp.int32)
    listing = labels.reshape(top, rows).T
    listing = listing[jax.random.permutation(jax.random.fold_in(own, 1), rows)]
    offset_by = jax.random.randint(jax.random.fold_in(own, 2), (rows, 1), 0, top)
    return jnp.take_along_axis(listing, (jnp.arange(top)[None, :] + offset_by) % top, axis=1)


def portions_of(amount, total, reach, slope, full):
    weights = [(1 << 20) // math.isqrt(standing ** slope) + 1 for standing in range(1, amount + 1)]
    largest = reach if full else min(reach, max(-(-total // amount), total * weights[0] // sum(weights)))
    least = 1 if total - largest >= amount - 1 else 0
    holding, surplus = [largest] + [least] * (amount - 1), total - largest - least * (amount - 1)
    while surplus > 0:
        movable = [i for i in range(1, amount) if holding[i] < largest] or [i for i in range(1, amount) if holding[i] < reach]
        pool, left = sum([weights[i] for i in movable]), surplus
        for i in movable:
            more = min(reach - holding[i], max(1, left * weights[i] // pool), surplus)
            holding[i] = holding[i] + more
            surplus = surplus - more
    return np.array(holding)


def noise(rng, shape, width, most, cuts=(), held_as=jnp.bfloat16):
    factor_of = level_of(rng, shape, cuts, -0.22, 0.18) if cuts else 1.0
    drawn = jax.random.normal(rng, shape, jnp.float32) * width * factor_of
    return jnp.minimum(jnp.maximum(drawn, -most), most).astype(held_as)


def setup_inputs(seed: int = 0) -> dict:
    key_list = jax.random.split(jax.random.key(seed), 16)
    tokens = noise(key_list[0], (TOKENS, D), 1.0, 6.0, ((0, 128),))
    gain_one = jnp.clip(1.0 + 0.1 * jax.random.normal(key_list[1], (D,), jnp.float32), 0.5, 1.5).astype(jnp.bfloat16)
    w_query = noise(key_list[2], (D, HEADS * HEAD_DIM), (D // 2) ** -0.5, 0.25, ((0, 128),))
    w_key = noise(key_list[3], (D, KV_HEADS * HEAD_DIM), (D // 2) ** -0.5, 0.25, ((0, 128),))
    w_value = noise(key_list[4], (D, KV_HEADS * HEAD_DIM), D ** -0.5, 0.1875, ((0, 128),))
    w_out = noise(key_list[5], (HEADS * HEAD_DIM, D), (D // 32) ** -0.5, 1.0, ((0, 128),))
    gain_two = jnp.clip(1.0 + 0.1 * jax.random.normal(key_list[6], (D,), jnp.float32), 0.5, 1.5).astype(jnp.bfloat16)
    w_router = noise(key_list[7], (D, EXPERTS), (4 * D) ** -0.5, 0.09375, ((0, 128),))
    w_gate = noise(key_list[8], (EXPERTS, D, FF), D ** -0.5, 0.1875, ((0, 32),))
    w_up = noise(key_list[9], (EXPERTS, D, FF), D ** -0.5, 0.1875, ((0, 32),))
    w_down = noise(key_list[10], (EXPERTS, FF, D), (FF // 16) ** -0.5, 1.0, ((0, 32),))
    dealt_order = draw_dealt_order(jax.random.fold_in(key_list[15], 71), 0)
    lengths = draw_lengths(jax.random.fold_in(key_list[15], 71), 0)
    routes_keys = jax.random.split(jax.random.fold_in(key_list[13], 1), TOKENS // TOK_DEV)
    routes_turns = jax.random.permutation(jax.random.fold_in(key_list[13], 3), TOKENS // TOK_DEV)
    routes = jax.vmap(lambda own, number: assign_block(jax.random.fold_in(key_list[13], 2), own, number, TOK_DEV, EXPERTS, TOP, CAP, 1))(routes_keys, routes_turns).reshape((TOKENS, TOP))
    cotangent = noise(key_list[14], (TOKENS, D), 1.0, 6.0, ((0, 128),))
    return {"tokens": tokens, "gain_one": gain_one, "w_query": w_query, "w_key": w_key, "w_value": w_value, "w_out": w_out, "gain_two": gain_two, "w_router": w_router, "w_gate": w_gate, "w_up": w_up, "w_down": w_down, "dealt_order": dealt_order, "lengths": lengths, "routes": routes, "cotangent": cotangent}


@jax.custom_vjp
def low(v):
    return lax.optimization_barrier(v.astype(jnp.bfloat16)).astype(jnp.float32)

@jax.custom_vjp
def low_back(v):
    return v

def low_keep(v):
    return (low(v), None)

def low_pass(kept, grad):
    return (grad,)

def back_keep(v):
    return (v, None)

def back_low(kept, grad):
    return (low(grad),)
low.defvjp(low_keep, low_pass)
low_back.defvjp(back_keep, back_low)
EPSILON = 1e-06
ROPE_BASE = 10000.0
HIGHEST = lax.Precision.HIGHEST

def normalize(values, scale_gain):
    inverse_rms = lax.rsqrt(lax.optimization_barrier(jnp.mean(values * values, axis=-1, keepdims=True)) + EPSILON)
    return values * inverse_rms * scale_gain

def places(dealt_order, lengths):
    ends_at = jnp.cumsum(lengths).astype(jnp.int32)
    passed = ends_at[None, :] <= dealt_order[:, None]
    segment = lax.optimization_barrier(jnp.sum(passed.astype(jnp.int32), axis=1)).astype(jnp.int32)
    offset = lax.optimization_barrier(jnp.sum(jnp.where(passed, lengths[None, :], 0), axis=1)).astype(jnp.int32)
    return (segment, (dealt_order - offset).astype(jnp.int32))

def rotate(values, position, direction):
    half_dim = values.shape[-1] // 2
    frequency = ROPE_BASE ** (-jnp.arange(half_dim, dtype=jnp.float32) / half_dim)
    angles = position.astype(jnp.float32)[:, None] * frequency[None, :]
    cosine = jnp.cos(angles)[:, None, :]
    sine_part = direction * jnp.sin(angles)[:, None, :]
    first_half = values[..., :half_dim]
    second_half = values[..., half_dim:]
    return jnp.concatenate([first_half * cosine - second_half * sine_part, second_half * cosine + first_half * sine_part], axis=-1)

def forward(tokens, gain_one, w_query, w_key, w_value, w_out, gain_two, w_router, w_gate, w_up, w_down, segment, position, dealt_order, routes):
    row_count = tokens.shape[0]
    head_ratio = HEADS // KV_HEADS
    normed = low(normalize(tokens, gain_one))
    query_pre = low_back(jnp.dot(normed, w_query, precision=HIGHEST))
    key_pre = low_back(jnp.dot(normed, w_key, precision=HIGHEST))
    value_rows = low(low_back(jnp.dot(normed, w_value, precision=HIGHEST))).reshape(row_count, KV_HEADS, HEAD_DIM)
    query_rot = low(rotate(query_pre.reshape(row_count, HEADS, HEAD_DIM), position, 1.0)).reshape(row_count, KV_HEADS, head_ratio, HEAD_DIM)
    key_rot = low(rotate(key_pre.reshape(row_count, KV_HEADS, HEAD_DIM), position, 1.0))
    key_norm = lax.optimization_barrier(jnp.max(jnp.sqrt(lax.optimization_barrier(jnp.sum(key_rot * key_rot, axis=-1))), axis=0))
    shift_all = jnp.ceil(jnp.sqrt(lax.optimization_barrier(jnp.sum(query_rot * query_rot, axis=-1))) * key_norm[None, :, None] * 0.125)
    query_blocks = row_count // GROUP
    key_blocks = row_count // KEYBLK
    key_split = key_rot.reshape(key_blocks, KEYBLK, KV_HEADS, HEAD_DIM)
    value_split = value_rows.reshape(key_blocks, KEYBLK, KV_HEADS, HEAD_DIM)
    segment_split = segment.reshape(key_blocks, KEYBLK)
    order_split = dealt_order.reshape(key_blocks, KEYBLK)

    def attend(pieces):
        query_block, shift_block, segment_block, order_block = pieces
        shift_row = shift_block.transpose(1, 2, 0)[..., None]

        def key_step(running, key_piece):
            weighted_sum, normalizer = running
            key_block, value_block, key_segment, key_order = key_piece
            scores = low_back(jnp.einsum('qjgd,kjd->jgqk', query_block, key_block, precision=HIGHEST) * 0.125)
            allowed = (segment_block[:, None] == key_segment[None, :]) & (key_order[None, :] <= order_block[:, None])
            exponent = jnp.where(allowed[None, None], jnp.exp(scores - shift_row), 0.0)
            weighted_sum = weighted_sum + jnp.einsum('jgqk,kjd->qjgd', low(exponent), value_block, precision=HIGHEST)
            normalizer = normalizer + lax.optimization_barrier(jnp.sum(exponent, axis=-1))
            return ((weighted_sum, normalizer), None)
        initial = (jnp.zeros(query_block.shape, jnp.float32), jnp.zeros(shift_row.shape[:3], jnp.float32))
        (weighted_sum, normalizer), _ = lax.scan(jax.checkpoint(key_step), initial, (key_split, value_split, segment_split, order_split))
        return low_back(weighted_sum) / normalizer.transpose(2, 0, 1)[..., None]
    attended = lax.map(jax.checkpoint(attend), (query_rot.reshape(query_blocks, GROUP, KV_HEADS, head_ratio, HEAD_DIM), shift_all.reshape(query_blocks, GROUP, KV_HEADS, head_ratio), segment.reshape(query_blocks, GROUP), dealt_order.reshape(query_blocks, GROUP)))
    attended = attended.reshape(row_count, HEADS * HEAD_DIM)
    sent_tokens = low_back(low(attended))
    residual_mid = tokens + low_back(jnp.dot(sent_tokens, w_out, precision=HIGHEST))
    mixed_in = low(normalize(residual_mid, gain_two))
    logits = low_back(jnp.dot(mixed_in, w_router, precision=HIGHEST))
    chosen = jnp.take_along_axis(logits, routes, axis=1)
    gate_probs = jax.nn.softmax(chosen, axis=-1)
    share_all = lax.optimization_barrier(jnp.sum(jax.nn.one_hot(routes, EXPERTS, dtype=jnp.float32) * gate_probs[..., None], axis=1))

    def expert(pieces):
        gate_weight, up_weight, down_weight, share_col = pieces
        inputs = low_back(mixed_in)
        gate_pre = low_back(jnp.dot(inputs, gate_weight, precision=HIGHEST))
        up_pre = low_back(jnp.dot(inputs, up_weight, precision=HIGHEST))
        hidden = low(jax.nn.silu(gate_pre) * up_pre)
        result = low_back(low(jnp.dot(hidden, down_weight, precision=HIGHEST)))
        return share_col[:, None] * result

    def accumulate(running_sum, pieces):
        return (running_sum + jax.checkpoint(expert)(pieces), None)
    expert_sum, _ = lax.scan(accumulate, jnp.zeros_like(residual_mid), (w_gate, w_up, w_down, share_all.T))
    return residual_mid + expert_sum

def reference(tokens, gain_one, w_query, w_key, w_value, w_out, gain_two, w_router, w_gate, w_up, w_down, dealt_order, lengths, routes, cotangent):
    segment, position = places(dealt_order, lengths)
    floats = (tokens, gain_one, w_query, w_key, w_value, w_out, gain_two, w_router, w_gate, w_up, w_down)
    floats = tuple((member.astype(jnp.float32) for member in floats))

    def layer_pass(tokens_in, gain_first, query_weight, key_weight, value_weight, out_weight, gain_second, router_weight, gate_weight, up_weight, down_weight):
        return forward(tokens_in, gain_first, query_weight, key_weight, value_weight, out_weight, gain_second, router_weight, gate_weight, up_weight, down_weight, segment, position, dealt_order, routes)
    result, pullback = jax.vjp(layer_pass, *floats)
    gradients = pullback(cotangent.astype(jnp.float32))
    return (result.astype(jnp.bfloat16), gradients[0], gradients[1], gradients[2], gradients[3], gradients[4], gradients[5], gradients[6], gradients[7], gradients[8], gradients[9], gradients[10])
```

```python
import functools
import math

import jax
import jax.numpy as jnp
import ml_dtypes
import numpy as np
from jax import lax
from jax.experimental import pallas as pl
from jax.experimental.pallas import tpu as pltpu
from jax.sharding import Mesh
from jax.sharding import PartitionSpec as P

D = 1024
HEADS = 16
KV_HEADS = 8
HEAD_DIM = 64
EXPERTS = 32
FF = 512
CAP = 36
SLOT = 40
SLOTS = EXPERTS * SLOT
ROWS = 128
CHIP_ROWS = 1024
RUN = 256
TOKENS = 16384
NSEQ = 5
EPSILON = 1e-06
ROPE_BASE = 10000.0
FAR = float(2.0**100)
SIZE = {"x": 4, "y": 4, "z": 4, "c": 2}
AXES = ("x", "y", "z", "c")
MESH = pl.DeviceIdType.MESH
BF16 = jnp.bfloat16
F32 = jnp.float32
NN = (((1,), (0,)), ((), ()))
NT = (((1,), (1,)), ((), ()))
TN = (((0,), (0,)), ((), ()))
VMEM_BYTES = 56 * 1024 * 1024


def mm(a, b, dims=NN):
    return lax.dot_general(a, b, dims, preferred_element_type=F32)


def halves(value):
    high = value.astype(BF16)
    return high, (value - high.astype(F32)).astype(BF16)


def local_call(kernel, outs, scratch=(), grid=None, in_specs=None, out_specs=None, flops=0, moved=0):
    extra = {}
    if grid is not None:
        extra = {"grid": grid, "in_specs": in_specs, "out_specs": out_specs}
    elif in_specs is not None:
        extra = {"in_specs": in_specs}
    return pl.pallas_call(
        kernel,
        out_shape=outs,
        scratch_shapes=list(scratch),
        compiler_params=pltpu.CompilerParams(vmem_limit_bytes=VMEM_BYTES),
        cost_estimate=pl.CostEstimate(flops=flops, bytes_accessed=moved, transcendentals=0),
        **extra,
    )


def flat_index(coords, order):
    index = 0
    for axis in order:
        index = index * SIZE[axis] + coords[axis]
    return index


PLANE_ORDER = (
    (2, 2), (2, 3), (2, 1), (3, 2), (1, 2), (0, 2), (2, 0), (3, 1), (1, 3),
    (3, 3), (1, 1), (0, 3), (0, 1), (3, 0), (1, 0), (0, 0),
)
PLANE_OFFSETS = tuple({"y": dy, "z": dz} for dy, dz in PLANE_ORDER[:-1])
SPREAD_OFFSETS = tuple(
    {"y": dy, "z": dz, "c": (dc + i + 1) % 2}
    for i, (dy, dz) in enumerate(PLANE_ORDER)
    for dc in range(2)
    if (dy, dz, (dc + i + 1) % 2) != (0, 0, 0)
)
LINE_OFFSETS = tuple(
    {"x": dx, "c": dc} for dx, dc in ((2, 0), (2, 1), (1, 0), (3, 0), (1, 1), (3, 1), (0, 1))
)
OFFSETS = {("y", "z"): PLANE_OFFSETS, ("y", "z", "c"): SPREAD_OFFSETS, ("x", "c"): LINE_OFFSETS}


def position(axes):
    return {axis: lax.axis_index(axis) for axis in axes}


def moved(me, offset):
    return {axis: lax.rem(me[axis] + by, SIZE[axis]) if by else me[axis] for axis, by in offset.items()}


def greet(me, offsets):
    barrier = pltpu.get_barrier_semaphore()
    for offset in offsets:
        pl.semaphore_signal(barrier, inc=1, device_id=moved(me, offset), device_id_type=MESH)
    pl.semaphore_wait(barrier, len(offsets))


def remote(src, dst, send, recv, slot, to):
    return pltpu.make_async_remote_copy(
        src_ref=src,
        dst_ref=dst,
        send_sem=send.at[slot],
        recv_sem=recv.at[slot],
        device_id=to,
        device_id_type=MESH,
    )


def exchange_kernel(axes, dest_order, src_order, arrays, *refs):
    x_refs, o_refs = refs[:arrays], refs[arrays : 2 * arrays]
    send, recv, local = refs[2 * arrays :]
    me = position(axes)
    offsets = OFFSETS[axes]
    greet(me, offsets)
    here = flat_index(me, src_order)
    copies = []
    for offset in offsets:
        to = moved(me, offset)
        for x_ref, o_ref in zip(x_refs, o_refs):
            copies.append(
                remote(
                    x_ref.at[flat_index(to, dest_order)], o_ref.at[here], send, recv, len(copies), to
                )
            )
            copies[-1].start()
    kept = [
        pltpu.make_async_copy(
            x_ref.at[flat_index(me, dest_order)], o_ref.at[here], local.at[i]
        )
        for i, (x_ref, o_ref) in enumerate(zip(x_refs, o_refs))
    ]
    for item in kept:
        item.start()
    for item in kept + copies:
        item.wait()


def exchange(data, axes, cid, dest_order=None, src_order=None):
    single = not isinstance(data, (tuple, list))
    data = [data] if single else list(data)
    dest_order = dest_order or axes
    src_order = src_order or axes
    arrays = len(data)
    count = len(OFFSETS[axes]) * arrays
    out = pl.pallas_call(
        functools.partial(exchange_kernel, axes, dest_order, src_order, arrays),
        out_shape=[jax.ShapeDtypeStruct(item.shape, item.dtype) for item in data],
        in_specs=[pl.BlockSpec(memory_space=pl.ANY)] * arrays,
        out_specs=[pl.BlockSpec(memory_space=pl.ANY)] * arrays,
        scratch_shapes=[
            pltpu.SemaphoreType.DMA((count,)),
            pltpu.SemaphoreType.DMA((count,)),
            pltpu.SemaphoreType.DMA((arrays,)),
        ],
        compiler_params=pltpu.CompilerParams(collective_id=cid, has_side_effects=True),
    )(*data)
    return out[0] if single else out


def start_kernel(tok_ref, w_ref, o_tok, o_w, send, recv, local):
    me = position(AXES)
    x, y, z, c = (me[axis] for axis in AXES)
    offsets = LINE_OFFSETS + PLANE_OFFSETS
    greet(me, offsets)
    plus, minus, far = lax.rem(x + 1, 4), lax.rem(x + 3, 4), lax.rem(x + 2, 4)
    other = 1 - c
    lower, upper = pl.ds(0, 64), pl.ds(64, 64)
    used = [0]

    def go(src, dst, to):
        item = remote(src, dst, send, recv, used[0], to)
        used[0] += 1
        item.start()
        return item

    own_tok = pltpu.make_async_copy(tok_ref, o_tok.at[c, x], local.at[0])
    own_w = pltpu.make_async_copy(w_ref.at[x * 2 + c], o_w.at[x, y, z, c], local.at[1])
    own_tok.start()
    own_w.start()
    first_w = []
    for offset in LINE_OFFSETS:
        to = moved(me, offset)
        first_w.append(go(w_ref.at[to["x"] * 2 + to["c"]], o_w.at[x, y, z, c], to))
    to_plus = go(tok_ref, o_tok.at[c, x], {"x": plus})
    to_minus = go(tok_ref, o_tok.at[c, x], {"x": minus})
    sides = [go(tok_ref, o_tok.at[c, x], {"c": other})]
    own_w.wait()
    for item in first_w:
        item.wait()
    second_w = [
        go(o_w.at[:, y, z], o_w.at[:, y, z], moved(me, offset)) for offset in PLANE_OFFSETS
    ]
    to_plus.wait()
    next_plus = go(o_tok.at[c, minus, lower], o_tok.at[c, minus, lower], {"x": plus})
    sides.append(go(o_tok.at[c, minus], o_tok.at[c, minus], {"c": other}))
    to_minus.wait()
    next_minus = go(o_tok.at[c, plus, upper], o_tok.at[c, plus, upper], {"x": minus})
    sides.append(go(o_tok.at[c, plus], o_tok.at[c, plus], {"c": other}))
    next_plus.wait()
    next_minus.wait()
    sides.append(go(o_tok.at[c, far], o_tok.at[c, far], {"c": other}))
    for item in sides + second_w + [own_tok]:
        item.wait()


def start_rows(tokens, packed, cid):
    count = 3 + 7 + 15 + 2 + 3
    rows, weights = pl.pallas_call(
        start_kernel,
        out_shape=[
            jax.ShapeDtypeStruct((2, 4, ROWS, D), BF16),
            jax.ShapeDtypeStruct((4, 4, 4, 2, 8, 384), BF16),
        ],
        in_specs=[pl.BlockSpec(memory_space=pl.ANY)] * 2,
        out_specs=[pl.BlockSpec(memory_space=pl.ANY)] * 2,
        scratch_shapes=[
            pltpu.SemaphoreType.DMA((count,)),
            pltpu.SemaphoreType.DMA((count,)),
            pltpu.SemaphoreType.DMA((2,)),
        ],
        compiler_params=pltpu.CompilerParams(collective_id=cid, has_side_effects=True),
    )(tokens, packed)
    return rows.reshape(CHIP_ROWS, D), weights.reshape(D, 384)


AROUND = ({"y": 1, "z": 0}, {"y": 3, "z": 0}, {"y": 0, "z": 1}, {"y": 0, "z": 3})


def gather_plane_kernel(x_ref, o_ref, send, recv, local):
    me = position(("y", "z"))
    y, z = me["y"], me["z"]
    greet(me, AROUND)
    own = pltpu.make_async_copy(x_ref, o_ref.at[y, z], local)
    own.start()
    half = x_ref.shape[1] // 2
    lower, upper = pl.ds(0, half), pl.ds(half, half)
    used = [0]

    def go(src, dst, to):
        item = remote(src, dst, send, recv, used[0], to)
        used[0] += 1
        item.start()
        return item

    def place(t, a, b):
        return o_ref.at[a, b, 0] if t == 0 else o_ref.at[b, a, 1]

    axis = (("y", "z"), ("z", "y"))
    here = tuple((me[a], me[b]) for a, b in axis)
    step = {"plus": 1, "minus": 3, "far": 2, "own": 0}

    def at(t, which, name):
        return lax.rem(here[t][which] + step[name], 4)

    def send_second(t, src, name):
        dst = place(t, at(t, 0, name), here[t][1])
        src = dst if src is None else src
        return (
            go(src, dst, {axis[t][1]: at(t, 1, "plus")}),
            go(src, dst, {axis[t][1]: at(t, 1, "minus")}),
        )

    def pass_on(t, which, a_name, b_name, part, direction):
        ref = place(t, at(t, 0, a_name), at(t, 1, b_name)).at[part]
        return go(ref, ref, {axis[t][which]: at(t, which, direction)})

    def forward_second(t, name, pair):
        pair[0].wait()
        a = pass_on(t, 1, name, "minus", lower, "plus")
        pair[1].wait()
        b = pass_on(t, 1, name, "plus", upper, "minus")
        return [a, b]

    first, second, last = {}, {}, []
    for t in (0, 1):
        dst = place(t, *here[t])
        first[t] = (
            go(x_ref.at[t], dst, {axis[t][0]: at(t, 0, "plus")}),
            go(x_ref.at[t], dst, {axis[t][0]: at(t, 0, "minus")}),
        )
    for t in (0, 1):
        second[t, "own"] = send_second(t, x_ref.at[t], "own")
    far = {}
    for t in (0, 1):
        first[t][0].wait()
        a = pass_on(t, 0, "minus", "own", lower, "plus")
        second[t, "minus"] = send_second(t, None, "minus")
        first[t][1].wait()
        b = pass_on(t, 0, "plus", "own", upper, "minus")
        second[t, "plus"] = send_second(t, None, "plus")
        far[t] = (a, b)
    for t in (0, 1):
        last += forward_second(t, "own", second[t, "own"])
    for t in (0, 1):
        far[t][0].wait()
        far[t][1].wait()
        second[t, "far"] = send_second(t, None, "far")
    for name in ("minus", "plus", "far"):
        for t in (0, 1):
            last += forward_second(t, name, second[t, name])
    for item in last + [own]:
        item.wait()


def gather_plane(data, cid):
    rows = data.shape[0] // 2
    out = pl.pallas_call(
        gather_plane_kernel,
        out_shape=jax.ShapeDtypeStruct((4, 4, 2, rows, 128), data.dtype),
        in_specs=[pl.BlockSpec(memory_space=pl.ANY)],
        out_specs=pl.BlockSpec(memory_space=pl.ANY),
        scratch_shapes=[
            pltpu.SemaphoreType.DMA((40,)),
            pltpu.SemaphoreType.DMA((40,)),
            pltpu.SemaphoreType.DMA,
        ],
        compiler_params=pltpu.CompilerParams(collective_id=cid, has_side_effects=True),
    )(data.reshape(2, rows, 128))
    return out.reshape(32 * rows, 128)


def scatter_plane_kernel(p_ref, sent_ref, branch_ref, o_ref, grad_ref, far_a, near_a, out_a, sum_a, far_b, near_b, out_b, send, recv):
    me = position(("y", "z"))
    greet(me, AROUND)
    half = p_ref.shape[3] // 2
    lower, upper = pl.ds(0, half), pl.ds(half, half)
    axis = (("y", "z"), ("z", "y"))
    used = [0]

    def go(src, dst, t, which, by):
        to = {axis[t][which]: lax.rem(me[axis[t][which]] + by, 4)}
        item = remote(src, dst, send, recv, used[0], to)
        used[0] += 1
        item.start()
        return item

    def part(t, first, second):
        a = lax.rem(me[axis[t][0]] + first, 4)
        b = lax.rem(me[axis[t][1]] + second, 4)
        return p_ref.at[a, b, 0] if t == 0 else p_ref.at[b, a, 1]

    turns = (2, 1, 3, 0)
    both = (0, 1)
    far, near = {}, {}
    for k, by in enumerate(turns):
        for t in both:
            far[k, t] = (
                go(part(t, 2, by).at[lower], far_a.at[t, k, 0], t, 0, 1),
                go(part(t, 2, by).at[upper], far_a.at[t, k, 1], t, 0, 3),
            )
    grad_ref[...] = mm(sent_ref[...], branch_ref[...], TN)
    for k, by in enumerate(turns):
        for t in both:
            ahead, behind = part(t, 1, by), part(t, 3, by)
            far[k, t][0].wait()
            out_a[t, k, 0, 0:half] = (ahead[0:half].astype(F32) + far_a[t, k, 0].astype(F32)).astype(BF16)
            out_a[t, k, 0, half : 2 * half] = ahead[half : 2 * half]
            first = go(out_a.at[t, k, 0], near_a.at[t, k, 0], t, 0, 1)
            far[k, t][1].wait()
            out_a[t, k, 1, 0:half] = behind[0:half]
            out_a[t, k, 1, half : 2 * half] = (
                behind[half : 2 * half].astype(F32) + far_a[t, k, 1].astype(F32)
            ).astype(BF16)
            near[k, t] = (first, go(out_a.at[t, k, 1], near_a.at[t, k, 1], t, 0, 3))

    def summed(k, t):
        near[k, t][0].wait()
        near[k, t][1].wait()
        return (
            part(t, 0, turns[k])[...].astype(F32)
            + near_a[t, k, 0].astype(F32)
            + near_a[t, k, 1].astype(F32)
        )

    far_two, near_two = {}, {}
    for t in both:
        value = summed(0, t).astype(BF16)
        out_b[t, 0] = value
        far_two[t] = (
            go(out_b.at[t, 0, lower], far_b.at[t, 0], t, 1, 1),
            go(out_b.at[t, 0, upper], far_b.at[t, 1], t, 1, 3),
        )
    for k in (1, 2):
        for t in both:
            sum_a[t, k - 1] = summed(k, t)
    for t in both:
        far_two[t][0].wait()
        out_b[t, 1, 0:half] = (sum_a[t, 0, 0:half] + far_b[t, 0].astype(F32)).astype(BF16)
        out_b[t, 1, half : 2 * half] = sum_a[t, 0, half : 2 * half].astype(BF16)
        first = go(out_b.at[t, 1], near_b.at[t, 0], t, 1, 1)
        far_two[t][1].wait()
        out_b[t, 2, 0:half] = sum_a[t, 1, 0:half].astype(BF16)
        out_b[t, 2, half : 2 * half] = (
            sum_a[t, 1, half : 2 * half] + far_b[t, 1].astype(F32)
        ).astype(BF16)
        near_two[t] = (first, go(out_b.at[t, 2], near_b.at[t, 1], t, 1, 3))
    for t in both:
        value = summed(3, t)
        near_two[t][0].wait()
        near_two[t][1].wait()
        o_ref[t] = value + near_b[t, 0].astype(F32) + near_b[t, 1].astype(F32)


def scatter_plane(data, sent, branch_rows, cid):
    rows = data.shape[0] // 32
    whole = pl.BlockSpec(memory_space=pltpu.VMEM)
    out, grad_out = pl.pallas_call(
        scatter_plane_kernel,
        out_shape=[
            jax.ShapeDtypeStruct((2, rows, 128), F32),
            jax.ShapeDtypeStruct((ROWS, D), F32),
        ],
        in_specs=[whole] * 3,
        out_specs=[whole] * 2,
        scratch_shapes=[
            pltpu.VMEM((2, 4, 2, rows // 2, 128), BF16),
            pltpu.VMEM((2, 4, 2, rows, 128), BF16),
            pltpu.VMEM((2, 4, 2, rows, 128), BF16),
            pltpu.VMEM((2, 2, rows, 128), F32),
            pltpu.VMEM((2, 2, rows // 2, 128), BF16),
            pltpu.VMEM((2, 2, rows, 128), BF16),
            pltpu.VMEM((2, 3, rows, 128), BF16),
            pltpu.SemaphoreType.DMA((40,)),
            pltpu.SemaphoreType.DMA((40,)),
        ],
        compiler_params=pltpu.CompilerParams(
            collective_id=cid, has_side_effects=True, vmem_limit_bytes=VMEM_BYTES
        ),
    )(data.reshape(4, 4, 2, rows, 128), sent, branch_rows)
    return out.reshape(2 * rows, 128), grad_out


def lane_index(shape):
    return lax.broadcasted_iota(jnp.int32, shape, 1)


def turned(values):
    lane = lane_index(values.shape)
    up = pltpu.roll(values, 32, axis=1)
    down = pltpu.roll(values, 96, axis=1)
    return jnp.where(lane % 64 < 32, -down, up)


def project_kernel(tok_ref, w_ref, cos_ref, sin_ref, normed_ref, q_ref, kv_ref, gain_ref):
    gain = w_ref[:, 256:384].astype(F32).T[0:1, :]
    gain_ref[...] = gain
    for part in range(4):
        rows = pl.ds(part * 256, 256)
        tok = tok_ref[rows, :].astype(F32)
        scale = lax.rsqrt(jnp.mean(tok * tok, axis=-1, keepdims=True) + EPSILON)
        normed = (tok * scale * gain).astype(BF16)
        normed_ref[rows, :] = normed
        pre = mm(normed, w_ref[:, 0:256])
        cos, sin = cos_ref[rows, :], sin_ref[rows, :]
        low_lanes = lane_index((256, 128)) < 64
        q_pre, kv_pre = pre[:, :128], pre[:, 128:]
        query = (q_pre * cos + turned(q_pre) * sin).astype(BF16).astype(F32) * 0.125
        q_ref[0, rows, :] = jnp.where(low_lanes, query, 0.0).astype(BF16)
        q_ref[1, rows, :] = jnp.where(low_lanes, pltpu.roll(query, 64, axis=1), 0.0).astype(BF16)
        key = kv_pre * cos + turned(kv_pre) * sin
        kv_ref[rows, :] = jnp.where(low_lanes, key, kv_pre).astype(BF16)


def order_pair(order_ref, index):
    row = jnp.broadcast_to(order_ref[index : index + 1, :], (RUN, RUN))
    return row, row.T


def attend_kernel(
    first_ref, count_ref, kv_ref, aux_ref, own_kv_ref, own_aux_ref, q_ref, order_ref,
    att_ref, norm_ref, sent_ref, qx_ref, acc_ref,
):
    def largest(step, best):
        tile = kv_ref[pl.ds(pl.multiple_of(step * 512, 512), 512), :].astype(F32)
        square = jnp.sum(jnp.where(lane_index((512, 128)) < 64, tile * tile, 0.0), axis=1, keepdims=True)
        return jnp.maximum(best, square)

    best = lax.fori_loop(0, TOKENS // 512, largest, jnp.zeros((512, 1), F32))
    key_norm = jnp.sqrt(jnp.max(best, axis=0, keepdims=True))
    lane = lane_index((RUN, 128))
    lane_tall = lane_index((2 * RUN, 128))

    def weights(keys, aux, qx):
        return jnp.exp(mm(qx, jnp.concatenate([keys, aux], axis=1), NT))

    def right(keys):
        return jnp.where(lane_index(keys.shape) < 64, jnp.ones_like(keys), keys)

    for part in range(4):
        rows = pl.ds(part * RUN, RUN)
        own_aux = own_aux_ref[rows, :].astype(F32)
        for head in range(2):
            query = q_ref[head, rows, :]
            wide = query.astype(F32)
            shift = jnp.ceil(jnp.sqrt(jnp.sum(wide * wide, axis=1, keepdims=True)) * key_norm)
            top = shift.astype(BF16).astype(F32)
            middle = (shift - top).astype(BF16).astype(F32)
            rest = shift - top - middle
            ext = jnp.where(lane < 3 + NSEQ, (own_aux - 1.0) * FAR, 0.0)
            ext = jnp.where(lane == 0, -top, ext)
            ext = jnp.where(lane == 1, -middle, ext)
            ext = jnp.where(lane == 2, -rest, ext)
            here = pl.ds(head * RUN, RUN)
            qx_ref[part, here, 0:128] = query
            qx_ref[part, here, 128:256] = ext.astype(BF16)
        qx = qx_ref[part]
        order_key, order_query = order_pair(order_ref, part)
        allowed = order_key <= order_query
        keys = own_kv_ref[rows, :]
        e = weights(keys, own_aux_ref[rows, :], qx)
        e = jnp.where(jnp.concatenate([allowed, allowed], axis=0), e, 0.0)
        acc_ref[...] = mm(e.astype(BF16), right(keys))
        base = (part % 2) * 32

        def tiles(step):
            start = pl.multiple_of(first_ref[base + step], RUN)
            return kv_ref[pl.ds(start, RUN), :], aux_ref[pl.ds(start, RUN), :]

        def pair(step, carry):
            keys_a, aux_a = tiles(2 * step)
            keys_b, aux_b = tiles(2 * step + 1)
            keys = jnp.concatenate([keys_a, keys_b], axis=0)
            aux = jnp.concatenate([aux_a, aux_b], axis=0)
            acc_ref[...] += mm(weights(keys, aux, qx).astype(BF16), right(keys))
            return carry

        number = count_ref[part]
        lax.fori_loop(0, number // 2, pair, 0)

        @pl.when(number % 2 == 1)
        def _():
            keys, aux = tiles(number - 1)
            acc_ref[...] += mm(weights(keys, aux, qx).astype(BF16), right(keys))

        total = acc_ref[...]
        other = pltpu.roll(total, 64, axis=1)
        norm = jnp.where(lane_tall < 64, total, other)
        value = jnp.where(lane_tall < 64, other, total) / norm
        low_lanes = lane < 64
        att = jnp.where(low_lanes, value[:RUN], value[RUN:])
        att_ref[rows, :] = att
        norm_ref[rows, :] = jnp.where(low_lanes, norm[:RUN], norm[RUN:])
        sent_ref[rows, :] = att.astype(BF16)


def attend_back_kernel(
    first_ref, count_ref, base_ref, kv_ref, aux_ref, own_kv_ref, own_aux_ref, qx_ref, order_ref,
    gsent_ref, att_ref, norm_ref, dq_ref, dkv_ref, acc_ref, dq_acc, gx_ref, rhs_ref,
):
    def clear(step, carry):
        acc_ref[pl.ds(pl.multiple_of(step * 512, 512), 512), :] = jnp.zeros((512, 128), F32)
        return carry

    lax.fori_loop(0, TOKENS // 512, clear, 0)
    lane = lane_index((RUN, 128))
    low_lanes = lane < 64
    for part in range(4):
        rows = pl.ds(part * RUN, RUN)
        gsent = gsent_ref[rows, :].astype(F32)
        norm = norm_ref[rows, :]
        product = gsent * att_ref[rows, :] / norm
        scaled = (gsent / norm).astype(BF16).astype(F32)
        for head in range(2):
            mask = low_lanes if head == 0 else jnp.logical_not(low_lanes)
            delta = jnp.sum(jnp.where(mask, product, 0.0), axis=1, keepdims=True)
            top = delta.astype(BF16).astype(F32)
            middle = (delta - top).astype(BF16).astype(F32)
            rest = delta - top - middle
            ext = jnp.where(lane == 0, -top, 0.0)
            ext = jnp.where(lane == 1, -middle, ext)
            ext = jnp.where(lane == 2, -rest, ext)
            grad = pltpu.roll(scaled, 64, axis=1) if head == 0 else scaled
            grad = jnp.where(low_lanes, 0.0, grad).astype(BF16)
            here = pl.ds(head * RUN, RUN)
            gx_ref[here, 0:128] = grad
            gx_ref[here, 128:256] = ext.astype(BF16)
            rhs_ref[pl.ds(head * RUN, RUN), :] = qx_ref[part, here, 0:128]
            rhs_ref[pl.ds((2 + head) * RUN, RUN), :] = grad
        order_key, order_query = order_pair(order_ref, part)
        allowed = order_query <= order_key
        dq_acc[...] = jnp.zeros_like(dq_acc)

        def tile(start, keys, aux, mask):
            both = jnp.concatenate([keys, aux], axis=1)
            e = jnp.exp(mm(both, qx_ref[part], NT))
            if mask is not None:
                e = jnp.where(mask, e, 0.0)
            ds = (e * mm(both, gx_ref[...], NT)).astype(BF16)
            left = jnp.concatenate([ds, e.astype(BF16)], axis=1)
            acc_ref[pl.ds(start, RUN), :] += mm(left, rhs_ref[...])
            dq_acc[...] += mm(keys.T[:64], ds)

        tile(
            pl.multiple_of(base_ref[0] + part * RUN, RUN),
            own_kv_ref[rows, :],
            own_aux_ref[rows, :],
            jnp.concatenate([allowed, allowed], axis=1),
        )
        base = (part % 2) * 32

        def step_tile(step, carry):
            start = pl.multiple_of(first_ref[base + step], RUN)
            tile(start, kv_ref[pl.ds(start, RUN), :], aux_ref[pl.ds(start, RUN), :], None)
            return carry

        lax.fori_loop(0, count_ref[part], step_tile, 0)
        total = dq_acc[...] * 0.125
        dq_ref[rows, :] = jnp.concatenate([total[:, :RUN], total[:, RUN:]], axis=0).T

    def finish(step, carry):
        rows = pl.ds(pl.multiple_of(step * 512, 512), 512)
        dkv_ref[rows, :] = acc_ref[rows, :].astype(BF16)
        return carry

    lax.fori_loop(0, TOKENS // 512, finish, 0)


SLOT_EXPERT = np.arange(SLOTS) // SLOT
SLOT_PLACE = np.arange(SLOTS) % SLOT


def constant(array):
    return jnp.asarray(np.asarray(array).astype(ml_dtypes.bfloat16))


def expand_matrix():
    return constant(np.arange(128)[:, None] == SLOT_EXPERT[None, :])


def place_matrix():
    return constant(SLOT_PLACE[:, None] == np.arange(128)[None, :])


def pick_matrix(place):
    return constant((SLOT_EXPERT[:, None] == np.arange(128)[None, :]) & (SLOT_PLACE[:, None] == place))


def place_column():
    used = np.where(SLOT_PLACE < CAP, SLOT_PLACE, -5)
    return constant(np.broadcast_to(used[:, None], (SLOTS, 128)))


def place_row():
    used = np.where(SLOT_PLACE < CAP, SLOT_PLACE, -5)
    return jnp.asarray(used[None, :].astype(np.float32))


def prepare_kernel(routes_ref, cot_ref, expand_ref, expand_t_ref, col_ref, row_ref, member_ref, put_ref, take_ref, out_ref):
    lane = lane_index((ROWS, 128))
    routes = routes_ref[...]
    member = jnp.zeros((ROWS, 128), F32)
    for choice in range(8):
        member += jnp.where(routes[:, choice : choice + 1] == lane, 1.0, 0.0)
    below = lax.broadcasted_iota(jnp.int32, (ROWS, ROWS), 0) > lane_index((ROWS, ROWS))
    earlier = mm(jnp.where(below, 1.0, 0.0).astype(BF16), member.astype(BF16))
    slot = jnp.where(member > 0.5, earlier, -1.0).astype(BF16)
    member_ref[...] = member
    take = jnp.where(mm(slot, expand_ref[...]) == row_ref[...], 1.0, 0.0)
    take_ref[...] = take.astype(BF16)
    put = jnp.where(mm(expand_t_ref[...], slot, NT) == col_ref[...].astype(F32), 1.0, 0.0)
    put = put.astype(BF16)
    put_ref[...] = put
    for part in range(4):
        columns = pl.ds(part * 256, 256)
        out_ref[:, columns] = mm(put, cot_ref[:, columns]).astype(BF16)


def middle_kernel(
    sent_ref, tok_ref, w_out_ref, router_ref, member_ref, put_ref, take_ref, expand_ref,
    place_ref, pick_high_ref, pick_low_ref,
    residual_ref, mixed_ref, gate_ref, out_ref, weigh_high_ref, weigh_low_ref,
):
    sent = jnp.concatenate([sent_ref[i] for i in range(8)], axis=1)
    residual = tok_ref[...].astype(F32) + mm(sent, w_out_ref[...])
    residual_ref[...] = residual
    scale = lax.rsqrt(jnp.mean(residual * residual, axis=-1, keepdims=True) + EPSILON)
    gain = router_ref[...].astype(F32).T[EXPERTS : EXPERTS + 1, :]
    mixed = (residual * scale * gain).astype(BF16)
    mixed_ref[...] = mixed
    logits = mm(mixed, router_ref[...])
    member = member_ref[...]
    masked = jnp.where(member > 0.5, logits, -FAR)
    top = jnp.max(masked, axis=1, keepdims=True)
    power = jnp.where(member > 0.5, jnp.exp(masked - top), 0.0)
    gate = power / jnp.sum(power, axis=1, keepdims=True)
    gate_ref[...] = gate
    gate_high, gate_low = halves(gate)
    spread = mm(gate_high, expand_ref[...]) + mm(gate_low, expand_ref[...])
    weigh = take_ref[...].astype(F32) * spread
    weigh_high, weigh_low = halves(weigh)
    weigh_high_ref[...] = weigh_high
    weigh_low_ref[...] = weigh_low
    total = jnp.sum(weigh, axis=0, keepdims=True)
    by_expert = expand_ref[...].astype(F32) * total
    rows_high, rows_low = halves(by_expert)
    rows_high = mm(rows_high, place_ref[...]).astype(BF16)
    rows_low = mm(rows_low, place_ref[...]).astype(BF16)
    gate_rows = mm(pick_high_ref[...], rows_high) + mm(pick_low_ref[...], rows_low)
    put = put_ref[...]
    out_ref[:, 0:128] = (mm(put, mixed[:, 0:128]) + gate_rows).astype(BF16)
    out_ref[:, 128:512] = mm(put, mixed[:, 128:512]).astype(BF16)
    out_ref[:, 512:1024] = mm(put, mixed[:, 512:1024]).astype(BF16)


BLOCK = 8 * SLOT
BLOCK_SOURCE = np.arange(BLOCK) // SLOT
BLOCK_PLACE = np.arange(BLOCK) % SLOT


def block_matrix(places):
    hit = np.isin(BLOCK_PLACE, places)[None, :] & (BLOCK_SOURCE[:, None] == BLOCK_SOURCE[None, :])
    return constant(hit)


def expert_kernel(
    x_ref, g_ref, gate_w_ref, up_w_ref, down_w_ref, select_ref, place_ref, high_ref, low_ref,
    y_ref, back_ref, grad_gate_ref, grad_up_ref, grad_down_ref, sum_gate, sum_up, sum_down,
):
    step = pl.program_id(0)

    @pl.when(step == 0)
    def _():
        sum_gate[...] = jnp.zeros_like(sum_gate)
        sum_up[...] = jnp.zeros_like(sum_up)
        sum_down[...] = jnp.zeros_like(sum_down)

    x = x_ref[...]
    g = g_ref[...]
    place = place_ref[...].astype(F32)
    gate = jnp.sum(mm(select_ref[...], x[:, :128]) * place, axis=1, keepdims=True)
    a = mm(x, gate_w_ref[...])
    b = mm(x, up_w_ref[...])
    s = 1.0 / (1.0 + jnp.exp(-a))
    silu = a * s
    hidden = (silu * b).astype(BF16)
    y = mm(hidden, down_w_ref[...]).astype(BF16)
    y_ref[...] = y
    g_wide = g.astype(F32)
    dgate = jnp.sum(y.astype(F32) * g_wide, axis=1, keepdims=True)
    gy = (g_wide * gate).astype(BF16)
    dhidden = mm(gy, down_w_ref[...], NT)
    da = (dhidden * b * (s * (1.0 + a * (1.0 - s)))).astype(BF16)
    db = (dhidden * silu).astype(BF16)
    back = mm(da, gate_w_ref[...], NT) + mm(db, up_w_ref[...], NT)
    dgate_high, dgate_low = halves(dgate * place)
    back_ref[:, 0:128] = (
        back[:, 0:128] + mm(high_ref[...], dgate_high) + mm(low_ref[...], dgate_low)
    ).astype(BF16)
    back_ref[:, 128:1024] = back[:, 128:1024].astype(BF16)
    sum_gate[...] += mm(x, da, TN)
    sum_up[...] += mm(x, db, TN)
    sum_down[...] += mm(hidden, gy, TN)

    @pl.when(step == pl.num_programs(0) - 1)
    def _():
        grad_gate_ref[...] = sum_gate[...].astype(BF16)
        grad_up_ref[...] = sum_up[...].astype(BF16)
        grad_down_ref[...] = sum_down[...].astype(BF16)


def return_kernel(
    back_ref, take_ref, gate_ref, cot_ref, residual_ref, mixed_ref, router_ref, w_out_ref,
    expand_ref, expand_t_ref, place_t_ref, pick_t_ref,
    gmid_ref, branch_ref, gsent_ref, grad_ref,
):
    back = back_ref[...]
    take = take_ref[...]
    rows = mm(pick_t_ref[...], back[:, 0:128])
    rows_high, rows_low = halves(rows)
    spread = mm(rows_high, place_t_ref[...]) + mm(rows_low, place_t_ref[...])
    along = jnp.sum(spread * expand_ref[...].astype(F32), axis=0, keepdims=True)
    found_high, found_low = halves(take.astype(F32) * along)
    dgate = mm(found_high, expand_t_ref[...]) + mm(found_low, expand_t_ref[...])
    gate = gate_ref[...]
    dlogits = gate * (dgate - jnp.sum(gate * dgate, axis=1, keepdims=True))
    dlogits = dlogits.astype(BF16)
    dmixed = mm(take, back) + mm(dlogits, router_ref[...], NT)
    residual = residual_ref[...]
    scale = lax.rsqrt(jnp.mean(residual * residual, axis=-1, keepdims=True) + EPSILON)
    gain = router_ref[...].astype(F32).T[EXPERTS : EXPERTS + 1, :]
    weighted = dmixed * gain
    inner = jnp.mean(weighted * residual, axis=-1, keepdims=True)
    gmid = cot_ref[...].astype(F32) + scale * weighted - residual * (scale * scale * scale) * inner
    gmid_ref[...] = gmid
    branch = gmid.astype(BF16)
    branch_ref[...] = branch
    gsent = mm(branch, w_out_ref[...], NT).astype(BF16)
    for i in range(8):
        gsent_ref[i] = gsent[:, i * 128 : (i + 1) * 128]
    gain_grad = jnp.sum(dmixed * residual * scale, axis=0, keepdims=True)
    grads = mm(dlogits, mixed_ref[...], TN)
    row = lax.broadcasted_iota(jnp.int32, (128, D), 0)
    grads = jnp.where(row == EXPERTS, gain_grad, grads)
    grad_ref[...] = grads.T.astype(BF16)


def finish_kernel(
    dq_ref, dkv_ref, cos_ref, sin_ref, normed_ref, w_ref,
    y_ref, weigh_high_ref, weigh_low_ref, residual_ref, out_ref, side_ref,
    dnormed_out, mixed_out, grads_out, early_out,
    dqkv, part_out, part_in, part_own, line_out, line_in, share_out, share_in, total,
    out_in, side_in, send, recv, local, out_recv,
):
    me = position(AXES)
    x, y, z, c = (me[axis] for axis in AXES)
    mine = y * 4 + z
    alone = jnp.where(c == lax.div(y, 2), 1, 0)
    barrier = pltpu.get_barrier_semaphore()

    def owner(k):
        at = lax.rem(lax.rem(y, 2) * 8 + z * 2 + c + k, 16)
        to = {"y": 2 * c + lax.div(at, 8), "z": lax.rem(lax.div(at, 2), 4), "c": lax.rem(at, 2)}
        return at, to

    def origin(k):
        at = lax.rem(mine + k, 16)
        return at, {"y": lax.div(at, 4), "z": lax.rem(at, 4), "c": lax.div(y, 2)}

    for k in range(1, 16):
        pl.semaphore_signal(barrier, inc=1, device_id=origin(k)[1], device_id_type=MESH)

    @pl.when(alone == 0)
    def _():
        pl.semaphore_signal(barrier, inc=1, device_id=origin(0)[1], device_id_type=MESH)

    offsets = LINE_OFFSETS + PLANE_OFFSETS
    for offset in offsets:
        pl.semaphore_signal(barrier, inc=1, device_id=moved(me, offset), device_id_type=MESH)
    pl.semaphore_wait(barrier, len(offsets) + 16 - alone)
    used = [0]

    def go(src, dst, to):
        item = remote(src, dst, send, recv, used[0], to)
        used[0] += 1
        item.start()
        return item

    other = 1 - c
    low_lanes = lane_index((256, 128)) < 64

    def out_copy(k):
        at, to = owner(k)
        return pltpu.make_async_remote_copy(
            src_ref=out_ref.at[at], dst_ref=out_in.at[mine], send_sem=send.at[used[0] + k],
            recv_sem=out_recv.at[mine], device_id=to, device_id_type=MESH,
        )

    def out_kept():
        return pltpu.make_async_copy(out_ref.at[owner(0)[0]], out_in.at[mine], local.at[1])

    out_copies = [out_copy(k) for k in range(16)]
    used[0] += 16
    out_arrivals = []
    for k in range(16):
        at, to = origin(k)
        out_arrivals.append(
            pltpu.make_async_remote_copy(
                src_ref=out_ref.at[0], dst_ref=out_in.at[at], send_sem=send.at[0],
                recv_sem=out_recv.at[at], device_id=to, device_id_type=MESH,
            )
        )

    @pl.when(alone == 0)
    def _():
        out_copies[0].start()

    @pl.when(alone == 1)
    def _():
        out_kept().start()

    for item in out_copies[1:]:
        item.start()
    early = []
    for offset in PLANE_OFFSETS:
        to = moved(me, offset)
        early.append(go(side_ref.at[to["y"] * 4 + to["z"]], side_in.at[mine], to))
    side_kept = pltpu.make_async_copy(side_ref.at[mine], side_in.at[mine], local.at[2])
    side_kept.start()
    early.append(side_kept)

    def turn_back(first):
        rows = pl.ds(pl.multiple_of(first, 256), 256)
        cos, sin = cos_ref[rows, :], sin_ref[rows, :]
        dq, dkv = dq_ref[rows, :], dkv_ref[rows, :]
        dq = (dq * cos - turned(dq) * sin).astype(BF16)
        dkv = jnp.where(low_lanes, dkv * cos - turned(dkv) * sin, dkv).astype(BF16)
        both = jnp.concatenate([dq, dkv], axis=1)
        dqkv[rows, :] = both
        return mm(both, w_ref[:, 0:256], NT)

    crossing = []
    for i in range(2):
        value = turn_back(other * 512 + i * 256).astype(BF16)
        part_out[2 * i] = value[:ROWS]
        part_out[2 * i + 1] = value[ROWS:]
        span = pl.ds(2 * i, 2)
        crossing.append(go(part_out.at[span], part_in.at[span], {"c": other}))
    for i in range(2):
        value = turn_back(c * 512 + i * 256)
        part_own[2 * i] = value[:ROWS]
        part_own[2 * i + 1] = value[ROWS:]
    for item in crossing:
        item.wait()
    along = []
    for i, by in enumerate((2, 1, 3)):
        to = lax.rem(x + by, 4)
        line_out[i] = (part_own[to] + part_in[to].astype(F32)).astype(BF16)
        along.append(go(line_out.at[i], line_in.at[i], {"x": to}))
    for i in range(4):
        columns = pl.ds(i * 256, 256)
        grad = mm(normed_ref[:, columns], dqkv[...], TN).astype(BF16)
        share_out[i] = grad.reshape(16, 16, 256)
    spread = []
    for offset in PLANE_OFFSETS:
        to = moved(me, offset)
        spread.append(go(share_out.at[:, to["y"] * 4 + to["z"]], share_in.at[mine], to))
    kept = pltpu.make_async_copy(share_out.at[:, mine], share_in.at[mine], local.at[0])
    kept.start()
    mixed = mm(weigh_high_ref[...], y_ref[...]) + mm(weigh_low_ref[...], y_ref[...])
    mixed_out[...] = (residual_ref[...] + mixed).astype(BF16)
    for item in spread + [kept]:
        item.wait()
    for i in range(4):
        value = share_in[0, i].astype(F32)
        for j in range(1, 16):
            value += share_in[j, i].astype(F32)
        total[i] = value.reshape(2, 8, 256)
    ends = []
    here = x * 2 + c
    for offset in LINE_OFFSETS:
        to = moved(me, offset)
        ends.append(go(total.at[to["x"], to["c"]], grads_out.at[here], to))
    kept = pltpu.make_async_copy(total.at[x, c], grads_out.at[here], local.at[0])
    kept.start()
    for item in out_copies[1:]:
        item.wait_send()
    for item in out_arrivals[1:]:
        item.wait_recv()

    @pl.when(alone == 0)
    def _():
        out_copies[0].wait_send()
        out_arrivals[0].wait_recv()

    @pl.when(alone == 1)
    def _():
        out_kept().wait()

    for item in early:
        item.wait()
    out_total, side_total = out_in[0], side_in[0]
    for j in range(1, 16):
        out_total += out_in[j]
        side_total += side_in[j]
    early_out[:, 0:D] = out_total
    early_out[:, D : D + 128] = side_total
    for item in along:
        item.wait()
    dnormed = part_own[x] + part_in[x].astype(F32)
    for i in range(3):
        dnormed += line_in[i].astype(F32)
    dnormed_out[...] = dnormed
    for item in ends + [kept]:
        item.wait()


def finish(inputs, cid):
    count = 2 + 3 + 15 + 7 + 16 + 15
    return pl.pallas_call(
        finish_kernel,
        out_shape=[
            jax.ShapeDtypeStruct((ROWS, D), F32),
            jax.ShapeDtypeStruct((ROWS, D), BF16),
            jax.ShapeDtypeStruct((8, 8, 256), F32),
            jax.ShapeDtypeStruct((8, D + 128), F32),
        ],
        in_specs=[pl.BlockSpec(memory_space=pltpu.VMEM)] * 12,
        out_specs=[pl.BlockSpec(memory_space=pltpu.VMEM)] * 4,
        scratch_shapes=[
            pltpu.VMEM((CHIP_ROWS, 256), BF16),
            pltpu.VMEM((4, ROWS, D), BF16),
            pltpu.VMEM((4, ROWS, D), BF16),
            pltpu.VMEM((4, ROWS, D), F32),
            pltpu.VMEM((3, ROWS, D), BF16),
            pltpu.VMEM((3, ROWS, D), BF16),
            pltpu.VMEM((4, 16, 16, 256), BF16),
            pltpu.VMEM((16, 4, 16, 256), BF16),
            pltpu.VMEM((4, 2, 8, 256), F32),
            pltpu.VMEM((16, 8, D), F32),
            pltpu.VMEM((16, 8, 128), F32),
            pltpu.SemaphoreType.DMA((count,)),
            pltpu.SemaphoreType.DMA((count,)),
            pltpu.SemaphoreType.DMA((3,)),
            pltpu.SemaphoreType.DMA((16,)),
        ],
        compiler_params=pltpu.CompilerParams(
            collective_id=cid, has_side_effects=True, vmem_limit_bytes=VMEM_BYTES
        ),
    )(*inputs)


def last_kernel(
    dnormed_ref, tok_ref, gain_ref, gmid_ref, mixed_ref, rows_ref, w_ref, own_gain_ref, early_ref,
    gate_ref, up_ref, down_ref,
    tokens_out, mixed_out, query_out, key_out, value_out, gains_out, grad_out, router_out,
    gate_out, up_out, down_out,
):
    tok = tok_ref[...].astype(F32)
    scale = lax.rsqrt(jnp.mean(tok * tok, axis=-1, keepdims=True) + EPSILON)
    weighted = dnormed_ref[...] * gain_ref[...]
    inner = jnp.mean(weighted * tok, axis=-1, keepdims=True)
    tokens_out[...] = gmid_ref[...] + scale * weighted - tok * (scale * scale * scale) * inner
    mixed_out[...] = mixed_ref[...]
    total = jnp.zeros((8, 256), F32)
    for i in range(8):
        rows = rows_ref[i]
        query_out[:, i * 128 : (i + 1) * 128] = rows[:, :128]
        total += rows * w_ref[:, i * 256 : (i + 1) * 256].astype(F32)
    lanes = lane_index((8, 128)) < 64
    for i in range(4):
        first, second = rows_ref[2 * i][:, 128:], rows_ref[2 * i + 1][:, 128:]
        key_out[:, i * 128 : (i + 1) * 128] = jnp.where(lanes, first, pltpu.roll(second, 64, axis=1))
        value_out[:, i * 128 : (i + 1) * 128] = jnp.where(lanes, pltpu.roll(first, 64, axis=1), second)
    gain_one = jnp.broadcast_to(jnp.sum(total, axis=1, keepdims=True), (8, 128)).T[0:1, :]
    side = early_ref[:, D : D + 128]
    gain_two = side.T[EXPERTS : EXPERTS + 1, :]
    gains_out[0:1, :] = gain_one[:, 0:8] / own_gain_ref[...]
    gains_out[1:2, :] = gain_two[:, 0:8]
    grad_out[...] = early_ref[:, 0:D]
    router_out[...] = side[:, 0:EXPERTS]
    gate_out[...] = gate_ref[...].astype(F32)
    up_out[...] = up_ref[...].astype(F32)
    down_out[...] = down_ref[...].astype(F32)


WHOLE = pl.BlockSpec(memory_space=pltpu.VMEM)
OUT_BLOCK = pl.BlockSpec((D, D), lambda i: (0, 0))
SIDE_BLOCK = pl.BlockSpec((D, 128), lambda i: (0, 8))


def shape(dims, dtype):
    return jax.ShapeDtypeStruct(dims, dtype)


def rotation_tables(order, lengths):
    ends = jnp.cumsum(lengths)
    passed = ends[None, :] <= order[:, None]
    position = order - jnp.sum(jnp.where(passed, lengths[None, :], 0), axis=1)
    frequency = ROPE_BASE ** (-jnp.arange(32, dtype=F32) / 32)
    angles = position.astype(F32)[:, None] * jnp.tile(frequency, 4)[None, :]
    return jnp.cos(angles), jnp.sin(angles)


def body(
    tokens,
    gain_one,
    w_query,
    w_key,
    w_value,
    w_out,
    gain_two,
    w_router,
    w_gate,
    w_up,
    w_down,
    dealt_order,
    lengths,
    routes,
    cotangent,
):
    x_at, y_at, z_at, c_at = (lax.axis_index(axis) for axis in AXES)
    chip = y_at * 4 + z_at
    first_row = chip * CHIP_ROWS

    grouped = jnp.concatenate(
        [
            w_query.reshape(8, 8, 128),
            w_key.reshape(8, 8, 64),
            w_value.reshape(8, 8, 64),
        ],
        axis=2,
    )
    gain_lane = jnp.where(jnp.arange(128)[None, :] == 0, gain_one[:, None], 0).astype(BF16)
    first_pack = jnp.concatenate(
        [grouped.transpose(1, 0, 2), jnp.broadcast_to(gain_lane[None], (8, 8, 128))], axis=2
    )
    token_rows, w_mine = start_rows(tokens, first_pack, 10)
    second_pack = jnp.concatenate(
        [w_out, w_router, gain_two[:, None], jnp.zeros((8, 95), BF16)], axis=1
    )
    second_pack, token_rows = lax.optimization_barrier((second_pack, token_rows))
    w_late = lax.all_gather(second_pack, AXES, axis=0, tiled=True)

    order_own = lax.dynamic_slice_in_dim(dealt_order, first_row, CHIP_ROWS)
    cos, sin = rotation_tables(order_own, lengths)
    ends = jnp.cumsum(lengths)
    within = (dealt_order[None, :] < ends[:, None]) & (
        dealt_order[None, :] >= (ends - lengths)[:, None]
    )
    aux_t = jnp.concatenate([jnp.ones((3, TOKENS), BF16), within.astype(BF16)], axis=0)
    aux = mm(aux_t, jnp.eye(8, 128, dtype=BF16), TN).astype(BF16)
    own_aux = lax.dynamic_slice_in_dim(aux, first_row, CHIP_ROWS)
    order_rows = order_own.astype(F32).reshape(4, RUN)
    run_of = dealt_order.reshape(32, 512)[:, 0] // RUN
    block_ids = jnp.arange(32, dtype=jnp.int32)
    block_of = jnp.sum(
        jnp.where(run_of[None, :] == block_ids[:, None], block_ids[None, :], 0), axis=1
    )
    first_rows = jnp.concatenate([block_of * 512, block_of[::-1] * 512 + RUN])
    mine = lax.dynamic_slice_in_dim(run_of, chip * 2, 2)
    counts = jnp.stack([mine[0], 31 - mine[0], mine[1], 31 - mine[1]])
    base = first_row.reshape(1).astype(jnp.int32)

    expand, expand_t = expand_matrix(), expand_matrix().T
    place, place_t = place_matrix(), place_matrix().T
    pick_high, pick_low = pick_matrix(CAP), pick_matrix(CAP + 1)
    member, put, take, g_out = local_call(
        prepare_kernel,
        (
            shape((ROWS, 128), F32),
            shape((SLOTS, ROWS), BF16),
            shape((ROWS, SLOTS), BF16),
            shape((SLOTS, D), BF16),
        ),
    )(routes, cotangent, expand, expand_t, place_column(), place_row())
    plane = ("y", "z", "c")

    normed, query, kv, gain_first = local_call(
        project_kernel,
        (
            shape((CHIP_ROWS, D), BF16),
            shape((2, CHIP_ROWS, 128), BF16),
            shape((CHIP_ROWS, 128), BF16),
            shape((1, D), F32),
        ),
    )(token_rows, w_mine, cos, sin)
    kv_all = gather_plane(kv, 1)
    g_out, kv_all = lax.optimization_barrier((g_out, kv_all))
    g_in = lax.all_to_all(
        g_out.reshape(EXPERTS, SLOT, D), plane, split_axis=0, concat_axis=0, tiled=True
    ).reshape(SLOTS, D)
    smem = pl.BlockSpec(memory_space=pltpu.SMEM)
    vmem = pl.BlockSpec(memory_space=pltpu.VMEM)
    att, norm, sent, query_ext = local_call(
        attend_kernel,
        (
            shape((CHIP_ROWS, 128), F32),
            shape((CHIP_ROWS, 128), F32),
            shape((CHIP_ROWS, 128), BF16),
            shape((4, 2 * RUN, 256), BF16),
        ),
        scratch=[pltpu.VMEM((2 * RUN, 128), F32)],
        in_specs=[smem] * 2 + [vmem] * 6,
        flops=2 * 66 * 512 * 256 * 512,
        moved=10 << 20,
    )(first_rows, counts, kv_all, aux, kv, own_aux, query, order_rows)
    sent_tok = exchange(
        sent.reshape(8, ROWS, 128), ("x", "c"), 2, dest_order=("c", "x"), src_order=("x", "c")
    )

    residual, mixed_in, gate, outgoing, weigh_high, weigh_low = local_call(
        middle_kernel,
        (
            shape((ROWS, D), F32),
            shape((ROWS, D), BF16),
            shape((ROWS, 128), F32),
            shape((SLOTS, D), BF16),
            shape((ROWS, SLOTS), BF16),
            shape((ROWS, SLOTS), BF16),
        ),
        grid=(1,),
        in_specs=[WHOLE] * 2 + [OUT_BLOCK, SIDE_BLOCK] + [WHOLE] * 7,
        out_specs=[WHOLE] * 6,
    )(
        sent_tok, tokens, w_late, w_late, member, put, take, expand, place,
        pick_high, pick_low,
    )
    arrived = exchange(outgoing.reshape(EXPERTS, SLOT, D), plane, 3).reshape(SLOTS, D)
    row_block = pl.BlockSpec((BLOCK, D), lambda i: (i, 0))

    def fixed(dims):
        return pl.BlockSpec(dims, lambda i: (0,) * len(dims))

    y_out, back_out, grad_gate, grad_up, grad_down = local_call(
        expert_kernel,
        (
            shape((SLOTS, D), BF16),
            shape((SLOTS, D), BF16),
            shape((D, FF), BF16),
            shape((D, FF), BF16),
            shape((FF, D), BF16),
        ),
        scratch=[pltpu.VMEM((D, FF), F32), pltpu.VMEM((D, FF), F32), pltpu.VMEM((FF, D), F32)],
        grid=(SLOTS // BLOCK,),
        in_specs=[
            row_block,
            row_block,
            fixed((D, FF)),
            fixed((D, FF)),
            fixed((FF, D)),
            fixed((BLOCK, BLOCK)),
            fixed((BLOCK, 128)),
            fixed((BLOCK, BLOCK)),
            fixed((BLOCK, BLOCK)),
        ],
        out_specs=[row_block, row_block, fixed((D, FF)), fixed((D, FF)), fixed((FF, D))],
    )(
        arrived,
        g_in,
        w_gate[0],
        w_up[0],
        w_down[0],
        block_matrix((CAP, CAP + 1)),
        place[:BLOCK],
        block_matrix((CAP,)).T * constant(BLOCK_PLACE == CAP)[:, None],
        block_matrix((CAP + 1,)).T * constant(BLOCK_PLACE == CAP + 1)[:, None],
    )
    returned = exchange(back_out.reshape(EXPERTS, SLOT, D), plane, 4).reshape(SLOTS, D)
    y_in = lax.all_to_all(
        y_out.reshape(EXPERTS, SLOT, D), plane, split_axis=0, concat_axis=0, tiled=True
    ).reshape(SLOTS, D)
    grad_gate, grad_up, grad_down = (
        lax.psum_scatter(grad, "x", scatter_dimension=0, tiled=True)
        for grad in (grad_gate, grad_up, grad_down)
    )

    gmid, branch, gsent, side_grad = local_call(
        return_kernel,
        (
            shape((ROWS, D), F32),
            shape((ROWS, D), BF16),
            shape((8, ROWS, 128), BF16),
            shape((D, 128), BF16),
        ),
        grid=(1,),
        in_specs=[WHOLE] * 6 + [SIDE_BLOCK, OUT_BLOCK] + [WHOLE] * 4,
        out_specs=[WHOLE] * 4,
    )(
        returned, take, gate, cotangent, residual, mixed_in, w_late, w_late,
        expand, expand_t, place_t, (pick_high + pick_low).T,
    )
    side_rows = side_grad.reshape(4, 16, 2, 8, 128).transpose(0, 2, 1, 3, 4).reshape(8, ROWS, 128)
    gsent_own, side_rows = exchange(
        [gsent, side_rows], ("x", "c"), 5, dest_order=("x", "c"), src_order=("c", "x")
    )
    gsent_own = gsent_own.reshape(CHIP_ROWS, 128)
    branch_rows = lax.all_gather(branch, ("c", "x"), axis=0, tiled=True)
    side_sum = jnp.sum(side_rows.astype(F32), axis=0)

    dq, dkv = local_call(
        attend_back_kernel,
        (shape((CHIP_ROWS, 128), F32), shape((TOKENS, 128), BF16)),
        scratch=[
            pltpu.VMEM((TOKENS, 128), F32),
            pltpu.VMEM((64, 2 * RUN), F32),
            pltpu.VMEM((2 * RUN, 256), BF16),
            pltpu.VMEM((4 * RUN, 128), BF16),
        ],
        in_specs=[smem] * 3 + [vmem] * 9,
        flops=5 * 66 * 512 * 256 * 512,
        moved=20 << 20,
    )(
        first_rows, counts, base, kv_all, aux, kv, own_aux, query_ext, order_rows, gsent_own, att,
        norm,
    )
    dkv_own, grad_out = scatter_plane(dkv, sent, branch_rows, 6)

    dnormed, mixed, qkv_rows, early = finish(
        (
            dq, dkv_own, cos, sin, normed, w_mine, y_in, weigh_high, weigh_low, residual,
            grad_out.reshape(16, 8, D), side_sum.reshape(16, 8, 128),
        ),
        7,
    )
    (
        grad_tokens, mixed, grad_query, grad_key, grad_value, gains, grad_out_rows, grad_router,
        grad_gate, grad_up, grad_down,
    ) = local_call(
        last_kernel,
        (
            shape((ROWS, D), F32),
            shape((ROWS, D), BF16),
            shape((8, D), F32),
            shape((8, 512), F32),
            shape((8, 512), F32),
            shape((2, 8), F32),
            shape((8, D), F32),
            shape((8, EXPERTS), F32),
            shape((256, FF), F32),
            shape((256, FF), F32),
            shape((128, D), F32),
        ),
    )(
        dnormed, tokens, gain_first, gmid, mixed, qkv_rows, grouped.reshape(8, 2048),
        gain_one.astype(F32).reshape(1, 8), early, grad_gate, grad_up, grad_down,
    )
    grad_gain_one, grad_gain_two = gains[0], gains[1]
    grad_gate, grad_up, grad_down = grad_gate[None], grad_up[None], grad_down[None]
    return (
        mixed,
        grad_tokens,
        grad_gain_one,
        grad_query,
        grad_key,
        grad_value,
        grad_out_rows,
        grad_gain_two,
        grad_router,
        grad_gate,
        grad_up,
        grad_down,
    )


def solution(mesh):
    grid = Mesh(mesh.devices.reshape(4, 4, 4, 2), AXES)
    rows = P(("y", "z", "c", "x"), None)
    vector = P(AXES)
    matrix = P(AXES, None)
    expert = P(("y", "z", "c"), None, None)
    in_specs = (
        rows, vector, matrix, matrix, matrix, matrix, vector, matrix, expert, expert, expert,
        P(), P(), rows, rows,
    )
    grads = P(("y", "z", "c"), "x", None)
    out_specs = (
        rows, rows, vector, matrix, matrix, matrix, matrix, vector, matrix, grads, grads, grads,
    )
    return jax.shard_map(body, mesh=grid, in_specs=in_specs, out_specs=out_specs, check_vma=False)
```

```python
import functools
import math

import jax
import jax.numpy as jnp
import ml_dtypes
import numpy as np
from jax import lax
from jax.experimental import pallas as pl
from jax.experimental.pallas import tpu as pltpu
from jax.sharding import Mesh
from jax.sharding import PartitionSpec as P

D = 1024
HEADS = 16
KV_HEADS = 8
HEAD_DIM = 64
EXPERTS = 32
FF = 512
CAP = 36
SLOT = 40
SLOTS = EXPERTS * SLOT
ROWS = 128
CHIP_ROWS = 1024
RUN = 256
TOKENS = 16384
NSEQ = 5
EPSILON = 1e-06
ROPE_BASE = 10000.0
FAR = float(2.0**100)
SIZE = {"x": 4, "y": 4, "z": 4, "c": 2}
AXES = ("x", "y", "z", "c")
MESH = pl.DeviceIdType.MESH
BF16 = jnp.bfloat16
F32 = jnp.float32
NN = (((1,), (0,)), ((), ()))
NT = (((1,), (1,)), ((), ()))
TN = (((0,), (0,)), ((), ()))
VMEM_BYTES = 56 * 1024 * 1024


def mm(a, b, dims=NN):
    return lax.dot_general(a, b, dims, preferred_element_type=F32)


def halves(value):
    high = value.astype(BF16)
    return high, (value - high.astype(F32)).astype(BF16)


def local_call(kernel, outs, scratch=(), grid=None, in_specs=None, out_specs=None):
    extra = {}
    if grid is not None:
        extra = {"grid": grid, "in_specs": in_specs, "out_specs": out_specs}
    elif in_specs is not None:
        extra = {"in_specs": in_specs}
    return pl.pallas_call(
        kernel,
        out_shape=outs,
        scratch_shapes=list(scratch),
        compiler_params=pltpu.CompilerParams(vmem_limit_bytes=VMEM_BYTES),
        **extra,
    )


def flat_index(coords, order):
    index = 0
    for axis in order:
        index = index * SIZE[axis] + coords[axis]
    return index


PLANE_ORDER = (
    (2, 2), (2, 3), (2, 1), (3, 2), (1, 2), (0, 2), (2, 0), (3, 1), (1, 3),
    (3, 3), (1, 1), (0, 3), (0, 1), (3, 0), (1, 0), (0, 0),
)
PLANE_OFFSETS = tuple({"y": dy, "z": dz} for dy, dz in PLANE_ORDER[:-1])
SPREAD_OFFSETS = tuple(
    {"y": dy, "z": dz, "c": (dc + i + 1) % 2}
    for i, (dy, dz) in enumerate(PLANE_ORDER)
    for dc in range(2)
    if (dy, dz, (dc + i + 1) % 2) != (0, 0, 0)
)
LINE_OFFSETS = tuple(
    {"x": dx, "c": dc} for dx, dc in ((2, 0), (2, 1), (1, 0), (3, 0), (1, 1), (3, 1), (0, 1))
)
OFFSETS = {("y", "z"): PLANE_OFFSETS, ("y", "z", "c"): SPREAD_OFFSETS, ("x", "c"): LINE_OFFSETS}


def position(axes):
    return {axis: lax.axis_index(axis) for axis in axes}


def moved(me, offset):
    return {axis: lax.rem(me[axis] + by, SIZE[axis]) if by else me[axis] for axis, by in offset.items()}


def greet(me, offsets):
    barrier = pltpu.get_barrier_semaphore()
    for offset in offsets:
        pl.semaphore_signal(barrier, inc=1, device_id=moved(me, offset), device_id_type=MESH)
    pl.semaphore_wait(barrier, len(offsets))


def remote(src, dst, send, recv, slot, to):
    return pltpu.make_async_remote_copy(
        src_ref=src,
        dst_ref=dst,
        send_sem=send.at[slot],
        recv_sem=recv.at[slot],
        device_id=to,
        device_id_type=MESH,
    )


def exchange_kernel(axes, dest_order, src_order, arrays, *refs):
    x_refs, o_refs = refs[:arrays], refs[arrays : 2 * arrays]
    send, recv, local = refs[2 * arrays :]
    me = position(axes)
    offsets = OFFSETS[axes]
    greet(me, offsets)
    here = flat_index(me, src_order)
    copies = []
    for offset in offsets:
        to = moved(me, offset)
        for x_ref, o_ref in zip(x_refs, o_refs):
            copies.append(
                remote(
                    x_ref.at[flat_index(to, dest_order)], o_ref.at[here], send, recv, len(copies), to
                )
            )
            copies[-1].start()
    kept = [
        pltpu.make_async_copy(
            x_ref.at[flat_index(me, dest_order)], o_ref.at[here], local.at[i]
        )
        for i, (x_ref, o_ref) in enumerate(zip(x_refs, o_refs))
    ]
    for item in kept:
        item.start()
    for item in kept + copies:
        item.wait()


def exchange(data, axes, cid, dest_order=None, src_order=None):
    single = not isinstance(data, (tuple, list))
    data = [data] if single else list(data)
    dest_order = dest_order or axes
    src_order = src_order or axes
    arrays = len(data)
    count = len(OFFSETS[axes]) * arrays
    out = pl.pallas_call(
        functools.partial(exchange_kernel, axes, dest_order, src_order, arrays),
        out_shape=[jax.ShapeDtypeStruct(item.shape, item.dtype) for item in data],
        in_specs=[pl.BlockSpec(memory_space=pl.ANY)] * arrays,
        out_specs=[pl.BlockSpec(memory_space=pl.ANY)] * arrays,
        scratch_shapes=[
            pltpu.SemaphoreType.DMA((count,)),
            pltpu.SemaphoreType.DMA((count,)),
            pltpu.SemaphoreType.DMA((arrays,)),
        ],
        compiler_params=pltpu.CompilerParams(collective_id=cid, has_side_effects=True),
    )(*data)
    return out[0] if single else out


def start_kernel(tok_ref, w_ref, o_tok, o_w, send, recv, local):
    me = position(AXES)
    x, y, z, c = (me[axis] for axis in AXES)
    offsets = LINE_OFFSETS + PLANE_OFFSETS
    greet(me, offsets)
    plus, minus, far = lax.rem(x + 1, 4), lax.rem(x + 3, 4), lax.rem(x + 2, 4)
    other = 1 - c
    lower, upper = pl.ds(0, 64), pl.ds(64, 64)
    used = [0]

    def go(src, dst, to):
        item = remote(src, dst, send, recv, used[0], to)
        used[0] += 1
        item.start()
        return item

    own_tok = pltpu.make_async_copy(tok_ref, o_tok.at[c, x], local.at[0])
    own_w = pltpu.make_async_copy(w_ref.at[x * 2 + c], o_w.at[x, y, z, c], local.at[1])
    own_tok.start()
    own_w.start()
    first_w = []
    for offset in LINE_OFFSETS:
        to = moved(me, offset)
        first_w.append(go(w_ref.at[to["x"] * 2 + to["c"]], o_w.at[x, y, z, c], to))
    to_plus = go(tok_ref, o_tok.at[c, x], {"x": plus})
    to_minus = go(tok_ref, o_tok.at[c, x], {"x": minus})
    sides = [go(tok_ref, o_tok.at[c, x], {"c": other})]
    own_w.wait()
    for item in first_w:
        item.wait()
    second_w = [
        go(o_w.at[:, y, z], o_w.at[:, y, z], moved(me, offset)) for offset in PLANE_OFFSETS
    ]
    to_plus.wait()
    next_plus = go(o_tok.at[c, minus, lower], o_tok.at[c, minus, lower], {"x": plus})
    sides.append(go(o_tok.at[c, minus], o_tok.at[c, minus], {"c": other}))
    to_minus.wait()
    next_minus = go(o_tok.at[c, plus, upper], o_tok.at[c, plus, upper], {"x": minus})
    sides.append(go(o_tok.at[c, plus], o_tok.at[c, plus], {"c": other}))
    next_plus.wait()
    next_minus.wait()
    sides.append(go(o_tok.at[c, far], o_tok.at[c, far], {"c": other}))
    for item in sides + second_w + [own_tok]:
        item.wait()


def start_rows(tokens, packed, cid):
    count = 3 + 7 + 15 + 2 + 3
    rows, weights = pl.pallas_call(
        start_kernel,
        out_shape=[
            jax.ShapeDtypeStruct((2, 4, ROWS, D), BF16),
            jax.ShapeDtypeStruct((4, 4, 4, 2, 8, 384), BF16),
        ],
        in_specs=[pl.BlockSpec(memory_space=pl.ANY)] * 2,
        out_specs=[pl.BlockSpec(memory_space=pl.ANY)] * 2,
        scratch_shapes=[
            pltpu.SemaphoreType.DMA((count,)),
            pltpu.SemaphoreType.DMA((count,)),
            pltpu.SemaphoreType.DMA((2,)),
        ],
        compiler_params=pltpu.CompilerParams(collective_id=cid, has_side_effects=True),
    )(tokens, packed)
    return rows.reshape(CHIP_ROWS, D), weights.reshape(D, 384)


AROUND = ({"y": 1, "z": 0}, {"y": 3, "z": 0}, {"y": 0, "z": 1}, {"y": 0, "z": 3})


def gather_plane_kernel(x_ref, o_ref, send, recv, local):
    me = position(("y", "z"))
    y, z = me["y"], me["z"]
    greet(me, AROUND)
    own = pltpu.make_async_copy(x_ref, o_ref.at[y, z], local)
    own.start()
    half = x_ref.shape[1] // 2
    lower, upper = pl.ds(0, half), pl.ds(half, half)
    used = [0]

    def go(src, dst, to):
        item = remote(src, dst, send, recv, used[0], to)
        used[0] += 1
        item.start()
        return item

    def place(t, a, b):
        return o_ref.at[a, b, 0] if t == 0 else o_ref.at[b, a, 1]

    axis = (("y", "z"), ("z", "y"))
    here = tuple((me[a], me[b]) for a, b in axis)
    step = {"plus": 1, "minus": 3, "far": 2, "own": 0}

    def at(t, which, name):
        return lax.rem(here[t][which] + step[name], 4)

    def send_second(t, src, name):
        dst = place(t, at(t, 0, name), here[t][1])
        src = dst if src is None else src
        return (
            go(src, dst, {axis[t][1]: at(t, 1, "plus")}),
            go(src, dst, {axis[t][1]: at(t, 1, "minus")}),
        )

    def pass_on(t, which, a_name, b_name, part, direction):
        ref = place(t, at(t, 0, a_name), at(t, 1, b_name)).at[part]
        return go(ref, ref, {axis[t][which]: at(t, which, direction)})

    def forward_second(t, name, pair):
        pair[0].wait()
        a = pass_on(t, 1, name, "minus", lower, "plus")
        pair[1].wait()
        b = pass_on(t, 1, name, "plus", upper, "minus")
        return [a, b]

    first, second, last = {}, {}, []
    for t in (0, 1):
        dst = place(t, *here[t])
        first[t] = (
            go(x_ref.at[t], dst, {axis[t][0]: at(t, 0, "plus")}),
            go(x_ref.at[t], dst, {axis[t][0]: at(t, 0, "minus")}),
        )
    for t in (0, 1):
        second[t, "own"] = send_second(t, x_ref.at[t], "own")
    far = {}
    for t in (0, 1):
        first[t][0].wait()
        a = pass_on(t, 0, "minus", "own", lower, "plus")
        second[t, "minus"] = send_second(t, None, "minus")
        first[t][1].wait()
        b = pass_on(t, 0, "plus", "own", upper, "minus")
        second[t, "plus"] = send_second(t, None, "plus")
        far[t] = (a, b)
    for t in (0, 1):
        last += forward_second(t, "own", second[t, "own"])
    for t in (0, 1):
        far[t][0].wait()
        far[t][1].wait()
        second[t, "far"] = send_second(t, None, "far")
    for name in ("minus", "plus", "far"):
        for t in (0, 1):
            last += forward_second(t, name, second[t, name])
    for item in last + [own]:
        item.wait()


def gather_plane(data, cid):
    rows = data.shape[0] // 2
    out = pl.pallas_call(
        gather_plane_kernel,
        out_shape=jax.ShapeDtypeStruct((4, 4, 2, rows, 128), data.dtype),
        in_specs=[pl.BlockSpec(memory_space=pl.ANY)],
        out_specs=pl.BlockSpec(memory_space=pl.ANY),
        scratch_shapes=[
            pltpu.SemaphoreType.DMA((40,)),
            pltpu.SemaphoreType.DMA((40,)),
            pltpu.SemaphoreType.DMA,
        ],
        compiler_params=pltpu.CompilerParams(collective_id=cid, has_side_effects=True),
    )(data.reshape(2, rows, 128))
    return out.reshape(32 * rows, 128)


def scatter_plane_kernel(p_ref, sent_ref, branch_ref, o_ref, grad_ref, far_a, near_a, out_a, sum_a, far_b, near_b, out_b, send, recv):
    me = position(("y", "z"))
    greet(me, AROUND)
    half = p_ref.shape[3] // 2
    lower, upper = pl.ds(0, half), pl.ds(half, half)
    axis = (("y", "z"), ("z", "y"))
    used = [0]

    def go(src, dst, t, which, by):
        to = {axis[t][which]: lax.rem(me[axis[t][which]] + by, 4)}
        item = remote(src, dst, send, recv, used[0], to)
        used[0] += 1
        item.start()
        return item

    def part(t, first, second):
        a = lax.rem(me[axis[t][0]] + first, 4)
        b = lax.rem(me[axis[t][1]] + second, 4)
        return p_ref.at[a, b, 0] if t == 0 else p_ref.at[b, a, 1]

    turns = (2, 1, 3, 0)
    both = (0, 1)
    far, near = {}, {}
    for k, by in enumerate(turns):
        for t in both:
            far[k, t] = (
                go(part(t, 2, by).at[lower], far_a.at[t, k, 0], t, 0, 1),
                go(part(t, 2, by).at[upper], far_a.at[t, k, 1], t, 0, 3),
            )
    grad_ref[...] = mm(sent_ref[...], branch_ref[...], TN)
    for k, by in enumerate(turns):
        for t in both:
            ahead, behind = part(t, 1, by), part(t, 3, by)
            far[k, t][0].wait()
            out_a[t, k, 0, 0:half] = (ahead[0:half].astype(F32) + far_a[t, k, 0].astype(F32)).astype(BF16)
            out_a[t, k, 0, half : 2 * half] = ahead[half : 2 * half]
            first = go(out_a.at[t, k, 0], near_a.at[t, k, 0], t, 0, 1)
            far[k, t][1].wait()
            out_a[t, k, 1, 0:half] = behind[0:half]
            out_a[t, k, 1, half : 2 * half] = (
                behind[half : 2 * half].astype(F32) + far_a[t, k, 1].astype(F32)
            ).astype(BF16)
            near[k, t] = (first, go(out_a.at[t, k, 1], near_a.at[t, k, 1], t, 0, 3))

    def summed(k, t):
        near[k, t][0].wait()
        near[k, t][1].wait()
        return (
            part(t, 0, turns[k])[...].astype(F32)
            + near_a[t, k, 0].astype(F32)
            + near_a[t, k, 1].astype(F32)
        )

    far_two, near_two = {}, {}
    for t in both:
        value = summed(0, t).astype(BF16)
        out_b[t, 0] = value
        far_two[t] = (
            go(out_b.at[t, 0, lower], far_b.at[t, 0], t, 1, 1),
            go(out_b.at[t, 0, upper], far_b.at[t, 1], t, 1, 3),
        )
    for k in (1, 2):
        for t in both:
            sum_a[t, k - 1] = summed(k, t)
    for t in both:
        far_two[t][0].wait()
        out_b[t, 1, 0:half] = (sum_a[t, 0, 0:half] + far_b[t, 0].astype(F32)).astype(BF16)
        out_b[t, 1, half : 2 * half] = sum_a[t, 0, half : 2 * half].astype(BF16)
        first = go(out_b.at[t, 1], near_b.at[t, 0], t, 1, 1)
        far_two[t][1].wait()
        out_b[t, 2, 0:half] = sum_a[t, 1, 0:half].astype(BF16)
        out_b[t, 2, half : 2 * half] = (
            sum_a[t, 1, half : 2 * half] + far_b[t, 1].astype(F32)
        ).astype(BF16)
        near_two[t] = (first, go(out_b.at[t, 2], near_b.at[t, 1], t, 1, 3))
    for t in both:
        value = summed(3, t)
        near_two[t][0].wait()
        near_two[t][1].wait()
        o_ref[t] = value + near_b[t, 0].astype(F32) + near_b[t, 1].astype(F32)


def scatter_plane(data, sent, branch_rows, cid):
    rows = data.shape[0] // 32
    whole = pl.BlockSpec(memory_space=pltpu.VMEM)
    out, grad_out = pl.pallas_call(
        scatter_plane_kernel,
        out_shape=[
            jax.ShapeDtypeStruct((2, rows, 128), F32),
            jax.ShapeDtypeStruct((ROWS, D), F32),
        ],
        in_specs=[whole] * 3,
        out_specs=[whole] * 2,
        scratch_shapes=[
            pltpu.VMEM((2, 4, 2, rows // 2, 128), BF16),
            pltpu.VMEM((2, 4, 2, rows, 128), BF16),
            pltpu.VMEM((2, 4, 2, rows, 128), BF16),
            pltpu.VMEM((2, 2, rows, 128), F32),
            pltpu.VMEM((2, 2, rows // 2, 128), BF16),
            pltpu.VMEM((2, 2, rows, 128), BF16),
            pltpu.VMEM((2, 3, rows, 128), BF16),
            pltpu.SemaphoreType.DMA((40,)),
            pltpu.SemaphoreType.DMA((40,)),
        ],
        compiler_params=pltpu.CompilerParams(
            collective_id=cid, has_side_effects=True, vmem_limit_bytes=VMEM_BYTES
        ),
    )(data.reshape(4, 4, 2, rows, 128), sent, branch_rows)
    return out.reshape(2 * rows, 128), grad_out


def lane_index(shape):
    return lax.broadcasted_iota(jnp.int32, shape, 1)


def turned(values):
    lane = lane_index(values.shape)
    up = pltpu.roll(values, 32, axis=1)
    down = pltpu.roll(values, 96, axis=1)
    return jnp.where(lane % 64 < 32, -down, up)


def project_kernel(tok_ref, w_ref, cos_ref, sin_ref, normed_ref, q_ref, kv_ref, gain_ref):
    gain = w_ref[:, 256:384].astype(F32).T[0:1, :]
    gain_ref[...] = gain
    for part in range(4):
        rows = pl.ds(part * 256, 256)
        tok = tok_ref[rows, :].astype(F32)
        scale = lax.rsqrt(jnp.mean(tok * tok, axis=-1, keepdims=True) + EPSILON)
        normed = (tok * scale * gain).astype(BF16)
        normed_ref[rows, :] = normed
        pre = mm(normed, w_ref[:, 0:256])
        cos, sin = cos_ref[rows, :], sin_ref[rows, :]
        low_lanes = lane_index((256, 128)) < 64
        q_pre, kv_pre = pre[:, :128], pre[:, 128:]
        query = (q_pre * cos + turned(q_pre) * sin).astype(BF16).astype(F32) * 0.125
        q_ref[0, rows, :] = jnp.where(low_lanes, query, 0.0).astype(BF16)
        q_ref[1, rows, :] = jnp.where(low_lanes, pltpu.roll(query, 64, axis=1), 0.0).astype(BF16)
        key = kv_pre * cos + turned(kv_pre) * sin
        kv_ref[rows, :] = jnp.where(low_lanes, key, kv_pre).astype(BF16)


def order_pair(order_ref, index):
    row = jnp.broadcast_to(order_ref[index : index + 1, :], (RUN, RUN))
    return row, row.T


def attend_kernel(
    first_ref, count_ref, kv_ref, aux_ref, own_kv_ref, own_aux_ref, q_ref, order_ref,
    att_ref, norm_ref, sent_ref, qx_ref, acc_ref,
):
    def largest(step, best):
        tile = kv_ref[pl.ds(pl.multiple_of(step * 512, 512), 512), :].astype(F32)
        square = jnp.sum(jnp.where(lane_index((512, 128)) < 64, tile * tile, 0.0), axis=1, keepdims=True)
        return jnp.maximum(best, square)

    best = lax.fori_loop(0, TOKENS // 512, largest, jnp.zeros((512, 1), F32))
    key_norm = jnp.sqrt(jnp.max(best, axis=0, keepdims=True))
    lane = lane_index((RUN, 128))
    lane_tall = lane_index((2 * RUN, 128))

    def weights(keys, aux, qx):
        return jnp.exp(mm(qx, jnp.concatenate([keys, aux], axis=1), NT))

    def right(keys):
        return jnp.where(lane_index(keys.shape) < 64, jnp.ones_like(keys), keys)

    for part in range(4):
        rows = pl.ds(part * RUN, RUN)
        own_aux = own_aux_ref[rows, :].astype(F32)
        for head in range(2):
            query = q_ref[head, rows, :]
            wide = query.astype(F32)
            shift = jnp.ceil(jnp.sqrt(jnp.sum(wide * wide, axis=1, keepdims=True)) * key_norm)
            top = shift.astype(BF16).astype(F32)
            middle = (shift - top).astype(BF16).astype(F32)
            rest = shift - top - middle
            ext = jnp.where(lane < 3 + NSEQ, (own_aux - 1.0) * FAR, 0.0)
            ext = jnp.where(lane == 0, -top, ext)
            ext = jnp.where(lane == 1, -middle, ext)
            ext = jnp.where(lane == 2, -rest, ext)
            here = pl.ds(head * RUN, RUN)
            qx_ref[part, here, 0:128] = query
            qx_ref[part, here, 128:256] = ext.astype(BF16)
        qx = qx_ref[part]
        order_key, order_query = order_pair(order_ref, part)
        allowed = order_key <= order_query
        keys = own_kv_ref[rows, :]
        e = weights(keys, own_aux_ref[rows, :], qx)
        e = jnp.where(jnp.concatenate([allowed, allowed], axis=0), e, 0.0)
        acc_ref[...] = mm(e.astype(BF16), right(keys))
        base = (part % 2) * 32

        def tiles(step):
            start = pl.multiple_of(first_ref[base + step], RUN)
            return kv_ref[pl.ds(start, RUN), :], aux_ref[pl.ds(start, RUN), :]

        def pair(step, carry):
            keys_a, aux_a = tiles(2 * step)
            keys_b, aux_b = tiles(2 * step + 1)
            keys = jnp.concatenate([keys_a, keys_b], axis=0)
            aux = jnp.concatenate([aux_a, aux_b], axis=0)
            acc_ref[...] += mm(weights(keys, aux, qx).astype(BF16), right(keys))
            return carry

        number = count_ref[part]
        lax.fori_loop(0, number // 2, pair, 0)

        @pl.when(number % 2 == 1)
        def _():
            keys, aux = tiles(number - 1)
            acc_ref[...] += mm(weights(keys, aux, qx).astype(BF16), right(keys))

        total = acc_ref[...]
        other = pltpu.roll(total, 64, axis=1)
        norm = jnp.where(lane_tall < 64, total, other)
        value = jnp.where(lane_tall < 64, other, total) / norm
        low_lanes = lane < 64
        att = jnp.where(low_lanes, value[:RUN], value[RUN:])
        att_ref[rows, :] = att
        norm_ref[rows, :] = jnp.where(low_lanes, norm[:RUN], norm[RUN:])
        sent_ref[rows, :] = att.astype(BF16)


def attend_back_kernel(
    first_ref, count_ref, base_ref, kv_ref, aux_ref, own_kv_ref, own_aux_ref, qx_ref, order_ref,
    gsent_ref, att_ref, norm_ref, dq_ref, dkv_ref, acc_ref, dq_acc, gx_ref, rhs_ref,
):
    def clear(step, carry):
        acc_ref[pl.ds(pl.multiple_of(step * 512, 512), 512), :] = jnp.zeros((512, 128), F32)
        return carry

    lax.fori_loop(0, TOKENS // 512, clear, 0)
    lane = lane_index((RUN, 128))
    low_lanes = lane < 64
    for part in range(4):
        rows = pl.ds(part * RUN, RUN)
        gsent = gsent_ref[rows, :].astype(F32)
        norm = norm_ref[rows, :]
        product = gsent * att_ref[rows, :] / norm
        scaled = (gsent / norm).astype(BF16).astype(F32)
        for head in range(2):
            mask = low_lanes if head == 0 else jnp.logical_not(low_lanes)
            delta = jnp.sum(jnp.where(mask, product, 0.0), axis=1, keepdims=True)
            top = delta.astype(BF16).astype(F32)
            middle = (delta - top).astype(BF16).astype(F32)
            rest = delta - top - middle
            ext = jnp.where(lane == 0, -top, 0.0)
            ext = jnp.where(lane == 1, -middle, ext)
            ext = jnp.where(lane == 2, -rest, ext)
            grad = pltpu.roll(scaled, 64, axis=1) if head == 0 else scaled
            grad = jnp.where(low_lanes, 0.0, grad).astype(BF16)
            here = pl.ds(head * RUN, RUN)
            gx_ref[here, 0:128] = grad
            gx_ref[here, 128:256] = ext.astype(BF16)
            rhs_ref[pl.ds(head * RUN, RUN), :] = qx_ref[part, here, 0:128]
            rhs_ref[pl.ds((2 + head) * RUN, RUN), :] = grad
        order_key, order_query = order_pair(order_ref, part)
        allowed = order_query <= order_key
        dq_acc[...] = jnp.zeros_like(dq_acc)

        def tile(start, keys, aux, mask):
            both = jnp.concatenate([keys, aux], axis=1)
            e = jnp.exp(mm(both, qx_ref[part], NT))
            if mask is not None:
                e = jnp.where(mask, e, 0.0)
            ds = (e * mm(both, gx_ref[...], NT)).astype(BF16)
            left = jnp.concatenate([ds, e.astype(BF16)], axis=1)
            acc_ref[pl.ds(start, RUN), :] += mm(left, rhs_ref[...])
            dq_acc[...] += mm(keys.T[:64], ds)

        tile(
            pl.multiple_of(base_ref[0] + part * RUN, RUN),
            own_kv_ref[rows, :],
            own_aux_ref[rows, :],
            jnp.concatenate([allowed, allowed], axis=1),
        )
        base = (part % 2) * 32

        def step_tile(step, carry):
            start = pl.multiple_of(first_ref[base + step], RUN)
            tile(start, kv_ref[pl.ds(start, RUN), :], aux_ref[pl.ds(start, RUN), :], None)
            return carry

        lax.fori_loop(0, count_ref[part], step_tile, 0)
        total = dq_acc[...] * 0.125
        dq_ref[rows, :] = jnp.concatenate([total[:, :RUN], total[:, RUN:]], axis=0).T

    def finish(step, carry):
        rows = pl.ds(pl.multiple_of(step * 512, 512), 512)
        dkv_ref[rows, :] = acc_ref[rows, :].astype(BF16)
        return carry

    lax.fori_loop(0, TOKENS // 512, finish, 0)


SLOT_EXPERT = np.arange(SLOTS) // SLOT
SLOT_PLACE = np.arange(SLOTS) % SLOT


def constant(array):
    return jnp.asarray(np.asarray(array).astype(ml_dtypes.bfloat16))


def expand_matrix():
    return constant(np.arange(128)[:, None] == SLOT_EXPERT[None, :])


def place_matrix():
    return constant(SLOT_PLACE[:, None] == np.arange(128)[None, :])


def pick_matrix(place):
    return constant((SLOT_EXPERT[:, None] == np.arange(128)[None, :]) & (SLOT_PLACE[:, None] == place))


def place_column():
    used = np.where(SLOT_PLACE < CAP, SLOT_PLACE, -5)
    return constant(np.broadcast_to(used[:, None], (SLOTS, 128)))


def place_row():
    used = np.where(SLOT_PLACE < CAP, SLOT_PLACE, -5)
    return jnp.asarray(used[None, :].astype(np.float32))


def prepare_kernel(routes_ref, cot_ref, expand_ref, expand_t_ref, col_ref, row_ref, member_ref, put_ref, take_ref, out_ref):
    lane = lane_index((ROWS, 128))
    routes = routes_ref[...]
    member = jnp.zeros((ROWS, 128), F32)
    for choice in range(8):
        member += jnp.where(routes[:, choice : choice + 1] == lane, 1.0, 0.0)
    below = lax.broadcasted_iota(jnp.int32, (ROWS, ROWS), 0) > lane_index((ROWS, ROWS))
    earlier = mm(jnp.where(below, 1.0, 0.0).astype(BF16), member.astype(BF16))
    slot = jnp.where(member > 0.5, earlier, -1.0).astype(BF16)
    member_ref[...] = member
    take = jnp.where(mm(slot, expand_ref[...]) == row_ref[...], 1.0, 0.0)
    take_ref[...] = take.astype(BF16)
    put = jnp.where(mm(expand_t_ref[...], slot, NT) == col_ref[...].astype(F32), 1.0, 0.0)
    put = put.astype(BF16)
    put_ref[...] = put
    for part in range(4):
        columns = pl.ds(part * 256, 256)
        out_ref[:, columns] = mm(put, cot_ref[:, columns]).astype(BF16)


BLOCK = 8 * SLOT
BLOCK_SOURCE = np.arange(BLOCK) // SLOT
BLOCK_PLACE = np.arange(BLOCK) % SLOT


def block_matrix(places):
    hit = np.isin(BLOCK_PLACE, places)[None, :] & (BLOCK_SOURCE[:, None] == BLOCK_SOURCE[None, :])
    return constant(hit)


def packed_pairs(values):
    total = sum(int(value) << (2 * i) for i, value in enumerate(values))
    return np.uint32(total).astype(np.int32)


STEP_Y = packed_pairs([dy for dy, _ in PLANE_ORDER])
STEP_Z = packed_pairs([dz for _, dz in PLANE_ORDER])


def moe_kernel(
    sent_ref, tok_ref, w_out_ref, router_ref, member_ref, put_ref, take_ref, expand_ref,
    expand_t_ref, place_ref, place_t_ref, pick_high_ref, pick_low_ref, pick_t_ref, cot_ref,
    select_ref, block_place_ref, high_ref, low_ref, g_hbm, gate_hbm, up_hbm, down_hbm,
    residual_ref, weigh_high_ref, weigh_low_ref, gmid_ref, branch_ref, gsent_in, side_in,
    y_hbm, grad_gate_hbm, grad_up_hbm, grad_down_hbm,
    sent_in, x_out, x_in, g_v, y_v, back_out, back_in, gate_v, up_v, down_v,
    sum_gate, sum_up, sum_down, grad_gate, grad_up, grad_down, mixed_v, gate_probs, gsent_out, side_out,
    x_send, x_recv, back_send, back_recv, line_send, line_recv, local,
):
    me = position(AXES)
    x_at, y_at, z_at, c_at = (me[axis] for axis in AXES)
    expert = (y_at * 4 + z_at) * 2 + c_at

    def offset(k):
        pair = lax.div(k, 2)
        dy = lax.shift_right_logical(jnp.int32(STEP_Y), 2 * pair) & 3
        dz = lax.shift_right_logical(jnp.int32(STEP_Z), 2 * pair) & 3
        return dy, dz, lax.rem(k + pair, 2)

    def toward(k):
        dy, dz, dc = offset(k)
        return {"y": lax.rem(y_at + dy, 4), "z": lax.rem(z_at + dz, 4), "c": lax.rem(c_at + dc, 2)}

    def source(k):
        dy, dz, dc = offset(k)
        return {
            "y": lax.rem(y_at + 4 - dy, 4),
            "z": lax.rem(z_at + 4 - dz, 4),
            "c": lax.rem(c_at + dc, 2),
        }

    def number(at):
        return (at["y"] * 4 + at["z"]) * 2 + at["c"]

    loads = [
        pltpu.make_async_copy(src, dst, local.at[i])
        for i, (src, dst) in enumerate(
            ((g_hbm, g_v), (gate_hbm, gate_v), (up_hbm, up_v), (down_hbm, down_v))
        )
    ]
    for item in loads:
        item.start()
    barrier = pltpu.get_barrier_semaphore()
    for by in LINE_OFFSETS:
        pl.semaphore_signal(barrier, inc=1, device_id=moved(me, by), device_id_type=MESH)

    def hello(k, carry):
        pl.semaphore_signal(barrier, inc=1, device_id=toward(k), device_id_type=MESH)
        return carry

    lax.fori_loop(0, 31, hello, 0)
    pl.semaphore_wait(barrier, 31 + len(LINE_OFFSETS))

    here_line = x_at * 2 + c_at
    moves = []
    for i, by in enumerate(LINE_OFFSETS):
        to = moved(me, by)
        moves.append(
            remote(sent_ref.at[to["c"] * 4 + to["x"]], sent_in.at[here_line], line_send, line_recv, i, to)
        )
        moves[-1].start()
    kept = pltpu.make_async_copy(sent_ref.at[c_at * 4 + x_at], sent_in.at[here_line], local.at[4])
    kept.start()
    for item in moves + [kept]:
        item.wait()
    sent = jnp.concatenate([sent_in[i] for i in range(8)], axis=1)
    residual = tok_ref[...].astype(F32) + mm(sent, w_out_ref[...])
    residual_ref[...] = residual
    gain = router_ref[...].astype(F32).T[EXPERTS : EXPERTS + 1, :]
    scale = lax.rsqrt(jnp.mean(residual * residual, axis=-1, keepdims=True) + EPSILON)
    mixed = (residual * scale * gain).astype(BF16)
    mixed_v[...] = mixed
    logits = mm(mixed, router_ref[...])
    member = member_ref[...]
    masked = jnp.where(member > 0.5, logits, -FAR)
    top = jnp.max(masked, axis=1, keepdims=True)
    power = jnp.where(member > 0.5, jnp.exp(masked - top), 0.0)
    gate = power / jnp.sum(power, axis=1, keepdims=True)
    gate_probs[...] = gate
    gate_high, gate_low = halves(gate)
    spread = mm(gate_high, expand_ref[...]) + mm(gate_low, expand_ref[...])
    weigh = take_ref[...].astype(F32) * spread
    weigh_high, weigh_low = halves(weigh)
    weigh_high_ref[...] = weigh_high
    weigh_low_ref[...] = weigh_low
    total = jnp.sum(weigh, axis=0, keepdims=True)
    rows_high, rows_low = halves(expand_ref[...].astype(F32) * total)
    rows_high = mm(rows_high, place_ref[...]).astype(BF16)
    rows_low = mm(rows_low, place_ref[...]).astype(BF16)
    gate_rows = mm(pick_high_ref[...], rows_high) + mm(pick_low_ref[...], rows_low)
    put = put_ref[...]

    def slots(value):
        return value.reshape(EXPERTS, SLOT, value.shape[1]).astype(BF16)

    x_out[:, :, 0:128] = slots(mm(put, mixed[:, 0:128]) + gate_rows)
    x_out[:, :, 128:512] = slots(mm(put, mixed[:, 128:512]))
    x_out[:, :, 512:1024] = slots(mm(put, mixed[:, 512:1024]))

    def x_copy(k):
        to = toward(k)
        return remote(x_out.at[number(to)], x_in.at[k], x_send, x_recv, k, to)

    def x_start(k, carry):
        x_copy(k).start()
        return carry

    lax.fori_loop(0, 31, x_start, 0)
    kept = pltpu.make_async_copy(x_out.at[expert], x_in.at[31], local.at[4])
    kept.start()
    kept.wait()
    sum_gate[...] = jnp.zeros_like(sum_gate)
    sum_up[...] = jnp.zeros_like(sum_up)
    sum_down[...] = jnp.zeros_like(sum_down)
    for item in loads:
        item.wait()

    def back_copy(k):
        to = source(k)
        return remote(back_out.at[k], back_in.at[expert], back_send, back_recv, k, to)

    def back_kept():
        return pltpu.make_async_copy(back_out.at[31], back_in.at[expert], local.at[4])

    def group(step, carry):
        first = step * 8
        for i in range(8):
            k = first + i

            @pl.when(k < 31)
            def _():
                x_copy(k).wait_recv()

        x = x_in[pl.ds(first, 8)].astype(F32).reshape(BLOCK, D).astype(BF16)
        g = jnp.concatenate([g_v[number(source(first + i))].astype(F32) for i in range(8)], axis=0)
        place = block_place_ref[...].astype(F32)
        share = jnp.sum(mm(select_ref[...], x[:, :128]) * place, axis=1, keepdims=True)
        a = mm(x, gate_v[...])
        b = mm(x, up_v[...])
        s = 1.0 / (1.0 + jnp.exp(-a))
        silu = a * s
        hidden = (silu * b).astype(BF16)
        y = mm(hidden, down_v[...]).astype(BF16).astype(F32)
        dgate = jnp.sum(y * g, axis=1, keepdims=True)
        y = y.reshape(8, SLOT, D)
        for i in range(8):
            y_v[number(source(first + i))] = y[i].astype(BF16)
        gy = (g * share).astype(BF16)
        dhidden = mm(gy, down_v[...], NT)
        da = (dhidden * b * (s * (1.0 + a * (1.0 - s)))).astype(BF16)
        db = (dhidden * silu).astype(BF16)
        back = mm(da, gate_v[...], NT) + mm(db, up_v[...], NT)
        dgate_high, dgate_low = halves(dgate * place)
        lead = back[:, 0:128] + mm(high_ref[...], dgate_high) + mm(low_ref[...], dgate_low)
        span = pl.ds(first, 8)
        back_out[span, :, 0:128] = lead.reshape(8, SLOT, 128).astype(BF16)
        back_out[span, :, 128:1024] = back[:, 128:1024].reshape(8, SLOT, 896).astype(BF16)
        for i in range(8):
            k = first + i

            @pl.when(k < 31)
            def _():
                back_copy(k).start()

            @pl.when(k == 31)
            def _():
                back_kept().start()

        sum_gate[...] += mm(x, da, TN)
        sum_up[...] += mm(x, db, TN)
        sum_down[...] += mm(hidden, gy, TN)
        return carry

    lax.fori_loop(0, 4, group, 0)
    grad_gate[...] = sum_gate[...].astype(BF16)
    grad_up[...] = sum_up[...].astype(BF16)
    grad_down[...] = sum_down[...].astype(BF16)
    stores = [
        pltpu.make_async_copy(src, dst, local.at[i])
        for i, (src, dst) in enumerate(
            ((y_v, y_hbm), (grad_gate, grad_gate_hbm), (grad_up, grad_up_hbm), (grad_down, grad_down_hbm))
        )
    ]
    for item in stores:
        item.start()

    def settle(k, carry):
        x_copy(k).wait_send()
        back_copy(k).wait()
        return carry

    lax.fori_loop(0, 31, settle, 0)
    back_kept().wait()

    take = take_ref[...]
    rows_high, rows_low = halves(
        sum(
            mm(
                pick_t_ref[:, i * 640 : (i + 1) * 640],
                back_in[i * 16 : (i + 1) * 16, :, 0:128].astype(F32).reshape(640, 128).astype(BF16),
            )
            for i in range(2)
        )
    )
    spread = mm(rows_high, place_t_ref[...]) + mm(rows_low, place_t_ref[...])
    along = jnp.sum(spread * expand_ref[...].astype(F32), axis=0, keepdims=True)
    found_high, found_low = halves(take.astype(F32) * along)
    dgate = mm(found_high, expand_t_ref[...]) + mm(found_low, expand_t_ref[...])
    gate = gate_probs[...]
    dlogits = gate * (dgate - jnp.sum(gate * dgate, axis=1, keepdims=True))
    dlogits = dlogits.astype(BF16)
    dmixed = mm(dlogits, router_ref[...], NT)
    for i in range(2):
        rows = back_in[i * 16 : (i + 1) * 16].astype(F32).reshape(640, D).astype(BF16)
        dmixed += mm(take[:, i * 640 : (i + 1) * 640], rows)
    residual = residual_ref[...]
    scale = lax.rsqrt(jnp.mean(residual * residual, axis=-1, keepdims=True) + EPSILON)
    gain = router_ref[...].astype(F32).T[EXPERTS : EXPERTS + 1, :]
    weighted = dmixed * gain
    inner = jnp.mean(weighted * residual, axis=-1, keepdims=True)
    gmid = cot_ref[...].astype(F32) + scale * weighted - residual * (scale * scale * scale) * inner
    gmid_ref[...] = gmid
    branch = gmid.astype(BF16)
    branch_ref[...] = branch
    gsent = mm(branch, w_out_ref[...], NT).astype(BF16)
    for i in range(8):
        gsent_out[i] = gsent[:, i * 128 : (i + 1) * 128]
    back_line = c_at * 4 + x_at
    moves = []
    for i, by in enumerate(LINE_OFFSETS):
        to = moved(me, by)
        moves.append(
            remote(
                gsent_out.at[to["x"] * 2 + to["c"]], gsent_in.at[back_line], line_send, line_recv, 7 + i, to
            )
        )
        moves[-1].start()
    kept = pltpu.make_async_copy(gsent_out.at[here_line], gsent_in.at[back_line], local.at[4])
    kept.start()
    moves.append(kept)
    gain_grad = jnp.sum(dmixed * residual * scale, axis=0, keepdims=True)
    grads = mm(dlogits, mixed_v[...], TN)
    row = lax.broadcasted_iota(jnp.int32, (128, D), 0)
    grads = jnp.where(row == EXPERTS, gain_grad, grads).T.reshape(4, 16, 2, 8, 128)
    for i in range(8):
        side_out[i] = grads[i // 2, :, i % 2].reshape(ROWS, 128).astype(BF16)
    for i, by in enumerate(LINE_OFFSETS):
        to = moved(me, by)
        moves.append(
            remote(
                side_out.at[to["x"] * 2 + to["c"]], side_in.at[back_line], line_send, line_recv, 14 + i, to
            )
        )
        moves[-1].start()
    kept = pltpu.make_async_copy(side_out.at[here_line], side_in.at[back_line], local.at[5])
    kept.start()
    for item in moves + [kept] + stores:
        item.wait()


def moe(inputs, cid):
    vmem = pl.BlockSpec(memory_space=pltpu.VMEM)
    hbm = pl.BlockSpec(memory_space=pl.ANY)
    slots = (EXPERTS, SLOT, D)
    up, down = (D, FF), (FF, D)
    dma = pltpu.SemaphoreType.DMA
    return pl.pallas_call(
        moe_kernel,
        grid=(1,),
        out_shape=[
            shape((ROWS, D), F32),
            shape((ROWS, SLOTS), BF16),
            shape((ROWS, SLOTS), BF16),
            shape((ROWS, D), F32),
            shape((ROWS, D), BF16),
            shape((8, ROWS, 128), BF16),
            shape((8, ROWS, 128), BF16),
            shape(slots, BF16),
            shape(up, BF16),
            shape(up, BF16),
            shape(down, BF16),
        ],
        in_specs=[vmem] * 2 + [OUT_BLOCK, SIDE_BLOCK] + [vmem] * 15 + [hbm] * 4,
        out_specs=[vmem] * 7 + [hbm] * 4,
        scratch_shapes=[
            pltpu.VMEM((8, ROWS, 128), BF16),
            pltpu.VMEM(slots, BF16),
            pltpu.VMEM(slots, BF16),
            pltpu.VMEM(slots, BF16),
            pltpu.VMEM(slots, BF16),
            pltpu.VMEM(slots, BF16),
            pltpu.VMEM(slots, BF16),
            pltpu.VMEM(up, BF16),
            pltpu.VMEM(up, BF16),
            pltpu.VMEM(down, BF16),
            pltpu.VMEM(up, F32),
            pltpu.VMEM(up, F32),
            pltpu.VMEM(down, F32),
            pltpu.VMEM(up, BF16),
            pltpu.VMEM(up, BF16),
            pltpu.VMEM(down, BF16),
            pltpu.VMEM((ROWS, D), BF16),
            pltpu.VMEM((ROWS, 128), F32),
            pltpu.VMEM((8, ROWS, 128), BF16),
            pltpu.VMEM((8, ROWS, 128), BF16),
            dma((31,)),
            dma((31,)),
            dma((31,)),
            dma((31,)),
            dma((21,)),
            dma((21,)),
            dma((6,)),
        ],
        compiler_params=pltpu.CompilerParams(
            collective_id=cid, has_side_effects=True, vmem_limit_bytes=VMEM_BYTES
        ),
    )(*inputs)


def finish_kernel(
    dq_ref, dkv_ref, cos_ref, sin_ref, normed_ref, w_ref,
    y_ref, weigh_high_ref, weigh_low_ref, residual_ref, out_ref, side_ref,
    dnormed_out, mixed_out, grads_out, early_out,
    dqkv, part_out, part_in, part_own, line_out, line_in, share_out, share_in, total,
    out_in, side_in, send, recv, local, out_recv,
):
    me = position(AXES)
    x, y, z, c = (me[axis] for axis in AXES)
    mine = y * 4 + z
    alone = jnp.where(c == lax.div(y, 2), 1, 0)
    barrier = pltpu.get_barrier_semaphore()

    def owner(k):
        at = lax.rem(lax.rem(y, 2) * 8 + z * 2 + c + k, 16)
        to = {"y": 2 * c + lax.div(at, 8), "z": lax.rem(lax.div(at, 2), 4), "c": lax.rem(at, 2)}
        return at, to

    def origin(k):
        at = lax.rem(mine + k, 16)
        return at, {"y": lax.div(at, 4), "z": lax.rem(at, 4), "c": lax.div(y, 2)}

    for k in range(1, 16):
        pl.semaphore_signal(barrier, inc=1, device_id=origin(k)[1], device_id_type=MESH)

    @pl.when(alone == 0)
    def _():
        pl.semaphore_signal(barrier, inc=1, device_id=origin(0)[1], device_id_type=MESH)

    offsets = LINE_OFFSETS + PLANE_OFFSETS
    for offset in offsets:
        pl.semaphore_signal(barrier, inc=1, device_id=moved(me, offset), device_id_type=MESH)
    pl.semaphore_wait(barrier, len(offsets) + 16 - alone)
    used = [0]

    def go(src, dst, to):
        item = remote(src, dst, send, recv, used[0], to)
        used[0] += 1
        item.start()
        return item

    other = 1 - c
    low_lanes = lane_index((256, 128)) < 64

    def out_copy(k):
        at, to = owner(k)
        return pltpu.make_async_remote_copy(
            src_ref=out_ref.at[at], dst_ref=out_in.at[mine], send_sem=send.at[used[0] + k],
            recv_sem=out_recv.at[mine], device_id=to, device_id_type=MESH,
        )

    def out_kept():
        return pltpu.make_async_copy(out_ref.at[owner(0)[0]], out_in.at[mine], local.at[1])

    out_copies = [out_copy(k) for k in range(16)]
    used[0] += 16
    out_arrivals = []
    for k in range(16):
        at, to = origin(k)
        out_arrivals.append(
            pltpu.make_async_remote_copy(
                src_ref=out_ref.at[0], dst_ref=out_in.at[at], send_sem=send.at[0],
                recv_sem=out_recv.at[at], device_id=to, device_id_type=MESH,
            )
        )

    @pl.when(alone == 0)
    def _():
        out_copies[0].start()

    @pl.when(alone == 1)
    def _():
        out_kept().start()

    for item in out_copies[1:]:
        item.start()
    early = []
    for offset in PLANE_OFFSETS:
        to = moved(me, offset)
        early.append(go(side_ref.at[to["y"] * 4 + to["z"]], side_in.at[mine], to))
    side_kept = pltpu.make_async_copy(side_ref.at[mine], side_in.at[mine], local.at[2])
    side_kept.start()
    early.append(side_kept)

    def turn_back(first):
        rows = pl.ds(pl.multiple_of(first, 256), 256)
        cos, sin = cos_ref[rows, :], sin_ref[rows, :]
        dq, dkv = dq_ref[rows, :], dkv_ref[rows, :]
        dq = (dq * cos - turned(dq) * sin).astype(BF16)
        dkv = jnp.where(low_lanes, dkv * cos - turned(dkv) * sin, dkv).astype(BF16)
        both = jnp.concatenate([dq, dkv], axis=1)
        dqkv[rows, :] = both
        return mm(both, w_ref[:, 0:256], NT)

    crossing = []
    for i in range(2):
        value = turn_back(other * 512 + i * 256).astype(BF16)
        part_out[2 * i] = value[:ROWS]
        part_out[2 * i + 1] = value[ROWS:]
        span = pl.ds(2 * i, 2)
        crossing.append(go(part_out.at[span], part_in.at[span], {"c": other}))
    for i in range(2):
        value = turn_back(c * 512 + i * 256)
        part_own[2 * i] = value[:ROWS]
        part_own[2 * i + 1] = value[ROWS:]
    for item in crossing:
        item.wait()
    along = []
    for i, by in enumerate((2, 1, 3)):
        to = lax.rem(x + by, 4)
        line_out[i] = (part_own[to] + part_in[to].astype(F32)).astype(BF16)
        along.append(go(line_out.at[i], line_in.at[i], {"x": to}))
    for i in range(4):
        columns = pl.ds(i * 256, 256)
        grad = mm(normed_ref[:, columns], dqkv[...], TN).astype(BF16)
        share_out[i] = grad.reshape(16, 16, 256)
    spread = []
    for offset in PLANE_OFFSETS:
        to = moved(me, offset)
        spread.append(go(share_out.at[:, to["y"] * 4 + to["z"]], share_in.at[mine], to))
    kept = pltpu.make_async_copy(share_out.at[:, mine], share_in.at[mine], local.at[0])
    kept.start()
    mixed = mm(weigh_high_ref[...], y_ref[...]) + mm(weigh_low_ref[...], y_ref[...])
    mixed_out[...] = (residual_ref[...] + mixed).astype(BF16)
    for item in spread + [kept]:
        item.wait()
    for i in range(4):
        value = share_in[0, i].astype(F32)
        for j in range(1, 16):
            value += share_in[j, i].astype(F32)
        total[i] = value.reshape(2, 8, 256)
    ends = []
    here = x * 2 + c
    for offset in LINE_OFFSETS:
        to = moved(me, offset)
        ends.append(go(total.at[to["x"], to["c"]], grads_out.at[here], to))
    kept = pltpu.make_async_copy(total.at[x, c], grads_out.at[here], local.at[0])
    kept.start()
    for item in out_copies[1:]:
        item.wait_send()
    for item in out_arrivals[1:]:
        item.wait_recv()

    @pl.when(alone == 0)
    def _():
        out_copies[0].wait_send()
        out_arrivals[0].wait_recv()

    @pl.when(alone == 1)
    def _():
        out_kept().wait()

    for item in early:
        item.wait()
    out_total, side_total = out_in[0], side_in[0]
    for j in range(1, 16):
        out_total += out_in[j]
        side_total += side_in[j]
    early_out[:, 0:D] = out_total
    early_out[:, D : D + 128] = side_total
    for item in along:
        item.wait()
    dnormed = part_own[x] + part_in[x].astype(F32)
    for i in range(3):
        dnormed += line_in[i].astype(F32)
    dnormed_out[...] = dnormed
    for item in ends + [kept]:
        item.wait()


def finish(inputs, cid):
    count = 2 + 3 + 15 + 7 + 16 + 15
    return pl.pallas_call(
        finish_kernel,
        out_shape=[
            jax.ShapeDtypeStruct((ROWS, D), F32),
            jax.ShapeDtypeStruct((ROWS, D), BF16),
            jax.ShapeDtypeStruct((8, 8, 256), F32),
            jax.ShapeDtypeStruct((8, D + 128), F32),
        ],
        in_specs=[pl.BlockSpec(memory_space=pltpu.VMEM)] * 12,
        out_specs=[pl.BlockSpec(memory_space=pltpu.VMEM)] * 4,
        scratch_shapes=[
            pltpu.VMEM((CHIP_ROWS, 256), BF16),
            pltpu.VMEM((4, ROWS, D), BF16),
            pltpu.VMEM((4, ROWS, D), BF16),
            pltpu.VMEM((4, ROWS, D), F32),
            pltpu.VMEM((3, ROWS, D), BF16),
            pltpu.VMEM((3, ROWS, D), BF16),
            pltpu.VMEM((4, 16, 16, 256), BF16),
            pltpu.VMEM((16, 4, 16, 256), BF16),
            pltpu.VMEM((4, 2, 8, 256), F32),
            pltpu.VMEM((16, 8, D), F32),
            pltpu.VMEM((16, 8, 128), F32),
            pltpu.SemaphoreType.DMA((count,)),
            pltpu.SemaphoreType.DMA((count,)),
            pltpu.SemaphoreType.DMA((3,)),
            pltpu.SemaphoreType.DMA((16,)),
        ],
        compiler_params=pltpu.CompilerParams(
            collective_id=cid, has_side_effects=True, vmem_limit_bytes=VMEM_BYTES
        ),
    )(*inputs)


def last_kernel(
    dnormed_ref, tok_ref, gain_ref, gmid_ref, mixed_ref, rows_ref, w_ref, own_gain_ref, early_ref,
    gate_ref, up_ref, down_ref,
    tokens_out, mixed_out, query_out, key_out, value_out, gains_out, grad_out, router_out,
    gate_out, up_out, down_out,
):
    tok = tok_ref[...].astype(F32)
    scale = lax.rsqrt(jnp.mean(tok * tok, axis=-1, keepdims=True) + EPSILON)
    weighted = dnormed_ref[...] * gain_ref[...]
    inner = jnp.mean(weighted * tok, axis=-1, keepdims=True)
    tokens_out[...] = gmid_ref[...] + scale * weighted - tok * (scale * scale * scale) * inner
    mixed_out[...] = mixed_ref[...]
    total = jnp.zeros((8, 256), F32)
    for i in range(8):
        rows = rows_ref[i]
        query_out[:, i * 128 : (i + 1) * 128] = rows[:, :128]
        total += rows * w_ref[:, i * 256 : (i + 1) * 256].astype(F32)
    lanes = lane_index((8, 128)) < 64
    for i in range(4):
        first, second = rows_ref[2 * i][:, 128:], rows_ref[2 * i + 1][:, 128:]
        key_out[:, i * 128 : (i + 1) * 128] = jnp.where(lanes, first, pltpu.roll(second, 64, axis=1))
        value_out[:, i * 128 : (i + 1) * 128] = jnp.where(lanes, pltpu.roll(first, 64, axis=1), second)
    gain_one = jnp.broadcast_to(jnp.sum(total, axis=1, keepdims=True), (8, 128)).T[0:1, :]
    side = early_ref[:, D : D + 128]
    gain_two = side.T[EXPERTS : EXPERTS + 1, :]
    gains_out[0:1, :] = gain_one[:, 0:8] / own_gain_ref[...]
    gains_out[1:2, :] = gain_two[:, 0:8]
    grad_out[...] = early_ref[:, 0:D]
    router_out[...] = side[:, 0:EXPERTS]
    gate_out[...] = gate_ref[...].astype(F32)
    up_out[...] = up_ref[...].astype(F32)
    down_out[...] = down_ref[...].astype(F32)


WHOLE = pl.BlockSpec(memory_space=pltpu.VMEM)
OUT_BLOCK = pl.BlockSpec((D, D), lambda i: (0, 0))
SIDE_BLOCK = pl.BlockSpec((D, 128), lambda i: (0, 8))


def shape(dims, dtype):
    return jax.ShapeDtypeStruct(dims, dtype)


def rotation_tables(order, lengths):
    ends = jnp.cumsum(lengths)
    passed = ends[None, :] <= order[:, None]
    position = order - jnp.sum(jnp.where(passed, lengths[None, :], 0), axis=1)
    frequency = ROPE_BASE ** (-jnp.arange(32, dtype=F32) / 32)
    angles = position.astype(F32)[:, None] * jnp.tile(frequency, 4)[None, :]
    return jnp.cos(angles), jnp.sin(angles)


def body(
    tokens,
    gain_one,
    w_query,
    w_key,
    w_value,
    w_out,
    gain_two,
    w_router,
    w_gate,
    w_up,
    w_down,
    dealt_order,
    lengths,
    routes,
    cotangent,
):
    x_at, y_at, z_at, c_at = (lax.axis_index(axis) for axis in AXES)
    chip = y_at * 4 + z_at
    first_row = chip * CHIP_ROWS

    grouped = jnp.concatenate(
        [
            w_query.reshape(8, 8, 128),
            w_key.reshape(8, 8, 64),
            w_value.reshape(8, 8, 64),
        ],
        axis=2,
    )
    gain_lane = jnp.where(jnp.arange(128)[None, :] == 0, gain_one[:, None], 0).astype(BF16)
    first_pack = jnp.concatenate(
        [grouped.transpose(1, 0, 2), jnp.broadcast_to(gain_lane[None], (8, 8, 128))], axis=2
    )
    token_rows, w_mine = start_rows(tokens, first_pack, 10)
    second_pack = jnp.concatenate(
        [w_out, w_router, gain_two[:, None], jnp.zeros((8, 95), BF16)], axis=1
    )
    second_pack, token_rows = lax.optimization_barrier((second_pack, token_rows))
    w_late = lax.all_gather(second_pack, AXES, axis=0, tiled=True)

    order_own = lax.dynamic_slice_in_dim(dealt_order, first_row, CHIP_ROWS)
    cos, sin = rotation_tables(order_own, lengths)
    ends = jnp.cumsum(lengths)
    within = (dealt_order[None, :] < ends[:, None]) & (
        dealt_order[None, :] >= (ends - lengths)[:, None]
    )
    aux_t = jnp.concatenate([jnp.ones((3, TOKENS), BF16), within.astype(BF16)], axis=0)
    aux = mm(aux_t, jnp.eye(8, 128, dtype=BF16), TN).astype(BF16)
    own_aux = lax.dynamic_slice_in_dim(aux, first_row, CHIP_ROWS)
    order_rows = order_own.astype(F32).reshape(4, RUN)
    run_of = dealt_order.reshape(32, 512)[:, 0] // RUN
    block_ids = jnp.arange(32, dtype=jnp.int32)
    block_of = jnp.sum(
        jnp.where(run_of[None, :] == block_ids[:, None], block_ids[None, :], 0), axis=1
    )
    first_rows = jnp.concatenate([block_of * 512, block_of[::-1] * 512 + RUN])
    mine = lax.dynamic_slice_in_dim(run_of, chip * 2, 2)
    counts = jnp.stack([mine[0], 31 - mine[0], mine[1], 31 - mine[1]])
    base = first_row.reshape(1).astype(jnp.int32)

    expand, expand_t = expand_matrix(), expand_matrix().T
    place, place_t = place_matrix(), place_matrix().T
    pick_high, pick_low = pick_matrix(CAP), pick_matrix(CAP + 1)
    member, put, take, g_out = local_call(
        prepare_kernel,
        (
            shape((ROWS, 128), F32),
            shape((SLOTS, ROWS), BF16),
            shape((ROWS, SLOTS), BF16),
            shape((SLOTS, D), BF16),
        ),
    )(routes, cotangent, expand, expand_t, place_column(), place_row())
    plane = ("y", "z", "c")

    normed, query, kv, gain_first = local_call(
        project_kernel,
        (
            shape((CHIP_ROWS, D), BF16),
            shape((2, CHIP_ROWS, 128), BF16),
            shape((CHIP_ROWS, 128), BF16),
            shape((1, D), F32),
        ),
    )(token_rows, w_mine, cos, sin)
    kv_all = gather_plane(kv, 1)
    g_out, kv_all = lax.optimization_barrier((g_out, kv_all))
    g_in = lax.all_to_all(
        g_out.reshape(EXPERTS, SLOT, D), plane, split_axis=0, concat_axis=0, tiled=True
    )
    smem = pl.BlockSpec(memory_space=pltpu.SMEM)
    vmem = pl.BlockSpec(memory_space=pltpu.VMEM)
    att, norm, sent, query_ext = local_call(
        attend_kernel,
        (
            shape((CHIP_ROWS, 128), F32),
            shape((CHIP_ROWS, 128), F32),
            shape((CHIP_ROWS, 128), BF16),
            shape((4, 2 * RUN, 256), BF16),
        ),
        scratch=[pltpu.VMEM((2 * RUN, 128), F32)],
        in_specs=[smem] * 2 + [vmem] * 6,
    )(first_rows, counts, kv_all, aux, kv, own_aux, query, order_rows)

    (
        residual, weigh_high, weigh_low, gmid, branch, gsent_own, side_rows, y_out,
        grad_gate, grad_up, grad_down,
    ) = moe(
        (
            sent.reshape(8, ROWS, 128), tokens, w_late, w_late, member, put, take, expand, expand_t,
            place, place_t, pick_high, pick_low, (pick_high + pick_low).T, cotangent,
            block_matrix((CAP, CAP + 1)),
            place[:BLOCK],
            block_matrix((CAP,)).T * constant(BLOCK_PLACE == CAP)[:, None],
            block_matrix((CAP + 1,)).T * constant(BLOCK_PLACE == CAP + 1)[:, None],
            g_in, w_gate[0], w_up[0], w_down[0],
        ),
        3,
    )
    y_in = lax.all_to_all(
        y_out, plane, split_axis=0, concat_axis=0, tiled=True
    ).reshape(SLOTS, D)
    grad_gate, grad_up, grad_down = (
        lax.psum_scatter(grad, "x", scatter_dimension=0, tiled=True)
        for grad in (grad_gate, grad_up, grad_down)
    )

    gsent_own = gsent_own.reshape(CHIP_ROWS, 128)
    branch_rows = lax.all_gather(branch, ("c", "x"), axis=0, tiled=True)
    side_sum = jnp.sum(side_rows.astype(F32), axis=0)

    dq, dkv = local_call(
        attend_back_kernel,
        (shape((CHIP_ROWS, 128), F32), shape((TOKENS, 128), BF16)),
        scratch=[
            pltpu.VMEM((TOKENS, 128), F32),
            pltpu.VMEM((64, 2 * RUN), F32),
            pltpu.VMEM((2 * RUN, 256), BF16),
            pltpu.VMEM((4 * RUN, 128), BF16),
        ],
        in_specs=[smem] * 3 + [vmem] * 9,
    )(
        first_rows, counts, base, kv_all, aux, kv, own_aux, query_ext, order_rows, gsent_own, att,
        norm,
    )
    dkv_own, grad_out = scatter_plane(dkv, sent, branch_rows, 6)

    dnormed, mixed, qkv_rows, early = finish(
        (
            dq, dkv_own, cos, sin, normed, w_mine, y_in, weigh_high, weigh_low, residual,
            grad_out.reshape(16, 8, D), side_sum.reshape(16, 8, 128),
        ),
        7,
    )
    (
        grad_tokens, mixed, grad_query, grad_key, grad_value, gains, grad_out_rows, grad_router,
        grad_gate, grad_up, grad_down,
    ) = local_call(
        last_kernel,
        (
            shape((ROWS, D), F32),
            shape((ROWS, D), BF16),
            shape((8, D), F32),
            shape((8, 512), F32),
            shape((8, 512), F32),
            shape((2, 8), F32),
            shape((8, D), F32),
            shape((8, EXPERTS), F32),
            shape((256, FF), F32),
            shape((256, FF), F32),
            shape((128, D), F32),
        ),
    )(
        dnormed, tokens, gain_first, gmid, mixed, qkv_rows, grouped.reshape(8, 2048),
        gain_one.astype(F32).reshape(1, 8), early, grad_gate, grad_up, grad_down,
    )
    grad_gain_one, grad_gain_two = gains[0], gains[1]
    grad_gate, grad_up, grad_down = grad_gate[None], grad_up[None], grad_down[None]
    return (
        mixed,
        grad_tokens,
        grad_gain_one,
        grad_query,
        grad_key,
        grad_value,
        grad_out_rows,
        grad_gain_two,
        grad_router,
        grad_gate,
        grad_up,
        grad_down,
    )


def solution(mesh):
    grid = Mesh(mesh.devices.reshape(4, 4, 4, 2), AXES)
    rows = P(("y", "z", "c", "x"), None)
    vector = P(AXES)
    matrix = P(AXES, None)
    expert = P(("y", "z", "c"), None, None)
    in_specs = (
        rows, vector, matrix, matrix, matrix, matrix, vector, matrix, expert, expert, expert,
        P(), P(), rows, rows,
    )
    grads = P(("y", "z", "c"), "x", None)
    out_specs = (
        rows, rows, vector, matrix, matrix, matrix, matrix, vector, matrix, grads, grads, grads,
    )
    return jax.shard_map(body, mesh=grid, in_specs=in_specs, out_specs=out_specs, check_vma=False)
```

```python
import functools
import math

import jax
import jax.numpy as jnp
import ml_dtypes
import numpy as np
from jax import lax
from jax.experimental import pallas as pl
from jax.experimental.pallas import tpu as pltpu
from jax.sharding import Mesh
from jax.sharding import PartitionSpec as P

D = 1024
HEADS = 16
KV_HEADS = 8
HEAD_DIM = 64
EXPERTS = 32
FF = 512
CAP = 36
SLOT = 40
SLOTS = EXPERTS * SLOT
ROWS = 128
CHIP_ROWS = 1024
RUN = 256
TOKENS = 16384
NSEQ = 5
EPSILON = 1e-06
ROPE_BASE = 10000.0
FAR = float(2.0**100)
SIZE = {"x": 4, "y": 4, "z": 4, "c": 2}
AXES = ("x", "y", "z", "c")
MESH = pl.DeviceIdType.MESH
BF16 = jnp.bfloat16
F32 = jnp.float32
NN = (((1,), (0,)), ((), ()))
NT = (((1,), (1,)), ((), ()))
TN = (((0,), (0,)), ((), ()))
VMEM_BYTES = 56 * 1024 * 1024


def mm(a, b, dims=NN):
    return lax.dot_general(a, b, dims, preferred_element_type=F32)


def halves(value):
    high = value.astype(BF16)
    return high, (value - high.astype(F32)).astype(BF16)


def local_call(kernel, outs, scratch=(), grid=None, in_specs=None, out_specs=None):
    extra = {}
    if grid is not None:
        extra = {"grid": grid, "in_specs": in_specs, "out_specs": out_specs}
    elif in_specs is not None:
        extra = {"in_specs": in_specs}
    return pl.pallas_call(
        kernel,
        out_shape=outs,
        scratch_shapes=list(scratch),
        compiler_params=pltpu.CompilerParams(vmem_limit_bytes=VMEM_BYTES),
        **extra,
    )


def flat_index(coords, order):
    index = 0
    for axis in order:
        index = index * SIZE[axis] + coords[axis]
    return index


PLANE_ORDER = (
    (2, 2), (2, 3), (2, 1), (3, 2), (1, 2), (0, 2), (2, 0), (3, 1), (1, 3),
    (3, 3), (1, 1), (0, 3), (0, 1), (3, 0), (1, 0), (0, 0),
)
PLANE_OFFSETS = tuple({"y": dy, "z": dz} for dy, dz in PLANE_ORDER[:-1])
SPREAD_OFFSETS = tuple(
    {"y": dy, "z": dz, "c": (dc + i + 1) % 2}
    for i, (dy, dz) in enumerate(PLANE_ORDER)
    for dc in range(2)
    if (dy, dz, (dc + i + 1) % 2) != (0, 0, 0)
)
LINE_OFFSETS = tuple(
    {"x": dx, "c": dc} for dx, dc in ((2, 0), (2, 1), (1, 0), (3, 0), (1, 1), (3, 1), (0, 1))
)
OFFSETS = {("y", "z"): PLANE_OFFSETS, ("y", "z", "c"): SPREAD_OFFSETS, ("x", "c"): LINE_OFFSETS}


def position(axes):
    return {axis: lax.axis_index(axis) for axis in axes}


def moved(me, offset):
    return {axis: lax.rem(me[axis] + by, SIZE[axis]) if by else me[axis] for axis, by in offset.items()}


def greet(me, offsets):
    barrier = pltpu.get_barrier_semaphore()
    for offset in offsets:
        pl.semaphore_signal(barrier, inc=1, device_id=moved(me, offset), device_id_type=MESH)
    pl.semaphore_wait(barrier, len(offsets))


def remote(src, dst, send, recv, slot, to):
    return pltpu.make_async_remote_copy(
        src_ref=src,
        dst_ref=dst,
        send_sem=send.at[slot],
        recv_sem=recv.at[slot],
        device_id=to,
        device_id_type=MESH,
    )


def exchange_kernel(axes, dest_order, src_order, arrays, *refs):
    x_refs, o_refs = refs[:arrays], refs[arrays : 2 * arrays]
    send, recv, local = refs[2 * arrays :]
    me = position(axes)
    offsets = OFFSETS[axes]
    greet(me, offsets)
    here = flat_index(me, src_order)
    copies = []
    for offset in offsets:
        to = moved(me, offset)
        for x_ref, o_ref in zip(x_refs, o_refs):
            copies.append(
                remote(
                    x_ref.at[flat_index(to, dest_order)], o_ref.at[here], send, recv, len(copies), to
                )
            )
            copies[-1].start()
    kept = [
        pltpu.make_async_copy(
            x_ref.at[flat_index(me, dest_order)], o_ref.at[here], local.at[i]
        )
        for i, (x_ref, o_ref) in enumerate(zip(x_refs, o_refs))
    ]
    for item in kept:
        item.start()
    for item in kept + copies:
        item.wait()


def exchange(data, axes, cid, dest_order=None, src_order=None):
    single = not isinstance(data, (tuple, list))
    data = [data] if single else list(data)
    dest_order = dest_order or axes
    src_order = src_order or axes
    arrays = len(data)
    count = len(OFFSETS[axes]) * arrays
    out = pl.pallas_call(
        functools.partial(exchange_kernel, axes, dest_order, src_order, arrays),
        out_shape=[jax.ShapeDtypeStruct(item.shape, item.dtype) for item in data],
        in_specs=[pl.BlockSpec(memory_space=pl.ANY)] * arrays,
        out_specs=[pl.BlockSpec(memory_space=pl.ANY)] * arrays,
        scratch_shapes=[
            pltpu.SemaphoreType.DMA((count,)),
            pltpu.SemaphoreType.DMA((count,)),
            pltpu.SemaphoreType.DMA((arrays,)),
        ],
        compiler_params=pltpu.CompilerParams(collective_id=cid, has_side_effects=True),
    )(*data)
    return out[0] if single else out


AROUND = ({"y": 1, "z": 0}, {"y": 3, "z": 0}, {"y": 0, "z": 1}, {"y": 0, "z": 3})


def scatter_plane_kernel(p_ref, sent_ref, branch_ref, o_ref, grad_ref, far_a, near_a, out_a, sum_a, far_b, near_b, out_b, send, recv):
    me = position(("y", "z"))
    greet(me, AROUND)
    half = p_ref.shape[3] // 2
    lower, upper = pl.ds(0, half), pl.ds(half, half)
    axis = (("y", "z"), ("z", "y"))
    used = [0]

    def go(src, dst, t, which, by):
        to = {axis[t][which]: lax.rem(me[axis[t][which]] + by, 4)}
        item = remote(src, dst, send, recv, used[0], to)
        used[0] += 1
        item.start()
        return item

    def part(t, first, second):
        a = lax.rem(me[axis[t][0]] + first, 4)
        b = lax.rem(me[axis[t][1]] + second, 4)
        return p_ref.at[a, b, 0] if t == 0 else p_ref.at[b, a, 1]

    turns = (2, 1, 3, 0)
    both = (0, 1)
    far, near = {}, {}
    for k, by in enumerate(turns):
        for t in both:
            far[k, t] = (
                go(part(t, 2, by).at[lower], far_a.at[t, k, 0], t, 0, 1),
                go(part(t, 2, by).at[upper], far_a.at[t, k, 1], t, 0, 3),
            )
    grad_ref[...] = mm(sent_ref[...], branch_ref[...], TN)
    for k, by in enumerate(turns):
        for t in both:
            ahead, behind = part(t, 1, by), part(t, 3, by)
            far[k, t][0].wait()
            out_a[t, k, 0, 0:half] = (ahead[0:half].astype(F32) + far_a[t, k, 0].astype(F32)).astype(BF16)
            out_a[t, k, 0, half : 2 * half] = ahead[half : 2 * half]
            first = go(out_a.at[t, k, 0], near_a.at[t, k, 0], t, 0, 1)
            far[k, t][1].wait()
            out_a[t, k, 1, 0:half] = behind[0:half]
            out_a[t, k, 1, half : 2 * half] = (
                behind[half : 2 * half].astype(F32) + far_a[t, k, 1].astype(F32)
            ).astype(BF16)
            near[k, t] = (first, go(out_a.at[t, k, 1], near_a.at[t, k, 1], t, 0, 3))

    def summed(k, t):
        near[k, t][0].wait()
        near[k, t][1].wait()
        return (
            part(t, 0, turns[k])[...].astype(F32)
            + near_a[t, k, 0].astype(F32)
            + near_a[t, k, 1].astype(F32)
        )

    far_two, near_two = {}, {}
    for t in both:
        value = summed(0, t).astype(BF16)
        out_b[t, 0] = value
        far_two[t] = (
            go(out_b.at[t, 0, lower], far_b.at[t, 0], t, 1, 1),
            go(out_b.at[t, 0, upper], far_b.at[t, 1], t, 1, 3),
        )
    for k in (1, 2):
        for t in both:
            sum_a[t, k - 1] = summed(k, t)
    for t in both:
        far_two[t][0].wait()
        out_b[t, 1, 0:half] = (sum_a[t, 0, 0:half] + far_b[t, 0].astype(F32)).astype(BF16)
        out_b[t, 1, half : 2 * half] = sum_a[t, 0, half : 2 * half].astype(BF16)
        first = go(out_b.at[t, 1], near_b.at[t, 0], t, 1, 1)
        far_two[t][1].wait()
        out_b[t, 2, 0:half] = sum_a[t, 1, 0:half].astype(BF16)
        out_b[t, 2, half : 2 * half] = (
            sum_a[t, 1, half : 2 * half] + far_b[t, 1].astype(F32)
        ).astype(BF16)
        near_two[t] = (first, go(out_b.at[t, 2], near_b.at[t, 1], t, 1, 3))
    for t in both:
        value = summed(3, t)
        near_two[t][0].wait()
        near_two[t][1].wait()
        o_ref[t] = value + near_b[t, 0].astype(F32) + near_b[t, 1].astype(F32)


def scatter_plane(data, sent, branch_rows, cid):
    rows = data.shape[0] // 32
    whole = pl.BlockSpec(memory_space=pltpu.VMEM)
    out, grad_out = pl.pallas_call(
        scatter_plane_kernel,
        out_shape=[
            jax.ShapeDtypeStruct((2, rows, 128), F32),
            jax.ShapeDtypeStruct((ROWS, D), F32),
        ],
        in_specs=[whole] * 3,
        out_specs=[whole] * 2,
        scratch_shapes=[
            pltpu.VMEM((2, 4, 2, rows // 2, 128), BF16),
            pltpu.VMEM((2, 4, 2, rows, 128), BF16),
            pltpu.VMEM((2, 4, 2, rows, 128), BF16),
            pltpu.VMEM((2, 2, rows, 128), F32),
            pltpu.VMEM((2, 2, rows // 2, 128), BF16),
            pltpu.VMEM((2, 2, rows, 128), BF16),
            pltpu.VMEM((2, 3, rows, 128), BF16),
            pltpu.SemaphoreType.DMA((40,)),
            pltpu.SemaphoreType.DMA((40,)),
        ],
        compiler_params=pltpu.CompilerParams(
            collective_id=cid, has_side_effects=True, vmem_limit_bytes=VMEM_BYTES
        ),
    )(data.reshape(4, 4, 2, rows, 128), sent, branch_rows)
    return out.reshape(2 * rows, 128), grad_out


def lane_index(shape):
    return lax.broadcasted_iota(jnp.int32, shape, 1)


def turned(values):
    lane = lane_index(values.shape)
    up = pltpu.roll(values, 32, axis=1)
    down = pltpu.roll(values, 96, axis=1)
    return jnp.where(lane % 64 < 32, -down, up)


def gather_plane(kv_v, kv_hbm, go, me, own_sem, fillers):
    own = pltpu.make_async_copy(kv_v, kv_hbm.at[me["y"], me["z"]], own_sem)
    own.start()
    half = kv_v.shape[1] // 2
    lower, upper = pl.ds(0, half), pl.ds(half, half)
    axis = (("y", "z"), ("z", "y"))
    here = tuple((me[a], me[b]) for a, b in axis)
    step = {"plus": 1, "minus": 3, "far": 2, "own": 0}

    def place(t, a, b):
        return kv_hbm.at[a, b, 0] if t == 0 else kv_hbm.at[b, a, 1]

    def at(t, which, name):
        return lax.rem(here[t][which] + step[name], 4)

    def send_second(t, src, name):
        dst = place(t, at(t, 0, name), here[t][1])
        src = dst if src is None else src
        return (
            go(src, dst, {axis[t][1]: at(t, 1, "plus")}),
            go(src, dst, {axis[t][1]: at(t, 1, "minus")}),
        )

    def pass_on(t, which, a_name, b_name, part, direction):
        ref = place(t, at(t, 0, a_name), at(t, 1, b_name)).at[part]
        return go(ref, ref, {axis[t][which]: at(t, which, direction)})

    def forward_second(t, name, pair):
        pair[0].wait()
        a = pass_on(t, 1, name, "minus", lower, "plus")
        pair[1].wait()
        b = pass_on(t, 1, name, "plus", upper, "minus")
        return [a, b]

    first, second, last = {}, {}, []
    for t in (0, 1):
        dst = place(t, *here[t])
        first[t] = (
            go(kv_v.at[t], dst, {axis[t][0]: at(t, 0, "plus")}),
            go(kv_v.at[t], dst, {axis[t][0]: at(t, 0, "minus")}),
        )
    for t in (0, 1):
        second[t, "own"] = send_second(t, kv_v.at[t], "own")
    fillers[0]()
    far = {}
    for t in (0, 1):
        first[t][0].wait()
        a = pass_on(t, 0, "minus", "own", lower, "plus")
        second[t, "minus"] = send_second(t, None, "minus")
        first[t][1].wait()
        b = pass_on(t, 0, "plus", "own", upper, "minus")
        second[t, "plus"] = send_second(t, None, "plus")
        far[t] = (a, b)
    fillers[1]()
    for t in (0, 1):
        last += forward_second(t, "own", second[t, "own"])
    for t in (0, 1):
        far[t][0].wait()
        far[t][1].wait()
        second[t, "far"] = send_second(t, None, "far")
    fillers[2]()
    for name in ("minus", "plus", "far"):
        for t in (0, 1):
            last += forward_second(t, name, second[t, name])
    return last + [own]


def front_kernel(
    lengths_ref, tok_ref, w_ref, late_ref, order_ref, routes_ref, cot_ref, expand_ref, expand_t_ref,
    col_ref, row_ref, turn_high_ref, turn_low_ref,
    q_ref, kv_own_ref, gain_ref, cos_ref, sin_ref, w_out_ref, member_ref, put_ref, take_ref,
    own_aux_ref, order_rows_ref, kv_hbm, late_hbm, normed_hbm, g_hbm, aux_hbm,
    rows_v, w_v, normed_v, kv_v, g_v, aux_v, send, recv, local,
):
    me = position(AXES)
    x, y, z, c = (me[axis] for axis in AXES)
    greet(me, LINE_OFFSETS + PLANE_OFFSETS)
    plus, minus, far = lax.rem(x + 1, 4), lax.rem(x + 3, 4), lax.rem(x + 2, 4)
    other = 1 - c
    lower, upper = pl.ds(0, 64), pl.ds(64, 64)
    used = [0]

    def go(src, dst, to):
        item = remote(src, dst, send, recv, used[0], to)
        used[0] += 1
        item.start()
        return item

    def keep(src, dst, slot):
        item = pltpu.make_async_copy(src, dst, local.at[slot])
        item.start()
        return item

    own = [
        keep(w_ref.at[x * 2 + c], w_v.at[x, y, z, c], 0),
        keep(late_ref, late_hbm.at[x, y, z, c], 1),
    ]
    own_rows = keep(tok_ref, rows_v.at[c, x], 2)
    first_w = []
    for offset in LINE_OFFSETS:
        to = moved(me, offset)
        first_w.append(go(w_ref.at[to["x"] * 2 + to["c"]], w_v.at[x, y, z, c], to))
    first_late = [go(late_ref, late_hbm.at[x, y, z, c], {"x": to}) for to in (far, plus, minus)]
    to_plus = go(tok_ref, rows_v.at[c, x], {"x": plus})
    to_minus = go(tok_ref, rows_v.at[c, x], {"x": minus})
    sides = [go(tok_ref, rows_v.at[c, x], {"c": other})]

    for item in own + first_w:
        item.wait()
    second_w = [go(w_v.at[:, y, z], w_v.at[:, y, z], moved(me, by)) for by in PLANE_OFFSETS]
    for item in first_late:
        item.wait()
    second_late = [
        go(late_hbm.at[:, y, z, c], late_hbm.at[:, y, z, c], moved(me, by)) for by in PLANE_OFFSETS
    ]

    chip = y * 4 + z
    mine = order_ref[pl.ds(pl.multiple_of(chip * 8, 8), 8), :]
    ends, total = [], jnp.int32(0)
    for i in range(NSEQ):
        total = total + lengths_ref[i]
        ends.append(total)
    place = mine
    for i in range(NSEQ):
        place = place - jnp.where(mine >= ends[i], lengths_ref[i], 0)
    lane = lane_index((ROWS, 128))

    def table(ref, picked):
        return mm(picked, ref[0]) + mm(picked, ref[1]) + mm(picked, ref[2])

    for i in range(8):
        wide = jnp.broadcast_to(place[i : i + 1, :].astype(F32), (ROWS, 128)).T.astype(jnp.int32)
        high = table(turn_high_ref, jnp.where(lane == lax.shift_right_logical(wide, 7), 1.0, 0.0).astype(BF16))
        low = table(turn_low_ref, jnp.where(lane == (wide & 127), 1.0, 0.0).astype(BF16))
        cos_ref[pl.ds(i * 128, 128), :] = high[:, :128] * low[:, :128] - high[:, 128:] * low[:, 128:]
        sin_ref[pl.ds(i * 128, 128), :] = high[:, 128:] * low[:, :128] + high[:, :128] * low[:, 128:]
    for i in range(4):
        order_rows_ref[i : i + 1, 0:128] = mine[2 * i : 2 * i + 1, :].astype(F32)
        order_rows_ref[i : i + 1, 128:256] = mine[2 * i + 1 : 2 * i + 2, :].astype(F32)

    to_plus.wait()
    next_plus = go(rows_v.at[c, minus, lower], rows_v.at[c, minus, lower], {"x": plus})
    sides.append(go(rows_v.at[c, minus], rows_v.at[c, minus], {"c": other}))
    to_minus.wait()
    next_minus = go(rows_v.at[c, plus, upper], rows_v.at[c, plus, upper], {"x": minus})
    sides.append(go(rows_v.at[c, plus], rows_v.at[c, plus], {"c": other}))
    next_plus.wait()
    next_minus.wait()
    sides.append(go(rows_v.at[c, far], rows_v.at[c, far], {"c": other}))
    own_rows.wait()
    for item in second_w:
        item.wait()
    weights = w_v[...].astype(F32).reshape(D, 384)
    w_out_ref[...] = weights.astype(BF16)
    gain = weights[:, 256:384].T[0:1, :]
    gain_ref[...] = gain
    low_lanes = lane_index((256, 128)) < 64

    def project(block):
        for i in range(2):
            rows = pl.ds(pl.multiple_of(block * 512 + i * 256, 256), 256)
            tok = rows_v[block, pl.ds(2 * i, 2)].astype(F32).reshape(256, D)
            scale = lax.rsqrt(jnp.mean(tok * tok, axis=-1, keepdims=True) + EPSILON)
            normed = (tok * scale * gain).astype(BF16)
            normed_v[rows, :] = normed
            pre = mm(normed, w_out_ref[:, 0:256])
            cos, sin = cos_ref[rows, :], sin_ref[rows, :]
            q_pre, kv_pre = pre[:, :128], pre[:, 128:]
            query = (q_pre * cos + turned(q_pre) * sin).astype(BF16).astype(F32) * 0.125
            q_ref[0, rows, :] = jnp.where(low_lanes, query, 0.0).astype(BF16)
            q_ref[1, rows, :] = jnp.where(low_lanes, pltpu.roll(query, 64, axis=1), 0.0).astype(BF16)
            key = kv_pre * cos + turned(kv_pre) * sin
            kv = jnp.where(low_lanes, key, kv_pre).astype(BF16)
            kv_own_ref[rows, :] = kv
            kv_v[block, pl.ds(i * 256, 256), :] = kv

    project(c)
    for item in sides:
        item.wait()
    project(other)
    stores = [keep(normed_v, normed_hbm, 2)]

    def routing():
        routes = routes_ref[...]
        member = jnp.zeros((ROWS, 128), F32)
        for choice in range(8):
            member += jnp.where(routes[:, choice : choice + 1] == lane, 1.0, 0.0)
        below = lax.broadcasted_iota(jnp.int32, (ROWS, ROWS), 0) > lane_index((ROWS, ROWS))
        earlier = mm(jnp.where(below, 1.0, 0.0).astype(BF16), member.astype(BF16))
        slot = jnp.where(member > 0.5, earlier, -1.0).astype(BF16)
        member_ref[...] = member
        take = jnp.where(mm(slot, expand_ref[...]) == row_ref[...], 1.0, 0.0)
        take_ref[...] = take.astype(BF16)
        put = jnp.where(mm(expand_t_ref[...], slot, NT) == col_ref[...].astype(F32), 1.0, 0.0)
        put = put.astype(BF16)
        put_ref[...] = put
        for part in range(4):
            columns = pl.ds(part * 256, 256)
            g_v[:, :, columns] = mm(put, cot_ref[:, columns]).reshape(EXPERTS, SLOT, 256).astype(BF16)
        stores.append(keep(g_v, g_hbm, 0))

    def segments():
        sub = lax.broadcasted_iota(jnp.int32, (8, 128), 0)
        begin = jnp.zeros((8, 128), jnp.int32)
        end = jnp.full((8, 128), TOKENS, jnp.int32)
        for i in range(NSEQ):
            begin = jnp.where(sub == 3 + i, ends[i] - lengths_ref[i], begin)
            end = jnp.where(sub == 3 + i, ends[i], end)
        spot = jnp.where(sub == lane_index((8, 128)), 1.0, 0.0).astype(BF16)

        def block(step, carry):
            rows = order_ref[pl.ds(pl.multiple_of(step * 8, 8), 8), :]
            for i in range(8):
                order = jnp.broadcast_to(rows[i : i + 1, :], (8, 128))
                within = jnp.where((order >= begin) & (order < end), 1.0, 0.0).astype(BF16)
                here = pl.ds(pl.multiple_of(step * 1024 + i * 128, 128), 128)
                aux_v[here, :] = mm(within, spot, TN).astype(BF16)
            return carry

        lax.fori_loop(0, 16, block, 0)
        stores.append(keep(aux_v, aux_hbm, 1))
        own_aux_ref[...] = aux_v[pl.ds(pl.multiple_of(chip * CHIP_ROWS, CHIP_ROWS), CHIP_ROWS), :]

    def late():
        for item in second_late:
            item.wait()
        stores.append(go(late_hbm.at[:, :, :, c], late_hbm.at[:, :, :, c], {"c": other}))

    last = gather_plane(kv_v, kv_hbm, go, me, local.at[3], (routing, segments, late))
    for item in last + stores:
        item.wait()


def front(inputs, cid):
    count = 7 + 3 + 3 + 15 + 15 + 2 + 3 + 40 + 1
    vmem = pl.BlockSpec(memory_space=pltpu.VMEM)
    smem = pl.BlockSpec(memory_space=pltpu.SMEM)
    hbm = pl.BlockSpec(memory_space=pl.ANY)
    return pl.pallas_call(
        front_kernel,
        out_shape=[
            shape((2, CHIP_ROWS, 128), BF16),
            shape((CHIP_ROWS, 128), BF16),
            shape((1, D), F32),
            shape((CHIP_ROWS, 128), F32),
            shape((CHIP_ROWS, 128), F32),
            shape((D, 384), BF16),
            shape((ROWS, 128), F32),
            shape((SLOTS, ROWS), BF16),
            shape((ROWS, SLOTS), BF16),
            shape((CHIP_ROWS, 128), BF16),
            shape((4, RUN), F32),
            shape((4, 4, 2, 512, 128), BF16),
            shape((4, 4, 4, 2, 8, 1152), BF16),
            shape((CHIP_ROWS, D), BF16),
            shape((EXPERTS, SLOT, D), BF16),
            shape((TOKENS, 128), BF16),
        ],
        in_specs=[smem, vmem, hbm, hbm] + [vmem] * 9,
        out_specs=[vmem] * 11 + [hbm] * 5,
        scratch_shapes=[
            pltpu.VMEM((2, 4, ROWS, D), BF16),
            pltpu.VMEM((4, 4, 4, 2, 8, 384), BF16),
            pltpu.VMEM((CHIP_ROWS, D), BF16),
            pltpu.VMEM((2, 512, 128), BF16),
            pltpu.VMEM((EXPERTS, SLOT, D), BF16),
            pltpu.VMEM((TOKENS, 128), BF16),
            pltpu.SemaphoreType.DMA((count,)),
            pltpu.SemaphoreType.DMA((count,)),
            pltpu.SemaphoreType.DMA((4,)),
        ],
        compiler_params=pltpu.CompilerParams(
            collective_id=cid, has_side_effects=True, vmem_limit_bytes=VMEM_BYTES
        ),
    )(*inputs)


def turn_tables(step):
    frequency = (np.float32(ROPE_BASE) ** (-np.arange(32, dtype=np.float32) / np.float32(32))).astype(np.float64)
    angles = (np.arange(128) * step)[:, None] * np.tile(frequency, 4)[None, :]
    rest = np.concatenate([np.cos(angles), np.sin(angles)], axis=1)
    parts = []
    for _ in range(3):
        part = rest.astype(np.float32).astype(ml_dtypes.bfloat16)
        parts.append(part)
        rest = rest - part.astype(np.float64)
    return jnp.asarray(np.stack(parts))


def order_pair(order_ref, index):
    row = jnp.broadcast_to(order_ref[index : index + 1, :], (RUN, RUN))
    return row, row.T


def attend_kernel(
    first_ref, count_ref, kv_ref, aux_ref, own_kv_ref, own_aux_ref, q_ref, order_ref,
    att_ref, norm_ref, sent_ref, qx_ref, acc_ref,
):
    def largest(step, best):
        tile = kv_ref[pl.ds(pl.multiple_of(step * 512, 512), 512), :].astype(F32)
        square = jnp.sum(jnp.where(lane_index((512, 128)) < 64, tile * tile, 0.0), axis=1, keepdims=True)
        return jnp.maximum(best, square)

    best = lax.fori_loop(0, TOKENS // 512, largest, jnp.zeros((512, 1), F32))
    key_norm = jnp.sqrt(jnp.max(best, axis=0, keepdims=True))
    lane = lane_index((RUN, 128))
    lane_tall = lane_index((2 * RUN, 128))

    def weights(keys, aux, qx):
        return jnp.exp(mm(qx, jnp.concatenate([keys, aux], axis=1), NT))

    def right(keys):
        return jnp.where(lane_index(keys.shape) < 64, jnp.ones_like(keys), keys)

    for part in range(4):
        rows = pl.ds(part * RUN, RUN)
        own_aux = own_aux_ref[rows, :].astype(F32)
        for head in range(2):
            query = q_ref[head, rows, :]
            wide = query.astype(F32)
            shift = jnp.ceil(jnp.sqrt(jnp.sum(wide * wide, axis=1, keepdims=True)) * key_norm)
            top = shift.astype(BF16).astype(F32)
            middle = (shift - top).astype(BF16).astype(F32)
            rest = shift - top - middle
            ext = jnp.where(lane < 3 + NSEQ, (own_aux - 1.0) * FAR, 0.0)
            ext = jnp.where(lane == 0, -top, ext)
            ext = jnp.where(lane == 1, -middle, ext)
            ext = jnp.where(lane == 2, -rest, ext)
            here = pl.ds(head * RUN, RUN)
            qx_ref[part, here, 0:128] = query
            qx_ref[part, here, 128:256] = ext.astype(BF16)
        qx = qx_ref[part]
        order_key, order_query = order_pair(order_ref, part)
        allowed = order_key <= order_query
        keys = own_kv_ref[rows, :]
        e = weights(keys, own_aux_ref[rows, :], qx)
        e = jnp.where(jnp.concatenate([allowed, allowed], axis=0), e, 0.0)
        acc_ref[...] = mm(e.astype(BF16), right(keys))
        base = (part % 2) * 32

        def tiles(step):
            start = pl.multiple_of(first_ref[base + step], RUN)
            return kv_ref[pl.ds(start, RUN), :], aux_ref[pl.ds(start, RUN), :]

        def pair(step, carry):
            keys_a, aux_a = tiles(2 * step)
            keys_b, aux_b = tiles(2 * step + 1)
            keys = jnp.concatenate([keys_a, keys_b], axis=0)
            aux = jnp.concatenate([aux_a, aux_b], axis=0)
            acc_ref[...] += mm(weights(keys, aux, qx).astype(BF16), right(keys))
            return carry

        number = count_ref[part]
        lax.fori_loop(0, number // 2, pair, 0)

        @pl.when(number % 2 == 1)
        def _():
            keys, aux = tiles(number - 1)
            acc_ref[...] += mm(weights(keys, aux, qx).astype(BF16), right(keys))

        total = acc_ref[...]
        other = pltpu.roll(total, 64, axis=1)
        norm = jnp.where(lane_tall < 64, total, other)
        value = jnp.where(lane_tall < 64, other, total) / norm
        low_lanes = lane < 64
        att = jnp.where(low_lanes, value[:RUN], value[RUN:])
        att_ref[rows, :] = att
        norm_ref[rows, :] = jnp.where(low_lanes, norm[:RUN], norm[RUN:])
        sent_ref[rows, :] = att.astype(BF16)


def attend_back_kernel(
    first_ref, count_ref, base_ref, kv_ref, aux_ref, own_kv_ref, own_aux_ref, qx_ref, order_ref,
    gsent_ref, att_ref, norm_ref, dq_ref, dkv_ref, acc_ref, dq_acc, gx_ref, rhs_ref,
):
    def clear(step, carry):
        acc_ref[pl.ds(pl.multiple_of(step * 512, 512), 512), :] = jnp.zeros((512, 128), F32)
        return carry

    lax.fori_loop(0, TOKENS // 512, clear, 0)
    lane = lane_index((RUN, 128))
    low_lanes = lane < 64
    for part in range(4):
        rows = pl.ds(part * RUN, RUN)
        gsent = gsent_ref[rows, :].astype(F32)
        norm = norm_ref[rows, :]
        product = gsent * att_ref[rows, :] / norm
        scaled = (gsent / norm).astype(BF16).astype(F32)
        for head in range(2):
            mask = low_lanes if head == 0 else jnp.logical_not(low_lanes)
            delta = jnp.sum(jnp.where(mask, product, 0.0), axis=1, keepdims=True)
            top = delta.astype(BF16).astype(F32)
            middle = (delta - top).astype(BF16).astype(F32)
            rest = delta - top - middle
            ext = jnp.where(lane == 0, -top, 0.0)
            ext = jnp.where(lane == 1, -middle, ext)
            ext = jnp.where(lane == 2, -rest, ext)
            grad = pltpu.roll(scaled, 64, axis=1) if head == 0 else scaled
            grad = jnp.where(low_lanes, 0.0, grad).astype(BF16)
            here = pl.ds(head * RUN, RUN)
            gx_ref[here, 0:128] = grad
            gx_ref[here, 128:256] = ext.astype(BF16)
            rhs_ref[pl.ds(head * RUN, RUN), :] = qx_ref[part, here, 0:128]
            rhs_ref[pl.ds((2 + head) * RUN, RUN), :] = grad
        order_key, order_query = order_pair(order_ref, part)
        allowed = order_query <= order_key
        dq_acc[...] = jnp.zeros_like(dq_acc)

        def tile(start, keys, aux, mask):
            both = jnp.concatenate([keys, aux], axis=1)
            e = jnp.exp(mm(both, qx_ref[part], NT))
            if mask is not None:
                e = jnp.where(mask, e, 0.0)
            ds = (e * mm(both, gx_ref[...], NT)).astype(BF16)
            left = jnp.concatenate([ds, e.astype(BF16)], axis=1)
            acc_ref[pl.ds(start, RUN), :] += mm(left, rhs_ref[...])
            dq_acc[...] += mm(keys.T[:64], ds)

        tile(
            pl.multiple_of(base_ref[0] + part * RUN, RUN),
            own_kv_ref[rows, :],
            own_aux_ref[rows, :],
            jnp.concatenate([allowed, allowed], axis=1),
        )
        base = (part % 2) * 32

        def step_tile(step, carry):
            start = pl.multiple_of(first_ref[base + step], RUN)
            tile(start, kv_ref[pl.ds(start, RUN), :], aux_ref[pl.ds(start, RUN), :], None)
            return carry

        lax.fori_loop(0, count_ref[part], step_tile, 0)
        total = dq_acc[...] * 0.125
        dq_ref[rows, :] = jnp.concatenate([total[:, :RUN], total[:, RUN:]], axis=0).T

    def finish(step, carry):
        rows = pl.ds(pl.multiple_of(step * 512, 512), 512)
        dkv_ref[rows, :] = acc_ref[rows, :].astype(BF16)
        return carry

    lax.fori_loop(0, TOKENS // 512, finish, 0)


SLOT_EXPERT = np.arange(SLOTS) // SLOT
SLOT_PLACE = np.arange(SLOTS) % SLOT


def constant(array):
    return jnp.asarray(np.asarray(array).astype(ml_dtypes.bfloat16))


def expand_matrix():
    return constant(np.arange(128)[:, None] == SLOT_EXPERT[None, :])


def place_matrix():
    return constant(SLOT_PLACE[:, None] == np.arange(128)[None, :])


def pick_matrix(place):
    return constant((SLOT_EXPERT[:, None] == np.arange(128)[None, :]) & (SLOT_PLACE[:, None] == place))


def place_column():
    used = np.where(SLOT_PLACE < CAP, SLOT_PLACE, -5)
    return constant(np.broadcast_to(used[:, None], (SLOTS, 128)))


def place_row():
    used = np.where(SLOT_PLACE < CAP, SLOT_PLACE, -5)
    return jnp.asarray(used[None, :].astype(np.float32))


BLOCK = 8 * SLOT
BLOCK_SOURCE = np.arange(BLOCK) // SLOT
BLOCK_PLACE = np.arange(BLOCK) % SLOT


def block_matrix(places):
    hit = np.isin(BLOCK_PLACE, places)[None, :] & (BLOCK_SOURCE[:, None] == BLOCK_SOURCE[None, :])
    return constant(hit)


def packed_pairs(values):
    total = sum(int(value) << (2 * i) for i, value in enumerate(values))
    return np.uint32(total).astype(np.int32)


STEP_Y = packed_pairs([dy for dy, _ in PLANE_ORDER])
STEP_Z = packed_pairs([dz for _, dz in PLANE_ORDER])


def moe_kernel(
    sent_ref, tok_ref, w_out_ref, router_ref, member_ref, put_ref, take_ref, expand_ref,
    expand_t_ref, place_ref, place_t_ref, pick_high_ref, pick_low_ref, pick_t_ref, cot_ref,
    select_ref, block_place_ref, high_ref, low_ref, g_hbm, gate_hbm, up_hbm, down_hbm,
    residual_ref, weigh_high_ref, weigh_low_ref, gmid_ref, branch_ref, gsent_in, side_in,
    y_hbm, grad_gate_hbm, grad_up_hbm, grad_down_hbm,
    sent_in, x_out, x_in, g_v, y_v, back_out, back_in, gate_v, up_v, down_v,
    sum_gate, sum_up, sum_down, grad_gate, grad_up, grad_down, mixed_v, gate_probs, gsent_out, side_out,
    x_send, x_recv, back_send, back_recv, line_send, line_recv, local,
):
    me = position(AXES)
    x_at, y_at, z_at, c_at = (me[axis] for axis in AXES)
    expert = (y_at * 4 + z_at) * 2 + c_at

    def offset(k):
        pair = lax.div(k, 2)
        dy = lax.shift_right_logical(jnp.int32(STEP_Y), 2 * pair) & 3
        dz = lax.shift_right_logical(jnp.int32(STEP_Z), 2 * pair) & 3
        return dy, dz, lax.rem(k + pair, 2)

    def toward(k):
        dy, dz, dc = offset(k)
        return {"y": lax.rem(y_at + dy, 4), "z": lax.rem(z_at + dz, 4), "c": lax.rem(c_at + dc, 2)}

    def source(k):
        dy, dz, dc = offset(k)
        return {
            "y": lax.rem(y_at + 4 - dy, 4),
            "z": lax.rem(z_at + 4 - dz, 4),
            "c": lax.rem(c_at + dc, 2),
        }

    def number(at):
        return (at["y"] * 4 + at["z"]) * 2 + at["c"]

    loads = [
        pltpu.make_async_copy(src, dst, local.at[i])
        for i, (src, dst) in enumerate(
            ((g_hbm, g_v), (gate_hbm, gate_v), (up_hbm, up_v), (down_hbm, down_v))
        )
    ]
    for item in loads:
        item.start()
    barrier = pltpu.get_barrier_semaphore()
    for by in LINE_OFFSETS:
        pl.semaphore_signal(barrier, inc=1, device_id=moved(me, by), device_id_type=MESH)

    def hello(k, carry):
        pl.semaphore_signal(barrier, inc=1, device_id=toward(k), device_id_type=MESH)
        return carry

    lax.fori_loop(0, 31, hello, 0)
    pl.semaphore_wait(barrier, 31 + len(LINE_OFFSETS))

    here_line = x_at * 2 + c_at
    moves = []
    for i, by in enumerate(LINE_OFFSETS):
        to = moved(me, by)
        moves.append(
            remote(sent_ref.at[to["c"] * 4 + to["x"]], sent_in.at[here_line], line_send, line_recv, i, to)
        )
        moves[-1].start()
    kept = pltpu.make_async_copy(sent_ref.at[c_at * 4 + x_at], sent_in.at[here_line], local.at[4])
    kept.start()
    for item in moves + [kept]:
        item.wait()
    sent = jnp.concatenate([sent_in[i] for i in range(8)], axis=1)
    residual = tok_ref[...].astype(F32) + mm(sent, w_out_ref[...])
    residual_ref[...] = residual
    gain = router_ref[...].astype(F32).T[EXPERTS : EXPERTS + 1, :]
    scale = lax.rsqrt(jnp.mean(residual * residual, axis=-1, keepdims=True) + EPSILON)
    mixed = (residual * scale * gain).astype(BF16)
    mixed_v[...] = mixed
    logits = mm(mixed, router_ref[...])
    member = member_ref[...]
    masked = jnp.where(member > 0.5, logits, -FAR)
    top = jnp.max(masked, axis=1, keepdims=True)
    power = jnp.where(member > 0.5, jnp.exp(masked - top), 0.0)
    gate = power / jnp.sum(power, axis=1, keepdims=True)
    gate_probs[...] = gate
    gate_high, gate_low = halves(gate)
    spread = mm(gate_high, expand_ref[...]) + mm(gate_low, expand_ref[...])
    weigh = take_ref[...].astype(F32) * spread
    weigh_high, weigh_low = halves(weigh)
    weigh_high_ref[...] = weigh_high
    weigh_low_ref[...] = weigh_low
    total = jnp.sum(weigh, axis=0, keepdims=True)
    rows_high, rows_low = halves(expand_ref[...].astype(F32) * total)
    rows_high = mm(rows_high, place_ref[...]).astype(BF16)
    rows_low = mm(rows_low, place_ref[...]).astype(BF16)
    gate_rows = mm(pick_high_ref[...], rows_high) + mm(pick_low_ref[...], rows_low)
    put = put_ref[...]

    def slots(value):
        return value.reshape(EXPERTS, SLOT, value.shape[1]).astype(BF16)

    x_out[:, :, 0:128] = slots(mm(put, mixed[:, 0:128]) + gate_rows)
    x_out[:, :, 128:512] = slots(mm(put, mixed[:, 128:512]))
    x_out[:, :, 512:1024] = slots(mm(put, mixed[:, 512:1024]))

    def x_copy(k):
        to = toward(k)
        return remote(x_out.at[number(to)], x_in.at[k], x_send, x_recv, k, to)

    def x_start(k, carry):
        x_copy(k).start()
        return carry

    lax.fori_loop(0, 31, x_start, 0)
    kept = pltpu.make_async_copy(x_out.at[expert], x_in.at[31], local.at[4])
    kept.start()
    kept.wait()
    sum_gate[...] = jnp.zeros_like(sum_gate)
    sum_up[...] = jnp.zeros_like(sum_up)
    sum_down[...] = jnp.zeros_like(sum_down)
    for item in loads:
        item.wait()

    def back_copy(k):
        to = source(k)
        return remote(back_out.at[k], back_in.at[expert], back_send, back_recv, k, to)

    def back_kept():
        return pltpu.make_async_copy(back_out.at[31], back_in.at[expert], local.at[4])

    def group(step, carry):
        first = step * 8
        for i in range(8):
            k = first + i

            @pl.when(k < 31)
            def _():
                x_copy(k).wait_recv()

        x = x_in[pl.ds(first, 8)].astype(F32).reshape(BLOCK, D).astype(BF16)
        g = jnp.concatenate([g_v[number(source(first + i))].astype(F32) for i in range(8)], axis=0)
        place = block_place_ref[...].astype(F32)
        share = jnp.sum(mm(select_ref[...], x[:, :128]) * place, axis=1, keepdims=True)
        a = mm(x, gate_v[...])
        b = mm(x, up_v[...])
        s = 1.0 / (1.0 + jnp.exp(-a))
        silu = a * s
        hidden = (silu * b).astype(BF16)
        y = mm(hidden, down_v[...]).astype(BF16).astype(F32)
        dgate = jnp.sum(y * g, axis=1, keepdims=True)
        y = y.reshape(8, SLOT, D)
        for i in range(8):
            y_v[number(source(first + i))] = y[i].astype(BF16)
        gy = (g * share).astype(BF16)
        dhidden = mm(gy, down_v[...], NT)
        da = (dhidden * b * (s * (1.0 + a * (1.0 - s)))).astype(BF16)
        db = (dhidden * silu).astype(BF16)
        back = mm(da, gate_v[...], NT) + mm(db, up_v[...], NT)
        dgate_high, dgate_low = halves(dgate * place)
        lead = back[:, 0:128] + mm(high_ref[...], dgate_high) + mm(low_ref[...], dgate_low)
        span = pl.ds(first, 8)
        back_out[span, :, 0:128] = lead.reshape(8, SLOT, 128).astype(BF16)
        back_out[span, :, 128:1024] = back[:, 128:1024].reshape(8, SLOT, 896).astype(BF16)
        for i in range(8):
            k = first + i

            @pl.when(k < 31)
            def _():
                back_copy(k).start()

            @pl.when(k == 31)
            def _():
                back_kept().start()

        sum_gate[...] += mm(x, da, TN)
        sum_up[...] += mm(x, db, TN)
        sum_down[...] += mm(hidden, gy, TN)
        return carry

    lax.fori_loop(0, 4, group, 0)
    grad_gate[...] = sum_gate[...].astype(BF16)
    grad_up[...] = sum_up[...].astype(BF16)
    grad_down[...] = sum_down[...].astype(BF16)
    stores = [
        pltpu.make_async_copy(src, dst, local.at[i])
        for i, (src, dst) in enumerate(
            ((y_v, y_hbm), (grad_gate, grad_gate_hbm), (grad_up, grad_up_hbm), (grad_down, grad_down_hbm))
        )
    ]
    for item in stores:
        item.start()

    def settle(k, carry):
        x_copy(k).wait_send()
        back_copy(k).wait()
        return carry

    lax.fori_loop(0, 31, settle, 0)
    back_kept().wait()

    take = take_ref[...]
    rows_high, rows_low = halves(
        sum(
            mm(
                pick_t_ref[:, i * 640 : (i + 1) * 640],
                back_in[i * 16 : (i + 1) * 16, :, 0:128].astype(F32).reshape(640, 128).astype(BF16),
            )
            for i in range(2)
        )
    )
    spread = mm(rows_high, place_t_ref[...]) + mm(rows_low, place_t_ref[...])
    along = jnp.sum(spread * expand_ref[...].astype(F32), axis=0, keepdims=True)
    found_high, found_low = halves(take.astype(F32) * along)
    dgate = mm(found_high, expand_t_ref[...]) + mm(found_low, expand_t_ref[...])
    gate = gate_probs[...]
    dlogits = gate * (dgate - jnp.sum(gate * dgate, axis=1, keepdims=True))
    dlogits = dlogits.astype(BF16)
    dmixed = mm(dlogits, router_ref[...], NT)
    for i in range(2):
        rows = back_in[i * 16 : (i + 1) * 16].astype(F32).reshape(640, D).astype(BF16)
        dmixed += mm(take[:, i * 640 : (i + 1) * 640], rows)
    residual = residual_ref[...]
    scale = lax.rsqrt(jnp.mean(residual * residual, axis=-1, keepdims=True) + EPSILON)
    gain = router_ref[...].astype(F32).T[EXPERTS : EXPERTS + 1, :]
    weighted = dmixed * gain
    inner = jnp.mean(weighted * residual, axis=-1, keepdims=True)
    gmid = cot_ref[...].astype(F32) + scale * weighted - residual * (scale * scale * scale) * inner
    gmid_ref[...] = gmid
    branch = gmid.astype(BF16)
    branch_ref[...] = branch
    gsent = mm(branch, w_out_ref[...], NT).astype(BF16)
    for i in range(8):
        gsent_out[i] = gsent[:, i * 128 : (i + 1) * 128]
    back_line = c_at * 4 + x_at
    moves = []
    for i, by in enumerate(LINE_OFFSETS):
        to = moved(me, by)
        moves.append(
            remote(
                gsent_out.at[to["x"] * 2 + to["c"]], gsent_in.at[back_line], line_send, line_recv, 7 + i, to
            )
        )
        moves[-1].start()
    kept = pltpu.make_async_copy(gsent_out.at[here_line], gsent_in.at[back_line], local.at[4])
    kept.start()
    moves.append(kept)
    gain_grad = jnp.sum(dmixed * residual * scale, axis=0, keepdims=True)
    grads = mm(dlogits, mixed_v[...], TN)
    row = lax.broadcasted_iota(jnp.int32, (128, D), 0)
    grads = jnp.where(row == EXPERTS, gain_grad, grads).T.reshape(4, 16, 2, 8, 128)
    for i in range(8):
        side_out[i] = grads[i // 2, :, i % 2].reshape(ROWS, 128).astype(BF16)
    for i, by in enumerate(LINE_OFFSETS):
        to = moved(me, by)
        moves.append(
            remote(
                side_out.at[to["x"] * 2 + to["c"]], side_in.at[back_line], line_send, line_recv, 14 + i, to
            )
        )
        moves[-1].start()
    kept = pltpu.make_async_copy(side_out.at[here_line], side_in.at[back_line], local.at[5])
    kept.start()
    for item in moves + [kept] + stores:
        item.wait()


def moe(inputs, cid):
    vmem = pl.BlockSpec(memory_space=pltpu.VMEM)
    hbm = pl.BlockSpec(memory_space=pl.ANY)
    slots = (EXPERTS, SLOT, D)
    up, down = (D, FF), (FF, D)
    dma = pltpu.SemaphoreType.DMA
    return pl.pallas_call(
        moe_kernel,
        grid=(1,),
        out_shape=[
            shape((ROWS, D), F32),
            shape((ROWS, SLOTS), BF16),
            shape((ROWS, SLOTS), BF16),
            shape((ROWS, D), F32),
            shape((ROWS, D), BF16),
            shape((8, ROWS, 128), BF16),
            shape((8, ROWS, 128), BF16),
            shape(slots, BF16),
            shape(up, BF16),
            shape(up, BF16),
            shape(down, BF16),
        ],
        in_specs=[vmem] * 2 + [OUT_BLOCK, SIDE_BLOCK] + [vmem] * 15 + [hbm] * 4,
        out_specs=[vmem] * 7 + [hbm] * 4,
        scratch_shapes=[
            pltpu.VMEM((8, ROWS, 128), BF16),
            pltpu.VMEM(slots, BF16),
            pltpu.VMEM(slots, BF16),
            pltpu.VMEM(slots, BF16),
            pltpu.VMEM(slots, BF16),
            pltpu.VMEM(slots, BF16),
            pltpu.VMEM(slots, BF16),
            pltpu.VMEM(up, BF16),
            pltpu.VMEM(up, BF16),
            pltpu.VMEM(down, BF16),
            pltpu.VMEM(up, F32),
            pltpu.VMEM(up, F32),
            pltpu.VMEM(down, F32),
            pltpu.VMEM(up, BF16),
            pltpu.VMEM(up, BF16),
            pltpu.VMEM(down, BF16),
            pltpu.VMEM((ROWS, D), BF16),
            pltpu.VMEM((ROWS, 128), F32),
            pltpu.VMEM((8, ROWS, 128), BF16),
            pltpu.VMEM((8, ROWS, 128), BF16),
            dma((31,)),
            dma((31,)),
            dma((31,)),
            dma((31,)),
            dma((21,)),
            dma((21,)),
            dma((6,)),
        ],
        compiler_params=pltpu.CompilerParams(
            collective_id=cid, has_side_effects=True, vmem_limit_bytes=VMEM_BYTES
        ),
    )(*inputs)


def finish_kernel(
    dq_ref, dkv_ref, cos_ref, sin_ref, normed_ref, w_ref,
    y_ref, weigh_high_ref, weigh_low_ref, residual_ref, out_ref, side_ref,
    dnormed_out, mixed_out, grads_out, early_out,
    dqkv, part_out, part_in, part_own, line_out, line_in, share_out, share_in, total,
    out_in, side_in, send, recv, local, out_recv,
):
    me = position(AXES)
    x, y, z, c = (me[axis] for axis in AXES)
    mine = y * 4 + z
    alone = jnp.where(c == lax.div(y, 2), 1, 0)
    barrier = pltpu.get_barrier_semaphore()

    def owner(k):
        at = lax.rem(lax.rem(y, 2) * 8 + z * 2 + c + k, 16)
        to = {"y": 2 * c + lax.div(at, 8), "z": lax.rem(lax.div(at, 2), 4), "c": lax.rem(at, 2)}
        return at, to

    def origin(k):
        at = lax.rem(mine + k, 16)
        return at, {"y": lax.div(at, 4), "z": lax.rem(at, 4), "c": lax.div(y, 2)}

    for k in range(1, 16):
        pl.semaphore_signal(barrier, inc=1, device_id=origin(k)[1], device_id_type=MESH)

    @pl.when(alone == 0)
    def _():
        pl.semaphore_signal(barrier, inc=1, device_id=origin(0)[1], device_id_type=MESH)

    offsets = LINE_OFFSETS + PLANE_OFFSETS
    for offset in offsets:
        pl.semaphore_signal(barrier, inc=1, device_id=moved(me, offset), device_id_type=MESH)
    pl.semaphore_wait(barrier, len(offsets) + 16 - alone)
    used = [0]

    def go(src, dst, to):
        item = remote(src, dst, send, recv, used[0], to)
        used[0] += 1
        item.start()
        return item

    other = 1 - c
    low_lanes = lane_index((256, 128)) < 64

    def out_copy(k):
        at, to = owner(k)
        return pltpu.make_async_remote_copy(
            src_ref=out_ref.at[at], dst_ref=out_in.at[mine], send_sem=send.at[used[0] + k],
            recv_sem=out_recv.at[mine], device_id=to, device_id_type=MESH,
        )

    def out_kept():
        return pltpu.make_async_copy(out_ref.at[owner(0)[0]], out_in.at[mine], local.at[1])

    out_copies = [out_copy(k) for k in range(16)]
    used[0] += 16
    out_arrivals = []
    for k in range(16):
        at, to = origin(k)
        out_arrivals.append(
            pltpu.make_async_remote_copy(
                src_ref=out_ref.at[0], dst_ref=out_in.at[at], send_sem=send.at[0],
                recv_sem=out_recv.at[at], device_id=to, device_id_type=MESH,
            )
        )

    @pl.when(alone == 0)
    def _():
        out_copies[0].start()

    @pl.when(alone == 1)
    def _():
        out_kept().start()

    for item in out_copies[1:]:
        item.start()
    early = []
    for offset in PLANE_OFFSETS:
        to = moved(me, offset)
        early.append(go(side_ref.at[to["y"] * 4 + to["z"]], side_in.at[mine], to))
    side_kept = pltpu.make_async_copy(side_ref.at[mine], side_in.at[mine], local.at[2])
    side_kept.start()
    early.append(side_kept)

    def turn_back(first):
        rows = pl.ds(pl.multiple_of(first, 256), 256)
        cos, sin = cos_ref[rows, :], sin_ref[rows, :]
        dq, dkv = dq_ref[rows, :], dkv_ref[rows, :]
        dq = (dq * cos - turned(dq) * sin).astype(BF16)
        dkv = jnp.where(low_lanes, dkv * cos - turned(dkv) * sin, dkv).astype(BF16)
        both = jnp.concatenate([dq, dkv], axis=1)
        dqkv[rows, :] = both
        return mm(both, w_ref[:, 0:256], NT)

    crossing = []
    for i in range(2):
        value = turn_back(other * 512 + i * 256).astype(BF16)
        part_out[2 * i] = value[:ROWS]
        part_out[2 * i + 1] = value[ROWS:]
        span = pl.ds(2 * i, 2)
        crossing.append(go(part_out.at[span], part_in.at[span], {"c": other}))
    for i in range(2):
        value = turn_back(c * 512 + i * 256)
        part_own[2 * i] = value[:ROWS]
        part_own[2 * i + 1] = value[ROWS:]
    for item in crossing:
        item.wait()
    along = []
    for i, by in enumerate((2, 1, 3)):
        to = lax.rem(x + by, 4)
        line_out[i] = (part_own[to] + part_in[to].astype(F32)).astype(BF16)
        along.append(go(line_out.at[i], line_in.at[i], {"x": to}))
    for i in range(4):
        columns = pl.ds(i * 256, 256)
        grad = mm(normed_ref[:, columns], dqkv[...], TN).astype(BF16)
        share_out[i] = grad.reshape(16, 16, 256)
    spread = []
    for offset in PLANE_OFFSETS:
        to = moved(me, offset)
        spread.append(go(share_out.at[:, to["y"] * 4 + to["z"]], share_in.at[mine], to))
    kept = pltpu.make_async_copy(share_out.at[:, mine], share_in.at[mine], local.at[0])
    kept.start()
    mixed = mm(weigh_high_ref[...], y_ref[...]) + mm(weigh_low_ref[...], y_ref[...])
    mixed_out[...] = (residual_ref[...] + mixed).astype(BF16)
    for item in spread + [kept]:
        item.wait()
    for i in range(4):
        value = share_in[0, i].astype(F32)
        for j in range(1, 16):
            value += share_in[j, i].astype(F32)
        total[i] = value.reshape(2, 8, 256)
    ends = []
    here = x * 2 + c
    for offset in LINE_OFFSETS:
        to = moved(me, offset)
        ends.append(go(total.at[to["x"], to["c"]], grads_out.at[here], to))
    kept = pltpu.make_async_copy(total.at[x, c], grads_out.at[here], local.at[0])
    kept.start()
    for item in out_copies[1:]:
        item.wait_send()
    for item in out_arrivals[1:]:
        item.wait_recv()

    @pl.when(alone == 0)
    def _():
        out_copies[0].wait_send()
        out_arrivals[0].wait_recv()

    @pl.when(alone == 1)
    def _():
        out_kept().wait()

    for item in early:
        item.wait()
    out_total, side_total = out_in[0], side_in[0]
    for j in range(1, 16):
        out_total += out_in[j]
        side_total += side_in[j]
    early_out[:, 0:D] = out_total
    early_out[:, D : D + 128] = side_total
    for item in along:
        item.wait()
    dnormed = part_own[x] + part_in[x].astype(F32)
    for i in range(3):
        dnormed += line_in[i].astype(F32)
    dnormed_out[...] = dnormed
    for item in ends + [kept]:
        item.wait()


def finish(inputs, cid):
    count = 2 + 3 + 15 + 7 + 16 + 15
    return pl.pallas_call(
        finish_kernel,
        out_shape=[
            jax.ShapeDtypeStruct((ROWS, D), F32),
            jax.ShapeDtypeStruct((ROWS, D), BF16),
            jax.ShapeDtypeStruct((8, 8, 256), F32),
            jax.ShapeDtypeStruct((8, D + 128), F32),
        ],
        in_specs=[pl.BlockSpec(memory_space=pltpu.VMEM)] * 12,
        out_specs=[pl.BlockSpec(memory_space=pltpu.VMEM)] * 4,
        scratch_shapes=[
            pltpu.VMEM((CHIP_ROWS, 256), BF16),
            pltpu.VMEM((4, ROWS, D), BF16),
            pltpu.VMEM((4, ROWS, D), BF16),
            pltpu.VMEM((4, ROWS, D), F32),
            pltpu.VMEM((3, ROWS, D), BF16),
            pltpu.VMEM((3, ROWS, D), BF16),
            pltpu.VMEM((4, 16, 16, 256), BF16),
            pltpu.VMEM((16, 4, 16, 256), BF16),
            pltpu.VMEM((4, 2, 8, 256), F32),
            pltpu.VMEM((16, 8, D), F32),
            pltpu.VMEM((16, 8, 128), F32),
            pltpu.SemaphoreType.DMA((count,)),
            pltpu.SemaphoreType.DMA((count,)),
            pltpu.SemaphoreType.DMA((3,)),
            pltpu.SemaphoreType.DMA((16,)),
        ],
        compiler_params=pltpu.CompilerParams(
            collective_id=cid, has_side_effects=True, vmem_limit_bytes=VMEM_BYTES
        ),
    )(*inputs)


def last_kernel(
    dnormed_ref, tok_ref, gain_ref, gmid_ref, mixed_ref, rows_ref, w_ref, own_gain_ref, early_ref,
    gate_ref, up_ref, down_ref,
    tokens_out, mixed_out, query_out, key_out, value_out, gains_out, grad_out, router_out,
    gate_out, up_out, down_out,
):
    tok = tok_ref[...].astype(F32)
    scale = lax.rsqrt(jnp.mean(tok * tok, axis=-1, keepdims=True) + EPSILON)
    weighted = dnormed_ref[...] * gain_ref[...]
    inner = jnp.mean(weighted * tok, axis=-1, keepdims=True)
    tokens_out[...] = gmid_ref[...] + scale * weighted - tok * (scale * scale * scale) * inner
    mixed_out[...] = mixed_ref[...]
    total = jnp.zeros((8, 256), F32)
    for i in range(8):
        rows = rows_ref[i]
        query_out[:, i * 128 : (i + 1) * 128] = rows[:, :128]
        total += rows * w_ref[:, i * 256 : (i + 1) * 256].astype(F32)
    lanes = lane_index((8, 128)) < 64
    for i in range(4):
        first, second = rows_ref[2 * i][:, 128:], rows_ref[2 * i + 1][:, 128:]
        key_out[:, i * 128 : (i + 1) * 128] = jnp.where(lanes, first, pltpu.roll(second, 64, axis=1))
        value_out[:, i * 128 : (i + 1) * 128] = jnp.where(lanes, pltpu.roll(first, 64, axis=1), second)
    gain_one = jnp.broadcast_to(jnp.sum(total, axis=1, keepdims=True), (8, 128)).T[0:1, :]
    side = early_ref[:, D : D + 128]
    gain_two = side.T[EXPERTS : EXPERTS + 1, :]
    gains_out[0:1, :] = gain_one[:, 0:8] / own_gain_ref[...]
    gains_out[1:2, :] = gain_two[:, 0:8]
    grad_out[...] = early_ref[:, 0:D]
    router_out[...] = side[:, 0:EXPERTS]
    gate_out[...] = gate_ref[...].astype(F32)
    up_out[...] = up_ref[...].astype(F32)
    down_out[...] = down_ref[...].astype(F32)


WHOLE = pl.BlockSpec(memory_space=pltpu.VMEM)
OUT_BLOCK = pl.BlockSpec((D, D), lambda i: (0, 0))
SIDE_BLOCK = pl.BlockSpec((D, 128), lambda i: (0, 8))


def shape(dims, dtype):
    return jax.ShapeDtypeStruct(dims, dtype)


def body(
    tokens,
    gain_one,
    w_query,
    w_key,
    w_value,
    w_out,
    gain_two,
    w_router,
    w_gate,
    w_up,
    w_down,
    dealt_order,
    lengths,
    routes,
    cotangent,
):
    y_at, z_at = lax.axis_index("y"), lax.axis_index("z")
    first_row = (y_at * 4 + z_at) * CHIP_ROWS

    grouped = jnp.concatenate(
        [
            w_query.reshape(8, 8, 128),
            w_key.reshape(8, 8, 64),
            w_value.reshape(8, 8, 64),
        ],
        axis=2,
    )
    gain_lane = jnp.where(jnp.arange(128)[None, :] == 0, gain_one[:, None], 0).astype(BF16)
    first_pack = jnp.concatenate(
        [grouped.transpose(1, 0, 2), jnp.broadcast_to(gain_lane[None], (8, 8, 128))], axis=2
    )
    second_pack = jnp.concatenate(
        [w_out, w_router, gain_two[:, None], jnp.zeros((8, 95), BF16)], axis=1
    )
    expand, expand_t = expand_matrix(), expand_matrix().T
    place, place_t = place_matrix(), place_matrix().T
    pick_high, pick_low = pick_matrix(CAP), pick_matrix(CAP + 1)
    (
        query, kv, gain_first, cos, sin, w_mine, member, put, take, own_aux, order_rows,
        kv_all, w_late, normed, g_out, aux,
    ) = front(
        (
            lengths, tokens, first_pack, second_pack, dealt_order.reshape(128, 128), routes, cotangent,
            expand, expand_t, place_column(), place_row(), turn_tables(128), turn_tables(1),
        ),
        1,
    )
    kv_all = kv_all.reshape(TOKENS, 128)
    w_late = w_late.reshape(D, 1152)
    plane = ("y", "z", "c")
    g_in = lax.all_to_all(g_out, plane, split_axis=0, concat_axis=0, tiled=True)

    run_of = dealt_order.reshape(32, 512)[:, 0] // RUN
    block_ids = jnp.arange(32, dtype=jnp.int32)
    block_of = jnp.sum(
        jnp.where(run_of[None, :] == block_ids[:, None], block_ids[None, :], 0), axis=1
    )
    first_rows = jnp.concatenate([block_of * 512, block_of[::-1] * 512 + RUN])
    mine = lax.dynamic_slice_in_dim(run_of, (y_at * 4 + z_at) * 2, 2)
    counts = jnp.stack([mine[0], 31 - mine[0], mine[1], 31 - mine[1]])
    base = first_row.reshape(1).astype(jnp.int32)
    smem = pl.BlockSpec(memory_space=pltpu.SMEM)
    vmem = pl.BlockSpec(memory_space=pltpu.VMEM)
    att, norm, sent, query_ext = local_call(
        attend_kernel,
        (
            shape((CHIP_ROWS, 128), F32),
            shape((CHIP_ROWS, 128), F32),
            shape((CHIP_ROWS, 128), BF16),
            shape((4, 2 * RUN, 256), BF16),
        ),
        scratch=[pltpu.VMEM((2 * RUN, 128), F32)],
        in_specs=[smem] * 2 + [vmem] * 6,
    )(first_rows, counts, kv_all, aux, kv, own_aux, query, order_rows)

    (
        residual, weigh_high, weigh_low, gmid, branch, gsent_own, side_rows, y_out,
        grad_gate, grad_up, grad_down,
    ) = moe(
        (
            sent.reshape(8, ROWS, 128), tokens, w_late, w_late, member, put, take, expand, expand_t,
            place, place_t, pick_high, pick_low, (pick_high + pick_low).T, cotangent,
            block_matrix((CAP, CAP + 1)),
            place[:BLOCK],
            block_matrix((CAP,)).T * constant(BLOCK_PLACE == CAP)[:, None],
            block_matrix((CAP + 1,)).T * constant(BLOCK_PLACE == CAP + 1)[:, None],
            g_in, w_gate[0], w_up[0], w_down[0],
        ),
        3,
    )
    y_in = lax.all_to_all(
        y_out, plane, split_axis=0, concat_axis=0, tiled=True
    ).reshape(SLOTS, D)
    grad_gate, grad_up, grad_down = (
        lax.psum_scatter(grad, "x", scatter_dimension=0, tiled=True)
        for grad in (grad_gate, grad_up, grad_down)
    )

    gsent_own = gsent_own.reshape(CHIP_ROWS, 128)
    branch_rows = lax.all_gather(branch, ("c", "x"), axis=0, tiled=True)
    side_sum = jnp.sum(side_rows.astype(F32), axis=0)

    dq, dkv = local_call(
        attend_back_kernel,
        (shape((CHIP_ROWS, 128), F32), shape((TOKENS, 128), BF16)),
        scratch=[
            pltpu.VMEM((TOKENS, 128), F32),
            pltpu.VMEM((64, 2 * RUN), F32),
            pltpu.VMEM((2 * RUN, 256), BF16),
            pltpu.VMEM((4 * RUN, 128), BF16),
        ],
        in_specs=[smem] * 3 + [vmem] * 9,
    )(
        first_rows, counts, base, kv_all, aux, kv, own_aux, query_ext, order_rows, gsent_own, att,
        norm,
    )
    dkv_own, grad_out = scatter_plane(dkv, sent, branch_rows, 6)

    dnormed, mixed, qkv_rows, early = finish(
        (
            dq, dkv_own, cos, sin, normed, w_mine, y_in, weigh_high, weigh_low, residual,
            grad_out.reshape(16, 8, D), side_sum.reshape(16, 8, 128),
        ),
        7,
    )
    (
        grad_tokens, mixed, grad_query, grad_key, grad_value, gains, grad_out_rows, grad_router,
        grad_gate, grad_up, grad_down,
    ) = local_call(
        last_kernel,
        (
            shape((ROWS, D), F32),
            shape((ROWS, D), BF16),
            shape((8, D), F32),
            shape((8, 512), F32),
            shape((8, 512), F32),
            shape((2, 8), F32),
            shape((8, D), F32),
            shape((8, EXPERTS), F32),
            shape((256, FF), F32),
            shape((256, FF), F32),
            shape((128, D), F32),
        ),
    )(
        dnormed, tokens, gain_first, gmid, mixed, qkv_rows, grouped.reshape(8, 2048),
        gain_one.astype(F32).reshape(1, 8), early, grad_gate, grad_up, grad_down,
    )
    grad_gain_one, grad_gain_two = gains[0], gains[1]
    grad_gate, grad_up, grad_down = grad_gate[None], grad_up[None], grad_down[None]
    return (
        mixed,
        grad_tokens,
        grad_gain_one,
        grad_query,
        grad_key,
        grad_value,
        grad_out_rows,
        grad_gain_two,
        grad_router,
        grad_gate,
        grad_up,
        grad_down,
    )


def solution(mesh):
    grid = Mesh(mesh.devices.reshape(4, 4, 4, 2), AXES)
    rows = P(("y", "z", "c", "x"), None)
    vector = P(AXES)
    matrix = P(AXES, None)
    expert = P(("y", "z", "c"), None, None)
    in_specs = (
        rows, vector, matrix, matrix, matrix, matrix, vector, matrix, expert, expert, expert,
        P(), P(), rows, rows,
    )
    grads = P(("y", "z", "c"), "x", None)
    out_specs = (
        rows, rows, vector, matrix, matrix, matrix, matrix, vector, matrix, grads, grads, grads,
    )
    return jax.shard_map(body, mesh=grid, in_specs=in_specs, out_specs=out_specs, check_vma=False)
```

```python
import functools
import math

import jax
import jax.numpy as jnp
import ml_dtypes
import numpy as np
from jax import lax
from jax.experimental import pallas as pl
from jax.experimental.pallas import tpu as pltpu
from jax.sharding import Mesh
from jax.sharding import PartitionSpec as P

D = 1024
HEADS = 16
KV_HEADS = 8
HEAD_DIM = 64
EXPERTS = 32
FF = 512
CAP = 36
SLOT = 40
SLOTS = EXPERTS * SLOT
ROWS = 128
CHIP_ROWS = 1024
RUN = 256
TOKENS = 16384
NSEQ = 5
EPSILON = 1e-06
ROPE_BASE = 10000.0
FAR = float(2.0**100)
SIZE = {"x": 4, "y": 4, "z": 4, "c": 2}
AXES = ("x", "y", "z", "c")
MESH = pl.DeviceIdType.MESH
BF16 = jnp.bfloat16
F32 = jnp.float32
NN = (((1,), (0,)), ((), ()))
NT = (((1,), (1,)), ((), ()))
TN = (((0,), (0,)), ((), ()))
VMEM_BYTES = 56 * 1024 * 1024


def mm(a, b, dims=NN):
    return lax.dot_general(a, b, dims, preferred_element_type=F32)


def shape(dims, dtype):
    return jax.ShapeDtypeStruct(dims, dtype)


def halves(value):
    high = value.astype(BF16)
    return high, (value - high.astype(F32)).astype(BF16)


def local_call(kernel, outs, scratch=(), grid=None, in_specs=None, out_specs=None):
    extra = {}
    if grid is not None:
        extra = {"grid": grid, "in_specs": in_specs, "out_specs": out_specs}
    elif in_specs is not None:
        extra = {"in_specs": in_specs}
        if out_specs is not None:
            extra["out_specs"] = out_specs
    return pl.pallas_call(
        kernel,
        out_shape=outs,
        scratch_shapes=list(scratch),
        compiler_params=pltpu.CompilerParams(vmem_limit_bytes=VMEM_BYTES),
        **extra,
    )


class Late:
    def __init__(self, hbm, vmem, sem, columns):
        self.hbm, self.vmem = hbm, vmem
        source = hbm if columns is None else hbm.at[:, columns[0] : columns[1]]
        self.copy, self.ready = pltpu.make_async_copy(source, vmem, sem), False
        self.copy.start()

    def get(self):
        if not self.ready:
            self.copy.wait()
            self.ready = True
        return self.vmem

    def __getitem__(self, index):
        return self.get()[index]


class Early:
    def __init__(self, hbm, vmem, sem):
        self.vmem, self.copy = vmem, pltpu.make_async_copy(vmem, hbm, sem)

    def __getitem__(self, index):
        return self.vmem[index]

    def __setitem__(self, index, value):
        self.vmem[index] = value

    def store(self):
        self.copy.start()


def remote_call(kernel, inputs, kinds, outs, out_kinds, scratch, cid):
    spaces = {"s": pltpu.SMEM, "v": pltpu.VMEM}
    late = [(i, kind) for i, kind in enumerate(kinds) if kind not in ("s", "v", "h")]
    early = [i for i, kind in enumerate(out_kinds) if kind == "e"]

    def late_shape(i, kind):
        dims = inputs[i].shape if kind == "l" else (inputs[i].shape[0], kind[1] - kind[0])
        return pltpu.VMEM(dims, inputs[i].dtype)

    def wrapped(*refs):
        ins, rest = list(refs[: len(inputs)]), list(refs[len(inputs) :])
        results, rest = rest[: len(outs)], rest[len(outs) :]
        own, rest = rest[: len(scratch)], rest[len(scratch) :]
        late_v, rest = rest[: len(late)], rest[len(late) :]
        early_v, (late_sem, early_sem) = rest[: len(early)], rest[len(early) :]
        for n, (i, kind) in enumerate(late):
            ins[i] = Late(ins[i], late_v[n], late_sem.at[n], None if kind == "l" else kind)
        for n, i in enumerate(early):
            results[i] = Early(results[i], early_v[n], early_sem.at[n])
        kernel(*ins, *results, *own)
        for i, _ in late:
            ins[i].get()
        for i in early:
            results[i].copy.wait()

    return pl.pallas_call(
        wrapped,
        out_shape=list(outs),
        in_specs=[pl.BlockSpec(memory_space=spaces.get(kind, pl.ANY)) for kind in kinds],
        out_specs=[pl.BlockSpec(memory_space=spaces.get(kind, pl.ANY)) for kind in out_kinds],
        scratch_shapes=list(scratch)
        + [late_shape(i, kind) for i, kind in late]
        + [pltpu.VMEM(outs[i].shape, outs[i].dtype) for i in early]
        + [pltpu.SemaphoreType.DMA((max(1, len(late)),)), pltpu.SemaphoreType.DMA((max(1, len(early)),))],
        compiler_params=pltpu.CompilerParams(
            collective_id=cid, has_side_effects=True, vmem_limit_bytes=VMEM_BYTES
        ),
    )(*inputs)


def flat_index(coords, order):
    index = 0
    for axis in order:
        index = index * SIZE[axis] + coords[axis]
    return index


PLANE_ORDER = (
    (2, 2), (2, 3), (2, 1), (3, 2), (1, 2), (0, 2), (2, 0), (3, 1), (1, 3),
    (3, 3), (1, 1), (0, 3), (0, 1), (3, 0), (1, 0), (0, 0),
)
PLANE_OFFSETS = tuple({"y": dy, "z": dz} for dy, dz in PLANE_ORDER[:-1])
SPREAD_OFFSETS = tuple(
    {"y": dy, "z": dz, "c": (dc + i + 1) % 2}
    for i, (dy, dz) in enumerate(PLANE_ORDER)
    for dc in range(2)
    if (dy, dz, (dc + i + 1) % 2) != (0, 0, 0)
)
LINE_OFFSETS = tuple(
    {"x": dx, "c": dc} for dx, dc in ((2, 0), (2, 1), (1, 0), (3, 0), (1, 1), (3, 1), (0, 1))
)
OFFSETS = {("y", "z"): PLANE_OFFSETS, ("y", "z", "c"): SPREAD_OFFSETS, ("x", "c"): LINE_OFFSETS}


def position(axes):
    return {axis: lax.axis_index(axis) for axis in axes}


def moved(me, offset):
    return {axis: lax.rem(me[axis] + by, SIZE[axis]) if by else me[axis] for axis, by in offset.items()}


def greet(me, offsets):
    barrier = pltpu.get_barrier_semaphore()
    for offset in offsets:
        pl.semaphore_signal(barrier, inc=1, device_id=moved(me, offset), device_id_type=MESH)
    pl.semaphore_wait(barrier, len(offsets))


def remote(src, dst, send, recv, slot, to):
    return pltpu.make_async_remote_copy(
        src_ref=src,
        dst_ref=dst,
        send_sem=send.at[slot],
        recv_sem=recv.at[slot],
        device_id=to,
        device_id_type=MESH,
    )


def exchange_kernel(axes, dest_order, src_order, arrays, *refs):
    x_refs, o_refs = refs[:arrays], refs[arrays : 2 * arrays]
    send, recv, local = refs[2 * arrays :]
    me = position(axes)
    offsets = OFFSETS[axes]
    greet(me, offsets)
    here = flat_index(me, src_order)
    copies = []
    for offset in offsets:
        to = moved(me, offset)
        for x_ref, o_ref in zip(x_refs, o_refs):
            copies.append(
                remote(
                    x_ref.at[flat_index(to, dest_order)], o_ref.at[here], send, recv, len(copies), to
                )
            )
            copies[-1].start()
    kept = [
        pltpu.make_async_copy(
            x_ref.at[flat_index(me, dest_order)], o_ref.at[here], local.at[i]
        )
        for i, (x_ref, o_ref) in enumerate(zip(x_refs, o_refs))
    ]
    for item in kept:
        item.start()
    for item in kept + copies:
        item.wait()


def exchange(data, axes, cid, dest_order=None, src_order=None):
    single = not isinstance(data, (tuple, list))
    data = [data] if single else list(data)
    dest_order = dest_order or axes
    src_order = src_order or axes
    arrays = len(data)
    count = len(OFFSETS[axes]) * arrays
    out = pl.pallas_call(
        functools.partial(exchange_kernel, axes, dest_order, src_order, arrays),
        out_shape=[jax.ShapeDtypeStruct(item.shape, item.dtype) for item in data],
        in_specs=[pl.BlockSpec(memory_space=pl.ANY)] * arrays,
        out_specs=[pl.BlockSpec(memory_space=pl.ANY)] * arrays,
        scratch_shapes=[
            pltpu.SemaphoreType.DMA((count,)),
            pltpu.SemaphoreType.DMA((count,)),
            pltpu.SemaphoreType.DMA((arrays,)),
        ],
        compiler_params=pltpu.CompilerParams(collective_id=cid, has_side_effects=True),
    )(*data)
    return out[0] if single else out


AROUND = ({"y": 1, "z": 0}, {"y": 3, "z": 0}, {"y": 0, "z": 1}, {"y": 0, "z": 3})


def scatter_plane_kernel(p_ref, sent_ref, branch_ref, o_ref, grad_ref, far_a, near_a, out_a, sum_a, far_b, near_b, out_b, send, recv):
    me = position(("y", "z"))
    greet(me, AROUND)
    half = p_ref.vmem.shape[3] // 2
    lower, upper = pl.ds(0, half), pl.ds(half, half)
    axis = (("y", "z"), ("z", "y"))
    used = [0]

    def go(src, dst, t, which, by):
        to = {axis[t][which]: lax.rem(me[axis[t][which]] + by, 4)}
        item = remote(src, dst, send, recv, used[0], to)
        used[0] += 1
        item.start()
        return item

    def part(t, first, second, hbm=False):
        a = lax.rem(me[axis[t][0]] + first, 4)
        b = lax.rem(me[axis[t][1]] + second, 4)
        ref = p_ref.hbm if hbm else p_ref.get()
        return ref.at[a, b, 0] if t == 0 else ref.at[b, a, 1]

    turns = (2, 1, 3, 0)
    both = (0, 1)
    far, near = {}, {}
    for k, by in enumerate(turns):
        for t in both:
            far[k, t] = (
                go(part(t, 2, by, True).at[lower], far_a.at[t, k, 0], t, 0, 1),
                go(part(t, 2, by, True).at[upper], far_a.at[t, k, 1], t, 0, 3),
            )
    grad_ref[...] = mm(sent_ref[...], branch_ref[...], TN)
    for k, by in enumerate(turns):
        for t in both:
            ahead, behind = part(t, 1, by), part(t, 3, by)
            far[k, t][0].wait()
            out_a[t, k, 0, 0:half] = (ahead[0:half].astype(F32) + far_a[t, k, 0].astype(F32)).astype(BF16)
            out_a[t, k, 0, half : 2 * half] = ahead[half : 2 * half]
            first = go(out_a.at[t, k, 0], near_a.at[t, k, 0], t, 0, 1)
            far[k, t][1].wait()
            out_a[t, k, 1, 0:half] = behind[0:half]
            out_a[t, k, 1, half : 2 * half] = (
                behind[half : 2 * half].astype(F32) + far_a[t, k, 1].astype(F32)
            ).astype(BF16)
            near[k, t] = (first, go(out_a.at[t, k, 1], near_a.at[t, k, 1], t, 0, 3))

    def summed(k, t):
        near[k, t][0].wait()
        near[k, t][1].wait()
        return (
            part(t, 0, turns[k])[...].astype(F32)
            + near_a[t, k, 0].astype(F32)
            + near_a[t, k, 1].astype(F32)
        )

    far_two, near_two = {}, {}
    for t in both:
        value = summed(0, t).astype(BF16)
        out_b[t, 0] = value
        far_two[t] = (
            go(out_b.at[t, 0, lower], far_b.at[t, 0], t, 1, 1),
            go(out_b.at[t, 0, upper], far_b.at[t, 1], t, 1, 3),
        )
    for k in (1, 2):
        for t in both:
            sum_a[t, k - 1] = summed(k, t)
    for t in both:
        far_two[t][0].wait()
        out_b[t, 1, 0:half] = (sum_a[t, 0, 0:half] + far_b[t, 0].astype(F32)).astype(BF16)
        out_b[t, 1, half : 2 * half] = sum_a[t, 0, half : 2 * half].astype(BF16)
        first = go(out_b.at[t, 1], near_b.at[t, 0], t, 1, 1)
        far_two[t][1].wait()
        out_b[t, 2, 0:half] = sum_a[t, 1, 0:half].astype(BF16)
        out_b[t, 2, half : 2 * half] = (
            sum_a[t, 1, half : 2 * half] + far_b[t, 1].astype(F32)
        ).astype(BF16)
        near_two[t] = (first, go(out_b.at[t, 2], near_b.at[t, 1], t, 1, 3))
    for t in both:
        value = summed(3, t)
        near_two[t][0].wait()
        near_two[t][1].wait()
        o_ref[t] = value + near_b[t, 0].astype(F32) + near_b[t, 1].astype(F32)


def scatter_plane(data, sent, branch_rows, cid):
    rows = data.shape[0] // 32
    out, grad_out = remote_call(
        scatter_plane_kernel,
        (data.reshape(4, 4, 2, rows, 128), sent, branch_rows),
        ("l", "l", "l"),
        [shape((2, rows, 128), F32), shape((ROWS, D), F32)],
        ("v", "v"),
        [
            pltpu.VMEM((2, 4, 2, rows // 2, 128), BF16),
            pltpu.VMEM((2, 4, 2, rows, 128), BF16),
            pltpu.VMEM((2, 4, 2, rows, 128), BF16),
            pltpu.VMEM((2, 2, rows, 128), F32),
            pltpu.VMEM((2, 2, rows // 2, 128), BF16),
            pltpu.VMEM((2, 2, rows, 128), BF16),
            pltpu.VMEM((2, 3, rows, 128), BF16),
            pltpu.SemaphoreType.DMA((40,)),
            pltpu.SemaphoreType.DMA((40,)),
        ],
        cid,
    )
    return out.reshape(2 * rows, 128), grad_out


def lane_index(shape):
    return lax.broadcasted_iota(jnp.int32, shape, 1)


def turned(values):
    lane = lane_index(values.shape)
    up = pltpu.roll(values, 32, axis=1)
    down = pltpu.roll(values, 96, axis=1)
    return jnp.where(lane % 64 < 32, -down, up)


def gather_plane(kv_v, kv_hbm, go, me, own_sem, fillers):
    own = pltpu.make_async_copy(kv_v, kv_hbm.at[me["y"], me["z"]], own_sem)
    own.start()
    half = kv_v.shape[1] // 2
    lower, upper = pl.ds(0, half), pl.ds(half, half)
    axis = (("y", "z"), ("z", "y"))
    here = tuple((me[a], me[b]) for a, b in axis)
    step = {"plus": 1, "minus": 3, "far": 2, "own": 0}

    def place(t, a, b):
        return kv_hbm.at[a, b, 0] if t == 0 else kv_hbm.at[b, a, 1]

    def at(t, which, name):
        return lax.rem(here[t][which] + step[name], 4)

    def send_second(t, src, name):
        dst = place(t, at(t, 0, name), here[t][1])
        src = dst if src is None else src
        return (
            go(src, dst, {axis[t][1]: at(t, 1, "plus")}),
            go(src, dst, {axis[t][1]: at(t, 1, "minus")}),
        )

    def pass_on(t, which, a_name, b_name, part, direction):
        ref = place(t, at(t, 0, a_name), at(t, 1, b_name)).at[part]
        return go(ref, ref, {axis[t][which]: at(t, which, direction)})

    def forward_second(t, name, pair):
        pair[0].wait()
        a = pass_on(t, 1, name, "minus", lower, "plus")
        pair[1].wait()
        b = pass_on(t, 1, name, "plus", upper, "minus")
        return [a, b]

    first, second, last = {}, {}, []
    for t in (0, 1):
        dst = place(t, *here[t])
        first[t] = (
            go(kv_v.at[t], dst, {axis[t][0]: at(t, 0, "plus")}),
            go(kv_v.at[t], dst, {axis[t][0]: at(t, 0, "minus")}),
        )
    for t in (0, 1):
        second[t, "own"] = send_second(t, kv_v.at[t], "own")
    fillers[0]()
    far = {}
    for t in (0, 1):
        first[t][0].wait()
        a = pass_on(t, 0, "minus", "own", lower, "plus")
        second[t, "minus"] = send_second(t, None, "minus")
        first[t][1].wait()
        b = pass_on(t, 0, "plus", "own", upper, "minus")
        second[t, "plus"] = send_second(t, None, "plus")
        far[t] = (a, b)
    fillers[1]()
    for t in (0, 1):
        last += forward_second(t, "own", second[t, "own"])
    for t in (0, 1):
        far[t][0].wait()
        far[t][1].wait()
        second[t, "far"] = send_second(t, None, "far")
    fillers[2]()
    for name in ("minus", "plus", "far"):
        for t in (0, 1):
            last += forward_second(t, name, second[t, name])
    return last + [own]


def front_kernel(
    lengths_ref, tok_ref, wq_ref, wk_ref, wv_ref, wo_ref, router_ref, gain_one_ref, gain_two_ref,
    order_ref, routes_ref, cot_ref, expand_ref, expand_t_ref, col_ref, row_ref, turn_high_ref, turn_low_ref,
    q_ref, kv_own_ref, gain_ref, cos_ref, sin_ref, w_out_ref, member_ref, put_ref, take_ref,
    own_aux_ref, order_rows_ref, key_norm_ref, kv_hbm, late_hbm, normed_v, g_v, aux_v,
    rows_v, w_v, kv_v, long_v, side_v, w_ref, late_ref, send, recv, local,
):
    me = position(AXES)
    x, y, z, c = (me[axis] for axis in AXES)
    small = lane_index((8, 128))
    diagonal = lax.broadcasted_iota(jnp.int32, (8, 8), 0) == lane_index((8, 8))

    def column(ref):
        row = jnp.broadcast_to(ref[...].astype(F32), (8, 8))
        return jnp.sum(jnp.where(diagonal, row, 0.0), axis=1, keepdims=True)

    gain_lane = jnp.where(small == 0, column(gain_one_ref), 0.0).astype(BF16)
    for i in range(8):
        span = slice((i // 2) * 128, (i // 2 + 1) * 128)
        key, value = wk_ref[:, span].astype(F32), wv_ref[:, span].astype(F32)
        if i % 2 == 0:
            pair = jnp.where(small < 64, key, pltpu.roll(value, 64, axis=1))
        else:
            pair = jnp.where(small < 64, pltpu.roll(key, 64, axis=1), value)
        w_ref[i, :, 0:128] = wq_ref[:, i * 128 : (i + 1) * 128]
        w_ref[i, :, 128:256] = pair.astype(BF16)
        w_ref[i, :, 256:384] = gain_lane
    side_v[...] = jnp.zeros_like(side_v)
    side_v[:, 0:EXPERTS] = router_ref[...].astype(F32)
    late_ref[:, 0:D] = wo_ref[...]
    late_ref[:, D : D + 128] = jnp.where(small == EXPERTS, column(gain_two_ref), side_v[...]).astype(BF16)
    greet(me, LINE_OFFSETS + PLANE_OFFSETS)
    plus, minus, far = lax.rem(x + 1, 4), lax.rem(x + 3, 4), lax.rem(x + 2, 4)
    other = 1 - c
    lower, upper = pl.ds(0, 64), pl.ds(64, 64)
    used = [0]

    def go(src, dst, to):
        item = remote(src, dst, send, recv, used[0], to)
        used[0] += 1
        item.start()
        return item

    def keep(src, dst, slot):
        item = pltpu.make_async_copy(src, dst, local.at[slot])
        item.start()
        return item

    own = [
        keep(w_ref.at[x * 2 + c], w_v.at[x, y, z, c], 0),
        keep(late_ref, late_hbm.at[x, y, z, c], 1),
    ]
    own_rows = keep(tok_ref, rows_v.at[c, x], 2)
    first_w = []
    for offset in LINE_OFFSETS:
        to = moved(me, offset)
        first_w.append(go(w_ref.at[to["x"] * 2 + to["c"]], w_v.at[x, y, z, c], to))
    to_plus = go(tok_ref, rows_v.at[c, x], {"x": plus})
    to_minus = go(tok_ref, rows_v.at[c, x], {"x": minus})
    sides = [go(tok_ref, rows_v.at[c, x], {"c": other})]

    for item in own + first_w:
        item.wait()
    second_w = [go(w_v.at[:, y, z], w_v.at[:, y, z], moved(me, by)) for by in PLANE_OFFSETS]
    first_late = [go(late_ref, late_hbm.at[x, y, z, c], moved(me, by)) for by in PLANE_OFFSETS]

    chip = y * 4 + z
    mine = order_ref[pl.ds(pl.multiple_of(chip * 8, 8), 8), :]
    ends, total = [], jnp.int32(0)
    for i in range(NSEQ):
        total = total + lengths_ref[i]
        ends.append(total)
    place = mine
    for i in range(NSEQ):
        place = place - jnp.where(mine >= ends[i], lengths_ref[i], 0)
    lane = lane_index((ROWS, 128))

    def table(ref, picked):
        return mm(picked, ref[0]) + mm(picked, ref[1]) + mm(picked, ref[2])

    for i in range(8):
        wide = jnp.broadcast_to(place[i : i + 1, :].astype(F32), (ROWS, 128)).T.astype(jnp.int32)
        high = table(turn_high_ref, jnp.where(lane == lax.shift_right_logical(wide, 7), 1.0, 0.0).astype(BF16))
        low = table(turn_low_ref, jnp.where(lane == (wide & 127), 1.0, 0.0).astype(BF16))
        cos_ref[pl.ds(i * 128, 128), :] = high[:, :128] * low[:, :128] - high[:, 128:] * low[:, 128:]
        sin_ref[pl.ds(i * 128, 128), :] = high[:, 128:] * low[:, :128] + high[:, :128] * low[:, 128:]
    for i in range(4):
        order_rows_ref[i : i + 1, 0:128] = mine[2 * i : 2 * i + 1, :].astype(F32)
        order_rows_ref[i : i + 1, 128:256] = mine[2 * i + 1 : 2 * i + 2, :].astype(F32)

    to_plus.wait()
    next_plus = go(rows_v.at[c, minus, lower], rows_v.at[c, minus, lower], {"x": plus})
    sides.append(go(rows_v.at[c, minus], rows_v.at[c, minus], {"c": other}))
    to_minus.wait()
    next_minus = go(rows_v.at[c, plus, upper], rows_v.at[c, plus, upper], {"x": minus})
    sides.append(go(rows_v.at[c, plus], rows_v.at[c, plus], {"c": other}))
    next_plus.wait()
    next_minus.wait()
    sides.append(go(rows_v.at[c, far], rows_v.at[c, far], {"c": other}))
    own_rows.wait()
    for item in second_w:
        item.wait()
    weights = w_v[...].astype(F32).reshape(D, 384)
    w_out_ref[...] = weights.astype(BF16)
    gain = weights[:, 256:384].T[0:1, :]
    gain_ref[...] = gain
    low_lanes = lane_index((256, 128)) < 64

    def project(block):
        longest = jnp.zeros((256, 1), F32)
        for i in range(2):
            rows = pl.ds(pl.multiple_of(block * 512 + i * 256, 256), 256)
            tok = rows_v[block, pl.ds(2 * i, 2)].astype(F32).reshape(256, D)
            scale = lax.rsqrt(jnp.mean(tok * tok, axis=-1, keepdims=True) + EPSILON)
            normed = (tok * scale * gain).astype(BF16)
            normed_v[rows, :] = normed
            pre = mm(normed, w_out_ref[:, 0:256])
            cos, sin = cos_ref[rows, :], sin_ref[rows, :]
            q_pre, kv_pre = pre[:, :128], pre[:, 128:]
            query = (q_pre * cos + turned(q_pre) * sin).astype(BF16).astype(F32) * 0.125
            q_ref[0, rows, :] = jnp.where(low_lanes, query, 0.0).astype(BF16)
            q_ref[1, rows, :] = jnp.where(low_lanes, pltpu.roll(query, 64, axis=1), 0.0).astype(BF16)
            key = kv_pre * cos + turned(kv_pre) * sin
            kv = jnp.where(low_lanes, key, kv_pre).astype(BF16)
            kv_own_ref[rows, :] = kv
            kv_v[block, pl.ds(i * 256, 256), :] = kv
            rounded = kv.astype(F32)
            square = jnp.sum(jnp.where(low_lanes, rounded * rounded, 0.0), axis=1, keepdims=True)
            longest = jnp.maximum(longest, square)
        return jnp.max(longest, axis=0, keepdims=True)

    longest = project(c)
    for item in sides:
        item.wait()
    longest = jnp.maximum(longest, project(other))
    long_v[chip] = jnp.broadcast_to(longest, (8, 128))
    longs = [go(long_v.at[chip], long_v.at[chip], moved(me, by)) for by in PLANE_OFFSETS]
    stores = []
    for item in (q_ref, kv_own_ref, cos_ref, sin_ref, w_out_ref, normed_v):
        item.store()

    def routing():
        routes = jnp.concatenate([routes_ref[...].astype(F32), jnp.full((120, 128), -1.0, F32)], axis=0).T
        member = jnp.zeros((ROWS, 128), F32)
        for choice in range(8):
            member += jnp.where(routes[:, choice : choice + 1].astype(jnp.int32) == lane, 1.0, 0.0)
        below = lax.broadcasted_iota(jnp.int32, (ROWS, ROWS), 0) > lane_index((ROWS, ROWS))
        earlier = mm(jnp.where(below, 1.0, 0.0).astype(BF16), member.astype(BF16))
        slot = jnp.where(member > 0.5, earlier, -1.0).astype(BF16)
        member_ref[...] = member
        take = jnp.where(mm(slot, expand_ref[...]) == row_ref[...], 1.0, 0.0)
        take_ref[...] = take.astype(BF16)
        put = jnp.where(mm(expand_t_ref[...], slot, NT) == col_ref[...].astype(F32), 1.0, 0.0)
        put = put.astype(BF16)
        put_ref[...] = put
        for part in range(4):
            columns = pl.ds(part * 256, 256)
            g_v[:, :, columns] = mm(put, cot_ref[:, columns]).reshape(EXPERTS, SLOT, 256).astype(BF16)
        for item in (put_ref, take_ref, g_v):
            item.store()

    def segments():
        sub = lax.broadcasted_iota(jnp.int32, (8, 128), 0)
        begin = jnp.zeros((8, 128), jnp.int32)
        end = jnp.full((8, 128), TOKENS, jnp.int32)
        for i in range(NSEQ):
            begin = jnp.where(sub == 3 + i, ends[i] - lengths_ref[i], begin)
            end = jnp.where(sub == 3 + i, ends[i], end)
        spot = jnp.where(sub == lane_index((8, 128)), 1.0, 0.0).astype(BF16)

        def block(step, carry):
            rows = order_ref[pl.ds(pl.multiple_of(step * 8, 8), 8), :]
            for i in range(8):
                order = jnp.broadcast_to(rows[i : i + 1, :], (8, 128))
                within = jnp.where((order >= begin) & (order < end), 1.0, 0.0).astype(BF16)
                here = pl.ds(pl.multiple_of(step * 1024 + i * 128, 128), 128)
                aux_v[here, :] = mm(within, spot, TN).astype(BF16)
            return carry

        lax.fori_loop(0, 16, block, 0)
        aux_v.store()
        own_aux_ref[...] = aux_v[pl.ds(pl.multiple_of(chip * CHIP_ROWS, CHIP_ROWS), CHIP_ROWS), :]
        own_aux_ref.store()

    def late():
        for item in second_late:
            item.wait()
        stores.append(go(late_hbm.at[:, :, :, c], late_hbm.at[:, :, :, c], {"c": other}))

    for item in first_late:
        item.wait()
    second_late = [
        go(late_hbm.at[x, :, :, c], late_hbm.at[x, :, :, c], {"x": to}) for to in (far, plus, minus)
    ]

    last = gather_plane(kv_v, kv_hbm, go, me, local.at[3], (routing, segments, late))
    for item in longs:
        item.wait()
    longest = long_v[0]
    for i in range(1, 16):
        longest = jnp.maximum(longest, long_v[i])
    key_norm_ref[...] = jnp.sqrt(longest)
    for item in last + stores:
        item.wait()


def front(inputs, cid):
    count = 7 + 3 + 3 + 15 + 15 + 2 + 3 + 40 + 1 + 15
    return remote_call(
        front_kernel,
        inputs,
        ("s", "h") + ("v",) * 9 + ("l",) * 7,
        [
            shape((2, CHIP_ROWS, 128), BF16),
            shape((CHIP_ROWS, 128), BF16),
            shape((1, D), F32),
            shape((CHIP_ROWS, 128), F32),
            shape((CHIP_ROWS, 128), F32),
            shape((D, 384), BF16),
            shape((ROWS, 128), F32),
            shape((SLOTS, ROWS), BF16),
            shape((ROWS, SLOTS), BF16),
            shape((CHIP_ROWS, 128), BF16),
            shape((4, RUN), F32),
            shape((8, 128), F32),
            shape((4, 4, 2, 512, 128), BF16),
            shape((4, 4, 4, 2, 8, 1152), BF16),
            shape((CHIP_ROWS, D), BF16),
            shape((EXPERTS, SLOT, D), BF16),
            shape((TOKENS, 128), BF16),
        ],
        ("e", "e", "v", "e", "e", "e", "v", "e", "e", "e", "v", "v", "h", "h", "e", "e", "e"),
        [
            pltpu.VMEM((2, 4, ROWS, D), BF16),
            pltpu.VMEM((4, 4, 4, 2, 8, 384), BF16),
            pltpu.VMEM((2, 512, 128), BF16),
            pltpu.VMEM((16, 8, 128), F32),
            pltpu.VMEM((8, 128), F32),
            pltpu.VMEM((8, 8, 384), BF16),
            pltpu.VMEM((8, 1152), BF16),
            pltpu.SemaphoreType.DMA((count,)),
            pltpu.SemaphoreType.DMA((count,)),
            pltpu.SemaphoreType.DMA((4,)),
        ],
        cid,
    )


def turn_tables(step):
    frequency = (np.float32(ROPE_BASE) ** (-np.arange(32, dtype=np.float32) / np.float32(32))).astype(np.float64)
    angles = (np.arange(128) * step)[:, None] * np.tile(frequency, 4)[None, :]
    rest = np.concatenate([np.cos(angles), np.sin(angles)], axis=1)
    parts = []
    for _ in range(3):
        part = rest.astype(np.float32).astype(ml_dtypes.bfloat16)
        parts.append(part)
        rest = rest - part.astype(np.float64)
    return jnp.asarray(np.stack(parts))


def order_pair(order_ref, index):
    row = jnp.broadcast_to(order_ref[pl.ds(index, 1), :], (RUN, RUN))
    return row, row.T


WIDE = 3


def run_lists(order_ref, base, first_ref):
    def note(block, carry):
        run = lax.shift_right_logical(order_ref[block * 512], 8)
        first_ref[run] = block * 512
        first_ref[63 - run] = block * 512 + RUN
        return carry

    lax.fori_loop(0, 32, note, 0)

    def count(part):
        run = lax.shift_right_logical(order_ref[base + lax.div(part, 2) * 512], 8)
        return jnp.where(lax.rem(part, 2) == 0, run, 31 - run)

    return count


def group_places(first_ref, number, half, step):
    places = []
    for i in range(WIDE):
        index = step * WIDE + i
        at = jnp.where(index < number, half + index, 32 - half)
        places.append(pl.ds(pl.multiple_of(first_ref[at], RUN), RUN))
    return places


def attend_kernel(
    order_smem, base_ref, kv_hbm, aux_hbm, own_kv_ref, own_aux_ref, q_ref, order_ref, key_norm_ref,
    att_ref, norm_ref, sent_ref, qx_ref, kv_ref, aux_ref, acc_ref, first_ref, loads,
):
    copies = [
        pltpu.make_async_copy(kv_hbm, kv_ref, loads.at[0]),
        pltpu.make_async_copy(aux_hbm, aux_ref, loads.at[1]),
    ]
    for item in copies:
        item.start()
    count = run_lists(order_smem, base_ref[0], first_ref)
    key_norm = key_norm_ref[0:1, 0:1]
    lane = lane_index((RUN, 128))
    low_lanes = lane < 64
    low_tall = lane_index((2 * RUN, 128)) < 64

    def right(keys):
        return jnp.where(lane_index(keys.shape) < 64, jnp.ones_like(keys), keys)

    def prepare(part, carry):
        rows = pl.ds(pl.multiple_of(part * RUN, RUN), RUN)
        own_aux = own_aux_ref[rows, :]
        spread = jnp.where(lane < 3 + NSEQ, (own_aux.astype(F32) - 1.0) * FAR, 0.0)
        for head in range(2):
            query = q_ref[head, rows, :]
            wide = query.astype(F32)
            shift = jnp.ceil(jnp.sqrt(jnp.sum(wide * wide, axis=1, keepdims=True)) * key_norm)
            top = shift.astype(BF16).astype(F32)
            middle = (shift - top).astype(BF16).astype(F32)
            rest = shift - top - middle
            ext = jnp.where(lane == 0, -top, spread)
            ext = jnp.where(lane == 1, -middle, ext)
            ext = jnp.where(lane == 2, -rest, ext)
            here = pl.ds(head * RUN, RUN)
            qx_ref[part, here, 0:128] = query
            qx_ref[part, here, 128:256] = ext.astype(BF16)
        order_key, order_query = order_pair(order_ref, part)
        allowed = order_key <= order_query
        keys = own_kv_ref[rows, :]
        e = jnp.exp(mm(qx_ref[part], jnp.concatenate([keys, own_aux], axis=1), NT))
        e = jnp.where(jnp.concatenate([allowed, allowed], axis=0), e, 0.0)
        acc_ref[part] = mm(e.astype(BF16), right(keys))
        return carry

    lax.fori_loop(0, 4, prepare, 0)
    for item in copies:
        item.wait()

    def part_step(part, carry):
        number = count(part)
        half = lax.rem(part, 2) * 32

        def group(step, carry):
            places = group_places(first_ref, number, half, step)
            keys = jnp.concatenate([kv_ref[here, :] for here in places], axis=0)
            aux = jnp.concatenate([aux_ref[here, :] for here in places], axis=0)
            e = jnp.exp(mm(qx_ref[part], jnp.concatenate([keys, aux], axis=1), NT))
            acc_ref[part] += mm(e.astype(BF16), right(keys))
            return carry

        lax.fori_loop(0, lax.div(number + WIDE - 1, WIDE), group, 0)
        rows = pl.ds(pl.multiple_of(part * RUN, RUN), RUN)
        total = acc_ref[part]
        other = pltpu.roll(total, 64, axis=1)
        norm = jnp.where(low_tall, total, other)
        value = jnp.where(low_tall, other, total) / norm
        att = jnp.where(low_lanes, value[:RUN], value[RUN:])
        att_ref[rows, :] = att
        norm_ref[rows, :] = jnp.where(low_lanes, norm[:RUN], norm[RUN:])
        sent_ref[rows, :] = att.astype(BF16)
        return carry

    lax.fori_loop(0, 4, part_step, 0)


def attend(order, base, kv, aux, own_kv, own_aux, query, order_rows, key_norm):
    smem = pl.BlockSpec(memory_space=pltpu.SMEM)
    vmem = pl.BlockSpec(memory_space=pltpu.VMEM)
    hbm = pl.BlockSpec(memory_space=pl.ANY)
    return local_call(
        attend_kernel,
        (
            shape((CHIP_ROWS, 128), F32),
            shape((CHIP_ROWS, 128), F32),
            shape((CHIP_ROWS, 128), BF16),
            shape((4, 2 * RUN, 256), BF16),
        ),
        scratch=[
            pltpu.VMEM((TOKENS, 128), BF16),
            pltpu.VMEM((TOKENS, 128), BF16),
            pltpu.VMEM((4, 2 * RUN, 128), F32),
            pltpu.SMEM((64,), jnp.int32),
            pltpu.SemaphoreType.DMA((2,)),
        ],
        in_specs=[smem] * 2 + [hbm] * 2 + [vmem] * 5,
    )(order, base, kv, aux, own_kv, own_aux, query, order_rows, key_norm)


def attend_back_kernel(
    order_smem, base_ref, kv_hbm, aux_hbm, own_kv_ref, own_aux_ref, qx_ref, order_ref,
    gsent_ref, att_ref, norm_ref, dq_ref, dkv_hbm,
    kv_ref, aux_ref, acc_ref, dq_acc, gx_ref, rhs_ref, out_ref, first_ref, loads, stores,
):
    copies = [
        pltpu.make_async_copy(kv_hbm, kv_ref, loads.at[0]),
        pltpu.make_async_copy(aux_hbm, aux_ref, loads.at[1]),
    ]
    for item in copies:
        item.start()
    own_base = base_ref[0]
    count = run_lists(order_smem, own_base, first_ref)

    def clear(step, carry):
        acc_ref[pl.ds(pl.multiple_of(step * 512, 512), 512), :] = jnp.zeros((512, 128), F32)
        return carry

    lax.fori_loop(0, TOKENS // 512, clear, 0)
    lane = lane_index((RUN, 128))
    low_lanes = lane < 64

    def apply(part, here, e, prob):
        ds = (e * prob).astype(BF16)
        left = jnp.concatenate([ds, e.astype(BF16)], axis=1)
        acc_ref[here, :] += mm(left, rhs_ref[part])
        return ds

    def scores(part, keys, aux):
        both = jnp.concatenate([keys, aux], axis=1)
        return mm(both, qx_ref[part], NT), mm(both, gx_ref[part], NT)

    def prepare(part, carry):
        rows = pl.ds(pl.multiple_of(part * RUN, RUN), RUN)
        gsent = gsent_ref[rows, :].astype(F32)
        norm = norm_ref[rows, :]
        product = gsent * att_ref[rows, :] / norm
        scaled = (gsent / norm).astype(BF16).astype(F32)
        for head in range(2):
            mask = low_lanes if head == 0 else jnp.logical_not(low_lanes)
            delta = jnp.sum(jnp.where(mask, product, 0.0), axis=1, keepdims=True)
            top = delta.astype(BF16).astype(F32)
            middle = (delta - top).astype(BF16).astype(F32)
            rest = delta - top - middle
            ext = jnp.where(lane == 0, -top, 0.0)
            ext = jnp.where(lane == 1, -middle, ext)
            ext = jnp.where(lane == 2, -rest, ext)
            grad = pltpu.roll(scaled, 64, axis=1) if head == 0 else scaled
            grad = jnp.where(low_lanes, 0.0, grad).astype(BF16)
            here = pl.ds(head * RUN, RUN)
            gx_ref[part, here, 0:128] = grad
            gx_ref[part, here, 128:256] = ext.astype(BF16)
            rhs_ref[part, pl.ds(head * RUN, RUN), :] = qx_ref[part, here, 0:128]
            rhs_ref[part, pl.ds((2 + head) * RUN, RUN), :] = grad
        order_key, order_query = order_pair(order_ref, part)
        allowed = order_query <= order_key
        keys = own_kv_ref[rows, :]
        score, prob = scores(part, keys, own_aux_ref[rows, :])
        e = jnp.where(jnp.concatenate([allowed, allowed], axis=1), jnp.exp(score), 0.0)
        own = pl.ds(pl.multiple_of(own_base + part * RUN, RUN), RUN)
        dq_acc[part] = mm(keys.T[:64], apply(part, own, e, prob))
        return carry

    lax.fori_loop(0, 4, prepare, 0)
    for item in copies:
        item.wait()

    def part_step(part, carry):
        number = count(part)
        half = lax.rem(part, 2) * 32

        def group(step, carry):
            places = group_places(first_ref, number, half, step)
            parts = [scores(part, kv_ref[here, :], aux_ref[here, :]) for here in places]
            ds = [
                apply(part, here, jnp.exp(score), prob)
                for here, (score, prob) in zip(places, parts)
            ]
            keys = jnp.concatenate([kv_ref[here, :] for here in places], axis=0)
            dq_acc[part] += mm(keys.T[:64], jnp.concatenate(ds, axis=0))
            return carry

        lax.fori_loop(0, lax.div(number + WIDE - 1, WIDE), group, 0)
        rows = pl.ds(pl.multiple_of(part * RUN, RUN), RUN)
        total = dq_acc[part] * 0.125
        dq_ref[rows, :] = jnp.concatenate([total[:, :RUN], total[:, RUN:]], axis=0).T
        return carry

    lax.fori_loop(0, 4, part_step, 0)

    def store(step):
        rows = pl.ds(pl.multiple_of(step * 2048, 2048), 2048)
        return pltpu.make_async_copy(out_ref.at[rows], dkv_hbm.at[rows], stores.at[step])

    def narrow(step, carry):
        rows = pl.ds(pl.multiple_of(step * 2048, 2048), 2048)
        out_ref[rows, :] = acc_ref[rows, :].astype(BF16)
        store(step).start()
        return carry

    def settle(step, carry):
        store(step).wait()
        return carry

    lax.fori_loop(0, 8, narrow, 0)
    lax.fori_loop(0, 8, settle, 0)


def attend_back(order, base, kv, aux, own_kv, own_aux, query_ext, order_rows, gsent, att, norm):
    smem = pl.BlockSpec(memory_space=pltpu.SMEM)
    vmem = pl.BlockSpec(memory_space=pltpu.VMEM)
    hbm = pl.BlockSpec(memory_space=pl.ANY)
    return local_call(
        attend_back_kernel,
        (shape((CHIP_ROWS, 128), F32), shape((TOKENS, 128), BF16)),
        scratch=[
            pltpu.VMEM((TOKENS, 128), BF16),
            pltpu.VMEM((TOKENS, 128), BF16),
            pltpu.VMEM((TOKENS, 128), F32),
            pltpu.VMEM((4, 64, 2 * RUN), F32),
            pltpu.VMEM((4, 2 * RUN, 256), BF16),
            pltpu.VMEM((4, 4 * RUN, 128), BF16),
            pltpu.VMEM((TOKENS, 128), BF16),
            pltpu.SMEM((64,), jnp.int32),
            pltpu.SemaphoreType.DMA((2,)),
            pltpu.SemaphoreType.DMA((8,)),
        ],
        in_specs=[smem] * 2 + [hbm] * 2 + [vmem] * 7,
        out_specs=[vmem, hbm],
    )(order, base, kv, aux, own_kv, own_aux, query_ext, order_rows, gsent, att, norm)


SLOT_EXPERT = np.arange(SLOTS) // SLOT
SLOT_PLACE = np.arange(SLOTS) % SLOT


def constant(array):
    return jnp.asarray(np.asarray(array).astype(ml_dtypes.bfloat16))


def expand_matrix():
    return constant(np.arange(128)[:, None] == SLOT_EXPERT[None, :])


def place_matrix():
    return constant(SLOT_PLACE[:, None] == np.arange(128)[None, :])


def pick_matrix(place):
    return constant((SLOT_EXPERT[:, None] == np.arange(128)[None, :]) & (SLOT_PLACE[:, None] == place))


def place_column():
    used = np.where(SLOT_PLACE < CAP, SLOT_PLACE, -5)
    return constant(np.broadcast_to(used[:, None], (SLOTS, 128)))


def place_row():
    used = np.where(SLOT_PLACE < CAP, SLOT_PLACE, -5)
    return jnp.asarray(used[None, :].astype(np.float32))


BLOCK = 8 * SLOT
BLOCK_SOURCE = np.arange(BLOCK) // SLOT
BLOCK_PLACE = np.arange(BLOCK) % SLOT


def block_matrix(places):
    hit = np.isin(BLOCK_PLACE, places)[None, :] & (BLOCK_SOURCE[:, None] == BLOCK_SOURCE[None, :])
    return constant(hit)


def packed_pairs(values):
    total = sum(int(value) << (2 * i) for i, value in enumerate(values))
    return np.uint32(total).astype(np.int32)


STEP_Y = packed_pairs([dy for dy, _ in PLANE_ORDER])
STEP_Z = packed_pairs([dz for _, dz in PLANE_ORDER])


def moe_kernel(
    sent_ref, tok_ref, w_out_ref, router_ref, member_ref, put_ref, take_ref, expand_ref,
    expand_t_ref, place_ref, place_t_ref, pick_high_ref, pick_low_ref, pick_t_ref, cot_ref,
    select_ref, block_place_ref, high_ref, low_ref, g_hbm, gate_hbm, up_hbm, down_hbm,
    residual_ref, weigh_high_ref, weigh_low_ref, gmid_ref, branch_ref, gsent_in, side_in,
    y_hbm, grad_gate_hbm, grad_up_hbm, grad_down_hbm,
    sent_in, x_out, x_in, g_v, y_v, back_out, back_in, gate_v, up_v, down_v,
    sum_gate, sum_up, sum_down, grad_gate, grad_up, grad_down, mixed_v, gate_probs, gsent_out, side_out,
    x_send, x_recv, back_send, back_recv, line_send, line_recv, local,
):
    me = position(AXES)
    x_at, y_at, z_at, c_at = (me[axis] for axis in AXES)
    expert = (y_at * 4 + z_at) * 2 + c_at

    def offset(k):
        pair = lax.div(k, 2)
        dy = lax.shift_right_logical(jnp.int32(STEP_Y), 2 * pair) & 3
        dz = lax.shift_right_logical(jnp.int32(STEP_Z), 2 * pair) & 3
        return dy, dz, lax.rem(k + pair, 2)

    def toward(k):
        dy, dz, dc = offset(k)
        return {"y": lax.rem(y_at + dy, 4), "z": lax.rem(z_at + dz, 4), "c": lax.rem(c_at + dc, 2)}

    def source(k):
        dy, dz, dc = offset(k)
        return {
            "y": lax.rem(y_at + 4 - dy, 4),
            "z": lax.rem(z_at + 4 - dz, 4),
            "c": lax.rem(c_at + dc, 2),
        }

    def number(at):
        return (at["y"] * 4 + at["z"]) * 2 + at["c"]

    loads = [
        pltpu.make_async_copy(src, dst, local.at[i])
        for i, (src, dst) in enumerate(
            ((g_hbm, g_v), (gate_hbm, gate_v), (up_hbm, up_v), (down_hbm, down_v))
        )
    ]
    for item in loads:
        item.start()
    barrier = pltpu.get_barrier_semaphore()
    for by in LINE_OFFSETS:
        pl.semaphore_signal(barrier, inc=1, device_id=moved(me, by), device_id_type=MESH)

    def hello(k, carry):
        pl.semaphore_signal(barrier, inc=1, device_id=toward(k), device_id_type=MESH)
        return carry

    lax.fori_loop(0, 31, hello, 0)
    pl.semaphore_wait(barrier, 31 + len(LINE_OFFSETS))

    here_line = x_at * 2 + c_at
    moves = []
    for i, by in enumerate(LINE_OFFSETS):
        to = moved(me, by)
        moves.append(
            remote(sent_ref.at[to["c"] * 4 + to["x"]], sent_in.at[here_line], line_send, line_recv, i, to)
        )
        moves[-1].start()
    kept = pltpu.make_async_copy(sent_ref.at[c_at * 4 + x_at], sent_in.at[here_line], local.at[4])
    kept.start()
    for item in moves + [kept]:
        item.wait()
    sent = jnp.concatenate([sent_in[i] for i in range(8)], axis=1)
    residual = tok_ref[...].astype(F32) + mm(sent, w_out_ref[...])
    residual_ref[...] = residual
    residual_ref.store()
    gain = router_ref[...].astype(F32).T[EXPERTS : EXPERTS + 1, :]
    scale = lax.rsqrt(jnp.mean(residual * residual, axis=-1, keepdims=True) + EPSILON)
    mixed = (residual * scale * gain).astype(BF16)
    mixed_v[...] = mixed
    logits = mm(mixed, router_ref[...])
    member = member_ref[...]
    masked = jnp.where(member > 0.5, logits, -FAR)
    top = jnp.max(masked, axis=1, keepdims=True)
    power = jnp.where(member > 0.5, jnp.exp(masked - top), 0.0)
    gate = power / jnp.sum(power, axis=1, keepdims=True)
    gate_probs[...] = gate
    gate_high, gate_low = halves(gate)
    spread = mm(gate_high, expand_ref[...]) + mm(gate_low, expand_ref[...])
    weigh = take_ref[...].astype(F32) * spread
    weigh_high, weigh_low = halves(weigh)
    weigh_high_ref[...] = weigh_high
    weigh_low_ref[...] = weigh_low
    weigh_high_ref.store()
    weigh_low_ref.store()
    total = jnp.sum(weigh, axis=0, keepdims=True)
    rows_high, rows_low = halves(expand_ref[...].astype(F32) * total)
    rows_high = mm(rows_high, place_ref[...]).astype(BF16)
    rows_low = mm(rows_low, place_ref[...]).astype(BF16)
    gate_rows = mm(pick_high_ref[...], rows_high) + mm(pick_low_ref[...], rows_low)
    put = put_ref[...]

    def slots(value):
        return value.reshape(EXPERTS, SLOT, value.shape[1]).astype(BF16)

    x_out[:, :, 0:128] = slots(mm(put, mixed[:, 0:128]) + gate_rows)
    x_out[:, :, 128:512] = slots(mm(put, mixed[:, 128:512]))
    x_out[:, :, 512:1024] = slots(mm(put, mixed[:, 512:1024]))

    def x_copy(k):
        to = toward(k)
        return remote(x_out.at[number(to)], x_in.at[k], x_send, x_recv, k, to)

    def x_start(k, carry):
        x_copy(k).start()
        return carry

    lax.fori_loop(0, 31, x_start, 0)
    kept = pltpu.make_async_copy(x_out.at[expert], x_in.at[31], local.at[4])
    kept.start()
    kept.wait()
    sum_gate[...] = jnp.zeros_like(sum_gate)
    sum_up[...] = jnp.zeros_like(sum_up)
    sum_down[...] = jnp.zeros_like(sum_down)
    for item in loads:
        item.wait()
    for item in (block_place_ref, select_ref, high_ref, low_ref):
        item.get()

    def back_copy(k):
        to = source(k)
        return remote(back_out.at[k], back_in.at[expert], back_send, back_recv, k, to)

    def back_kept():
        return pltpu.make_async_copy(back_out.at[31], back_in.at[expert], local.at[4])

    def group(step, carry):
        first = step * 8
        for i in range(8):
            k = first + i

            @pl.when(k < 31)
            def _():
                x_copy(k).wait_recv()

        x = x_in[pl.ds(first, 8)].astype(F32).reshape(BLOCK, D).astype(BF16)
        g = jnp.concatenate([g_v[number(source(first + i))].astype(F32) for i in range(8)], axis=0)
        place = block_place_ref[...].astype(F32)
        share = jnp.sum(mm(select_ref[...], x[:, :128]) * place, axis=1, keepdims=True)
        a = mm(x, gate_v[...])
        b = mm(x, up_v[...])
        s = 1.0 / (1.0 + jnp.exp(-a))
        silu = a * s
        hidden = (silu * b).astype(BF16)
        y = mm(hidden, down_v[...]).astype(BF16).astype(F32)
        dgate = jnp.sum(y * g, axis=1, keepdims=True)
        y = y.reshape(8, SLOT, D)
        for i in range(8):
            y_v[number(source(first + i))] = y[i].astype(BF16)
        gy = (g * share).astype(BF16)
        dhidden = mm(gy, down_v[...], NT)
        da = (dhidden * b * (s * (1.0 + a * (1.0 - s)))).astype(BF16)
        db = (dhidden * silu).astype(BF16)
        back = mm(da, gate_v[...], NT) + mm(db, up_v[...], NT)
        dgate_high, dgate_low = halves(dgate * place)
        lead = back[:, 0:128] + mm(high_ref[...], dgate_high) + mm(low_ref[...], dgate_low)
        span = pl.ds(first, 8)
        back_out[span, :, 0:128] = lead.reshape(8, SLOT, 128).astype(BF16)
        back_out[span, :, 128:1024] = back[:, 128:1024].reshape(8, SLOT, 896).astype(BF16)
        for i in range(8):
            k = first + i

            @pl.when(k < 31)
            def _():
                back_copy(k).start()

            @pl.when(k == 31)
            def _():
                back_kept().start()

        sum_gate[...] += mm(x, da, TN)
        sum_up[...] += mm(x, db, TN)
        sum_down[...] += mm(hidden, gy, TN)
        return carry

    lax.fori_loop(0, 4, group, 0)
    grad_gate[...] = sum_gate[...].astype(BF16)
    grad_up[...] = sum_up[...].astype(BF16)
    grad_down[...] = sum_down[...].astype(BF16)
    stores = [
        pltpu.make_async_copy(src, dst, local.at[i])
        for i, (src, dst) in enumerate(
            ((y_v, y_hbm), (grad_gate, grad_gate_hbm), (grad_up, grad_up_hbm), (grad_down, grad_down_hbm))
        )
    ]
    for item in stores:
        item.start()

    def settle(k, carry):
        x_copy(k).wait_send()
        back_copy(k).wait()
        return carry

    lax.fori_loop(0, 31, settle, 0)
    back_kept().wait()

    take = take_ref[...]
    rows_high, rows_low = halves(
        sum(
            mm(
                pick_t_ref[:, i * 640 : (i + 1) * 640],
                back_in[i * 16 : (i + 1) * 16, :, 0:128].astype(F32).reshape(640, 128).astype(BF16),
            )
            for i in range(2)
        )
    )
    spread = mm(rows_high, place_t_ref[...]) + mm(rows_low, place_t_ref[...])
    along = jnp.sum(spread * expand_ref[...].astype(F32), axis=0, keepdims=True)
    found_high, found_low = halves(take.astype(F32) * along)
    dgate = mm(found_high, expand_t_ref[...]) + mm(found_low, expand_t_ref[...])
    gate = gate_probs[...]
    dlogits = gate * (dgate - jnp.sum(gate * dgate, axis=1, keepdims=True))
    dlogits = dlogits.astype(BF16)
    dmixed = mm(dlogits, router_ref[...], NT)
    for i in range(2):
        rows = back_in[i * 16 : (i + 1) * 16].astype(F32).reshape(640, D).astype(BF16)
        dmixed += mm(take[:, i * 640 : (i + 1) * 640], rows)
    residual = residual_ref[...]
    scale = lax.rsqrt(jnp.mean(residual * residual, axis=-1, keepdims=True) + EPSILON)
    gain = router_ref[...].astype(F32).T[EXPERTS : EXPERTS + 1, :]
    weighted = dmixed * gain
    inner = jnp.mean(weighted * residual, axis=-1, keepdims=True)
    gmid = cot_ref[...].astype(F32) + scale * weighted - residual * (scale * scale * scale) * inner
    gmid_ref[...] = gmid
    gmid_ref.store()
    branch = gmid.astype(BF16)
    branch_ref[...] = branch
    branch_ref.store()
    gsent = mm(branch, w_out_ref[...], NT).astype(BF16)
    for i in range(8):
        gsent_out[i] = gsent[:, i * 128 : (i + 1) * 128]
    back_line = c_at * 4 + x_at
    moves = []
    for i, by in enumerate(LINE_OFFSETS):
        to = moved(me, by)
        moves.append(
            remote(
                gsent_out.at[to["x"] * 2 + to["c"]], gsent_in.at[back_line], line_send, line_recv, 7 + i, to
            )
        )
        moves[-1].start()
    kept = pltpu.make_async_copy(gsent_out.at[here_line], gsent_in.at[back_line], local.at[4])
    kept.start()
    moves.append(kept)
    gain_grad = jnp.sum(dmixed * residual * scale, axis=0, keepdims=True)
    grads = mm(dlogits, mixed_v[...], TN)
    row = lax.broadcasted_iota(jnp.int32, (128, D), 0)
    grads = jnp.where(row == EXPERTS, gain_grad, grads).T.reshape(4, 16, 2, 8, 128)
    for i in range(8):
        side_out[i] = grads[i // 2, :, i % 2].reshape(ROWS, 128).astype(BF16)
    for i, by in enumerate(LINE_OFFSETS):
        to = moved(me, by)
        moves.append(
            remote(
                side_out.at[to["x"] * 2 + to["c"]], side_in.at[back_line], line_send, line_recv, 14 + i, to
            )
        )
        moves[-1].start()
    kept = pltpu.make_async_copy(side_out.at[here_line], side_in.at[back_line], local.at[5])
    kept.start()
    for item in moves + [kept] + stores:
        item.wait()


def moe(inputs, cid):
    slots = (EXPERTS, SLOT, D)
    up, down = (D, FF), (FF, D)
    dma = pltpu.SemaphoreType.DMA
    return remote_call(
        moe_kernel,
        inputs,
        ("h", "l", (0, D), (D, D + 128)) + ("l",) * 15 + ("h",) * 4,
        [
            shape((ROWS, D), F32),
            shape((ROWS, SLOTS), BF16),
            shape((ROWS, SLOTS), BF16),
            shape((ROWS, D), F32),
            shape((ROWS, D), BF16),
            shape((8, ROWS, 128), BF16),
            shape((8, ROWS, 128), BF16),
            shape(slots, BF16),
            shape(up, BF16),
            shape(up, BF16),
            shape(down, BF16),
        ],
        ("e", "e", "e", "e", "e", "v", "v", "h", "h", "h", "h"),
        [
            pltpu.VMEM((8, ROWS, 128), BF16),
            pltpu.VMEM(slots, BF16),
            pltpu.VMEM(slots, BF16),
            pltpu.VMEM(slots, BF16),
            pltpu.VMEM(slots, BF16),
            pltpu.VMEM(slots, BF16),
            pltpu.VMEM(slots, BF16),
            pltpu.VMEM(up, BF16),
            pltpu.VMEM(up, BF16),
            pltpu.VMEM(down, BF16),
            pltpu.VMEM(up, F32),
            pltpu.VMEM(up, F32),
            pltpu.VMEM(down, F32),
            pltpu.VMEM(up, BF16),
            pltpu.VMEM(up, BF16),
            pltpu.VMEM(down, BF16),
            pltpu.VMEM((ROWS, D), BF16),
            pltpu.VMEM((ROWS, 128), F32),
            pltpu.VMEM((8, ROWS, 128), BF16),
            pltpu.VMEM((8, ROWS, 128), BF16),
            dma((31,)),
            dma((31,)),
            dma((31,)),
            dma((31,)),
            dma((21,)),
            dma((21,)),
            dma((6,)),
        ],
        cid,
    )


def finish_kernel(
    dq_ref, dkv_ref, cos_ref, sin_ref, normed_ref, w_ref,
    y_ref, weigh_high_ref, weigh_low_ref, residual_ref, out_ref, side_ref,
    dnormed_out, mixed_out, grads_out, early_out,
    dqkv, part_out, part_in, part_own, line_out, line_in, share_out, share_in, total,
    out_in, side_in, send, recv, local, out_recv,
):
    me = position(AXES)
    x, y, z, c = (me[axis] for axis in AXES)
    mine = y * 4 + z
    alone = jnp.where(c == lax.div(y, 2), 1, 0)
    barrier = pltpu.get_barrier_semaphore()

    def owner(k):
        at = lax.rem(lax.rem(y, 2) * 8 + z * 2 + c + k, 16)
        to = {"y": 2 * c + lax.div(at, 8), "z": lax.rem(lax.div(at, 2), 4), "c": lax.rem(at, 2)}
        return at, to

    def origin(k):
        at = lax.rem(mine + k, 16)
        return at, {"y": lax.div(at, 4), "z": lax.rem(at, 4), "c": lax.div(y, 2)}

    for k in range(1, 16):
        pl.semaphore_signal(barrier, inc=1, device_id=origin(k)[1], device_id_type=MESH)

    @pl.when(alone == 0)
    def _():
        pl.semaphore_signal(barrier, inc=1, device_id=origin(0)[1], device_id_type=MESH)

    offsets = LINE_OFFSETS + PLANE_OFFSETS
    for offset in offsets:
        pl.semaphore_signal(barrier, inc=1, device_id=moved(me, offset), device_id_type=MESH)
    pl.semaphore_wait(barrier, len(offsets) + 16 - alone)
    used = [0]

    def go(src, dst, to):
        item = remote(src, dst, send, recv, used[0], to)
        used[0] += 1
        item.start()
        return item

    other = 1 - c
    low_lanes = lane_index((256, 128)) < 64

    def out_copy(k):
        at, to = owner(k)
        return pltpu.make_async_remote_copy(
            src_ref=out_ref.at[at], dst_ref=out_in.at[mine], send_sem=send.at[used[0] + k],
            recv_sem=out_recv.at[mine], device_id=to, device_id_type=MESH,
        )

    def out_kept():
        return pltpu.make_async_copy(out_ref.at[owner(0)[0]], out_in.at[mine], local.at[1])

    out_copies = [out_copy(k) for k in range(16)]
    used[0] += 16
    out_arrivals = []
    for k in range(16):
        at, to = origin(k)
        out_arrivals.append(
            pltpu.make_async_remote_copy(
                src_ref=out_ref.at[0], dst_ref=out_in.at[at], send_sem=send.at[0],
                recv_sem=out_recv.at[at], device_id=to, device_id_type=MESH,
            )
        )

    @pl.when(alone == 0)
    def _():
        out_copies[0].start()

    @pl.when(alone == 1)
    def _():
        out_kept().start()

    for item in out_copies[1:]:
        item.start()
    early = []
    for offset in PLANE_OFFSETS:
        to = moved(me, offset)
        early.append(go(side_ref.at[to["y"] * 4 + to["z"]], side_in.at[mine], to))
    side_kept = pltpu.make_async_copy(side_ref.at[mine], side_in.at[mine], local.at[2])
    side_kept.start()
    early.append(side_kept)

    def turn_back(first):
        rows = pl.ds(pl.multiple_of(first, 256), 256)
        cos, sin = cos_ref[rows, :], sin_ref[rows, :]
        dq, dkv = dq_ref[rows, :], dkv_ref[rows, :]
        dq = (dq * cos - turned(dq) * sin).astype(BF16)
        dkv = jnp.where(low_lanes, dkv * cos - turned(dkv) * sin, dkv).astype(BF16)
        both = jnp.concatenate([dq, dkv], axis=1)
        dqkv[rows, :] = both
        return mm(both, w_ref[...], NT)

    crossing = []
    for i in range(2):
        value = turn_back(other * 512 + i * 256).astype(BF16)
        part_out[2 * i] = value[:ROWS]
        part_out[2 * i + 1] = value[ROWS:]
        span = pl.ds(2 * i, 2)
        crossing.append(go(part_out.at[span], part_in.at[span], {"c": other}))
    for i in range(2):
        value = turn_back(c * 512 + i * 256)
        part_own[2 * i] = value[:ROWS]
        part_own[2 * i + 1] = value[ROWS:]
    for item in crossing:
        item.wait()
    along = []
    for i, by in enumerate((2, 1, 3)):
        to = lax.rem(x + by, 4)
        line_out[i] = (part_own[to] + part_in[to].astype(F32)).astype(BF16)
        along.append(go(line_out.at[i], line_in.at[i], {"x": to}))
    for i in range(4):
        columns = pl.ds(i * 256, 256)
        grad = mm(normed_ref[:, columns], dqkv[...], TN).astype(BF16)
        share_out[i] = grad.reshape(16, 16, 256)
    spread = []
    for offset in PLANE_OFFSETS:
        to = moved(me, offset)
        spread.append(go(share_out.at[:, to["y"] * 4 + to["z"]], share_in.at[mine], to))
    kept = pltpu.make_async_copy(share_out.at[:, mine], share_in.at[mine], local.at[0])
    kept.start()
    mixed = mm(weigh_high_ref[...], y_ref[...]) + mm(weigh_low_ref[...], y_ref[...])
    mixed_out[...] = (residual_ref[...] + mixed).astype(BF16)
    mixed_out.store()
    for item in spread + [kept]:
        item.wait()
    for i in range(4):
        value = share_in[0, i].astype(F32)
        for j in range(1, 16):
            value += share_in[j, i].astype(F32)
        total[i] = value.reshape(2, 8, 256)
    ends = []
    here = x * 2 + c
    for offset in LINE_OFFSETS:
        to = moved(me, offset)
        ends.append(go(total.at[to["x"], to["c"]], grads_out.at[here], to))
    kept = pltpu.make_async_copy(total.at[x, c], grads_out.at[here], local.at[0])
    kept.start()
    for item in out_copies[1:]:
        item.wait_send()
    for item in out_arrivals[1:]:
        item.wait_recv()

    @pl.when(alone == 0)
    def _():
        out_copies[0].wait_send()
        out_arrivals[0].wait_recv()

    @pl.when(alone == 1)
    def _():
        out_kept().wait()

    for item in early:
        item.wait()
    out_total, side_total = out_in[0], side_in[0]
    for j in range(1, 16):
        out_total += out_in[j]
        side_total += side_in[j]
    early_out[:, 0:D] = out_total
    early_out[:, D : D + 128] = side_total
    for item in along:
        item.wait()
    dnormed = part_own[x] + part_in[x].astype(F32)
    for i in range(3):
        dnormed += line_in[i].astype(F32)
    dnormed_out[...] = dnormed
    for item in ends + [kept]:
        item.wait()


def finish(inputs, cid):
    count = 2 + 3 + 15 + 7 + 16 + 15
    return remote_call(
        finish_kernel,
        inputs,
        ("l", "l", "l", "l", "l", (0, 256), "l", "l", "l", "l", "h", "h"),
        [
            shape((ROWS, D), F32),
            shape((ROWS, D), BF16),
            shape((8, 8, 256), F32),
            shape((8, D + 128), F32),
        ],
        ("v", "e", "v", "v"),
        [
            pltpu.VMEM((CHIP_ROWS, 256), BF16),
            pltpu.VMEM((4, ROWS, D), BF16),
            pltpu.VMEM((4, ROWS, D), BF16),
            pltpu.VMEM((4, ROWS, D), F32),
            pltpu.VMEM((3, ROWS, D), BF16),
            pltpu.VMEM((3, ROWS, D), BF16),
            pltpu.VMEM((4, 16, 16, 256), BF16),
            pltpu.VMEM((16, 4, 16, 256), BF16),
            pltpu.VMEM((4, 2, 8, 256), F32),
            pltpu.VMEM((16, 8, D), F32),
            pltpu.VMEM((16, 8, 128), F32),
            pltpu.SemaphoreType.DMA((count,)),
            pltpu.SemaphoreType.DMA((count,)),
            pltpu.SemaphoreType.DMA((3,)),
            pltpu.SemaphoreType.DMA((16,)),
        ],
        cid,
    )


def last_kernel(
    dnormed_ref, tok_ref, gain_ref, gmid_ref, mixed_ref, rows_ref, wq_ref, wk_ref, wv_ref, own_gain_ref, early_ref,
    gate_ref, up_ref, down_ref,
    tokens_out, mixed_out, query_out, key_out, value_out, gains_out, grad_out, router_out,
    gate_out, up_out, down_out,
):
    tok = tok_ref[...].astype(F32)
    scale = lax.rsqrt(jnp.mean(tok * tok, axis=-1, keepdims=True) + EPSILON)
    weighted = dnormed_ref[...] * gain_ref[...]
    inner = jnp.mean(weighted * tok, axis=-1, keepdims=True)
    tokens_out[...] = gmid_ref[...] + scale * weighted - tok * (scale * scale * scale) * inner
    mixed_out[...] = mixed_ref[...]
    for i in range(8):
        query_out[:, i * 128 : (i + 1) * 128] = rows_ref[i][:, :128]
    lanes = lane_index((8, 128)) < 64
    for i in range(4):
        first, second = rows_ref[2 * i][:, 128:], rows_ref[2 * i + 1][:, 128:]
        key_out[:, i * 128 : (i + 1) * 128] = jnp.where(lanes, first, pltpu.roll(second, 64, axis=1))
        value_out[:, i * 128 : (i + 1) * 128] = jnp.where(lanes, pltpu.roll(first, 64, axis=1), second)
    total = (
        jnp.sum(query_out[...] * wq_ref[...].astype(F32), axis=1, keepdims=True)
        + jnp.sum(key_out[...] * wk_ref[...].astype(F32), axis=1, keepdims=True)
        + jnp.sum(value_out[...] * wv_ref[...].astype(F32), axis=1, keepdims=True)
    )
    gain_one = jnp.broadcast_to(total, (8, 128)).T[0:1, :]
    side = early_ref[:, D : D + 128]
    gain_two = side.T[EXPERTS : EXPERTS + 1, :]
    gains_out[0:1, :] = gain_one[:, 0:8] / own_gain_ref[...].astype(F32)
    gains_out[1:2, :] = gain_two[:, 0:8]
    grad_out[...] = early_ref[:, 0:D]
    router_out[...] = side[:, 0:EXPERTS]
    gate_out[...] = gate_ref[...].astype(F32)
    up_out[...] = up_ref[...].astype(F32)
    down_out[...] = down_ref[...].astype(F32)


def body(
    tokens,
    gain_one,
    w_query,
    w_key,
    w_value,
    w_out,
    gain_two,
    w_router,
    w_gate,
    w_up,
    w_down,
    dealt_order,
    lengths,
    routes,
    cotangent,
):
    y_at, z_at = lax.axis_index("y"), lax.axis_index("z")
    first_row = (y_at * 4 + z_at) * CHIP_ROWS

    expand, expand_t = expand_matrix(), expand_matrix().T
    place, place_t = place_matrix(), place_matrix().T
    pick_high, pick_low = pick_matrix(CAP), pick_matrix(CAP + 1)
    (
        query, kv, gain_first, cos, sin, w_mine, member, put, take, own_aux, order_rows, key_norm,
        kv_all, w_late, normed, g_out, aux,
    ) = front(
        (
            lengths, tokens, w_query, w_key, w_value, w_out, w_router, gain_one.reshape(1, 8),
            gain_two.reshape(1, 8), dealt_order.reshape(128, 128), routes.T, cotangent,
            expand, expand_t, place_column(), place_row(), turn_tables(128), turn_tables(1),
        ),
        1,
    )
    kv_all = kv_all.reshape(TOKENS, 128)
    w_late = w_late.reshape(D, 1152)
    plane = ("y", "z", "c")
    g_in = lax.all_to_all(g_out, plane, split_axis=0, concat_axis=0, tiled=True)

    base = first_row.reshape(1).astype(jnp.int32)
    att, norm, sent, query_ext = attend(
        dealt_order, base, kv_all, aux, kv, own_aux, query, order_rows, key_norm
    )

    (
        residual, weigh_high, weigh_low, gmid, branch, gsent_own, side_rows, y_out,
        grad_gate, grad_up, grad_down,
    ) = moe(
        (
            sent.reshape(8, ROWS, 128), tokens, w_late, w_late, member, put, take, expand, expand_t,
            place, place_t, pick_high, pick_low, (pick_high + pick_low).T, cotangent,
            block_matrix((CAP, CAP + 1)),
            place[:BLOCK],
            block_matrix((CAP,)).T * constant(BLOCK_PLACE == CAP)[:, None],
            block_matrix((CAP + 1,)).T * constant(BLOCK_PLACE == CAP + 1)[:, None],
            g_in, w_gate[0], w_up[0], w_down[0],
        ),
        3,
    )
    y_in = lax.all_to_all(
        y_out, plane, split_axis=0, concat_axis=0, tiled=True
    ).reshape(SLOTS, D)
    grad_gate, grad_up, grad_down = (
        lax.psum_scatter(grad, "x", scatter_dimension=0, tiled=True)
        for grad in (grad_gate, grad_up, grad_down)
    )

    gsent_own = gsent_own.reshape(CHIP_ROWS, 128)
    branch_rows = lax.all_gather(branch, ("c", "x"), axis=0, tiled=True)
    side_sum = jnp.sum(side_rows.astype(F32), axis=0)

    dq, dkv = attend_back(
        dealt_order, base, kv_all, aux, kv, own_aux, query_ext, order_rows, gsent_own, att, norm
    )
    dkv_own, grad_out = scatter_plane(dkv, sent, branch_rows, 6)

    dnormed, mixed, qkv_rows, early = finish(
        (
            dq, dkv_own, cos, sin, normed, w_mine, y_in, weigh_high, weigh_low, residual,
            grad_out.reshape(16, 8, D), side_sum.reshape(16, 8, 128),
        ),
        7,
    )
    (
        grad_tokens, mixed, grad_query, grad_key, grad_value, gains, grad_out_rows, grad_router,
        grad_gate, grad_up, grad_down,
    ) = local_call(
        last_kernel,
        (
            shape((ROWS, D), F32),
            shape((ROWS, D), BF16),
            shape((8, D), F32),
            shape((8, 512), F32),
            shape((8, 512), F32),
            shape((2, 8), F32),
            shape((8, D), F32),
            shape((8, EXPERTS), F32),
            shape((256, FF), F32),
            shape((256, FF), F32),
            shape((128, D), F32),
        ),
    )(
        dnormed, tokens, gain_first, gmid, mixed, qkv_rows, w_query, w_key, w_value,
        gain_one.reshape(1, 8), early, grad_gate, grad_up, grad_down,
    )
    grad_gain_one, grad_gain_two = gains[0], gains[1]
    grad_gate, grad_up, grad_down = grad_gate[None], grad_up[None], grad_down[None]
    return (
        mixed,
        grad_tokens,
        grad_gain_one,
        grad_query,
        grad_key,
        grad_value,
        grad_out_rows,
        grad_gain_two,
        grad_router,
        grad_gate,
        grad_up,
        grad_down,
    )


def solution(mesh):
    grid = Mesh(mesh.devices.reshape(4, 4, 4, 2), AXES)
    rows = P(("y", "z", "c", "x"), None)
    vector = P(AXES)
    matrix = P(AXES, None)
    expert = P(("y", "z", "c"), None, None)
    in_specs = (
        rows, vector, matrix, matrix, matrix, matrix, vector, matrix, expert, expert, expert,
        P(), P(), rows, rows,
    )
    grads = P(("y", "z", "c"), "x", None)
    out_specs = (
        rows, rows, vector, matrix, matrix, matrix, matrix, vector, matrix, grads, grads, grads,
    )
    return jax.shard_map(body, mesh=grid, in_specs=in_specs, out_specs=out_specs, check_vma=False)
```

```python
import functools
import math

import jax
import jax.numpy as jnp
import ml_dtypes
import numpy as np
from jax import lax
from jax.experimental import pallas as pl
from jax.experimental.pallas import tpu as pltpu
from jax.sharding import Mesh
from jax.sharding import PartitionSpec as P

D = 1024
HEADS = 16
KV_HEADS = 8
HEAD_DIM = 64
EXPERTS = 32
FF = 512
CAP = 36
SLOT = 40
SLOTS = EXPERTS * SLOT
ROWS = 128
CHIP_ROWS = 1024
RUN = 256
TOKENS = 16384
NSEQ = 5
EPSILON = 1e-06
ROPE_BASE = 10000.0
FAR = float(2.0**100)
SIZE = {"x": 4, "y": 4, "z": 4, "c": 2}
AXES = ("x", "y", "z", "c")
MESH = pl.DeviceIdType.MESH
BF16 = jnp.bfloat16
F32 = jnp.float32
NN = (((1,), (0,)), ((), ()))
NT = (((1,), (1,)), ((), ()))
TN = (((0,), (0,)), ((), ()))
VMEM_BYTES = 56 * 1024 * 1024


def mm(a, b, dims=NN):
    return lax.dot_general(a, b, dims, preferred_element_type=F32)


def shape(dims, dtype):
    return jax.ShapeDtypeStruct(dims, dtype)


def halves(value):
    high = value.astype(BF16)
    return high, (value - high.astype(F32)).astype(BF16)


def local_call(kernel, outs, scratch=(), grid=None, in_specs=None, out_specs=None):
    extra = {}
    if grid is not None:
        extra = {"grid": grid, "in_specs": in_specs, "out_specs": out_specs}
    elif in_specs is not None:
        extra = {"in_specs": in_specs}
        if out_specs is not None:
            extra["out_specs"] = out_specs
    return pl.pallas_call(
        kernel,
        out_shape=outs,
        scratch_shapes=list(scratch),
        compiler_params=pltpu.CompilerParams(vmem_limit_bytes=VMEM_BYTES),
        **extra,
    )


class Late:
    def __init__(self, hbm, vmem, sem, columns):
        self.hbm, self.vmem = hbm, vmem
        source = hbm if columns is None else hbm.at[:, columns[0] : columns[1]]
        self.copy, self.ready = pltpu.make_async_copy(source, vmem, sem), False
        self.copy.start()

    def get(self):
        if not self.ready:
            self.copy.wait()
            self.ready = True
        return self.vmem

    def __getitem__(self, index):
        return self.get()[index]


class Early:
    def __init__(self, hbm, vmem, sem):
        self.vmem, self.copy = vmem, pltpu.make_async_copy(vmem, hbm, sem)

    def __getitem__(self, index):
        return self.vmem[index]

    def __setitem__(self, index, value):
        self.vmem[index] = value

    def store(self):
        self.copy.start()


def remote_call(kernel, inputs, kinds, outs, out_kinds, scratch, cid):
    spaces = {"s": pltpu.SMEM, "v": pltpu.VMEM}
    late = [(i, kind) for i, kind in enumerate(kinds) if kind not in ("s", "v", "h")]
    early = [i for i, kind in enumerate(out_kinds) if kind == "e"]

    def late_shape(i, kind):
        dims = inputs[i].shape if kind == "l" else (inputs[i].shape[0], kind[1] - kind[0])
        return pltpu.VMEM(dims, inputs[i].dtype)

    def wrapped(*refs):
        ins, rest = list(refs[: len(inputs)]), list(refs[len(inputs) :])
        results, rest = rest[: len(outs)], rest[len(outs) :]
        own, rest = rest[: len(scratch)], rest[len(scratch) :]
        late_v, rest = rest[: len(late)], rest[len(late) :]
        early_v, (late_sem, early_sem) = rest[: len(early)], rest[len(early) :]
        for n, (i, kind) in enumerate(late):
            ins[i] = Late(ins[i], late_v[n], late_sem.at[n], None if kind == "l" else kind)
        for n, i in enumerate(early):
            results[i] = Early(results[i], early_v[n], early_sem.at[n])
        kernel(*ins, *results, *own)
        for i, _ in late:
            ins[i].get()
        for i in early:
            results[i].copy.wait()

    return pl.pallas_call(
        wrapped,
        out_shape=list(outs),
        in_specs=[pl.BlockSpec(memory_space=spaces.get(kind, pl.ANY)) for kind in kinds],
        out_specs=[pl.BlockSpec(memory_space=spaces.get(kind, pl.ANY)) for kind in out_kinds],
        scratch_shapes=list(scratch)
        + [late_shape(i, kind) for i, kind in late]
        + [pltpu.VMEM(outs[i].shape, outs[i].dtype) for i in early]
        + [pltpu.SemaphoreType.DMA((max(1, len(late)),)), pltpu.SemaphoreType.DMA((max(1, len(early)),))],
        compiler_params=pltpu.CompilerParams(
            collective_id=cid, has_side_effects=True, vmem_limit_bytes=VMEM_BYTES
        ),
    )(*inputs)


def flat_index(coords, order):
    index = 0
    for axis in order:
        index = index * SIZE[axis] + coords[axis]
    return index


PLANE_ORDER = (
    (2, 2), (2, 3), (2, 1), (3, 2), (1, 2), (0, 2), (2, 0), (3, 1), (1, 3),
    (3, 3), (1, 1), (0, 3), (0, 1), (3, 0), (1, 0), (0, 0),
)
PLANE_OFFSETS = tuple({"y": dy, "z": dz} for dy, dz in PLANE_ORDER[:-1])
SPREAD_OFFSETS = tuple(
    {"y": dy, "z": dz, "c": (dc + i + 1) % 2}
    for i, (dy, dz) in enumerate(PLANE_ORDER)
    for dc in range(2)
    if (dy, dz, (dc + i + 1) % 2) != (0, 0, 0)
)
LINE_OFFSETS = tuple(
    {"x": dx, "c": dc} for dx, dc in ((2, 0), (2, 1), (1, 0), (3, 0), (1, 1), (3, 1), (0, 1))
)
OFFSETS = {("y", "z"): PLANE_OFFSETS, ("y", "z", "c"): SPREAD_OFFSETS, ("x", "c"): LINE_OFFSETS}


def position(axes):
    return {axis: lax.axis_index(axis) for axis in axes}


def moved(me, offset):
    return {axis: lax.rem(me[axis] + by, SIZE[axis]) if by else me[axis] for axis, by in offset.items()}


def greet(me, offsets):
    barrier = pltpu.get_barrier_semaphore()
    for offset in offsets:
        pl.semaphore_signal(barrier, inc=1, device_id=moved(me, offset), device_id_type=MESH)
    return lambda: pl.semaphore_wait(barrier, len(offsets))


def remote(src, dst, send, recv, slot, to):
    return pltpu.make_async_remote_copy(
        src_ref=src,
        dst_ref=dst,
        send_sem=send.at[slot],
        recv_sem=recv.at[slot],
        device_id=to,
        device_id_type=MESH,
    )


def scatter_plane(me, p_ref, o_ref, far_a, near_a, out_a, sum_a, far_b, near_b, out_b, send, recv):
    half = p_ref.vmem.shape[3] // 2
    lower, upper = pl.ds(0, half), pl.ds(half, half)
    axis = (("y", "z"), ("z", "y"))
    used = [0]

    def go(src, dst, t, which, by):
        to = {axis[t][which]: lax.rem(me[axis[t][which]] + by, 4)}
        item = remote(src, dst, send, recv, used[0], to)
        used[0] += 1
        item.start()
        return item

    def part(t, first, second, hbm=False):
        a = lax.rem(me[axis[t][0]] + first, 4)
        b = lax.rem(me[axis[t][1]] + second, 4)
        ref = p_ref.hbm if hbm else p_ref.get()
        return ref.at[a, b, 0] if t == 0 else ref.at[b, a, 1]

    turns = (2, 1, 3, 0)
    both = (0, 1)
    far, near = {}, {}
    for k, by in enumerate(turns):
        for t in both:
            far[k, t] = (
                go(part(t, 2, by, True).at[lower], far_a.at[t, k, 0], t, 0, 1),
                go(part(t, 2, by, True).at[upper], far_a.at[t, k, 1], t, 0, 3),
            )
    for k, by in enumerate(turns):
        for t in both:
            ahead, behind = part(t, 1, by), part(t, 3, by)
            far[k, t][0].wait()
            out_a[t, k, 0, 0:half] = (ahead[0:half].astype(F32) + far_a[t, k, 0].astype(F32)).astype(BF16)
            out_a[t, k, 0, half : 2 * half] = ahead[half : 2 * half]
            first = go(out_a.at[t, k, 0], near_a.at[t, k, 0], t, 0, 1)
            far[k, t][1].wait()
            out_a[t, k, 1, 0:half] = behind[0:half]
            out_a[t, k, 1, half : 2 * half] = (
                behind[half : 2 * half].astype(F32) + far_a[t, k, 1].astype(F32)
            ).astype(BF16)
            near[k, t] = (first, go(out_a.at[t, k, 1], near_a.at[t, k, 1], t, 0, 3))

    def summed(k, t):
        near[k, t][0].wait()
        near[k, t][1].wait()
        return (
            part(t, 0, turns[k])[...].astype(F32)
            + near_a[t, k, 0].astype(F32)
            + near_a[t, k, 1].astype(F32)
        )

    far_two, near_two = {}, {}
    for t in both:
        value = summed(0, t).astype(BF16)
        out_b[t, 0] = value
        far_two[t] = (
            go(out_b.at[t, 0, lower], far_b.at[t, 0], t, 1, 1),
            go(out_b.at[t, 0, upper], far_b.at[t, 1], t, 1, 3),
        )
    for k in (1, 2):
        for t in both:
            sum_a[t, k - 1] = summed(k, t)
    for t in both:
        far_two[t][0].wait()
        out_b[t, 1, 0:half] = (sum_a[t, 0, 0:half] + far_b[t, 0].astype(F32)).astype(BF16)
        out_b[t, 1, half : 2 * half] = sum_a[t, 0, half : 2 * half].astype(BF16)
        first = go(out_b.at[t, 1], near_b.at[t, 0], t, 1, 1)
        far_two[t][1].wait()
        out_b[t, 2, 0:half] = sum_a[t, 1, 0:half].astype(BF16)
        out_b[t, 2, half : 2 * half] = (
            sum_a[t, 1, half : 2 * half] + far_b[t, 1].astype(F32)
        ).astype(BF16)
        near_two[t] = (first, go(out_b.at[t, 2], near_b.at[t, 1], t, 1, 3))
    for t in both:
        value = summed(3, t)
        near_two[t][0].wait()
        near_two[t][1].wait()
        o_ref[t] = value + near_b[t, 0].astype(F32) + near_b[t, 1].astype(F32)


def lane_index(shape):
    return lax.broadcasted_iota(jnp.int32, shape, 1)


def turned(values):
    lane = lane_index(values.shape)
    up = pltpu.roll(values, 32, axis=1)
    down = pltpu.roll(values, 96, axis=1)
    return jnp.where(lane % 64 < 32, -down, up)


def gather_plane(kv_v, kv_hbm, go, me, own_sem, fillers):
    own = pltpu.make_async_copy(kv_v, kv_hbm.at[me["y"], me["z"]], own_sem)
    own.start()
    half = kv_v.shape[1] // 2
    lower, upper = pl.ds(0, half), pl.ds(half, half)
    axis = (("y", "z"), ("z", "y"))
    here = tuple((me[a], me[b]) for a, b in axis)
    step = {"plus": 1, "minus": 3, "far": 2, "own": 0}

    def place(t, a, b):
        return kv_hbm.at[a, b, 0] if t == 0 else kv_hbm.at[b, a, 1]

    def at(t, which, name):
        return lax.rem(here[t][which] + step[name], 4)

    def send_second(t, src, name):
        dst = place(t, at(t, 0, name), here[t][1])
        src = dst if src is None else src
        return (
            go(src, dst, {axis[t][1]: at(t, 1, "plus")}),
            go(src, dst, {axis[t][1]: at(t, 1, "minus")}),
        )

    def pass_on(t, which, a_name, b_name, part, direction):
        ref = place(t, at(t, 0, a_name), at(t, 1, b_name)).at[part]
        return go(ref, ref, {axis[t][which]: at(t, which, direction)})

    def forward_second(t, name, pair):
        pair[0].wait()
        a = pass_on(t, 1, name, "minus", lower, "plus")
        pair[1].wait()
        b = pass_on(t, 1, name, "plus", upper, "minus")
        return [a, b]

    first, second, last = {}, {}, []
    for t in (0, 1):
        dst = place(t, *here[t])
        first[t] = (
            go(kv_v.at[t], dst, {axis[t][0]: at(t, 0, "plus")}),
            go(kv_v.at[t], dst, {axis[t][0]: at(t, 0, "minus")}),
        )
    for t in (0, 1):
        second[t, "own"] = send_second(t, kv_v.at[t], "own")
    fillers[0]()
    far = {}
    for t in (0, 1):
        first[t][0].wait()
        a = pass_on(t, 0, "minus", "own", lower, "plus")
        second[t, "minus"] = send_second(t, None, "minus")
        first[t][1].wait()
        b = pass_on(t, 0, "plus", "own", upper, "minus")
        second[t, "plus"] = send_second(t, None, "plus")
        far[t] = (a, b)
    fillers[1]()
    for t in (0, 1):
        last += forward_second(t, "own", second[t, "own"])
    for t in (0, 1):
        far[t][0].wait()
        far[t][1].wait()
        second[t, "far"] = send_second(t, None, "far")
    fillers[2]()
    for name in ("minus", "plus", "far"):
        for t in (0, 1):
            last += forward_second(t, name, second[t, name])
    return last + [own]


def front_kernel(
    lengths_ref, tok_ref, wq_ref, wk_ref, wv_ref, wo_ref, router_ref, gain_one_ref, gain_two_ref,
    order_ref, routes_ref, expand_ref, expand_t_ref, col_ref, row_ref, turn_high_ref, turn_low_ref,
    q_ref, kv_own_ref, gain_ref, cos_ref, sin_ref, w_out_ref, member_ref, put_ref, take_ref,
    own_aux_ref, order_rows_ref, key_norm_ref, kv_hbm, late_hbm, normed_v, aux_v,
    rows_v, w_v, kv_v, long_v, side_v, w_ref, late_ref, send, recv, local,
):
    me = position(AXES)
    x, y, z, c = (me[axis] for axis in AXES)
    arrived = greet(me, LINE_OFFSETS + PLANE_OFFSETS)
    small = lane_index((8, 128))
    diagonal = lax.broadcasted_iota(jnp.int32, (8, 8), 0) == lane_index((8, 8))

    def column(ref):
        row = jnp.broadcast_to(ref[...].astype(F32), (8, 8))
        return jnp.sum(jnp.where(diagonal, row, 0.0), axis=1, keepdims=True)

    gain_lane = jnp.where(small == 0, column(gain_one_ref), 0.0).astype(BF16)
    for i in range(8):
        span = slice((i // 2) * 128, (i // 2 + 1) * 128)
        key, value = wk_ref[:, span].astype(F32), wv_ref[:, span].astype(F32)
        if i % 2 == 0:
            pair = jnp.where(small < 64, key, pltpu.roll(value, 64, axis=1))
        else:
            pair = jnp.where(small < 64, pltpu.roll(key, 64, axis=1), value)
        w_ref[i, :, 0:128] = wq_ref[:, i * 128 : (i + 1) * 128]
        w_ref[i, :, 128:256] = pair.astype(BF16)
        w_ref[i, :, 256:384] = gain_lane
    side_v[...] = jnp.zeros_like(side_v)
    side_v[:, 0:EXPERTS] = router_ref[...].astype(F32)
    late_ref[:, 0:D] = wo_ref[...]
    late_ref[:, D : D + 128] = jnp.where(small == EXPERTS, column(gain_two_ref), side_v[...]).astype(BF16)
    arrived()
    plus, minus, far = lax.rem(x + 1, 4), lax.rem(x + 3, 4), lax.rem(x + 2, 4)
    other = 1 - c
    lower, upper = pl.ds(0, 64), pl.ds(64, 64)
    used = [0]

    def go(src, dst, to):
        item = remote(src, dst, send, recv, used[0], to)
        used[0] += 1
        item.start()
        return item

    def keep(src, dst, slot):
        item = pltpu.make_async_copy(src, dst, local.at[slot])
        item.start()
        return item

    own = [
        keep(w_ref.at[x * 2 + c], w_v.at[x, y, z, c], 0),
        keep(late_ref, late_hbm.at[x, y, z, c], 1),
    ]
    own_rows = keep(tok_ref, rows_v.at[c, x], 2)
    first_w = []
    for offset in LINE_OFFSETS:
        to = moved(me, offset)
        first_w.append(go(w_ref.at[to["x"] * 2 + to["c"]], w_v.at[x, y, z, c], to))
    to_plus = go(tok_ref, rows_v.at[c, x], {"x": plus})
    to_minus = go(tok_ref, rows_v.at[c, x], {"x": minus})
    sides = [go(tok_ref, rows_v.at[c, x], {"c": other})]

    for item in own + first_w:
        item.wait()
    second_w = [go(w_v.at[:, y, z], w_v.at[:, y, z], moved(me, by)) for by in PLANE_OFFSETS]
    first_late = [go(late_ref, late_hbm.at[x, y, z, c], moved(me, by)) for by in PLANE_OFFSETS]

    chip = y * 4 + z
    mine = order_ref[pl.ds(pl.multiple_of(chip * 8, 8), 8), :]
    ends, total = [], jnp.int32(0)
    for i in range(NSEQ):
        total = total + lengths_ref[i]
        ends.append(total)
    place = mine
    for i in range(NSEQ):
        place = place - jnp.where(mine >= ends[i], lengths_ref[i], 0)
    lane = lane_index((ROWS, 128))

    def table(ref, picked):
        return mm(picked, ref[0]) + mm(picked, ref[1]) + mm(picked, ref[2])

    for i in range(8):
        wide = jnp.broadcast_to(place[i : i + 1, :].astype(F32), (ROWS, 128)).T.astype(jnp.int32)
        high = table(turn_high_ref, jnp.where(lane == lax.shift_right_logical(wide, 7), 1.0, 0.0).astype(BF16))
        low = table(turn_low_ref, jnp.where(lane == (wide & 127), 1.0, 0.0).astype(BF16))
        cos_ref[pl.ds(i * 128, 128), :] = high[:, :128] * low[:, :128] - high[:, 128:] * low[:, 128:]
        sin_ref[pl.ds(i * 128, 128), :] = high[:, 128:] * low[:, :128] + high[:, :128] * low[:, 128:]
    for i in range(4):
        order_rows_ref[i : i + 1, 0:128] = mine[2 * i : 2 * i + 1, :].astype(F32)
        order_rows_ref[i : i + 1, 128:256] = mine[2 * i + 1 : 2 * i + 2, :].astype(F32)

    to_plus.wait()
    next_plus = go(rows_v.at[c, minus, lower], rows_v.at[c, minus, lower], {"x": plus})
    sides.append(go(rows_v.at[c, minus], rows_v.at[c, minus], {"c": other}))
    to_minus.wait()
    next_minus = go(rows_v.at[c, plus, upper], rows_v.at[c, plus, upper], {"x": minus})
    sides.append(go(rows_v.at[c, plus], rows_v.at[c, plus], {"c": other}))
    next_plus.wait()
    next_minus.wait()
    sides.append(go(rows_v.at[c, far], rows_v.at[c, far], {"c": other}))
    own_rows.wait()
    for item in second_w:
        item.wait()
    weights = w_v[...].astype(F32).reshape(D, 384)
    w_out_ref[...] = weights.astype(BF16)
    gain = weights[:, 256:384].T[0:1, :]
    gain_ref[...] = gain
    low_lanes = lane_index((256, 128)) < 64

    def project(block):
        longest = jnp.zeros((256, 1), F32)
        for i in range(2):
            rows = pl.ds(pl.multiple_of(block * 512 + i * 256, 256), 256)
            tok = rows_v[block, pl.ds(2 * i, 2)].astype(F32).reshape(256, D)
            scale = lax.rsqrt(jnp.mean(tok * tok, axis=-1, keepdims=True) + EPSILON)
            normed = (tok * scale * gain).astype(BF16)
            normed_v[rows, :] = normed
            pre = mm(normed, w_out_ref[:, 0:256])
            cos, sin = cos_ref[rows, :], sin_ref[rows, :]
            q_pre, kv_pre = pre[:, :128], pre[:, 128:]
            query = (q_pre * cos + turned(q_pre) * sin).astype(BF16).astype(F32) * 0.125
            q_ref[0, rows, :] = jnp.where(low_lanes, query, 0.0).astype(BF16)
            q_ref[1, rows, :] = jnp.where(low_lanes, pltpu.roll(query, 64, axis=1), 0.0).astype(BF16)
            key = kv_pre * cos + turned(kv_pre) * sin
            kv = jnp.where(low_lanes, key, kv_pre).astype(BF16)
            kv_own_ref[rows, :] = kv
            kv_v[block, pl.ds(i * 256, 256), :] = kv
            rounded = kv.astype(F32)
            square = jnp.sum(jnp.where(low_lanes, rounded * rounded, 0.0), axis=1, keepdims=True)
            longest = jnp.maximum(longest, square)
        return jnp.max(longest, axis=0, keepdims=True)

    longest = project(c)
    for item in sides:
        item.wait()
    longest = jnp.maximum(longest, project(other))
    long_v[chip] = jnp.broadcast_to(longest, (8, 128))
    longs = [go(long_v.at[chip], long_v.at[chip], moved(me, by)) for by in PLANE_OFFSETS]
    stores = []
    for item in (q_ref, kv_own_ref, cos_ref, sin_ref, w_out_ref, normed_v):
        item.store()

    def routing():
        routes = jnp.concatenate([routes_ref[...].astype(F32), jnp.full((120, 128), -1.0, F32)], axis=0).T
        member = jnp.zeros((ROWS, 128), F32)
        for choice in range(8):
            member += jnp.where(routes[:, choice : choice + 1].astype(jnp.int32) == lane, 1.0, 0.0)
        below = lax.broadcasted_iota(jnp.int32, (ROWS, ROWS), 0) > lane_index((ROWS, ROWS))
        earlier = mm(jnp.where(below, 1.0, 0.0).astype(BF16), member.astype(BF16))
        slot = jnp.where(member > 0.5, earlier, -1.0).astype(BF16)
        member_ref[...] = member
        take = jnp.where(mm(slot, expand_ref[...]) == row_ref[...], 1.0, 0.0)
        take_ref[...] = take.astype(BF16)
        put = jnp.where(mm(expand_t_ref[...], slot, NT) == col_ref[...].astype(F32), 1.0, 0.0)
        put = put.astype(BF16)
        put_ref[...] = put
        for item in (put_ref, take_ref):
            item.store()

    def segments():
        sub = lax.broadcasted_iota(jnp.int32, (8, 128), 0)
        begin = jnp.zeros((8, 128), jnp.int32)
        end = jnp.full((8, 128), TOKENS, jnp.int32)
        for i in range(NSEQ):
            begin = jnp.where(sub == 3 + i, ends[i] - lengths_ref[i], begin)
            end = jnp.where(sub == 3 + i, ends[i], end)
        spot = jnp.where(sub == lane_index((8, 128)), 1.0, 0.0).astype(BF16)

        def block(step, carry):
            rows = order_ref[pl.ds(pl.multiple_of(step * 8, 8), 8), :]
            for i in range(8):
                order = jnp.broadcast_to(rows[i : i + 1, :], (8, 128))
                within = jnp.where((order >= begin) & (order < end), 1.0, 0.0).astype(BF16)
                here = pl.ds(pl.multiple_of(step * 1024 + i * 128, 128), 128)
                aux_v[here, :] = mm(within, spot, TN).astype(BF16)
            return carry

        lax.fori_loop(0, 16, block, 0)
        aux_v.store()
        own_aux_ref[...] = aux_v[pl.ds(pl.multiple_of(chip * CHIP_ROWS, CHIP_ROWS), CHIP_ROWS), :]
        own_aux_ref.store()

    def late():
        for item in second_late:
            item.wait()
        stores.append(go(late_hbm.at[:, :, :, c], late_hbm.at[:, :, :, c], {"c": other}))

    for item in first_late:
        item.wait()
    second_late = [
        go(late_hbm.at[x, :, :, c], late_hbm.at[x, :, :, c], {"x": to}) for to in (far, plus, minus)
    ]

    last = gather_plane(kv_v, kv_hbm, go, me, local.at[3], (routing, segments, late))
    for item in longs:
        item.wait()
    longest = long_v[0]
    for i in range(1, 16):
        longest = jnp.maximum(longest, long_v[i])
    key_norm_ref[...] = jnp.sqrt(longest)
    for item in last + stores:
        item.wait()


def front(inputs, cid):
    count = 7 + 3 + 3 + 15 + 15 + 2 + 3 + 40 + 1 + 15
    return remote_call(
        front_kernel,
        inputs,
        ("s", "h") + ("v",) * 9 + ("l",) * 6,
        [
            shape((2, CHIP_ROWS, 128), BF16),
            shape((CHIP_ROWS, 128), BF16),
            shape((1, D), F32),
            shape((CHIP_ROWS, 128), F32),
            shape((CHIP_ROWS, 128), F32),
            shape((D, 384), BF16),
            shape((ROWS, 128), F32),
            shape((SLOTS, ROWS), BF16),
            shape((ROWS, SLOTS), BF16),
            shape((CHIP_ROWS, 128), BF16),
            shape((4, RUN), F32),
            shape((8, 128), F32),
            shape((4, 4, 2, 512, 128), BF16),
            shape((4, 4, 4, 2, 8, 1152), BF16),
            shape((CHIP_ROWS, D), BF16),
            shape((TOKENS, 128), BF16),
        ],
        ("e", "e", "v", "e", "e", "e", "v", "e", "e", "e", "v", "v", "h", "h", "e", "e"),
        [
            pltpu.VMEM((2, 4, ROWS, D), BF16),
            pltpu.VMEM((4, 4, 4, 2, 8, 384), BF16),
            pltpu.VMEM((2, 512, 128), BF16),
            pltpu.VMEM((16, 8, 128), F32),
            pltpu.VMEM((8, 128), F32),
            pltpu.VMEM((8, 8, 384), BF16),
            pltpu.VMEM((8, 1152), BF16),
            pltpu.SemaphoreType.DMA((count,)),
            pltpu.SemaphoreType.DMA((count,)),
            pltpu.SemaphoreType.DMA((4,)),
        ],
        cid,
    )


def turn_tables(step):
    frequency = (np.float32(ROPE_BASE) ** (-np.arange(32, dtype=np.float32) / np.float32(32))).astype(np.float64)
    angles = (np.arange(128) * step)[:, None] * np.tile(frequency, 4)[None, :]
    rest = np.concatenate([np.cos(angles), np.sin(angles)], axis=1)
    parts = []
    for _ in range(3):
        part = rest.astype(np.float32).astype(ml_dtypes.bfloat16)
        parts.append(part)
        rest = rest - part.astype(np.float64)
    return jnp.asarray(np.stack(parts))


def order_pair(order_ref, index):
    row = jnp.broadcast_to(order_ref[pl.ds(index, 1), :], (RUN, RUN))
    return row, row.T


WIDE = 6
WIDE_BACK = 3


def run_lists(order_ref, base, first_ref):
    def note(block, carry):
        run = lax.shift_right_logical(order_ref[block * 512], 8)
        first_ref[run] = block * 512
        first_ref[63 - run] = block * 512 + RUN
        return carry

    lax.fori_loop(0, 32, note, 0)

    def count(part):
        run = lax.shift_right_logical(order_ref[base + lax.div(part, 2) * 512], 8)
        return jnp.where(lax.rem(part, 2) == 0, run, 31 - run)

    return count


def group_places(first_ref, number, half, step, wide):
    places = []
    for i in range(wide):
        index = step * wide + i
        at = jnp.where(index < number, half + index, 32 - half)
        places.append(pl.ds(pl.multiple_of(first_ref[at], RUN), RUN))
    return places


def attend_kernel(
    order_smem, base_ref, kv_hbm, aux_hbm, own_kv_ref, own_aux_ref, q_ref, order_ref, key_norm_ref,
    att_ref, norm_ref, sent_ref, qx_ref, kv_ref, aux_ref, acc_ref, first_ref, loads,
):
    copies = [
        pltpu.make_async_copy(kv_hbm, kv_ref, loads.at[0]),
        pltpu.make_async_copy(aux_hbm, aux_ref, loads.at[1]),
    ]
    for item in copies:
        item.start()
    count = run_lists(order_smem, base_ref[0], first_ref)
    key_norm = key_norm_ref[0:1, 0:1]
    lane = lane_index((RUN, 128))

    def right(keys):
        turned_keys = keys.T
        row = lax.broadcasted_iota(jnp.int32, turned_keys.shape, 0)
        return jnp.where(row < 64, jnp.ones_like(turned_keys), turned_keys)[56:]

    def prepare(part, carry):
        rows = pl.ds(pl.multiple_of(part * RUN, RUN), RUN)
        own_aux = own_aux_ref[rows, :]
        spread = jnp.where(lane < 3 + NSEQ, (own_aux.astype(F32) - 1.0) * FAR, 0.0)
        for head in range(2):
            query = q_ref[head, rows, :]
            wide = query.astype(F32)
            shift = jnp.ceil(jnp.sqrt(jnp.sum(wide * wide, axis=1, keepdims=True)) * key_norm)
            top = shift.astype(BF16).astype(F32)
            middle = (shift - top).astype(BF16).astype(F32)
            rest = shift - top - middle
            ext = jnp.where(lane == 0, -top, spread)
            ext = jnp.where(lane == 1, -middle, ext)
            ext = jnp.where(lane == 2, -rest, ext)
            here = pl.ds(head * RUN, RUN)
            qx_ref[part, here, 0:128] = query
            qx_ref[part, here, 128:256] = ext.astype(BF16)
        order_key, order_query = order_pair(order_ref, part)
        allowed = order_query <= order_key
        keys = own_kv_ref[rows, :]
        e = jnp.exp(mm(jnp.concatenate([keys, own_aux], axis=1), qx_ref[part], NT))
        e = jnp.where(jnp.concatenate([allowed, allowed], axis=1), e, 0.0)
        acc_ref[part] = mm(right(keys), e.astype(BF16))
        return carry

    lax.fori_loop(0, 4, prepare, 0)
    for item in copies:
        item.wait()

    def part_step(part, carry):
        number = count(part)
        half = lax.rem(part, 2) * 32

        def group(step, carry):
            places = group_places(first_ref, number, half, step, WIDE)
            keys = jnp.concatenate([kv_ref[here, :] for here in places], axis=0)
            aux = jnp.concatenate([aux_ref[here, :] for here in places], axis=0)
            e = jnp.exp(mm(jnp.concatenate([keys, aux], axis=1), qx_ref[part], NT))
            acc_ref[part] += mm(right(keys), e.astype(BF16))
            return carry

        lax.fori_loop(0, lax.div(number + WIDE - 1, WIDE), group, 0)
        rows = pl.ds(pl.multiple_of(part * RUN, RUN), RUN)
        total = acc_ref[part]
        value = total[8:72] / total[0:1]
        att = jnp.concatenate([value[:, :RUN], value[:, RUN:]], axis=0).T
        norm = jnp.broadcast_to(total[0:1], (64, 2 * RUN))
        norm = jnp.concatenate([norm[:, :RUN], norm[:, RUN:]], axis=0).T
        att_ref[rows, :] = att
        norm_ref[rows, :] = norm
        sent_ref[rows, :] = att.astype(BF16)
        return carry

    lax.fori_loop(0, 4, part_step, 0)


def attend(order, base, kv, aux, own_kv, own_aux, query, order_rows, key_norm):
    smem = pl.BlockSpec(memory_space=pltpu.SMEM)
    vmem = pl.BlockSpec(memory_space=pltpu.VMEM)
    hbm = pl.BlockSpec(memory_space=pl.ANY)
    return local_call(
        attend_kernel,
        (
            shape((CHIP_ROWS, 128), F32),
            shape((CHIP_ROWS, 128), F32),
            shape((CHIP_ROWS, 128), BF16),
            shape((4, 2 * RUN, 256), BF16),
        ),
        scratch=[
            pltpu.VMEM((TOKENS, 128), BF16),
            pltpu.VMEM((TOKENS, 128), BF16),
            pltpu.VMEM((4, 72, 2 * RUN), F32),
            pltpu.SMEM((64,), jnp.int32),
            pltpu.SemaphoreType.DMA((2,)),
        ],
        in_specs=[smem] * 2 + [hbm] * 2 + [vmem] * 5,
    )(order, base, kv, aux, own_kv, own_aux, query, order_rows, key_norm)


def attend_back_kernel(
    order_smem, base_ref, kv_hbm, aux_hbm, own_kv_ref, own_aux_ref, qx_ref, order_ref,
    gsent_ref, att_ref, norm_ref, dq_ref, dkv_hbm,
    kv_ref, aux_ref, acc_ref, dq_acc, gx_ref, rhs_ref, out_ref, first_ref, loads, stores,
):
    copies = [
        pltpu.make_async_copy(kv_hbm, kv_ref, loads.at[0]),
        pltpu.make_async_copy(aux_hbm, aux_ref, loads.at[1]),
    ]
    for item in copies:
        item.start()
    own_base = base_ref[0]
    count = run_lists(order_smem, own_base, first_ref)

    def clear(step, carry):
        acc_ref[pl.ds(pl.multiple_of(step * 512, 512), 512), :] = jnp.zeros((512, 128), F32)
        return carry

    lax.fori_loop(0, TOKENS // 512, clear, 0)
    lane = lane_index((RUN, 128))
    low_lanes = lane < 64

    def apply(part, here, e, prob):
        ds = (e * prob).astype(BF16)
        left = jnp.concatenate([ds, e.astype(BF16)], axis=1)
        acc_ref[here, :] += mm(left, rhs_ref[part])
        return ds

    def scores(part, keys, aux):
        both = jnp.concatenate([keys, aux], axis=1)
        return mm(both, qx_ref[part], NT), mm(both, gx_ref[part], NT)

    def prepare(part, carry):
        rows = pl.ds(pl.multiple_of(part * RUN, RUN), RUN)
        gsent = gsent_ref[rows, :].astype(F32)
        norm = norm_ref[rows, :]
        product = gsent * att_ref[rows, :] / norm
        scaled = (gsent / norm).astype(BF16).astype(F32)
        for head in range(2):
            mask = low_lanes if head == 0 else jnp.logical_not(low_lanes)
            delta = jnp.sum(jnp.where(mask, product, 0.0), axis=1, keepdims=True)
            top = delta.astype(BF16).astype(F32)
            middle = (delta - top).astype(BF16).astype(F32)
            rest = delta - top - middle
            ext = jnp.where(lane == 0, -top, 0.0)
            ext = jnp.where(lane == 1, -middle, ext)
            ext = jnp.where(lane == 2, -rest, ext)
            grad = pltpu.roll(scaled, 64, axis=1) if head == 0 else scaled
            grad = jnp.where(low_lanes, 0.0, grad).astype(BF16)
            here = pl.ds(head * RUN, RUN)
            gx_ref[part, here, 0:128] = grad
            gx_ref[part, here, 128:256] = ext.astype(BF16)
            rhs_ref[part, pl.ds(head * RUN, RUN), :] = qx_ref[part, here, 0:128]
            rhs_ref[part, pl.ds((2 + head) * RUN, RUN), :] = grad
        order_key, order_query = order_pair(order_ref, part)
        allowed = order_query <= order_key
        keys = own_kv_ref[rows, :]
        score, prob = scores(part, keys, own_aux_ref[rows, :])
        e = jnp.where(jnp.concatenate([allowed, allowed], axis=1), jnp.exp(score), 0.0)
        own = pl.ds(pl.multiple_of(own_base + part * RUN, RUN), RUN)
        dq_acc[part] = mm(keys.T[:64], apply(part, own, e, prob))
        return carry

    lax.fori_loop(0, 4, prepare, 0)
    for item in copies:
        item.wait()

    def part_step(part, carry):
        number = count(part)
        half = lax.rem(part, 2) * 32

        def group(step, carry):
            places = group_places(first_ref, number, half, step, WIDE_BACK)
            parts = [scores(part, kv_ref[here, :], aux_ref[here, :]) for here in places]
            ds = [
                apply(part, here, jnp.exp(score), prob)
                for here, (score, prob) in zip(places, parts)
            ]
            keys = jnp.concatenate([kv_ref[here, :] for here in places], axis=0)
            dq_acc[part] += mm(keys.T[:64], jnp.concatenate(ds, axis=0))
            return carry

        lax.fori_loop(0, lax.div(number + WIDE_BACK - 1, WIDE_BACK), group, 0)
        rows = pl.ds(pl.multiple_of(part * RUN, RUN), RUN)
        total = dq_acc[part] * 0.125
        dq_ref[rows, :] = jnp.concatenate([total[:, :RUN], total[:, RUN:]], axis=0).T
        return carry

    lax.fori_loop(0, 4, part_step, 0)

    def store(step):
        rows = pl.ds(pl.multiple_of(step * 2048, 2048), 2048)
        return pltpu.make_async_copy(out_ref.at[rows], dkv_hbm.at[rows], stores.at[step])

    def narrow(step, carry):
        rows = pl.ds(pl.multiple_of(step * 2048, 2048), 2048)
        out_ref[rows, :] = acc_ref[rows, :].astype(BF16)
        store(step).start()
        return carry

    def settle(step, carry):
        store(step).wait()
        return carry

    lax.fori_loop(0, 8, narrow, 0)
    lax.fori_loop(0, 8, settle, 0)


def attend_back(order, base, kv, aux, own_kv, own_aux, query_ext, order_rows, gsent, att, norm):
    smem = pl.BlockSpec(memory_space=pltpu.SMEM)
    vmem = pl.BlockSpec(memory_space=pltpu.VMEM)
    hbm = pl.BlockSpec(memory_space=pl.ANY)
    return local_call(
        attend_back_kernel,
        (shape((CHIP_ROWS, 128), F32), shape((TOKENS, 128), BF16)),
        scratch=[
            pltpu.VMEM((TOKENS, 128), BF16),
            pltpu.VMEM((TOKENS, 128), BF16),
            pltpu.VMEM((TOKENS, 128), F32),
            pltpu.VMEM((4, 64, 2 * RUN), F32),
            pltpu.VMEM((4, 2 * RUN, 256), BF16),
            pltpu.VMEM((4, 4 * RUN, 128), BF16),
            pltpu.VMEM((TOKENS, 128), BF16),
            pltpu.SMEM((64,), jnp.int32),
            pltpu.SemaphoreType.DMA((2,)),
            pltpu.SemaphoreType.DMA((8,)),
        ],
        in_specs=[smem] * 2 + [hbm] * 2 + [vmem] * 7,
        out_specs=[vmem, hbm],
    )(order, base, kv, aux, own_kv, own_aux, query_ext, order_rows, gsent, att, norm)


SLOT_EXPERT = np.arange(SLOTS) // SLOT
SLOT_PLACE = np.arange(SLOTS) % SLOT


def constant(array):
    return jnp.asarray(np.asarray(array).astype(ml_dtypes.bfloat16))


def expand_matrix():
    return constant(np.arange(128)[:, None] == SLOT_EXPERT[None, :])


def place_matrix():
    return constant(SLOT_PLACE[:, None] == np.arange(128)[None, :])


def pick_matrix(place):
    return constant((SLOT_EXPERT[:, None] == np.arange(128)[None, :]) & (SLOT_PLACE[:, None] == place))


def place_column():
    used = np.where(SLOT_PLACE < CAP, SLOT_PLACE, -5)
    return constant(np.broadcast_to(used[:, None], (SLOTS, 128)))


def place_row():
    used = np.where(SLOT_PLACE < CAP, SLOT_PLACE, -5)
    return jnp.asarray(used[None, :].astype(np.float32))


BLOCK = 8 * SLOT
BLOCK_SOURCE = np.arange(BLOCK) // SLOT
BLOCK_PLACE = np.arange(BLOCK) % SLOT


def block_matrix(places):
    hit = np.isin(BLOCK_PLACE, places)[None, :] & (BLOCK_SOURCE[:, None] == BLOCK_SOURCE[None, :])
    return constant(hit)


def packed_pairs(values):
    total = sum(int(value) << (2 * i) for i, value in enumerate(values))
    return np.uint32(total).astype(np.int32)


STEP_Y = packed_pairs([dy for dy, _ in PLANE_ORDER])
STEP_Z = packed_pairs([dz for _, dz in PLANE_ORDER])


def moe_kernel(
    sent_ref, tok_ref, w_out_ref, router_ref, member_ref, put_ref, take_ref, expand_ref,
    expand_t_ref, place_ref, place_t_ref, cot_ref, cots_hbm, gate_hbm, up_hbm, down_hbm,
    residual_ref, weigh_high_ref, weigh_low_ref, gmid_ref, branch_ref, gsent_in, side_in,
    y_hbm, grads_hbm,
    sent_in, x_out, x_in, y_v, back_out, back_in, gate_v, up_v, down_v,
    sum_gate, sum_up, sum_down, grads_v, mixed_v, gate_probs, gsent_out, side_out, cots_v,
    note_out, note_in, answer_out, answer_in,
    x_send, x_recv, back_send, back_recv, note_send, note_recv, answer_send, answer_recv,
    line_send, line_recv, local,
):
    me = position(AXES)
    x_at, y_at, z_at, c_at = (me[axis] for axis in AXES)
    expert = (y_at * 4 + z_at) * 2 + c_at

    def offset(k):
        pair = lax.div(k, 2)
        dy = lax.shift_right_logical(jnp.int32(STEP_Y), 2 * pair) & 3
        dz = lax.shift_right_logical(jnp.int32(STEP_Z), 2 * pair) & 3
        return dy, dz, lax.rem(k + pair, 2)

    def toward(k):
        dy, dz, dc = offset(k)
        return {"y": lax.rem(y_at + dy, 4), "z": lax.rem(z_at + dz, 4), "c": lax.rem(c_at + dc, 2)}

    def source(k):
        dy, dz, dc = offset(k)
        return {
            "y": lax.rem(y_at + 4 - dy, 4),
            "z": lax.rem(z_at + 4 - dz, 4),
            "c": lax.rem(c_at + dc, 2),
        }

    def number(at):
        return (at["y"] * 4 + at["z"]) * 2 + at["c"]

    loads = [
        pltpu.make_async_copy(src, dst, local.at[i])
        for i, (src, dst) in enumerate(
            ((cots_hbm, cots_v), (gate_hbm, gate_v), (up_hbm, up_v), (down_hbm, down_v))
        )
    ]
    for item in loads:
        item.start()
    barrier = pltpu.get_barrier_semaphore()
    for by in LINE_OFFSETS:
        pl.semaphore_signal(barrier, inc=1, device_id=moved(me, by), device_id_type=MESH)

    def hello(k, carry):
        pl.semaphore_signal(barrier, inc=1, device_id=toward(k), device_id_type=MESH)
        return carry

    lax.fori_loop(0, 31, hello, 0)
    sum_gate[...] = jnp.zeros_like(sum_gate)
    sum_up[...] = jnp.zeros_like(sum_up)
    sum_down[...] = jnp.zeros_like(sum_down)
    pl.semaphore_wait(barrier, 31 + len(LINE_OFFSETS))

    here_line = x_at * 2 + c_at
    moves = []
    for i, by in enumerate(LINE_OFFSETS):
        to = moved(me, by)
        moves.append(
            remote(sent_ref.at[to["c"] * 4 + to["x"]], sent_in.at[here_line], line_send, line_recv, i, to)
        )
        moves[-1].start()
    kept = pltpu.make_async_copy(sent_ref.at[c_at * 4 + x_at], sent_in.at[here_line], local.at[4])
    kept.start()
    for item in moves + [kept]:
        item.wait()
    sent = jnp.concatenate([sent_in[i] for i in range(8)], axis=1)
    residual = tok_ref[...].astype(F32) + mm(sent, w_out_ref[...])
    residual_ref[...] = residual
    residual_ref.store()
    gain = router_ref[...].astype(F32).T[EXPERTS : EXPERTS + 1, :]
    scale = lax.rsqrt(jnp.mean(residual * residual, axis=-1, keepdims=True) + EPSILON)
    mixed = (residual * scale * gain).astype(BF16)
    mixed_v[...] = mixed
    put = put_ref[...]

    def slots(value):
        return value.reshape(EXPERTS, SLOT, value.shape[1]).astype(BF16)

    x_out[:, :, 0:512] = slots(mm(put, mixed[:, 0:512]))
    x_out[:, :, 512:1024] = slots(mm(put, mixed[:, 512:1024]))

    def x_copy(k):
        to = toward(k)
        return remote(x_out.at[number(to)], x_in.at[k], x_send, x_recv, k, to)

    def note_copy(k):
        to = toward(k)
        return remote(note_out.at[number(to)], note_in.at[k], note_send, note_recv, k, to)

    def x_start(k, carry):
        x_copy(k).start()
        return carry

    lax.fori_loop(0, 8, x_start, 0)
    kept = pltpu.make_async_copy(x_out.at[expert], x_in.at[31], local.at[4])
    kept.start()
    logits = mm(mixed, router_ref[...])
    member = member_ref[...]
    masked = jnp.where(member > 0.5, logits, -FAR)
    top = jnp.max(masked, axis=1, keepdims=True)
    power = jnp.where(member > 0.5, jnp.exp(masked - top), 0.0)
    gate = power / jnp.sum(power, axis=1, keepdims=True)
    gate_probs[...] = gate
    gate_high, gate_low = halves(gate)
    spread = mm(gate_high, expand_ref[...]) + mm(gate_low, expand_ref[...])
    weigh = take_ref[...].astype(F32) * spread
    weigh_high, weigh_low = halves(weigh)
    weigh_high_ref[...] = weigh_high
    weigh_low_ref[...] = weigh_low
    weigh_high_ref.store()
    weigh_low_ref.store()
    wide_expand = expand_ref[...].astype(F32)
    rows_high, rows_low = halves(wide_expand * jnp.sum(weigh, axis=0, keepdims=True))
    gates = mm(rows_high, place_ref[...]) + mm(rows_low, place_ref[...])
    token = lax.broadcasted_iota(jnp.int32, (ROWS, SLOTS), 0).astype(F32)
    token = jnp.sum(take_ref[...].astype(F32) * token, axis=0, keepdims=True)
    token = mm((wide_expand * token).astype(BF16), place_ref[...])
    top_row = lax.broadcasted_iota(jnp.int32, (8, 128), 0) == 0
    for i in range(EXPERTS):
        note_out[i] = jnp.where(
            top_row,
            jnp.broadcast_to(gates[i : i + 1], (8, 128)),
            jnp.broadcast_to(token[i : i + 1], (8, 128)),
        )

    def note_start(k, carry):
        note_copy(k).start()
        return carry

    lax.fori_loop(0, 31, note_start, 0)
    lax.fori_loop(8, 31, x_start, 0)
    note_in[31] = note_out[expert]
    kept.wait()
    for item in loads:
        item.wait()

    def cot_of(at):
        return cots_v[number(at)]

    slot_lane = lane_index((SLOT, 128))
    own_lane = slot_lane == lax.broadcasted_iota(jnp.int32, (SLOT, 128), 0)

    def answer_copy(k):
        return remote(answer_out.at[k], answer_in.at[expert], answer_send, answer_recv, k, source(k))

    def back_copy(k):
        to = source(k)
        return remote(back_out.at[k], back_in.at[expert], back_send, back_recv, k, to)

    def back_kept():
        return pltpu.make_async_copy(back_out.at[31], back_in.at[expert], local.at[4])

    def group(step, carry):
        first = step * 8
        for i in range(8):
            k = first + i

            @pl.when(k < 31)
            def _():
                x_copy(k).wait_recv()
                note_copy(k).wait_recv()

        x = x_in[pl.ds(first, 8)].astype(F32).reshape(BLOCK, D).astype(BF16)
        share, chosen = [], []
        for i in range(8):
            note = note_in[first + i]
            share.append(jnp.sum(jnp.where(own_lane, note[0:1], 0.0), axis=1, keepdims=True))
            row = jnp.sum(jnp.where(own_lane, note[1:2], 0.0), axis=1, keepdims=True)
            chosen.append(jnp.where(slot_lane.astype(F32) == row, 1.0, 0.0).astype(BF16))
        share = jnp.concatenate(share, axis=0)
        g = jnp.concatenate([mm(chosen[i], cot_of(source(first + i))) for i in range(8)], axis=0)
        a = mm(x, gate_v[...])
        b = mm(x, up_v[...])
        s = 1.0 / (1.0 + jnp.exp(-a))
        silu = a * s
        hidden = (silu * b).astype(BF16)
        y = mm(hidden, down_v[...]).astype(BF16).astype(F32)
        dgate = jnp.sum(y * g, axis=1, keepdims=True)
        for i in range(8):
            k = first + i
            own = dgate[i * SLOT : (i + 1) * SLOT]
            row = jnp.sum(jnp.where(own_lane, own, 0.0), axis=0, keepdims=True)
            answer_out[k] = jnp.broadcast_to(row, (8, 128))

            @pl.when(k < 31)
            def _():
                answer_copy(k).start()

        y = y.reshape(8, SLOT, D)
        for i in range(8):
            y_v[number(source(first + i))] = y[i].astype(BF16)
        gy = (g * share).astype(BF16)
        dhidden = mm(gy, down_v[...], NT)
        da = (dhidden * b * (s * (1.0 + a * (1.0 - s)))).astype(BF16)
        db = (dhidden * silu).astype(BF16)
        back = mm(da, gate_v[...], NT) + mm(db, up_v[...], NT)
        back_out[pl.ds(first, 8)] = back.reshape(8, SLOT, D).astype(BF16)
        for i in range(8):
            k = first + i

            @pl.when(k < 31)
            def _():
                back_copy(k).start()

            @pl.when(k == 31)
            def _():
                back_kept().start()

        sum_gate[...] += mm(x, da, TN)
        sum_up[...] += mm(x, db, TN)
        sum_down[...] += mm(hidden, gy, TN)
        return carry

    lax.fori_loop(0, 4, group, 0)
    answer_in[expert] = answer_out[31]
    for i in range(4):
        grads_v[i * 768 : i * 768 + 256] = sum_gate[i * 256 : (i + 1) * 256].astype(BF16)
        grads_v[i * 768 + 256 : i * 768 + 512] = sum_up[i * 256 : (i + 1) * 256].astype(BF16)
        down = sum_down[i * 128 : (i + 1) * 128].astype(BF16)
        grads_v[i * 768 + 512 : i * 768 + 640] = down[:, 0:FF]
        grads_v[i * 768 + 640 : i * 768 + 768] = down[:, FF:D]
    stores = [
        pltpu.make_async_copy(src, dst, local.at[i])
        for i, (src, dst) in enumerate(((y_v, y_hbm), (grads_v, grads_hbm)))
    ]
    for item in stores:
        item.start()

    def answers(k, carry):
        answer_copy(k).wait()
        return carry

    lax.fori_loop(0, 31, answers, 0)
    take = take_ref[...]
    rows_high, rows_low = halves(
        jnp.concatenate([answer_in[i][0:1] for i in range(EXPERTS)] + [jnp.zeros((96, 128), F32)], axis=0)
    )
    spread = mm(rows_high, place_t_ref[...]) + mm(rows_low, place_t_ref[...])
    along = jnp.sum(spread * expand_ref[...].astype(F32), axis=0, keepdims=True)
    found_high, found_low = halves(take.astype(F32) * along)
    dgate = mm(found_high, expand_t_ref[...]) + mm(found_low, expand_t_ref[...])
    gate = gate_probs[...]
    dlogits = gate * (dgate - jnp.sum(gate * dgate, axis=1, keepdims=True))
    dlogits = dlogits.astype(BF16)
    dmixed = mm(dlogits, router_ref[...], NT)

    def settle(k, carry):
        x_copy(k).wait_send()
        note_copy(k).wait_send()
        back_copy(k).wait()
        return carry

    lax.fori_loop(0, 31, settle, 0)
    back_kept().wait()

    for i in range(2):
        rows = back_in[i * 16 : (i + 1) * 16].astype(F32).reshape(640, D).astype(BF16)
        dmixed += mm(take[:, i * 640 : (i + 1) * 640], rows)
    residual = residual_ref[...]
    scale = lax.rsqrt(jnp.mean(residual * residual, axis=-1, keepdims=True) + EPSILON)
    gain = router_ref[...].astype(F32).T[EXPERTS : EXPERTS + 1, :]
    weighted = dmixed * gain
    inner = jnp.mean(weighted * residual, axis=-1, keepdims=True)
    gmid = cot_ref[...].astype(F32) + scale * weighted - residual * (scale * scale * scale) * inner
    gmid_ref[...] = gmid
    gmid_ref.store()
    branch = gmid.astype(BF16)
    branch_ref[...] = branch
    branch_ref.store()
    gsent = mm(branch, w_out_ref[...], NT).astype(BF16)
    for i in range(8):
        gsent_out[i] = gsent[:, i * 128 : (i + 1) * 128]
    back_line = c_at * 4 + x_at
    moves = []
    for i, by in enumerate(LINE_OFFSETS):
        to = moved(me, by)
        moves.append(
            remote(
                gsent_out.at[to["x"] * 2 + to["c"]], gsent_in.at[back_line], line_send, line_recv, 7 + i, to
            )
        )
        moves[-1].start()
    kept = pltpu.make_async_copy(gsent_out.at[here_line], gsent_in.at[back_line], local.at[4])
    kept.start()
    moves.append(kept)
    gain_grad = jnp.sum(dmixed * residual * scale, axis=0, keepdims=True)
    grads = mm(dlogits, mixed_v[...], TN)
    row = lax.broadcasted_iota(jnp.int32, (128, D), 0)
    grads = jnp.where(row == EXPERTS, gain_grad, grads).T.reshape(4, 16, 2, 8, 128)
    for i in range(8):
        side_out[i] = grads[i // 2, :, i % 2].reshape(ROWS, 128).astype(BF16)
    for i, by in enumerate(LINE_OFFSETS):
        to = moved(me, by)
        moves.append(
            remote(
                side_out.at[to["x"] * 2 + to["c"]], side_in.at[back_line], line_send, line_recv, 14 + i, to
            )
        )
        moves[-1].start()
    kept = pltpu.make_async_copy(side_out.at[here_line], side_in.at[back_line], local.at[5])
    kept.start()
    for item in moves + [kept] + stores:
        item.wait()


def moe(inputs, cid):
    slots = (EXPERTS, SLOT, D)
    up, down = (D, FF), (FF, D)
    dma = pltpu.SemaphoreType.DMA
    return remote_call(
        moe_kernel,
        inputs,
        ("h", "l", (0, D), (D, D + 128)) + ("l",) * 8 + ("h",) * 4,
        [
            shape((ROWS, D), F32),
            shape((ROWS, SLOTS), BF16),
            shape((ROWS, SLOTS), BF16),
            shape((ROWS, D), F32),
            shape((ROWS, D), BF16),
            shape((8, ROWS, 128), BF16),
            shape((8, ROWS, 128), BF16),
            shape(slots, BF16),
            shape((3 * D, FF), BF16),
        ],
        ("e", "e", "e", "e", "e", "v", "v", "h", "h"),
        [
            pltpu.VMEM((8, ROWS, 128), BF16),
            pltpu.VMEM(slots, BF16),
            pltpu.VMEM(slots, BF16),
            pltpu.VMEM(slots, BF16),
            pltpu.VMEM(slots, BF16),
            pltpu.VMEM(slots, BF16),
            pltpu.VMEM(up, BF16),
            pltpu.VMEM(up, BF16),
            pltpu.VMEM(down, BF16),
            pltpu.VMEM(up, F32),
            pltpu.VMEM(up, F32),
            pltpu.VMEM(down, F32),
            pltpu.VMEM((3 * D, FF), BF16),
            pltpu.VMEM((ROWS, D), BF16),
            pltpu.VMEM((ROWS, 128), F32),
            pltpu.VMEM((8, ROWS, 128), BF16),
            pltpu.VMEM((8, ROWS, 128), BF16),
            pltpu.VMEM((EXPERTS, ROWS, D), BF16),
            pltpu.VMEM((EXPERTS, 8, 128), F32),
            pltpu.VMEM((EXPERTS, 8, 128), F32),
            pltpu.VMEM((EXPERTS, 8, 128), F32),
            pltpu.VMEM((EXPERTS, 8, 128), F32),
        ]
        + [dma((31,))] * 8
        + [
            dma((21,)),
            dma((21,)),
            dma((6,)),
        ],
        cid,
    )


def tail_kernel(
    partial_ref, sent_ref, branch_ref, side_rows_ref, dq_ref, cos_ref, sin_ref, normed_ref, w_ref,
    y_ref, weigh_high_ref, weigh_low_ref, residual_ref,
    dnormed_out, mixed_out, grads_out, early_out,
    dqkv, part_out, part_in, part_own, line_out, line_in, share_out, share_in, total,
    out_in, side_in, dkv_ref, out_ref, side_ref, far_a, near_a, out_a, sum_a, far_b, near_b, out_b,
    plane_send, plane_recv, send, recv, local, out_recv,
):
    me = position(AXES)
    x, y, z, c = (me[axis] for axis in AXES)
    mine = y * 4 + z
    alone = jnp.where(c == lax.div(y, 2), 1, 0)
    barrier = pltpu.get_barrier_semaphore()

    def owner(k):
        at = lax.rem(lax.rem(y, 2) * 8 + z * 2 + c + k, 16)
        to = {"y": 2 * c + lax.div(at, 8), "z": lax.rem(lax.div(at, 2), 4), "c": lax.rem(at, 2)}
        return at, to

    def origin(k):
        at = lax.rem(mine + k, 16)
        return at, {"y": lax.div(at, 4), "z": lax.rem(at, 4), "c": lax.div(y, 2)}

    for k in range(1, 16):
        pl.semaphore_signal(barrier, inc=1, device_id=origin(k)[1], device_id_type=MESH)

    @pl.when(alone == 0)
    def _():
        pl.semaphore_signal(barrier, inc=1, device_id=origin(0)[1], device_id_type=MESH)

    offsets = LINE_OFFSETS + PLANE_OFFSETS
    for offset in offsets:
        pl.semaphore_signal(barrier, inc=1, device_id=moved(me, offset), device_id_type=MESH)
    grad_out = mm(sent_ref[...], branch_ref[...], TN)
    for j in range(16):
        out_ref[j] = grad_out[j * 8 : (j + 1) * 8]
    side = side_rows_ref[0].astype(F32)
    for i in range(1, 8):
        side += side_rows_ref[i].astype(F32)
    side_ref[...] = side.reshape(16, 8, 128)
    pl.semaphore_wait(barrier, len(offsets) + 16 - alone)
    scatter_plane(
        me, partial_ref, dkv_ref, far_a, near_a, out_a, sum_a, far_b, near_b, out_b, plane_send, plane_recv
    )
    used = [0]

    def go(src, dst, to):
        item = remote(src, dst, send, recv, used[0], to)
        used[0] += 1
        item.start()
        return item

    other = 1 - c
    low_lanes = lane_index((256, 128)) < 64

    def out_copy(k):
        at, to = owner(k)
        return pltpu.make_async_remote_copy(
            src_ref=out_ref.at[at], dst_ref=out_in.at[mine], send_sem=send.at[used[0] + k],
            recv_sem=out_recv.at[mine], device_id=to, device_id_type=MESH,
        )

    def out_kept():
        return pltpu.make_async_copy(out_ref.at[owner(0)[0]], out_in.at[mine], local.at[1])

    out_copies = [out_copy(k) for k in range(16)]
    used[0] += 16
    out_arrivals = []
    for k in range(16):
        at, to = origin(k)
        out_arrivals.append(
            pltpu.make_async_remote_copy(
                src_ref=out_ref.at[0], dst_ref=out_in.at[at], send_sem=send.at[0],
                recv_sem=out_recv.at[at], device_id=to, device_id_type=MESH,
            )
        )

    @pl.when(alone == 0)
    def _():
        out_copies[0].start()

    @pl.when(alone == 1)
    def _():
        out_kept().start()

    for item in out_copies[1:]:
        item.start()
    early = []
    for offset in PLANE_OFFSETS:
        to = moved(me, offset)
        early.append(go(side_ref.at[to["y"] * 4 + to["z"]], side_in.at[mine], to))
    side_kept = pltpu.make_async_copy(side_ref.at[mine], side_in.at[mine], local.at[2])
    side_kept.start()
    early.append(side_kept)

    def turn_back(first):
        rows = pl.ds(pl.multiple_of(first, 256), 256)
        cos, sin = cos_ref[rows, :], sin_ref[rows, :]
        dq, dkv = dq_ref[rows, :], dkv_ref[lax.div(first, 512), pl.ds(lax.rem(first, 512), 256), :]
        dq = (dq * cos - turned(dq) * sin).astype(BF16)
        dkv = jnp.where(low_lanes, dkv * cos - turned(dkv) * sin, dkv).astype(BF16)
        both = jnp.concatenate([dq, dkv], axis=1)
        dqkv[rows, :] = both
        return mm(both, w_ref[...], NT)

    crossing = []
    for i in range(2):
        value = turn_back(other * 512 + i * 256).astype(BF16)
        part_out[2 * i] = value[:ROWS]
        part_out[2 * i + 1] = value[ROWS:]
        span = pl.ds(2 * i, 2)
        crossing.append(go(part_out.at[span], part_in.at[span], {"c": other}))
    for i in range(2):
        value = turn_back(c * 512 + i * 256)
        part_own[2 * i] = value[:ROWS]
        part_own[2 * i + 1] = value[ROWS:]
    for item in crossing:
        item.wait()
    along = []
    for i, by in enumerate((2, 1, 3)):
        to = lax.rem(x + by, 4)
        line_out[i] = (part_own[to] + part_in[to].astype(F32)).astype(BF16)
        along.append(go(line_out.at[i], line_in.at[i], {"x": to}))
    for i in range(4):
        columns = pl.ds(i * 256, 256)
        grad = mm(normed_ref[:, columns], dqkv[...], TN).astype(BF16)
        share_out[i] = grad.reshape(16, 16, 256)
    spread = []
    for offset in PLANE_OFFSETS:
        to = moved(me, offset)
        spread.append(go(share_out.at[:, to["y"] * 4 + to["z"]], share_in.at[mine], to))
    kept = pltpu.make_async_copy(share_out.at[:, mine], share_in.at[mine], local.at[0])
    kept.start()
    mixed = mm(weigh_high_ref[...], y_ref[...]) + mm(weigh_low_ref[...], y_ref[...])
    mixed_out[...] = (residual_ref[...] + mixed).astype(BF16)
    mixed_out.store()
    for item in spread + [kept]:
        item.wait()
    for i in range(4):
        value = share_in[0, i].astype(F32)
        for j in range(1, 16):
            value += share_in[j, i].astype(F32)
        total[i] = value.reshape(2, 8, 256)
    ends = []
    here = x * 2 + c
    for offset in LINE_OFFSETS:
        to = moved(me, offset)
        ends.append(go(total.at[to["x"], to["c"]], grads_out.at[here], to))
    kept = pltpu.make_async_copy(total.at[x, c], grads_out.at[here], local.at[0])
    kept.start()
    for item in out_copies[1:]:
        item.wait_send()
    for item in out_arrivals[1:]:
        item.wait_recv()

    @pl.when(alone == 0)
    def _():
        out_copies[0].wait_send()
        out_arrivals[0].wait_recv()

    @pl.when(alone == 1)
    def _():
        out_kept().wait()

    for item in early:
        item.wait()
    out_total, side_total = out_in[0], side_in[0]
    for j in range(1, 16):
        out_total += out_in[j]
        side_total += side_in[j]
    early_out[:, 0:D] = out_total
    early_out[:, D : D + 128] = side_total
    for item in along:
        item.wait()
    dnormed = part_own[x] + part_in[x].astype(F32)
    for i in range(3):
        dnormed += line_in[i].astype(F32)
    dnormed_out[...] = dnormed
    for item in ends + [kept]:
        item.wait()


def tail(inputs, cid):
    count = 2 + 3 + 15 + 7 + 16 + 15
    return remote_call(
        tail_kernel,
        inputs,
        ("l",) * 8 + ((0, 256), "v", "l", "l", "l"),
        [
            shape((ROWS, D), F32),
            shape((ROWS, D), BF16),
            shape((8, 8, 256), F32),
            shape((8, D + 128), F32),
        ],
        ("v", "e", "v", "v"),
        [
            pltpu.VMEM((CHIP_ROWS, 256), BF16),
            pltpu.VMEM((4, ROWS, D), BF16),
            pltpu.VMEM((4, ROWS, D), BF16),
            pltpu.VMEM((4, ROWS, D), F32),
            pltpu.VMEM((3, ROWS, D), BF16),
            pltpu.VMEM((3, ROWS, D), BF16),
            pltpu.VMEM((4, 16, 16, 256), BF16),
            pltpu.VMEM((16, 4, 16, 256), BF16),
            pltpu.VMEM((4, 2, 8, 256), F32),
            pltpu.VMEM((16, 8, D), F32),
            pltpu.VMEM((16, 8, 128), F32),
            pltpu.VMEM((2, 512, 128), F32),
            pltpu.VMEM((16, 8, D), F32),
            pltpu.VMEM((16, 8, 128), F32),
            pltpu.VMEM((2, 4, 2, 256, 128), BF16),
            pltpu.VMEM((2, 4, 2, 512, 128), BF16),
            pltpu.VMEM((2, 4, 2, 512, 128), BF16),
            pltpu.VMEM((2, 2, 512, 128), F32),
            pltpu.VMEM((2, 2, 256, 128), BF16),
            pltpu.VMEM((2, 2, 512, 128), BF16),
            pltpu.VMEM((2, 3, 512, 128), BF16),
            pltpu.SemaphoreType.DMA((40,)),
            pltpu.SemaphoreType.DMA((40,)),
            pltpu.SemaphoreType.DMA((count,)),
            pltpu.SemaphoreType.DMA((count,)),
            pltpu.SemaphoreType.DMA((3,)),
            pltpu.SemaphoreType.DMA((16,)),
        ],
        cid,
    )


def last_kernel(
    dnormed_ref, tok_ref, gain_ref, gmid_ref, mixed_ref, rows_ref, wq_ref, wk_ref, wv_ref, own_gain_ref, early_ref,
    grads_ref,
    tokens_out, mixed_out, query_out, key_out, value_out, gains_out, grad_out, router_out,
    gate_out, up_out, down_out,
):
    tok = tok_ref[...].astype(F32)
    scale = lax.rsqrt(jnp.mean(tok * tok, axis=-1, keepdims=True) + EPSILON)
    weighted = dnormed_ref[...] * gain_ref[...]
    inner = jnp.mean(weighted * tok, axis=-1, keepdims=True)
    tokens_out[...] = gmid_ref[...] + scale * weighted - tok * (scale * scale * scale) * inner
    mixed_out[...] = mixed_ref[...]
    for i in range(8):
        query_out[:, i * 128 : (i + 1) * 128] = rows_ref[i][:, :128]
    lanes = lane_index((8, 128)) < 64
    for i in range(4):
        first, second = rows_ref[2 * i][:, 128:], rows_ref[2 * i + 1][:, 128:]
        key_out[:, i * 128 : (i + 1) * 128] = jnp.where(lanes, first, pltpu.roll(second, 64, axis=1))
        value_out[:, i * 128 : (i + 1) * 128] = jnp.where(lanes, pltpu.roll(first, 64, axis=1), second)
    total = (
        jnp.sum(query_out[...] * wq_ref[...].astype(F32), axis=1, keepdims=True)
        + jnp.sum(key_out[...] * wk_ref[...].astype(F32), axis=1, keepdims=True)
        + jnp.sum(value_out[...] * wv_ref[...].astype(F32), axis=1, keepdims=True)
    )
    gain_one = jnp.broadcast_to(total, (8, 128)).T[0:1, :]
    side = early_ref[:, D : D + 128]
    gain_two = side.T[EXPERTS : EXPERTS + 1, :]
    gains_out[0:1, :] = gain_one[:, 0:8] / own_gain_ref[...].astype(F32)
    gains_out[1:2, :] = gain_two[:, 0:8]
    grad_out[...] = early_ref[:, 0:D]
    router_out[...] = side[:, 0:EXPERTS]
    gate_out[...] = grads_ref[0:256].astype(F32)
    up_out[...] = grads_ref[256:512].astype(F32)
    down_out[:, 0:FF] = grads_ref[512:640].astype(F32)
    down_out[:, FF:D] = grads_ref[640:768].astype(F32)


def body(
    tokens,
    gain_one,
    w_query,
    w_key,
    w_value,
    w_out,
    gain_two,
    w_router,
    w_gate,
    w_up,
    w_down,
    dealt_order,
    lengths,
    routes,
    cotangent,
):
    y_at, z_at = lax.axis_index("y"), lax.axis_index("z")
    first_row = (y_at * 4 + z_at) * CHIP_ROWS

    cot_rows = lax.all_gather(cotangent, ("y", "z", "c"), axis=0, tiled=True)

    expand, expand_t = expand_matrix(), expand_matrix().T
    place, place_t = place_matrix(), place_matrix().T
    (
        query, kv, gain_first, cos, sin, w_mine, member, put, take, own_aux, order_rows, key_norm,
        kv_all, w_late, normed, aux,
    ) = front(
        (
            lengths, tokens, w_query, w_key, w_value, w_out, w_router, gain_one.reshape(1, 8),
            gain_two.reshape(1, 8), dealt_order.reshape(128, 128), routes.T,
            expand, expand_t, place_column(), place_row(), turn_tables(128), turn_tables(1),
        ),
        1,
    )
    kv_all = kv_all.reshape(TOKENS, 128)
    w_late = w_late.reshape(D, 1152)
    plane = ("y", "z", "c")

    base = first_row.reshape(1).astype(jnp.int32)
    att, norm, sent, query_ext = attend(
        dealt_order, base, kv_all, aux, kv, own_aux, query, order_rows, key_norm
    )

    (
        residual, weigh_high, weigh_low, gmid, branch, gsent_own, side_rows, y_out, expert_grads,
    ) = moe(
        (
            sent.reshape(8, ROWS, 128), tokens, w_late, w_late, member, put, take, expand, expand_t,
            place, place_t, cotangent,
            cot_rows.reshape(EXPERTS, ROWS, D), w_gate[0], w_up[0], w_down[0],
        ),
        3,
    )
    y_in = lax.all_to_all(
        y_out, plane, split_axis=0, concat_axis=0, tiled=True
    ).reshape(SLOTS, D)
    expert_grads = lax.psum_scatter(expert_grads, "x", scatter_dimension=0, tiled=True)

    gsent_own = gsent_own.reshape(CHIP_ROWS, 128)
    branch_rows = lax.all_gather(branch, ("c", "x"), axis=0, tiled=True)

    dq, dkv = attend_back(
        dealt_order, base, kv_all, aux, kv, own_aux, query_ext, order_rows, gsent_own, att, norm
    )

    dnormed, mixed, qkv_rows, early = tail(
        (
            dkv.reshape(4, 4, 2, 512, 128), sent, branch_rows, side_rows, dq, cos, sin, normed, w_mine,
            y_in, weigh_high, weigh_low, residual,
        ),
        7,
    )
    (
        grad_tokens, mixed, grad_query, grad_key, grad_value, gains, grad_out_rows, grad_router,
        grad_gate, grad_up, grad_down,
    ) = local_call(
        last_kernel,
        (
            shape((ROWS, D), F32),
            shape((ROWS, D), BF16),
            shape((8, D), F32),
            shape((8, 512), F32),
            shape((8, 512), F32),
            shape((2, 8), F32),
            shape((8, D), F32),
            shape((8, EXPERTS), F32),
            shape((256, FF), F32),
            shape((256, FF), F32),
            shape((128, D), F32),
        ),
    )(
        dnormed, tokens, gain_first, gmid, mixed, qkv_rows, w_query, w_key, w_value,
        gain_one.reshape(1, 8), early, expert_grads,
    )
    grad_gain_one, grad_gain_two = gains[0], gains[1]
    grad_gate, grad_up, grad_down = grad_gate[None], grad_up[None], grad_down[None]
    return (
        mixed,
        grad_tokens,
        grad_gain_one,
        grad_query,
        grad_key,
        grad_value,
        grad_out_rows,
        grad_gain_two,
        grad_router,
        grad_gate,
        grad_up,
        grad_down,
    )


def solution(mesh):
    grid = Mesh(mesh.devices.reshape(4, 4, 4, 2), AXES)
    rows = P(("y", "z", "c", "x"), None)
    vector = P(AXES)
    matrix = P(AXES, None)
    expert = P(("y", "z", "c"), None, None)
    in_specs = (
        rows, vector, matrix, matrix, matrix, matrix, vector, matrix, expert, expert, expert,
        P(), P(), rows, rows,
    )
    grads = P(("y", "z", "c"), "x", None)
    out_specs = (
        rows, rows, vector, matrix, matrix, matrix, matrix, vector, matrix, grads, grads, grads,
    )
    return jax.shard_map(body, mesh=grid, in_specs=in_specs, out_specs=out_specs, check_vma=False)
```

```python
import functools
import math

import jax
import jax.numpy as jnp
import ml_dtypes
import numpy as np
from jax import lax
from jax.experimental import pallas as pl
from jax.experimental.pallas import tpu as pltpu
from jax.sharding import Mesh
from jax.sharding import PartitionSpec as P

D = 1024
HEADS = 16
KV_HEADS = 8
HEAD_DIM = 64
EXPERTS = 32
FF = 512
CAP = 36
SLOT = CAP
SLOTS = EXPERTS * SLOT
ROWS = 128
CHIP_ROWS = 1024
RUN = 256
TOKENS = 16384
NSEQ = 5
EPSILON = 1e-06
ROPE_BASE = 10000.0
FAR = float(2.0**100)
SIZE = {"x": 4, "y": 4, "z": 4, "c": 2}
AXES = ("x", "y", "z", "c")
MESH = pl.DeviceIdType.MESH
BF16 = jnp.bfloat16
F32 = jnp.float32
NN = (((1,), (0,)), ((), ()))
NT = (((1,), (1,)), ((), ()))
TN = (((0,), (0,)), ((), ()))
VMEM_BYTES = 56 * 1024 * 1024


def mm(a, b, dims=NN):
    return lax.dot_general(a, b, dims, preferred_element_type=F32)


def shape(dims, dtype):
    return jax.ShapeDtypeStruct(dims, dtype)


def halves(value):
    high = value.astype(BF16)
    return high, (value - high.astype(F32)).astype(BF16)


def local_call(kernel, outs, scratch=(), grid=None, in_specs=None, out_specs=None):
    extra = {}
    if grid is not None:
        extra = {"grid": grid, "in_specs": in_specs, "out_specs": out_specs}
    elif in_specs is not None:
        extra = {"in_specs": in_specs}
        if out_specs is not None:
            extra["out_specs"] = out_specs
    return pl.pallas_call(
        kernel,
        out_shape=outs,
        scratch_shapes=list(scratch),
        compiler_params=pltpu.CompilerParams(vmem_limit_bytes=VMEM_BYTES),
        **extra,
    )


class Late:
    def __init__(self, hbm, vmem, sem, columns):
        self.hbm, self.vmem = hbm, vmem
        source = hbm if columns is None else hbm.at[:, columns[0] : columns[1]]
        self.copy, self.ready = pltpu.make_async_copy(source, vmem, sem), False
        self.copy.start()

    def get(self):
        if not self.ready:
            self.copy.wait()
            self.ready = True
        return self.vmem

    def __getitem__(self, index):
        return self.get()[index]


class Early:
    def __init__(self, hbm, vmem, sem):
        self.vmem, self.copy = vmem, pltpu.make_async_copy(vmem, hbm, sem)

    def __getitem__(self, index):
        return self.vmem[index]

    def __setitem__(self, index, value):
        self.vmem[index] = value

    def store(self):
        self.copy.start()


def remote_call(kernel, inputs, kinds, outs, out_kinds, scratch, cid):
    spaces = {"s": pltpu.SMEM, "v": pltpu.VMEM}
    late = [(i, kind) for i, kind in enumerate(kinds) if kind not in ("s", "v", "h")]
    early = [i for i, kind in enumerate(out_kinds) if kind == "e"]

    def late_shape(i, kind):
        dims = inputs[i].shape if kind == "l" else (inputs[i].shape[0], kind[1] - kind[0])
        return pltpu.VMEM(dims, inputs[i].dtype)

    def wrapped(*refs):
        ins, rest = list(refs[: len(inputs)]), list(refs[len(inputs) :])
        results, rest = rest[: len(outs)], rest[len(outs) :]
        own, rest = rest[: len(scratch)], rest[len(scratch) :]
        late_v, rest = rest[: len(late)], rest[len(late) :]
        early_v, (late_sem, early_sem) = rest[: len(early)], rest[len(early) :]
        for n, (i, kind) in enumerate(late):
            ins[i] = Late(ins[i], late_v[n], late_sem.at[n], None if kind == "l" else kind)
        for n, i in enumerate(early):
            results[i] = Early(results[i], early_v[n], early_sem.at[n])
        kernel(*ins, *results, *own)
        for i, _ in late:
            ins[i].get()
        for i in early:
            results[i].copy.wait()

    return pl.pallas_call(
        wrapped,
        out_shape=list(outs),
        in_specs=[pl.BlockSpec(memory_space=spaces.get(kind, pl.ANY)) for kind in kinds],
        out_specs=[pl.BlockSpec(memory_space=spaces.get(kind, pl.ANY)) for kind in out_kinds],
        scratch_shapes=list(scratch)
        + [late_shape(i, kind) for i, kind in late]
        + [pltpu.VMEM(outs[i].shape, outs[i].dtype) for i in early]
        + [pltpu.SemaphoreType.DMA((max(1, len(late)),)), pltpu.SemaphoreType.DMA((max(1, len(early)),))],
        compiler_params=pltpu.CompilerParams(
            collective_id=cid, has_side_effects=True, vmem_limit_bytes=VMEM_BYTES
        ),
    )(*inputs)


def flat_index(coords, order):
    index = 0
    for axis in order:
        index = index * SIZE[axis] + coords[axis]
    return index


PLANE_ORDER = (
    (2, 2), (2, 3), (2, 1), (3, 2), (1, 2), (0, 2), (2, 0), (3, 1), (1, 3),
    (3, 3), (1, 1), (0, 3), (0, 1), (3, 0), (1, 0), (0, 0),
)
PLANE_OFFSETS = tuple({"y": dy, "z": dz} for dy, dz in PLANE_ORDER[:-1])
SPREAD_OFFSETS = tuple(
    {"y": dy, "z": dz, "c": (dc + i + 1) % 2}
    for i, (dy, dz) in enumerate(PLANE_ORDER)
    for dc in range(2)
    if (dy, dz, (dc + i + 1) % 2) != (0, 0, 0)
)
LINE_OFFSETS = tuple(
    {"x": dx, "c": dc} for dx, dc in ((2, 0), (2, 1), (1, 0), (3, 0), (1, 1), (3, 1), (0, 1))
)
OFFSETS = {("y", "z"): PLANE_OFFSETS, ("y", "z", "c"): SPREAD_OFFSETS, ("x", "c"): LINE_OFFSETS}


def position(axes):
    return {axis: lax.axis_index(axis) for axis in axes}


def moved(me, offset):
    return {axis: lax.rem(me[axis] + by, SIZE[axis]) if by else me[axis] for axis, by in offset.items()}


def greet(me, offsets):
    barrier = pltpu.get_barrier_semaphore()
    for offset in offsets:
        pl.semaphore_signal(barrier, inc=1, device_id=moved(me, offset), device_id_type=MESH)
    return lambda: pl.semaphore_wait(barrier, len(offsets))


def remote(src, dst, send, recv, slot, to):
    return pltpu.make_async_remote_copy(
        src_ref=src,
        dst_ref=dst,
        send_sem=send.at[slot],
        recv_sem=recv.at[slot],
        device_id=to,
        device_id_type=MESH,
    )


def scatter_plane(me, p_ref, o_ref, far_a, near_a, out_a, sum_a, far_b, near_b, out_b, send, recv):
    half = p_ref.vmem.shape[3] // 2
    lower, upper = pl.ds(0, half), pl.ds(half, half)
    axis = (("y", "z"), ("z", "y"))
    used = [0]

    def go(src, dst, t, which, by):
        to = {axis[t][which]: lax.rem(me[axis[t][which]] + by, 4)}
        item = remote(src, dst, send, recv, used[0], to)
        used[0] += 1
        item.start()
        return item

    def part(t, first, second, hbm=False):
        a = lax.rem(me[axis[t][0]] + first, 4)
        b = lax.rem(me[axis[t][1]] + second, 4)
        ref = p_ref.hbm if hbm else p_ref.get()
        return ref.at[a, b, 0] if t == 0 else ref.at[b, a, 1]

    turns = (2, 1, 3, 0)
    both = (0, 1)
    far, near = {}, {}
    for k, by in enumerate(turns):
        for t in both:
            far[k, t] = (
                go(part(t, 2, by, True).at[lower], far_a.at[t, k, 0], t, 0, 1),
                go(part(t, 2, by, True).at[upper], far_a.at[t, k, 1], t, 0, 3),
            )
    for k, by in enumerate(turns):
        for t in both:
            ahead, behind = part(t, 1, by), part(t, 3, by)
            far[k, t][0].wait()
            out_a[t, k, 0, 0:half] = (ahead[0:half].astype(F32) + far_a[t, k, 0].astype(F32)).astype(BF16)
            out_a[t, k, 0, half : 2 * half] = ahead[half : 2 * half]
            first = go(out_a.at[t, k, 0], near_a.at[t, k, 0], t, 0, 1)
            far[k, t][1].wait()
            out_a[t, k, 1, 0:half] = behind[0:half]
            out_a[t, k, 1, half : 2 * half] = (
                behind[half : 2 * half].astype(F32) + far_a[t, k, 1].astype(F32)
            ).astype(BF16)
            near[k, t] = (first, go(out_a.at[t, k, 1], near_a.at[t, k, 1], t, 0, 3))

    def summed(k, t):
        near[k, t][0].wait()
        near[k, t][1].wait()
        return (
            part(t, 0, turns[k])[...].astype(F32)
            + near_a[t, k, 0].astype(F32)
            + near_a[t, k, 1].astype(F32)
        )

    far_two, near_two = {}, {}
    for t in both:
        value = summed(0, t).astype(BF16)
        out_b[t, 0] = value
        far_two[t] = (
            go(out_b.at[t, 0, lower], far_b.at[t, 0], t, 1, 1),
            go(out_b.at[t, 0, upper], far_b.at[t, 1], t, 1, 3),
        )
    for k in (1, 2):
        for t in both:
            sum_a[t, k - 1] = summed(k, t)
    for t in both:
        far_two[t][0].wait()
        out_b[t, 1, 0:half] = (sum_a[t, 0, 0:half] + far_b[t, 0].astype(F32)).astype(BF16)
        out_b[t, 1, half : 2 * half] = sum_a[t, 0, half : 2 * half].astype(BF16)
        first = go(out_b.at[t, 1], near_b.at[t, 0], t, 1, 1)
        far_two[t][1].wait()
        out_b[t, 2, 0:half] = sum_a[t, 1, 0:half].astype(BF16)
        out_b[t, 2, half : 2 * half] = (
            sum_a[t, 1, half : 2 * half] + far_b[t, 1].astype(F32)
        ).astype(BF16)
        near_two[t] = (first, go(out_b.at[t, 2], near_b.at[t, 1], t, 1, 3))
    for t in both:
        value = summed(3, t)
        near_two[t][0].wait()
        near_two[t][1].wait()
        o_ref[t] = value + near_b[t, 0].astype(F32) + near_b[t, 1].astype(F32)


def lane_index(shape):
    return lax.broadcasted_iota(jnp.int32, shape, 1)


def turned(values):
    lane = lane_index(values.shape)
    up = pltpu.roll(values, 32, axis=1)
    down = pltpu.roll(values, 96, axis=1)
    return jnp.where(lane % 64 < 32, -down, up)


def gather_plane(kv_v, kv_hbm, go, me, own_sem, fillers):
    own = pltpu.make_async_copy(kv_v, kv_hbm.at[me["y"], me["z"]], own_sem)
    own.start()
    half = kv_v.shape[1] // 2
    lower, upper = pl.ds(0, half), pl.ds(half, half)
    axis = (("y", "z"), ("z", "y"))
    here = tuple((me[a], me[b]) for a, b in axis)
    step = {"plus": 1, "minus": 3, "far": 2, "own": 0}

    def place(t, a, b):
        return kv_hbm.at[a, b, 0] if t == 0 else kv_hbm.at[b, a, 1]

    def at(t, which, name):
        return lax.rem(here[t][which] + step[name], 4)

    def send_second(t, src, name):
        dst = place(t, at(t, 0, name), here[t][1])
        src = dst if src is None else src
        return (
            go(src, dst, {axis[t][1]: at(t, 1, "plus")}),
            go(src, dst, {axis[t][1]: at(t, 1, "minus")}),
        )

    def pass_on(t, which, a_name, b_name, part, direction):
        ref = place(t, at(t, 0, a_name), at(t, 1, b_name)).at[part]
        return go(ref, ref, {axis[t][which]: at(t, which, direction)})

    def forward_second(t, name, pair):
        pair[0].wait()
        a = pass_on(t, 1, name, "minus", lower, "plus")
        pair[1].wait()
        b = pass_on(t, 1, name, "plus", upper, "minus")
        return [a, b]

    first, second, last = {}, {}, []
    for t in (0, 1):
        dst = place(t, *here[t])
        first[t] = (
            go(kv_v.at[t], dst, {axis[t][0]: at(t, 0, "plus")}),
            go(kv_v.at[t], dst, {axis[t][0]: at(t, 0, "minus")}),
        )
    for t in (0, 1):
        second[t, "own"] = send_second(t, kv_v.at[t], "own")
    fillers[0]()
    far = {}
    for t in (0, 1):
        first[t][0].wait()
        a = pass_on(t, 0, "minus", "own", lower, "plus")
        second[t, "minus"] = send_second(t, None, "minus")
        first[t][1].wait()
        b = pass_on(t, 0, "plus", "own", upper, "minus")
        second[t, "plus"] = send_second(t, None, "plus")
        far[t] = (a, b)
    fillers[1]()
    for t in (0, 1):
        last += forward_second(t, "own", second[t, "own"])
    for t in (0, 1):
        far[t][0].wait()
        far[t][1].wait()
        second[t, "far"] = send_second(t, None, "far")
    fillers[2]()
    for name in ("minus", "plus", "far"):
        for t in (0, 1):
            last += forward_second(t, name, second[t, name])
    return last + [own]


def front_kernel(
    lengths_ref, tok_ref, wq_ref, wk_ref, wv_ref, wo_ref, router_ref, gain_one_ref, gain_two_ref,
    order_ref, routes_ref, expand_ref, expand_t_ref, col_ref, row_ref, turn_high_ref, turn_low_ref,
    q_ref, kv_own_ref, gain_ref, cos_ref, sin_ref, w_out_ref, member_ref, put_ref, take_ref,
    own_aux_ref, order_rows_ref, key_norm_ref, kv_hbm, late_hbm, normed_v, aux_v,
    rows_v, w_v, kv_v, long_v, side_v, w_ref, late_ref, send, recv, local,
):
    me = position(AXES)
    x, y, z, c = (me[axis] for axis in AXES)
    arrived = greet(me, LINE_OFFSETS + PLANE_OFFSETS)
    small = lane_index((8, 128))
    diagonal = lax.broadcasted_iota(jnp.int32, (8, 8), 0) == lane_index((8, 8))

    def column(ref):
        row = jnp.broadcast_to(ref[...].astype(F32), (8, 8))
        return jnp.sum(jnp.where(diagonal, row, 0.0), axis=1, keepdims=True)

    gain_lane = jnp.where(small == 0, column(gain_one_ref), 0.0).astype(BF16)
    for i in range(8):
        span = slice((i // 2) * 128, (i // 2 + 1) * 128)
        key, value = wk_ref[:, span].astype(F32), wv_ref[:, span].astype(F32)
        if i % 2 == 0:
            pair = jnp.where(small < 64, key, pltpu.roll(value, 64, axis=1))
        else:
            pair = jnp.where(small < 64, pltpu.roll(key, 64, axis=1), value)
        w_ref[i, :, 0:128] = wq_ref[:, i * 128 : (i + 1) * 128]
        w_ref[i, :, 128:256] = pair.astype(BF16)
        w_ref[i, :, 256:384] = gain_lane
    side_v[...] = jnp.zeros_like(side_v)
    side_v[:, 0:EXPERTS] = router_ref[...].astype(F32)
    late_ref[:, 0:D] = wo_ref[...]
    late_ref[:, D : D + 128] = jnp.where(small == EXPERTS, column(gain_two_ref), side_v[...]).astype(BF16)
    arrived()
    plus, minus, far = lax.rem(x + 1, 4), lax.rem(x + 3, 4), lax.rem(x + 2, 4)
    other = 1 - c
    lower, upper = pl.ds(0, 64), pl.ds(64, 64)
    used = [0]

    def go(src, dst, to):
        item = remote(src, dst, send, recv, used[0], to)
        used[0] += 1
        item.start()
        return item

    def keep(src, dst, slot):
        item = pltpu.make_async_copy(src, dst, local.at[slot])
        item.start()
        return item

    own = [
        keep(w_ref.at[x * 2 + c], w_v.at[x, y, z, c], 0),
        keep(late_ref, late_hbm.at[x, y, z, c], 1),
    ]
    own_rows = keep(tok_ref, rows_v.at[c, x], 2)
    first_w = []
    for offset in LINE_OFFSETS:
        to = moved(me, offset)
        first_w.append(go(w_ref.at[to["x"] * 2 + to["c"]], w_v.at[x, y, z, c], to))
    to_plus = go(tok_ref, rows_v.at[c, x], {"x": plus})
    to_minus = go(tok_ref, rows_v.at[c, x], {"x": minus})
    sides = [go(tok_ref, rows_v.at[c, x], {"c": other})]

    for item in own + first_w:
        item.wait()
    second_w = [go(w_v.at[:, y, z], w_v.at[:, y, z], moved(me, by)) for by in PLANE_OFFSETS]
    first_late = [go(late_ref, late_hbm.at[x, y, z, c], moved(me, by)) for by in PLANE_OFFSETS]

    chip = y * 4 + z
    mine = order_ref[pl.ds(pl.multiple_of(chip * 8, 8), 8), :]
    ends, total = [], jnp.int32(0)
    for i in range(NSEQ):
        total = total + lengths_ref[i]
        ends.append(total)
    place = mine
    for i in range(NSEQ):
        place = place - jnp.where(mine >= ends[i], lengths_ref[i], 0)
    lane = lane_index((ROWS, 128))

    def table(ref, picked):
        return mm(picked, ref[0]) + mm(picked, ref[1]) + mm(picked, ref[2])

    for i in range(8):
        wide = jnp.broadcast_to(place[i : i + 1, :].astype(F32), (ROWS, 128)).T.astype(jnp.int32)
        high = table(turn_high_ref, jnp.where(lane == lax.shift_right_logical(wide, 7), 1.0, 0.0).astype(BF16))
        low = table(turn_low_ref, jnp.where(lane == (wide & 127), 1.0, 0.0).astype(BF16))
        cos_ref[pl.ds(i * 128, 128), :] = high[:, :128] * low[:, :128] - high[:, 128:] * low[:, 128:]
        sin_ref[pl.ds(i * 128, 128), :] = high[:, 128:] * low[:, :128] + high[:, :128] * low[:, 128:]
    for i in range(4):
        order_rows_ref[i : i + 1, 0:128] = mine[2 * i : 2 * i + 1, :].astype(F32)
        order_rows_ref[i : i + 1, 128:256] = mine[2 * i + 1 : 2 * i + 2, :].astype(F32)

    to_plus.wait()
    next_plus = go(rows_v.at[c, minus, lower], rows_v.at[c, minus, lower], {"x": plus})
    sides.append(go(rows_v.at[c, minus], rows_v.at[c, minus], {"c": other}))
    to_minus.wait()
    next_minus = go(rows_v.at[c, plus, upper], rows_v.at[c, plus, upper], {"x": minus})
    sides.append(go(rows_v.at[c, plus], rows_v.at[c, plus], {"c": other}))
    next_plus.wait()
    next_minus.wait()
    sides.append(go(rows_v.at[c, far], rows_v.at[c, far], {"c": other}))
    own_rows.wait()
    for item in second_w:
        item.wait()
    weights = w_v[...].astype(F32).reshape(D, 384)
    w_out_ref[...] = weights.astype(BF16)
    gain = weights[:, 256:384].T[0:1, :]
    gain_ref[...] = gain
    low_lanes = lane_index((256, 128)) < 64

    def project(block):
        longest = jnp.zeros((256, 1), F32)
        for i in range(2):
            rows = pl.ds(pl.multiple_of(block * 512 + i * 256, 256), 256)
            tok = rows_v[block, pl.ds(2 * i, 2)].astype(F32).reshape(256, D)
            scale = lax.rsqrt(jnp.mean(tok * tok, axis=-1, keepdims=True) + EPSILON)
            normed = (tok * scale * gain).astype(BF16)
            normed_v[rows, :] = normed
            pre = mm(normed, w_out_ref[:, 0:256])
            cos, sin = cos_ref[rows, :], sin_ref[rows, :]
            q_pre, kv_pre = pre[:, :128], pre[:, 128:]
            query = (q_pre * cos + turned(q_pre) * sin).astype(BF16).astype(F32) * 0.125
            q_ref[0, rows, :] = jnp.where(low_lanes, query, 0.0).astype(BF16)
            q_ref[1, rows, :] = jnp.where(low_lanes, pltpu.roll(query, 64, axis=1), 0.0).astype(BF16)
            key = kv_pre * cos + turned(kv_pre) * sin
            kv = jnp.where(low_lanes, key, kv_pre).astype(BF16)
            kv_own_ref[rows, :] = kv
            kv_v[block, pl.ds(i * 256, 256), :] = kv
            rounded = kv.astype(F32)
            square = jnp.sum(jnp.where(low_lanes, rounded * rounded, 0.0), axis=1, keepdims=True)
            longest = jnp.maximum(longest, square)
        return jnp.max(longest, axis=0, keepdims=True)

    longest = project(c)
    for item in sides:
        item.wait()
    longest = jnp.maximum(longest, project(other))
    long_v[chip] = jnp.broadcast_to(longest, (8, 128))
    longs = [go(long_v.at[chip], long_v.at[chip], moved(me, by)) for by in PLANE_OFFSETS]
    stores = []
    for item in (q_ref, kv_own_ref, cos_ref, sin_ref, w_out_ref, normed_v):
        item.store()

    def routing():
        routes = jnp.concatenate([routes_ref[...].astype(F32), jnp.full((120, 128), -1.0, F32)], axis=0).T
        member = jnp.zeros((ROWS, 128), F32)
        for choice in range(8):
            member += jnp.where(routes[:, choice : choice + 1].astype(jnp.int32) == lane, 1.0, 0.0)
        below = lax.broadcasted_iota(jnp.int32, (ROWS, ROWS), 0) > lane_index((ROWS, ROWS))
        earlier = mm(jnp.where(below, 1.0, 0.0).astype(BF16), member.astype(BF16))
        slot = jnp.where(member > 0.5, earlier, -1.0).astype(BF16)
        member_ref[...] = member
        take = jnp.where(mm(slot, expand_ref[...]) == row_ref[...], 1.0, 0.0)
        take_ref[...] = take.astype(BF16)
        put = jnp.where(mm(expand_t_ref[...], slot, NT) == col_ref[...].astype(F32), 1.0, 0.0)
        put = put.astype(BF16)
        put_ref[...] = put
        for item in (put_ref, take_ref):
            item.store()

    def segments():
        sub = lax.broadcasted_iota(jnp.int32, (8, 128), 0)
        begin = jnp.zeros((8, 128), jnp.int32)
        end = jnp.full((8, 128), TOKENS, jnp.int32)
        for i in range(NSEQ):
            begin = jnp.where(sub == 3 + i, ends[i] - lengths_ref[i], begin)
            end = jnp.where(sub == 3 + i, ends[i], end)
        spot = jnp.where(sub == lane_index((8, 128)), 1.0, 0.0).astype(BF16)

        def block(step, carry):
            rows = order_ref[pl.ds(pl.multiple_of(step * 8, 8), 8), :]
            for i in range(8):
                order = jnp.broadcast_to(rows[i : i + 1, :], (8, 128))
                within = jnp.where((order >= begin) & (order < end), 1.0, 0.0).astype(BF16)
                here = pl.ds(pl.multiple_of(step * 1024 + i * 128, 128), 128)
                aux_v[here, :] = mm(within, spot, TN).astype(BF16)
            return carry

        lax.fori_loop(0, 16, block, 0)
        aux_v.store()
        own_aux_ref[...] = aux_v[pl.ds(pl.multiple_of(chip * CHIP_ROWS, CHIP_ROWS), CHIP_ROWS), :]
        own_aux_ref.store()

    def late():
        for item in second_late:
            item.wait()
        stores.append(go(late_hbm.at[:, :, :, c], late_hbm.at[:, :, :, c], {"c": other}))

    for item in first_late:
        item.wait()
    second_late = [
        go(late_hbm.at[x, :, :, c], late_hbm.at[x, :, :, c], {"x": to}) for to in (far, plus, minus)
    ]

    last = gather_plane(kv_v, kv_hbm, go, me, local.at[3], (routing, segments, late))
    for item in longs:
        item.wait()
    longest = long_v[0]
    for i in range(1, 16):
        longest = jnp.maximum(longest, long_v[i])
    key_norm_ref[...] = jnp.sqrt(longest)
    for item in last + stores:
        item.wait()


def front(inputs, cid):
    count = 7 + 3 + 3 + 15 + 15 + 2 + 3 + 40 + 1 + 15
    return remote_call(
        front_kernel,
        inputs,
        ("s", "h") + ("v",) * 9 + ("l",) * 6,
        [
            shape((2, CHIP_ROWS, 128), BF16),
            shape((CHIP_ROWS, 128), BF16),
            shape((1, D), F32),
            shape((CHIP_ROWS, 128), F32),
            shape((CHIP_ROWS, 128), F32),
            shape((D, 384), BF16),
            shape((ROWS, 128), F32),
            shape((SLOTS, ROWS), BF16),
            shape((ROWS, SLOTS), BF16),
            shape((CHIP_ROWS, 128), BF16),
            shape((4, RUN), F32),
            shape((8, 128), F32),
            shape((4, 4, 2, 512, 128), BF16),
            shape((4, 4, 4, 2, 8, 1152), BF16),
            shape((CHIP_ROWS, D), BF16),
            shape((TOKENS, 128), BF16),
        ],
        ("e", "e", "v", "e", "e", "e", "v", "e", "e", "e", "v", "v", "h", "h", "e", "e"),
        [
            pltpu.VMEM((2, 4, ROWS, D), BF16),
            pltpu.VMEM((4, 4, 4, 2, 8, 384), BF16),
            pltpu.VMEM((2, 512, 128), BF16),
            pltpu.VMEM((16, 8, 128), F32),
            pltpu.VMEM((8, 128), F32),
            pltpu.VMEM((8, 8, 384), BF16),
            pltpu.VMEM((8, 1152), BF16),
            pltpu.SemaphoreType.DMA((count,)),
            pltpu.SemaphoreType.DMA((count,)),
            pltpu.SemaphoreType.DMA((4,)),
        ],
        cid,
    )


def turn_tables(step):
    frequency = (np.float32(ROPE_BASE) ** (-np.arange(32, dtype=np.float32) / np.float32(32))).astype(np.float64)
    angles = (np.arange(128) * step)[:, None] * np.tile(frequency, 4)[None, :]
    rest = np.concatenate([np.cos(angles), np.sin(angles)], axis=1)
    parts = []
    for _ in range(3):
        part = rest.astype(np.float32).astype(ml_dtypes.bfloat16)
        parts.append(part)
        rest = rest - part.astype(np.float64)
    return jnp.asarray(np.stack(parts))


def order_pair(order_ref, index):
    row = jnp.broadcast_to(order_ref[pl.ds(index, 1), :], (RUN, RUN))
    return row, row.T


WIDE = 6
WIDE_BACK = 3


def run_lists(order_ref, base, first_ref):
    def note(block, carry):
        run = lax.shift_right_logical(order_ref[block * 512], 8)
        first_ref[run] = block * 512
        first_ref[63 - run] = block * 512 + RUN
        return carry

    lax.fori_loop(0, 32, note, 0)

    def count(part):
        run = lax.shift_right_logical(order_ref[base + lax.div(part, 2) * 512], 8)
        return jnp.where(lax.rem(part, 2) == 0, run, 31 - run)

    return count


def group_places(first_ref, number, half, step, wide):
    places = []
    for i in range(wide):
        index = step * wide + i
        at = jnp.where(index < number, half + index, 32 - half)
        places.append(pl.ds(pl.multiple_of(first_ref[at], RUN), RUN))
    return places


def attend_kernel(
    order_smem, base_ref, kv_hbm, aux_hbm, own_kv_ref, own_aux_ref, q_ref, order_ref, key_norm_ref,
    att_ref, norm_ref, sent_ref, qx_ref, kv_ref, aux_ref, acc_ref, first_ref, loads,
):
    copies = [
        pltpu.make_async_copy(kv_hbm, kv_ref, loads.at[0]),
        pltpu.make_async_copy(aux_hbm, aux_ref, loads.at[1]),
    ]
    for item in copies:
        item.start()
    count = run_lists(order_smem, base_ref[0], first_ref)
    key_norm = key_norm_ref[0:1, 0:1]
    lane = lane_index((RUN, 128))

    def right(keys):
        turned_keys = keys.T
        row = lax.broadcasted_iota(jnp.int32, turned_keys.shape, 0)
        return jnp.where(row < 64, jnp.ones_like(turned_keys), turned_keys)[56:]

    def prepare(part, carry):
        rows = pl.ds(pl.multiple_of(part * RUN, RUN), RUN)
        own_aux = own_aux_ref[rows, :]
        spread = jnp.where(lane < 3 + NSEQ, (own_aux.astype(F32) - 1.0) * FAR, 0.0)
        for head in range(2):
            query = q_ref[head, rows, :]
            wide = query.astype(F32)
            shift = jnp.ceil(jnp.sqrt(jnp.sum(wide * wide, axis=1, keepdims=True)) * key_norm)
            top = shift.astype(BF16).astype(F32)
            middle = (shift - top).astype(BF16).astype(F32)
            rest = shift - top - middle
            ext = jnp.where(lane == 0, -top, spread)
            ext = jnp.where(lane == 1, -middle, ext)
            ext = jnp.where(lane == 2, -rest, ext)
            here = pl.ds(head * RUN, RUN)
            qx_ref[part, here, 0:128] = query
            qx_ref[part, here, 128:256] = ext.astype(BF16)
        order_key, order_query = order_pair(order_ref, part)
        allowed = order_query <= order_key
        keys = own_kv_ref[rows, :]
        e = jnp.exp(mm(jnp.concatenate([keys, own_aux], axis=1), qx_ref[part], NT))
        e = jnp.where(jnp.concatenate([allowed, allowed], axis=1), e, 0.0)
        acc_ref[part] = mm(right(keys), e.astype(BF16))
        return carry

    lax.fori_loop(0, 4, prepare, 0)
    for item in copies:
        item.wait()

    def part_step(part, carry):
        number = count(part)
        half = lax.rem(part, 2) * 32

        def group(step, carry):
            places = group_places(first_ref, number, half, step, WIDE)
            keys = jnp.concatenate([kv_ref[here, :] for here in places], axis=0)
            aux = jnp.concatenate([aux_ref[here, :] for here in places], axis=0)
            e = jnp.exp(mm(jnp.concatenate([keys, aux], axis=1), qx_ref[part], NT))
            acc_ref[part] += mm(right(keys), e.astype(BF16))
            return carry

        lax.fori_loop(0, lax.div(number + WIDE - 1, WIDE), group, 0)
        rows = pl.ds(pl.multiple_of(part * RUN, RUN), RUN)
        total = acc_ref[part]
        value = total[8:72] / total[0:1]
        att = jnp.concatenate([value[:, :RUN], value[:, RUN:]], axis=0).T
        norm = jnp.broadcast_to(total[0:1], (64, 2 * RUN))
        norm = jnp.concatenate([norm[:, :RUN], norm[:, RUN:]], axis=0).T
        att_ref[rows, :] = att
        norm_ref[rows, :] = norm
        sent_ref[rows, :] = att.astype(BF16)
        return carry

    lax.fori_loop(0, 4, part_step, 0)


def attend(order, base, kv, aux, own_kv, own_aux, query, order_rows, key_norm):
    smem = pl.BlockSpec(memory_space=pltpu.SMEM)
    vmem = pl.BlockSpec(memory_space=pltpu.VMEM)
    hbm = pl.BlockSpec(memory_space=pl.ANY)
    return local_call(
        attend_kernel,
        (
            shape((CHIP_ROWS, 128), F32),
            shape((CHIP_ROWS, 128), F32),
            shape((CHIP_ROWS, 128), BF16),
            shape((4, 2 * RUN, 256), BF16),
        ),
        scratch=[
            pltpu.VMEM((TOKENS, 128), BF16),
            pltpu.VMEM((TOKENS, 128), BF16),
            pltpu.VMEM((4, 72, 2 * RUN), F32),
            pltpu.SMEM((64,), jnp.int32),
            pltpu.SemaphoreType.DMA((2,)),
        ],
        in_specs=[smem] * 2 + [hbm] * 2 + [vmem] * 5,
    )(order, base, kv, aux, own_kv, own_aux, query, order_rows, key_norm)


def attend_back_kernel(
    order_smem, base_ref, kv_hbm, aux_hbm, own_kv_ref, own_aux_ref, qx_ref, order_ref,
    gsent_ref, att_ref, norm_ref, dq_ref, dkv_hbm,
    kv_ref, aux_ref, acc_ref, dq_acc, gx_ref, rhs_ref, out_ref, first_ref, loads, stores,
):
    copies = [
        pltpu.make_async_copy(kv_hbm, kv_ref, loads.at[0]),
        pltpu.make_async_copy(aux_hbm, aux_ref, loads.at[1]),
    ]
    for item in copies:
        item.start()
    own_base = base_ref[0]
    count = run_lists(order_smem, own_base, first_ref)

    def clear(step, carry):
        acc_ref[pl.ds(pl.multiple_of(step * 512, 512), 512), :] = jnp.zeros((512, 128), F32)
        return carry

    lax.fori_loop(0, TOKENS // 512, clear, 0)
    lane = lane_index((RUN, 128))
    low_lanes = lane < 64

    def apply(part, here, e, prob):
        ds = (e * prob).astype(BF16)
        left = jnp.concatenate([ds, e.astype(BF16)], axis=1)
        acc_ref[here, :] += mm(left, rhs_ref[part])
        return ds

    def scores(part, keys, aux):
        both = jnp.concatenate([keys, aux], axis=1)
        return mm(both, qx_ref[part], NT), mm(both, gx_ref[part], NT)

    def prepare(part, carry):
        rows = pl.ds(pl.multiple_of(part * RUN, RUN), RUN)
        gsent = gsent_ref[rows, :].astype(F32)
        norm = norm_ref[rows, :]
        product = gsent * att_ref[rows, :] / norm
        scaled = (gsent / norm).astype(BF16).astype(F32)
        for head in range(2):
            mask = low_lanes if head == 0 else jnp.logical_not(low_lanes)
            delta = jnp.sum(jnp.where(mask, product, 0.0), axis=1, keepdims=True)
            top = delta.astype(BF16).astype(F32)
            middle = (delta - top).astype(BF16).astype(F32)
            rest = delta - top - middle
            ext = jnp.where(lane == 0, -top, 0.0)
            ext = jnp.where(lane == 1, -middle, ext)
            ext = jnp.where(lane == 2, -rest, ext)
            grad = pltpu.roll(scaled, 64, axis=1) if head == 0 else scaled
            grad = jnp.where(low_lanes, 0.0, grad).astype(BF16)
            here = pl.ds(head * RUN, RUN)
            gx_ref[part, here, 0:128] = grad
            gx_ref[part, here, 128:256] = ext.astype(BF16)
            rhs_ref[part, pl.ds(head * RUN, RUN), :] = qx_ref[part, here, 0:128]
            rhs_ref[part, pl.ds((2 + head) * RUN, RUN), :] = grad
        order_key, order_query = order_pair(order_ref, part)
        allowed = order_query <= order_key
        keys = own_kv_ref[rows, :]
        score, prob = scores(part, keys, own_aux_ref[rows, :])
        e = jnp.where(jnp.concatenate([allowed, allowed], axis=1), jnp.exp(score), 0.0)
        own = pl.ds(pl.multiple_of(own_base + part * RUN, RUN), RUN)
        dq_acc[part] = mm(keys.T[:64], apply(part, own, e, prob))
        return carry

    lax.fori_loop(0, 4, prepare, 0)
    for item in copies:
        item.wait()

    def part_step(part, carry):
        number = count(part)
        half = lax.rem(part, 2) * 32

        def group(step, carry):
            places = group_places(first_ref, number, half, step, WIDE_BACK)
            parts = [scores(part, kv_ref[here, :], aux_ref[here, :]) for here in places]
            ds = [
                apply(part, here, jnp.exp(score), prob)
                for here, (score, prob) in zip(places, parts)
            ]
            keys = jnp.concatenate([kv_ref[here, :] for here in places], axis=0)
            dq_acc[part] += mm(keys.T[:64], jnp.concatenate(ds, axis=0))
            return carry

        lax.fori_loop(0, lax.div(number + WIDE_BACK - 1, WIDE_BACK), group, 0)
        rows = pl.ds(pl.multiple_of(part * RUN, RUN), RUN)
        total = dq_acc[part] * 0.125
        dq_ref[rows, :] = jnp.concatenate([total[:, :RUN], total[:, RUN:]], axis=0).T
        return carry

    lax.fori_loop(0, 4, part_step, 0)

    def store(step):
        rows = pl.ds(pl.multiple_of(step * 2048, 2048), 2048)
        return pltpu.make_async_copy(out_ref.at[rows], dkv_hbm.at[rows], stores.at[step])

    def narrow(step, carry):
        rows = pl.ds(pl.multiple_of(step * 2048, 2048), 2048)
        out_ref[rows, :] = acc_ref[rows, :].astype(BF16)
        store(step).start()
        return carry

    def settle(step, carry):
        store(step).wait()
        return carry

    lax.fori_loop(0, 8, narrow, 0)
    lax.fori_loop(0, 8, settle, 0)


def attend_back(order, base, kv, aux, own_kv, own_aux, query_ext, order_rows, gsent, att, norm):
    smem = pl.BlockSpec(memory_space=pltpu.SMEM)
    vmem = pl.BlockSpec(memory_space=pltpu.VMEM)
    hbm = pl.BlockSpec(memory_space=pl.ANY)
    return local_call(
        attend_back_kernel,
        (shape((CHIP_ROWS, 128), F32), shape((TOKENS, 128), BF16)),
        scratch=[
            pltpu.VMEM((TOKENS, 128), BF16),
            pltpu.VMEM((TOKENS, 128), BF16),
            pltpu.VMEM((TOKENS, 128), F32),
            pltpu.VMEM((4, 64, 2 * RUN), F32),
            pltpu.VMEM((4, 2 * RUN, 256), BF16),
            pltpu.VMEM((4, 4 * RUN, 128), BF16),
            pltpu.VMEM((TOKENS, 128), BF16),
            pltpu.SMEM((64,), jnp.int32),
            pltpu.SemaphoreType.DMA((2,)),
            pltpu.SemaphoreType.DMA((8,)),
        ],
        in_specs=[smem] * 2 + [hbm] * 2 + [vmem] * 7,
        out_specs=[vmem, hbm],
    )(order, base, kv, aux, own_kv, own_aux, query_ext, order_rows, gsent, att, norm)


SLOT_EXPERT = np.arange(SLOTS) // SLOT
SLOT_PLACE = np.arange(SLOTS) % SLOT


def constant(array):
    return jnp.asarray(np.asarray(array).astype(ml_dtypes.bfloat16))


def expand_matrix():
    return constant(np.arange(128)[:, None] == SLOT_EXPERT[None, :])


def place_matrix():
    return constant(SLOT_PLACE[:, None] == np.arange(128)[None, :])


def origin_matrix():
    return constant((np.arange(8 * SLOT) // SLOT)[:, None] == np.arange(128)[None, :])


def place_column():
    used = np.where(SLOT_PLACE < CAP, SLOT_PLACE, -5)
    return constant(np.broadcast_to(used[:, None], (SLOTS, 128)))


def place_row():
    used = np.where(SLOT_PLACE < CAP, SLOT_PLACE, -5)
    return jnp.asarray(used[None, :].astype(np.float32))


BLOCK = 8 * SLOT


def packed_pairs(values):
    total = sum(int(value) << (2 * i) for i, value in enumerate(values))
    return np.uint32(total).astype(np.int32)


STEP_Y = packed_pairs([dy for dy, _ in PLANE_ORDER])
STEP_Z = packed_pairs([dz for _, dz in PLANE_ORDER])


def moe_kernel(
    sent_ref, tok_ref, w_out_ref, router_ref, member_ref, put_ref, take_ref, expand_ref,
    expand_t_ref, place_ref, place_t_ref, origin_ref, block_place_ref, cot_ref, cots_hbm, gate_hbm, up_hbm, down_hbm,
    residual_ref, weigh_high_ref, weigh_low_ref, gmid_ref, branch_ref, gsent_in, side_in,
    y_hbm, grads_hbm,
    sent_in, x_out, x_in, y_v, back_out, back_in, gate_v, up_v, down_v,
    sum_gate, sum_up, sum_down, grads_v, mixed_v, gate_probs, gsent_out, side_out, cots_v,
    note_out, note_in, answer_out, answer_in,
    x_send, x_recv, back_send, back_recv, note_send, note_recv, answer_send, answer_recv,
    line_send, line_recv, local,
):
    me = position(AXES)
    x_at, y_at, z_at, c_at = (me[axis] for axis in AXES)
    expert = (y_at * 4 + z_at) * 2 + c_at

    def offset(k):
        pair = lax.div(k, 2)
        dy = lax.shift_right_logical(jnp.int32(STEP_Y), 2 * pair) & 3
        dz = lax.shift_right_logical(jnp.int32(STEP_Z), 2 * pair) & 3
        return dy, dz, lax.rem(k + pair, 2)

    def toward(k):
        dy, dz, dc = offset(k)
        return {"y": lax.rem(y_at + dy, 4), "z": lax.rem(z_at + dz, 4), "c": lax.rem(c_at + dc, 2)}

    def source(k):
        dy, dz, dc = offset(k)
        return {
            "y": lax.rem(y_at + 4 - dy, 4),
            "z": lax.rem(z_at + 4 - dz, 4),
            "c": lax.rem(c_at + dc, 2),
        }

    def number(at):
        return (at["y"] * 4 + at["z"]) * 2 + at["c"]

    loads = [
        pltpu.make_async_copy(src, dst, local.at[i])
        for i, (src, dst) in enumerate(
            ((cots_hbm, cots_v), (gate_hbm, gate_v), (up_hbm, up_v), (down_hbm, down_v))
        )
    ]
    for item in loads:
        item.start()
    barrier = pltpu.get_barrier_semaphore()
    for by in LINE_OFFSETS:
        pl.semaphore_signal(barrier, inc=1, device_id=moved(me, by), device_id_type=MESH)

    def hello(k, carry):
        pl.semaphore_signal(barrier, inc=1, device_id=toward(k), device_id_type=MESH)
        return carry

    lax.fori_loop(0, 31, hello, 0)
    sum_gate[...] = jnp.zeros_like(sum_gate)
    sum_up[...] = jnp.zeros_like(sum_up)
    sum_down[...] = jnp.zeros_like(sum_down)
    pl.semaphore_wait(barrier, 31 + len(LINE_OFFSETS))

    here_line = x_at * 2 + c_at
    moves = []
    for i, by in enumerate(LINE_OFFSETS):
        to = moved(me, by)
        moves.append(
            remote(sent_ref.at[to["c"] * 4 + to["x"]], sent_in.at[here_line], line_send, line_recv, i, to)
        )
        moves[-1].start()
    kept = pltpu.make_async_copy(sent_ref.at[c_at * 4 + x_at], sent_in.at[here_line], local.at[4])
    kept.start()
    for item in moves + [kept]:
        item.wait()
    sent = jnp.concatenate([sent_in[i] for i in range(8)], axis=1)
    residual = tok_ref[...].astype(F32) + mm(sent, w_out_ref[...])
    residual_ref[...] = residual
    residual_ref.store()
    gain = router_ref[...].astype(F32).T[EXPERTS : EXPERTS + 1, :]
    scale = lax.rsqrt(jnp.mean(residual * residual, axis=-1, keepdims=True) + EPSILON)
    mixed = (residual * scale * gain).astype(BF16)
    mixed_v[...] = mixed
    put = put_ref[...]

    def tiles(value):
        return value.reshape(8, SLOT, 8, 128).astype(BF16)

    def rows_of(value):
        return value.astype(F32).reshape(value.shape[0] * SLOT, D).astype(BF16)

    for i in range(4):
        x_out[i * 8 : (i + 1) * 8] = tiles(mm(put[i * BLOCK : (i + 1) * BLOCK], mixed))

    def x_copy(k):
        to = toward(k)
        return remote(x_out.at[number(to)], x_in.at[k], x_send, x_recv, k, to)

    def note_copy(k):
        to = toward(k)
        return remote(note_out.at[number(to)], note_in.at[k], note_send, note_recv, k, to)

    def x_start(k, carry):
        x_copy(k).start()
        return carry

    lax.fori_loop(0, 8, x_start, 0)
    kept = pltpu.make_async_copy(x_out.at[expert], x_in.at[31], local.at[4])
    kept.start()
    logits = mm(mixed, router_ref[...])
    member = member_ref[...]
    masked = jnp.where(member > 0.5, logits, -FAR)
    top = jnp.max(masked, axis=1, keepdims=True)
    power = jnp.where(member > 0.5, jnp.exp(masked - top), 0.0)
    gate = power / jnp.sum(power, axis=1, keepdims=True)
    gate_probs[...] = gate
    gate_high, gate_low = halves(gate)
    spread = mm(gate_high, expand_ref[...]) + mm(gate_low, expand_ref[...])
    weigh = take_ref[...].astype(F32) * spread
    weigh_high, weigh_low = halves(weigh)
    weigh_high_ref[...] = weigh_high
    weigh_low_ref[...] = weigh_low
    weigh_high_ref.store()
    weigh_low_ref.store()
    wide_expand = expand_ref[...].astype(F32)
    rows_high, rows_low = halves(wide_expand * jnp.sum(weigh, axis=0, keepdims=True))
    gates = mm(rows_high, place_ref[...]) + mm(rows_low, place_ref[...])
    token = lax.broadcasted_iota(jnp.int32, (ROWS, SLOTS), 0).astype(F32)
    token = jnp.sum(take_ref[...].astype(F32) * token, axis=0, keepdims=True)
    token = mm((wide_expand * token).astype(BF16), place_ref[...])
    top_row = lax.broadcasted_iota(jnp.int32, (8, 128), 0) == 0
    for i in range(EXPERTS):
        note_out[i] = jnp.where(
            top_row,
            jnp.broadcast_to(gates[i : i + 1], (8, 128)),
            jnp.broadcast_to(token[i : i + 1], (8, 128)),
        )

    def note_start(k, carry):
        note_copy(k).start()
        return carry

    lax.fori_loop(0, 31, note_start, 0)
    lax.fori_loop(8, 31, x_start, 0)
    note_in[31] = note_out[expert]
    kept.wait()
    for item in loads:
        item.wait()

    def cot_of(at):
        return cots_v[number(at)]

    block_row = lax.broadcasted_iota(jnp.int32, (BLOCK, 1), 0)
    block_start = jnp.zeros((BLOCK, 1), F32)
    for i in range(1, 8):
        block_start += jnp.where(block_row >= i * SLOT, 128.0, 0.0)
    origin_ref.get()
    block_place_ref.get()

    def answer_copy(k):
        return remote(answer_out.at[k], answer_in.at[expert], answer_send, answer_recv, k, source(k))

    def back_copy(k):
        to = source(k)
        return remote(back_out.at[k], back_in.at[expert], back_send, back_recv, k, to)

    def back_kept():
        return pltpu.make_async_copy(back_out.at[31], back_in.at[expert], local.at[4])

    def group(step, carry):
        first = step * 8
        for i in range(8):
            k = first + i

            @pl.when(k < 31)
            def _():
                x_copy(k).wait_recv()
                note_copy(k).wait_recv()

        x = rows_of(x_in[pl.ds(first, 8)])
        origin, place = origin_ref[...], block_place_ref[...].astype(F32)
        blank = jnp.zeros((120, 128), F32)
        gates = [note_in[first + i][0:1] for i in range(8)]
        gates_high, gates_low = halves(jnp.concatenate(gates + [blank], axis=0))
        share = mm(origin, gates_high) + mm(origin, gates_low)
        share = jnp.sum(share * place, axis=1, keepdims=True)
        tokens = [note_in[first + i][1:2] for i in range(8)]
        row = mm(origin, jnp.concatenate(tokens + [blank], axis=0).astype(BF16))
        row = jnp.sum(row * place, axis=1, keepdims=True) + block_start
        chosen = jnp.where(lane_index((BLOCK, D)).astype(F32) == row, 1.0, 0.0).astype(BF16)
        g = mm(chosen, jnp.concatenate([cot_of(source(first + i)) for i in range(8)], axis=0))
        a = mm(x, gate_v[...])
        b = mm(x, up_v[...])
        s = 1.0 / (1.0 + jnp.exp(-a))
        silu = a * s
        hidden = (silu * b).astype(BF16)
        y = mm(hidden, down_v[...]).astype(BF16).astype(F32)
        dgate = jnp.sum(y * g, axis=1, keepdims=True)
        dgate_high, dgate_low = halves(dgate * place)
        answers = mm(origin, dgate_high, TN) + mm(origin, dgate_low, TN)
        for i in range(8):
            k = first + i
            answer_out[k] = jnp.broadcast_to(answers[i : i + 1], (8, 128))

            @pl.when(k < 31)
            def _():
                answer_copy(k).start()

        y = tiles(y)
        for i in range(8):
            y_v[number(source(first + i))] = y[i]
        gy = (g * share).astype(BF16)
        dhidden = mm(gy, down_v[...], NT)
        da = (dhidden * b * (s * (1.0 + a * (1.0 - s)))).astype(BF16)
        db = (dhidden * silu).astype(BF16)
        back = mm(da, gate_v[...], NT) + mm(db, up_v[...], NT)
        back_out[pl.ds(first, 8)] = tiles(back)
        for i in range(8):
            k = first + i

            @pl.when(k < 31)
            def _():
                back_copy(k).start()

            @pl.when(k == 31)
            def _():
                back_kept().start()

        sum_gate[...] += mm(x, da, TN)
        sum_up[...] += mm(x, db, TN)
        sum_down[...] += mm(hidden, gy, TN)
        return carry

    lax.fori_loop(0, 4, group, 0)
    answer_in[expert] = answer_out[31]
    for i in range(4):
        grads_v[i * 768 : i * 768 + 256] = sum_gate[i * 256 : (i + 1) * 256].astype(BF16)
        grads_v[i * 768 + 256 : i * 768 + 512] = sum_up[i * 256 : (i + 1) * 256].astype(BF16)
        down = sum_down[i * 128 : (i + 1) * 128].astype(BF16)
        grads_v[i * 768 + 512 : i * 768 + 640] = down[:, 0:FF]
        grads_v[i * 768 + 640 : i * 768 + 768] = down[:, FF:D]
    stores = [
        pltpu.make_async_copy(src, dst, local.at[i])
        for i, (src, dst) in enumerate(((y_v, y_hbm), (grads_v, grads_hbm)))
    ]
    for item in stores:
        item.start()

    def answers(k, carry):
        answer_copy(k).wait()
        return carry

    lax.fori_loop(0, 31, answers, 0)
    take = take_ref[...]
    rows_high, rows_low = halves(
        jnp.concatenate([answer_in[i][0:1] for i in range(EXPERTS)] + [jnp.zeros((96, 128), F32)], axis=0)
    )
    spread = mm(rows_high, place_t_ref[...]) + mm(rows_low, place_t_ref[...])
    along = jnp.sum(spread * expand_ref[...].astype(F32), axis=0, keepdims=True)
    found_high, found_low = halves(take.astype(F32) * along)
    dgate = mm(found_high, expand_t_ref[...]) + mm(found_low, expand_t_ref[...])
    gate = gate_probs[...]
    dlogits = gate * (dgate - jnp.sum(gate * dgate, axis=1, keepdims=True))
    dlogits = dlogits.astype(BF16)
    dmixed = mm(dlogits, router_ref[...], NT)

    def settle(k, carry):
        x_copy(k).wait_send()
        note_copy(k).wait_send()
        back_copy(k).wait()
        return carry

    lax.fori_loop(0, 31, settle, 0)
    back_kept().wait()

    dmixed += mm(take, rows_of(back_in[...]))
    residual = residual_ref[...]
    scale = lax.rsqrt(jnp.mean(residual * residual, axis=-1, keepdims=True) + EPSILON)
    gain = router_ref[...].astype(F32).T[EXPERTS : EXPERTS + 1, :]
    weighted = dmixed * gain
    inner = jnp.mean(weighted * residual, axis=-1, keepdims=True)
    gmid = cot_ref[...].astype(F32) + scale * weighted - residual * (scale * scale * scale) * inner
    gmid_ref[...] = gmid
    gmid_ref.store()
    branch = gmid.astype(BF16)
    branch_ref[...] = branch
    branch_ref.store()
    gsent = mm(branch, w_out_ref[...], NT).astype(BF16)
    for i in range(8):
        gsent_out[i] = gsent[:, i * 128 : (i + 1) * 128]
    back_line = c_at * 4 + x_at
    moves = []
    for i, by in enumerate(LINE_OFFSETS):
        to = moved(me, by)
        moves.append(
            remote(
                gsent_out.at[to["x"] * 2 + to["c"]], gsent_in.at[back_line], line_send, line_recv, 7 + i, to
            )
        )
        moves[-1].start()
    kept = pltpu.make_async_copy(gsent_out.at[here_line], gsent_in.at[back_line], local.at[4])
    kept.start()
    moves.append(kept)
    gain_grad = jnp.sum(dmixed * residual * scale, axis=0, keepdims=True)
    grads = mm(dlogits, mixed_v[...], TN)
    row = lax.broadcasted_iota(jnp.int32, (128, D), 0)
    grads = jnp.where(row == EXPERTS, gain_grad, grads).T.reshape(4, 16, 2, 8, 128)
    for i in range(8):
        side_out[i] = grads[i // 2, :, i % 2].reshape(ROWS, 128).astype(BF16)
    for i, by in enumerate(LINE_OFFSETS):
        to = moved(me, by)
        moves.append(
            remote(
                side_out.at[to["x"] * 2 + to["c"]], side_in.at[back_line], line_send, line_recv, 14 + i, to
            )
        )
        moves[-1].start()
    kept = pltpu.make_async_copy(side_out.at[here_line], side_in.at[back_line], local.at[5])
    kept.start()
    for item in moves + [kept] + stores:
        item.wait()


def moe(inputs, cid):
    slots = (EXPERTS, SLOT, 8, 128)
    up, down = (D, FF), (FF, D)
    dma = pltpu.SemaphoreType.DMA
    return remote_call(
        moe_kernel,
        inputs,
        ("h", "l", (0, D), (D, D + 128)) + ("l",) * 10 + ("h",) * 4,
        [
            shape((ROWS, D), F32),
            shape((ROWS, SLOTS), BF16),
            shape((ROWS, SLOTS), BF16),
            shape((ROWS, D), F32),
            shape((ROWS, D), BF16),
            shape((8, ROWS, 128), BF16),
            shape((8, ROWS, 128), BF16),
            shape(slots, BF16),
            shape((3 * D, FF), BF16),
        ],
        ("e", "e", "e", "e", "e", "v", "v", "h", "h"),
        [
            pltpu.VMEM((8, ROWS, 128), BF16),
            pltpu.VMEM(slots, BF16),
            pltpu.VMEM(slots, BF16),
            pltpu.VMEM(slots, BF16),
            pltpu.VMEM(slots, BF16),
            pltpu.VMEM(slots, BF16),
            pltpu.VMEM(up, BF16),
            pltpu.VMEM(up, BF16),
            pltpu.VMEM(down, BF16),
            pltpu.VMEM(up, F32),
            pltpu.VMEM(up, F32),
            pltpu.VMEM(down, F32),
            pltpu.VMEM((3 * D, FF), BF16),
            pltpu.VMEM((ROWS, D), BF16),
            pltpu.VMEM((ROWS, 128), F32),
            pltpu.VMEM((8, ROWS, 128), BF16),
            pltpu.VMEM((8, ROWS, 128), BF16),
            pltpu.VMEM((EXPERTS, ROWS, D), BF16),
            pltpu.VMEM((EXPERTS, 8, 128), F32),
            pltpu.VMEM((EXPERTS, 8, 128), F32),
            pltpu.VMEM((EXPERTS, 8, 128), F32),
            pltpu.VMEM((EXPERTS, 8, 128), F32),
        ]
        + [dma((31,))] * 8
        + [
            dma((21,)),
            dma((21,)),
            dma((6,)),
        ],
        cid,
    )


def tail_kernel(
    partial_ref, sent_ref, branch_ref, side_rows_ref, dq_ref, cos_ref, sin_ref, normed_ref, w_ref,
    y_ref, weigh_high_ref, weigh_low_ref, residual_ref,
    dnormed_out, mixed_out, grads_out, early_out,
    dqkv, part_out, part_in, part_own, line_out, line_in, share_out, share_in, total,
    out_in, side_in, dkv_ref, out_ref, side_ref, far_a, near_a, out_a, sum_a, far_b, near_b, out_b,
    plane_send, plane_recv, send, recv, local, out_recv,
):
    me = position(AXES)
    x, y, z, c = (me[axis] for axis in AXES)
    mine = y * 4 + z
    alone = jnp.where(c == lax.div(y, 2), 1, 0)
    barrier = pltpu.get_barrier_semaphore()

    def owner(k):
        at = lax.rem(lax.rem(y, 2) * 8 + z * 2 + c + k, 16)
        to = {"y": 2 * c + lax.div(at, 8), "z": lax.rem(lax.div(at, 2), 4), "c": lax.rem(at, 2)}
        return at, to

    def origin(k):
        at = lax.rem(mine + k, 16)
        return at, {"y": lax.div(at, 4), "z": lax.rem(at, 4), "c": lax.div(y, 2)}

    for k in range(1, 16):
        pl.semaphore_signal(barrier, inc=1, device_id=origin(k)[1], device_id_type=MESH)

    @pl.when(alone == 0)
    def _():
        pl.semaphore_signal(barrier, inc=1, device_id=origin(0)[1], device_id_type=MESH)

    offsets = LINE_OFFSETS + PLANE_OFFSETS
    for offset in offsets:
        pl.semaphore_signal(barrier, inc=1, device_id=moved(me, offset), device_id_type=MESH)
    grad_out = mm(sent_ref[...], branch_ref[...], TN)
    for j in range(16):
        out_ref[j] = grad_out[j * 8 : (j + 1) * 8]
    side = side_rows_ref[0].astype(F32)
    for i in range(1, 8):
        side += side_rows_ref[i].astype(F32)
    side_ref[...] = side.reshape(16, 8, 128)
    pl.semaphore_wait(barrier, len(offsets) + 16 - alone)
    scatter_plane(
        me, partial_ref, dkv_ref, far_a, near_a, out_a, sum_a, far_b, near_b, out_b, plane_send, plane_recv
    )
    used = [0]

    def go(src, dst, to):
        item = remote(src, dst, send, recv, used[0], to)
        used[0] += 1
        item.start()
        return item

    other = 1 - c
    low_lanes = lane_index((256, 128)) < 64

    def out_copy(k):
        at, to = owner(k)
        return pltpu.make_async_remote_copy(
            src_ref=out_ref.at[at], dst_ref=out_in.at[mine], send_sem=send.at[used[0] + k],
            recv_sem=out_recv.at[mine], device_id=to, device_id_type=MESH,
        )

    def out_kept():
        return pltpu.make_async_copy(out_ref.at[owner(0)[0]], out_in.at[mine], local.at[1])

    out_copies = [out_copy(k) for k in range(16)]
    used[0] += 16
    out_arrivals = []
    for k in range(16):
        at, to = origin(k)
        out_arrivals.append(
            pltpu.make_async_remote_copy(
                src_ref=out_ref.at[0], dst_ref=out_in.at[at], send_sem=send.at[0],
                recv_sem=out_recv.at[at], device_id=to, device_id_type=MESH,
            )
        )

    @pl.when(alone == 0)
    def _():
        out_copies[0].start()

    @pl.when(alone == 1)
    def _():
        out_kept().start()

    for item in out_copies[1:]:
        item.start()
    early = []
    for offset in PLANE_OFFSETS:
        to = moved(me, offset)
        early.append(go(side_ref.at[to["y"] * 4 + to["z"]], side_in.at[mine], to))
    side_kept = pltpu.make_async_copy(side_ref.at[mine], side_in.at[mine], local.at[2])
    side_kept.start()
    early.append(side_kept)

    def turn_back(first):
        rows = pl.ds(pl.multiple_of(first, 256), 256)
        cos, sin = cos_ref[rows, :], sin_ref[rows, :]
        dq, dkv = dq_ref[rows, :], dkv_ref[lax.div(first, 512), pl.ds(lax.rem(first, 512), 256), :]
        dq = (dq * cos - turned(dq) * sin).astype(BF16)
        dkv = jnp.where(low_lanes, dkv * cos - turned(dkv) * sin, dkv).astype(BF16)
        both = jnp.concatenate([dq, dkv], axis=1)
        dqkv[rows, :] = both
        return mm(both, w_ref[...], NT)

    crossing = []
    for i in range(2):
        value = turn_back(other * 512 + i * 256).astype(BF16)
        part_out[2 * i] = value[:ROWS]
        part_out[2 * i + 1] = value[ROWS:]
        span = pl.ds(2 * i, 2)
        crossing.append(go(part_out.at[span], part_in.at[span], {"c": other}))
    for i in range(2):
        value = turn_back(c * 512 + i * 256)
        part_own[2 * i] = value[:ROWS]
        part_own[2 * i + 1] = value[ROWS:]
    for item in crossing:
        item.wait()
    along = []
    for i, by in enumerate((2, 1, 3)):
        to = lax.rem(x + by, 4)
        line_out[i] = (part_own[to] + part_in[to].astype(F32)).astype(BF16)
        along.append(go(line_out.at[i], line_in.at[i], {"x": to}))
    for i in range(4):
        columns = pl.ds(i * 256, 256)
        grad = mm(normed_ref[:, columns], dqkv[...], TN).astype(BF16)
        share_out[i] = grad.reshape(16, 16, 256)
    spread = []
    for offset in PLANE_OFFSETS:
        to = moved(me, offset)
        spread.append(go(share_out.at[:, to["y"] * 4 + to["z"]], share_in.at[mine], to))
    kept = pltpu.make_async_copy(share_out.at[:, mine], share_in.at[mine], local.at[0])
    kept.start()
    outs = y_ref[...].astype(F32).reshape(SLOTS, D).astype(BF16)
    mixed = mm(weigh_high_ref[...], outs) + mm(weigh_low_ref[...], outs)
    mixed_out[...] = (residual_ref[...] + mixed).astype(BF16)
    mixed_out.store()
    for item in spread + [kept]:
        item.wait()
    for i in range(4):
        value = share_in[0, i].astype(F32)
        for j in range(1, 16):
            value += share_in[j, i].astype(F32)
        total[i] = value.reshape(2, 8, 256)
    ends = []
    here = x * 2 + c
    for offset in LINE_OFFSETS:
        to = moved(me, offset)
        ends.append(go(total.at[to["x"], to["c"]], grads_out.at[here], to))
    kept = pltpu.make_async_copy(total.at[x, c], grads_out.at[here], local.at[0])
    kept.start()
    for item in out_copies[1:]:
        item.wait_send()
    for item in out_arrivals[1:]:
        item.wait_recv()

    @pl.when(alone == 0)
    def _():
        out_copies[0].wait_send()
        out_arrivals[0].wait_recv()

    @pl.when(alone == 1)
    def _():
        out_kept().wait()

    for item in early:
        item.wait()
    out_total, side_total = out_in[0], side_in[0]
    for j in range(1, 16):
        out_total += out_in[j]
        side_total += side_in[j]
    early_out[:, 0:D] = out_total
    early_out[:, D : D + 128] = side_total
    for item in along:
        item.wait()
    dnormed = part_own[x] + part_in[x].astype(F32)
    for i in range(3):
        dnormed += line_in[i].astype(F32)
    dnormed_out[...] = dnormed
    for item in ends + [kept]:
        item.wait()


def tail(inputs, cid):
    count = 2 + 3 + 15 + 7 + 16 + 15
    return remote_call(
        tail_kernel,
        inputs,
        ("l",) * 8 + ((0, 256), "v", "l", "l", "l"),
        [
            shape((ROWS, D), F32),
            shape((ROWS, D), BF16),
            shape((8, 8, 256), F32),
            shape((8, D + 128), F32),
        ],
        ("v", "e", "v", "v"),
        [
            pltpu.VMEM((CHIP_ROWS, 256), BF16),
            pltpu.VMEM((4, ROWS, D), BF16),
            pltpu.VMEM((4, ROWS, D), BF16),
            pltpu.VMEM((4, ROWS, D), F32),
            pltpu.VMEM((3, ROWS, D), BF16),
            pltpu.VMEM((3, ROWS, D), BF16),
            pltpu.VMEM((4, 16, 16, 256), BF16),
            pltpu.VMEM((16, 4, 16, 256), BF16),
            pltpu.VMEM((4, 2, 8, 256), F32),
            pltpu.VMEM((16, 8, D), F32),
            pltpu.VMEM((16, 8, 128), F32),
            pltpu.VMEM((2, 512, 128), F32),
            pltpu.VMEM((16, 8, D), F32),
            pltpu.VMEM((16, 8, 128), F32),
            pltpu.VMEM((2, 4, 2, 256, 128), BF16),
            pltpu.VMEM((2, 4, 2, 512, 128), BF16),
            pltpu.VMEM((2, 4, 2, 512, 128), BF16),
            pltpu.VMEM((2, 2, 512, 128), F32),
            pltpu.VMEM((2, 2, 256, 128), BF16),
            pltpu.VMEM((2, 2, 512, 128), BF16),
            pltpu.VMEM((2, 3, 512, 128), BF16),
            pltpu.SemaphoreType.DMA((40,)),
            pltpu.SemaphoreType.DMA((40,)),
            pltpu.SemaphoreType.DMA((count,)),
            pltpu.SemaphoreType.DMA((count,)),
            pltpu.SemaphoreType.DMA((3,)),
            pltpu.SemaphoreType.DMA((16,)),
        ],
        cid,
    )


def last_kernel(
    dnormed_ref, tok_ref, gain_ref, gmid_ref, mixed_ref, rows_ref, wq_ref, wk_ref, wv_ref, own_gain_ref, early_ref,
    grads_ref,
    tokens_out, mixed_out, query_out, key_out, value_out, gains_out, grad_out, router_out,
    gate_out, up_out, down_out,
):
    tok = tok_ref[...].astype(F32)
    scale = lax.rsqrt(jnp.mean(tok * tok, axis=-1, keepdims=True) + EPSILON)
    weighted = dnormed_ref[...] * gain_ref[...]
    inner = jnp.mean(weighted * tok, axis=-1, keepdims=True)
    tokens_out[...] = gmid_ref[...] + scale * weighted - tok * (scale * scale * scale) * inner
    mixed_out[...] = mixed_ref[...]
    for i in range(8):
        query_out[:, i * 128 : (i + 1) * 128] = rows_ref[i][:, :128]
    lanes = lane_index((8, 128)) < 64
    for i in range(4):
        first, second = rows_ref[2 * i][:, 128:], rows_ref[2 * i + 1][:, 128:]
        key_out[:, i * 128 : (i + 1) * 128] = jnp.where(lanes, first, pltpu.roll(second, 64, axis=1))
        value_out[:, i * 128 : (i + 1) * 128] = jnp.where(lanes, pltpu.roll(first, 64, axis=1), second)
    total = (
        jnp.sum(query_out[...] * wq_ref[...].astype(F32), axis=1, keepdims=True)
        + jnp.sum(key_out[...] * wk_ref[...].astype(F32), axis=1, keepdims=True)
        + jnp.sum(value_out[...] * wv_ref[...].astype(F32), axis=1, keepdims=True)
    )
    gain_one = jnp.broadcast_to(total, (8, 128)).T[0:1, :]
    side = early_ref[:, D : D + 128]
    gain_two = side.T[EXPERTS : EXPERTS + 1, :]
    gains_out[0:1, :] = gain_one[:, 0:8] / own_gain_ref[...].astype(F32)
    gains_out[1:2, :] = gain_two[:, 0:8]
    grad_out[...] = early_ref[:, 0:D]
    router_out[...] = side[:, 0:EXPERTS]
    gate_out[...] = grads_ref[0:256].astype(F32)
    up_out[...] = grads_ref[256:512].astype(F32)
    down_out[:, 0:FF] = grads_ref[512:640].astype(F32)
    down_out[:, FF:D] = grads_ref[640:768].astype(F32)


def body(
    tokens,
    gain_one,
    w_query,
    w_key,
    w_value,
    w_out,
    gain_two,
    w_router,
    w_gate,
    w_up,
    w_down,
    dealt_order,
    lengths,
    routes,
    cotangent,
):
    y_at, z_at = lax.axis_index("y"), lax.axis_index("z")
    first_row = (y_at * 4 + z_at) * CHIP_ROWS

    cot_rows = lax.all_gather(cotangent, ("y", "z", "c"), axis=0, tiled=True)

    expand, expand_t = expand_matrix(), expand_matrix().T
    place, place_t = place_matrix(), place_matrix().T
    (
        query, kv, gain_first, cos, sin, w_mine, member, put, take, own_aux, order_rows, key_norm,
        kv_all, w_late, normed, aux,
    ) = front(
        (
            lengths, tokens, w_query, w_key, w_value, w_out, w_router, gain_one.reshape(1, 8),
            gain_two.reshape(1, 8), dealt_order.reshape(128, 128), routes.T,
            expand, expand_t, place_column(), place_row(), turn_tables(128), turn_tables(1),
        ),
        1,
    )
    kv_all = kv_all.reshape(TOKENS, 128)
    w_late = w_late.reshape(D, 1152)
    plane = ("y", "z", "c")

    base = first_row.reshape(1).astype(jnp.int32)
    att, norm, sent, query_ext = attend(
        dealt_order, base, kv_all, aux, kv, own_aux, query, order_rows, key_norm
    )

    (
        residual, weigh_high, weigh_low, gmid, branch, gsent_own, side_rows, y_out, expert_grads,
    ) = moe(
        (
            sent.reshape(8, ROWS, 128), tokens, w_late, w_late, member, put, take, expand, expand_t,
            place, place_t, origin_matrix(), place[:BLOCK], cotangent,
            cot_rows.reshape(EXPERTS, ROWS, D), w_gate[0], w_up[0], w_down[0],
        ),
        3,
    )
    y_in = lax.all_to_all(y_out, plane, split_axis=0, concat_axis=0, tiled=True)
    expert_grads = lax.psum_scatter(expert_grads, "x", scatter_dimension=0, tiled=True)

    gsent_own = gsent_own.reshape(CHIP_ROWS, 128)
    branch_rows = lax.all_gather(branch, ("c", "x"), axis=0, tiled=True)

    dq, dkv = attend_back(
        dealt_order, base, kv_all, aux, kv, own_aux, query_ext, order_rows, gsent_own, att, norm
    )

    dnormed, mixed, qkv_rows, early = tail(
        (
            dkv.reshape(4, 4, 2, 512, 128), sent, branch_rows, side_rows, dq, cos, sin, normed, w_mine,
            y_in, weigh_high, weigh_low, residual,
        ),
        7,
    )
    (
        grad_tokens, mixed, grad_query, grad_key, grad_value, gains, grad_out_rows, grad_router,
        grad_gate, grad_up, grad_down,
    ) = local_call(
        last_kernel,
        (
            shape((ROWS, D), F32),
            shape((ROWS, D), BF16),
            shape((8, D), F32),
            shape((8, 512), F32),
            shape((8, 512), F32),
            shape((2, 8), F32),
            shape((8, D), F32),
            shape((8, EXPERTS), F32),
            shape((256, FF), F32),
            shape((256, FF), F32),
            shape((128, D), F32),
        ),
    )(
        dnormed, tokens, gain_first, gmid, mixed, qkv_rows, w_query, w_key, w_value,
        gain_one.reshape(1, 8), early, expert_grads,
    )
    grad_gain_one, grad_gain_two = gains[0], gains[1]
    grad_gate, grad_up, grad_down = grad_gate[None], grad_up[None], grad_down[None]
    return (
        mixed,
        grad_tokens,
        grad_gain_one,
        grad_query,
        grad_key,
        grad_value,
        grad_out_rows,
        grad_gain_two,
        grad_router,
        grad_gate,
        grad_up,
        grad_down,
    )


def solution(mesh):
    grid = Mesh(mesh.devices.reshape(4, 4, 4, 2), AXES)
    rows = P(("y", "z", "c", "x"), None)
    vector = P(AXES)
    matrix = P(AXES, None)
    expert = P(("y", "z", "c"), None, None)
    in_specs = (
        rows, vector, matrix, matrix, matrix, matrix, vector, matrix, expert, expert, expert,
        P(), P(), rows, rows,
    )
    grads = P(("y", "z", "c"), "x", None)
    out_specs = (
        rows, rows, vector, matrix, matrix, matrix, matrix, vector, matrix, grads, grads, grads,
    )
    return jax.shard_map(body, mesh=grid, in_specs=in_specs, out_specs=out_specs, check_vma=False)
```

```python
import functools
import math

import jax
import jax.numpy as jnp
import ml_dtypes
import numpy as np
from jax import lax
from jax.experimental import pallas as pl
from jax.experimental.pallas import tpu as pltpu
from jax.sharding import Mesh
from jax.sharding import PartitionSpec as P

D = 1024
HEADS = 16
KV_HEADS = 8
HEAD_DIM = 64
EXPERTS = 32
FF = 512
CAP = 36
SLOT = CAP
SLOTS = EXPERTS * SLOT
ROWS = 128
CHIP_ROWS = 1024
RUN = 256
TOKENS = 16384
NSEQ = 5
EPSILON = 1e-06
ROPE_BASE = 10000.0
FAR = float(2.0**100)
SIZE = {"x": 4, "y": 4, "z": 4, "c": 2}
AXES = ("x", "y", "z", "c")
MESH = pl.DeviceIdType.MESH
BF16 = jnp.bfloat16
F32 = jnp.float32
NN = (((1,), (0,)), ((), ()))
NT = (((1,), (1,)), ((), ()))
TN = (((0,), (0,)), ((), ()))
VMEM_BYTES = 56 * 1024 * 1024


def mm(a, b, dims=NN):
    return lax.dot_general(a, b, dims, preferred_element_type=F32)


def shape(dims, dtype):
    return jax.ShapeDtypeStruct(dims, dtype)


def halves(value):
    high = value.astype(BF16)
    return high, (value - high.astype(F32)).astype(BF16)


def local_call(kernel, outs, scratch=(), grid=None, in_specs=None, out_specs=None):
    extra = {}
    if grid is not None:
        extra = {"grid": grid, "in_specs": in_specs, "out_specs": out_specs}
    elif in_specs is not None:
        extra = {"in_specs": in_specs}
        if out_specs is not None:
            extra["out_specs"] = out_specs
    return pl.pallas_call(
        kernel,
        out_shape=outs,
        scratch_shapes=list(scratch),
        compiler_params=pltpu.CompilerParams(vmem_limit_bytes=VMEM_BYTES),
        **extra,
    )


class Late:
    def __init__(self, hbm, vmem, sem, columns, wait):
        self.hbm, self.vmem = hbm, vmem
        source = hbm if columns is None else hbm.at[:, columns[0] : columns[1]]
        self.copy, self.ready = pltpu.make_async_copy(source, vmem, sem), False
        if not wait:
            self.copy.start()

    def begin(self):
        self.copy.start()

    def get(self):
        if not self.ready:
            self.copy.wait()
            self.ready = True
        return self.vmem

    def __getitem__(self, index):
        return self.get()[index]


class Early:
    def __init__(self, hbm, vmem, sem):
        self.vmem, self.copy = vmem, pltpu.make_async_copy(vmem, hbm, sem)

    def __getitem__(self, index):
        return self.vmem[index]

    def __setitem__(self, index, value):
        self.vmem[index] = value

    def store(self):
        self.copy.start()


DEFERRED_COLUMNS = (0, 256)


def remote_call(kernel, inputs, kinds, outs, out_kinds, scratch, cid, room=VMEM_BYTES):
    spaces = {"s": pltpu.SMEM, "v": pltpu.VMEM}
    late = [(i, kind) for i, kind in enumerate(kinds) if kind not in ("s", "v", "h")]
    early = [i for i, kind in enumerate(out_kinds) if kind == "e"]

    def late_shape(i, kind):
        dims = inputs[i].shape if kind in ("l", "d") else (inputs[i].shape[0], kind[1] - kind[0])
        return pltpu.VMEM(dims, inputs[i].dtype)

    def wrapped(*refs):
        ins, rest = list(refs[: len(inputs)]), list(refs[len(inputs) :])
        results, rest = rest[: len(outs)], rest[len(outs) :]
        own, rest = rest[: len(scratch)], rest[len(scratch) :]
        late_v, rest = rest[: len(late)], rest[len(late) :]
        early_v, (late_sem, early_sem) = rest[: len(early)], rest[len(early) :]
        for n, (i, kind) in enumerate(late):
            columns = None if kind in ("l", "d") else kind
            ins[i] = Late(ins[i], late_v[n], late_sem.at[n], columns, kind == "d" or kind == DEFERRED_COLUMNS)
        for n, i in enumerate(early):
            results[i] = Early(results[i], early_v[n], early_sem.at[n])
        kernel(*ins, *results, *own)
        for i, _ in late:
            ins[i].get()
        for i in early:
            results[i].copy.wait()

    return pl.pallas_call(
        wrapped,
        out_shape=list(outs),
        in_specs=[pl.BlockSpec(memory_space=spaces.get(kind, pl.ANY)) for kind in kinds],
        out_specs=[pl.BlockSpec(memory_space=spaces.get(kind, pl.ANY)) for kind in out_kinds],
        scratch_shapes=list(scratch)
        + [late_shape(i, kind) for i, kind in late]
        + [pltpu.VMEM(outs[i].shape, outs[i].dtype) for i in early]
        + [pltpu.SemaphoreType.DMA((max(1, len(late)),)), pltpu.SemaphoreType.DMA((max(1, len(early)),))],
        compiler_params=pltpu.CompilerParams(
            collective_id=cid, has_side_effects=True, vmem_limit_bytes=room
        ),
    )(*inputs)


def flat_index(coords, order):
    index = 0
    for axis in order:
        index = index * SIZE[axis] + coords[axis]
    return index


PLANE_ORDER = (
    (2, 2), (2, 3), (2, 1), (3, 2), (1, 2), (0, 2), (2, 0), (3, 1), (1, 3),
    (3, 3), (1, 1), (0, 3), (0, 1), (3, 0), (1, 0), (0, 0),
)
PLANE_OFFSETS = tuple({"y": dy, "z": dz} for dy, dz in PLANE_ORDER[:-1])
SPREAD_OFFSETS = tuple(
    {"y": dy, "z": dz, "c": (dc + i + 1) % 2}
    for i, (dy, dz) in enumerate(PLANE_ORDER)
    for dc in range(2)
    if (dy, dz, (dc + i + 1) % 2) != (0, 0, 0)
)
LINE_OFFSETS = tuple(
    {"x": dx, "c": dc} for dx, dc in ((2, 0), (2, 1), (1, 0), (3, 0), (1, 1), (3, 1), (0, 1))
)
OFFSETS = {("y", "z"): PLANE_OFFSETS, ("y", "z", "c"): SPREAD_OFFSETS, ("x", "c"): LINE_OFFSETS}


def position(axes):
    return {axis: lax.axis_index(axis) for axis in axes}


def moved(me, offset):
    return {axis: lax.rem(me[axis] + by, SIZE[axis]) if by else me[axis] for axis, by in offset.items()}


def greet(me, offsets):
    barrier = pltpu.get_barrier_semaphore()
    for offset in offsets:
        pl.semaphore_signal(barrier, inc=1, device_id=moved(me, offset), device_id_type=MESH)
    return lambda: pl.semaphore_wait(barrier, len(offsets))


def remote(src, dst, send, recv, slot, to):
    return pltpu.make_async_remote_copy(
        src_ref=src,
        dst_ref=dst,
        send_sem=send.at[slot],
        recv_sem=recv.at[slot],
        device_id=to,
        device_id_type=MESH,
    )


def scatter_plane(me, begun, p_ref, o_ref, far_a, near_a, out_a, sum_a, far_b, near_b, out_b, send, recv):
    half = p_ref.vmem.shape[3] // 2
    lower, upper = pl.ds(0, half), pl.ds(half, half)
    axis = (("y", "z"), ("z", "y"))
    used = [0]

    def go(src, dst, t, which, by):
        to = {axis[t][which]: lax.rem(me[axis[t][which]] + by, 4)}
        item = remote(src, dst, send, recv, used[0], to)
        used[0] += 1
        item.start()
        return item

    def part(t, first, second, hbm=False):
        a = lax.rem(me[axis[t][0]] + first, 4)
        b = lax.rem(me[axis[t][1]] + second, 4)
        ref = p_ref.hbm if hbm else p_ref.get()
        return ref.at[a, b, 0] if t == 0 else ref.at[b, a, 1]

    turns = (2, 1, 3, 0)
    both = (0, 1)
    far, near = {}, {}
    for k, by in enumerate(turns):
        for t in both:
            far[k, t] = (
                go(part(t, 2, by, True).at[lower], far_a.at[t, k, 0], t, 0, 1),
                go(part(t, 2, by, True).at[upper], far_a.at[t, k, 1], t, 0, 3),
            )
    begun()
    for k, by in enumerate(turns):
        for t in both:
            ahead, behind = part(t, 1, by), part(t, 3, by)
            far[k, t][0].wait()
            out_a[t, k, 0, 0:half] = (ahead[0:half].astype(F32) + far_a[t, k, 0].astype(F32)).astype(BF16)
            out_a[t, k, 0, half : 2 * half] = ahead[half : 2 * half]
            first = go(out_a.at[t, k, 0], near_a.at[t, k, 0], t, 0, 1)
            far[k, t][1].wait()
            out_a[t, k, 1, 0:half] = behind[0:half]
            out_a[t, k, 1, half : 2 * half] = (
                behind[half : 2 * half].astype(F32) + far_a[t, k, 1].astype(F32)
            ).astype(BF16)
            near[k, t] = (first, go(out_a.at[t, k, 1], near_a.at[t, k, 1], t, 0, 3))

    def summed(k, t):
        near[k, t][0].wait()
        near[k, t][1].wait()
        return (
            part(t, 0, turns[k])[...].astype(F32)
            + near_a[t, k, 0].astype(F32)
            + near_a[t, k, 1].astype(F32)
        )

    far_two, near_two = {}, {}
    for t in both:
        value = summed(0, t).astype(BF16)
        out_b[t, 0] = value
        far_two[t] = (
            go(out_b.at[t, 0, lower], far_b.at[t, 0], t, 1, 1),
            go(out_b.at[t, 0, upper], far_b.at[t, 1], t, 1, 3),
        )
    for k in (1, 2):
        for t in both:
            sum_a[t, k - 1] = summed(k, t)
    for t in both:
        far_two[t][0].wait()
        out_b[t, 1, 0:half] = (sum_a[t, 0, 0:half] + far_b[t, 0].astype(F32)).astype(BF16)
        out_b[t, 1, half : 2 * half] = sum_a[t, 0, half : 2 * half].astype(BF16)
        first = go(out_b.at[t, 1], near_b.at[t, 0], t, 1, 1)
        far_two[t][1].wait()
        out_b[t, 2, 0:half] = sum_a[t, 1, 0:half].astype(BF16)
        out_b[t, 2, half : 2 * half] = (
            sum_a[t, 1, half : 2 * half] + far_b[t, 1].astype(F32)
        ).astype(BF16)
        near_two[t] = (first, go(out_b.at[t, 2], near_b.at[t, 1], t, 1, 3))
    for t in both:
        value = summed(3, t)
        near_two[t][0].wait()
        near_two[t][1].wait()
        o_ref[t] = value + near_b[t, 0].astype(F32) + near_b[t, 1].astype(F32)


def lane_index(shape):
    return lax.broadcasted_iota(jnp.int32, shape, 1)


def turned(values):
    lane = lane_index(values.shape)
    up = pltpu.roll(values, 32, axis=1)
    down = pltpu.roll(values, 96, axis=1)
    return jnp.where(lane % 64 < 32, -down, up)


def gather_plane(kv_v, kv_hbm, go, me, own_sem, fillers):
    own = pltpu.make_async_copy(kv_v, kv_hbm.at[me["y"], me["z"]], own_sem)
    own.start()
    half = kv_v.shape[1] // 2
    lower, upper = pl.ds(0, half), pl.ds(half, half)
    axis = (("y", "z"), ("z", "y"))
    here = tuple((me[a], me[b]) for a, b in axis)
    step = {"plus": 1, "minus": 3, "far": 2, "own": 0}

    def place(t, a, b):
        return kv_hbm.at[a, b, 0] if t == 0 else kv_hbm.at[b, a, 1]

    def at(t, which, name):
        return lax.rem(here[t][which] + step[name], 4)

    def send_second(t, src, name):
        dst = place(t, at(t, 0, name), here[t][1])
        src = dst if src is None else src
        return (
            go(src, dst, {axis[t][1]: at(t, 1, "plus")}),
            go(src, dst, {axis[t][1]: at(t, 1, "minus")}),
        )

    def pass_on(t, which, a_name, b_name, part, direction):
        ref = place(t, at(t, 0, a_name), at(t, 1, b_name)).at[part]
        return go(ref, ref, {axis[t][which]: at(t, which, direction)})

    def forward_second(t, name, pair):
        pair[0].wait()
        a = pass_on(t, 1, name, "minus", lower, "plus")
        pair[1].wait()
        b = pass_on(t, 1, name, "plus", upper, "minus")
        return [a, b]

    first, second, last = {}, {}, []
    for t in (0, 1):
        dst = place(t, *here[t])
        first[t] = (
            go(kv_v.at[t], dst, {axis[t][0]: at(t, 0, "plus")}),
            go(kv_v.at[t], dst, {axis[t][0]: at(t, 0, "minus")}),
        )
    for t in (0, 1):
        second[t, "own"] = send_second(t, kv_v.at[t], "own")
    fillers[0]()
    far = {}
    for t in (0, 1):
        first[t][0].wait()
        a = pass_on(t, 0, "minus", "own", lower, "plus")
        second[t, "minus"] = send_second(t, None, "minus")
        first[t][1].wait()
        b = pass_on(t, 0, "plus", "own", upper, "minus")
        second[t, "plus"] = send_second(t, None, "plus")
        far[t] = (a, b)
    fillers[1]()
    for t in (0, 1):
        last += forward_second(t, "own", second[t, "own"])
    for t in (0, 1):
        far[t][0].wait()
        far[t][1].wait()
        second[t, "far"] = send_second(t, None, "far")
    fillers[2]()
    for name in ("minus", "plus", "far"):
        for t in (0, 1):
            last += forward_second(t, name, second[t, name])
    return last + [own]


def front_kernel(
    lengths_ref, tok_ref, wq_ref, wk_ref, wv_ref, wo_ref, router_ref, gain_one_ref, gain_two_ref,
    order_ref, routes_ref, expand_ref, expand_t_ref, col_ref, row_ref, turn_high_ref, turn_low_ref,
    q_ref, kv_own_ref, gain_ref, cos_ref, sin_ref, w_out_ref, member_ref, put_ref, take_ref,
    own_aux_ref, order_rows_ref, key_norm_ref, heads_ref, kv_hbm, late_hbm, normed_v, aux_v,
    rows_v, w_v, kv_v, long_v, side_v, w_ref, late_ref, send, recv, local,
):
    me = position(AXES)
    x, y, z, c = (me[axis] for axis in AXES)
    arrived = greet(me, LINE_OFFSETS + PLANE_OFFSETS)
    small = lane_index((8, 128))
    diagonal = lax.broadcasted_iota(jnp.int32, (8, 8), 0) == lane_index((8, 8))

    def column(ref):
        row = jnp.broadcast_to(ref[...].astype(F32), (8, 8))
        return jnp.sum(jnp.where(diagonal, row, 0.0), axis=1, keepdims=True)

    gain_lane = jnp.where(small == 0, column(gain_one_ref), 0.0).astype(BF16)
    for i in range(8):
        span = slice((i // 2) * 128, (i // 2 + 1) * 128)
        key, value = wk_ref[:, span].astype(F32), wv_ref[:, span].astype(F32)
        if i % 2 == 0:
            pair = jnp.where(small < 64, key, pltpu.roll(value, 64, axis=1))
        else:
            pair = jnp.where(small < 64, pltpu.roll(key, 64, axis=1), value)
        w_ref[i, :, 0:128] = wq_ref[:, i * 128 : (i + 1) * 128]
        w_ref[i, :, 128:256] = pair.astype(BF16)
        w_ref[i, :, 256:384] = gain_lane
    side_v[...] = jnp.zeros_like(side_v)
    side_v[:, 0:EXPERTS] = router_ref[...].astype(F32)
    late_ref[:, 0:D] = wo_ref[...]
    late_ref[:, D : D + 128] = jnp.where(small == EXPERTS, column(gain_two_ref), side_v[...]).astype(BF16)
    arrived()
    plus, minus, far = lax.rem(x + 1, 4), lax.rem(x + 3, 4), lax.rem(x + 2, 4)
    other = 1 - c
    lower, upper = pl.ds(0, 64), pl.ds(64, 64)
    used = [0]

    def go(src, dst, to):
        item = remote(src, dst, send, recv, used[0], to)
        used[0] += 1
        item.start()
        return item

    def keep(src, dst, slot):
        item = pltpu.make_async_copy(src, dst, local.at[slot])
        item.start()
        return item

    own = [
        keep(w_ref.at[x * 2 + c], w_v.at[x, y, z, c], 0),
        keep(late_ref, late_hbm.at[x, y, z, c], 1),
    ]
    own_rows = keep(tok_ref, rows_v.at[c, x], 2)
    first_w = []
    for offset in LINE_OFFSETS:
        to = moved(me, offset)
        first_w.append(go(w_ref.at[to["x"] * 2 + to["c"]], w_v.at[x, y, z, c], to))
    to_plus = go(tok_ref, rows_v.at[c, x], {"x": plus})
    to_minus = go(tok_ref, rows_v.at[c, x], {"x": minus})
    sides = [go(tok_ref, rows_v.at[c, x], {"c": other})]

    for item in own + first_w:
        item.wait()
    second_w = [go(w_v.at[:, y, z], w_v.at[:, y, z], moved(me, by)) for by in PLANE_OFFSETS]
    first_late = [go(late_ref, late_hbm.at[x, y, z, c], moved(me, by)) for by in PLANE_OFFSETS]

    chip = y * 4 + z
    mine = order_ref[pl.ds(pl.multiple_of(chip * 8, 8), 8), :]
    ends, total = [], jnp.int32(0)
    for i in range(NSEQ):
        total = total + lengths_ref[i]
        ends.append(total)
    place = mine
    for i in range(NSEQ):
        place = place - jnp.where(mine >= ends[i], lengths_ref[i], 0)
    lane = lane_index((ROWS, 128))

    def table(ref, picked):
        return mm(picked, ref[0]) + mm(picked, ref[1]) + mm(picked, ref[2])

    for i in range(8):
        wide = jnp.broadcast_to(place[i : i + 1, :].astype(F32), (ROWS, 128)).T.astype(jnp.int32)
        high = table(turn_high_ref, jnp.where(lane == lax.shift_right_logical(wide, 7), 1.0, 0.0).astype(BF16))
        low = table(turn_low_ref, jnp.where(lane == (wide & 127), 1.0, 0.0).astype(BF16))
        cos_ref[pl.ds(i * 128, 128), :] = high[:, :128] * low[:, :128] - high[:, 128:] * low[:, 128:]
        sin_ref[pl.ds(i * 128, 128), :] = high[:, 128:] * low[:, :128] + high[:, :128] * low[:, 128:]
    heads_ref[...] = order_ref[pl.ds(0, 32, stride=4), :]
    order_rows_ref[...] = mine.astype(F32)

    to_plus.wait()
    next_plus = go(rows_v.at[c, minus, lower], rows_v.at[c, minus, lower], {"x": plus})
    sides.append(go(rows_v.at[c, minus], rows_v.at[c, minus], {"c": other}))
    to_minus.wait()
    next_minus = go(rows_v.at[c, plus, upper], rows_v.at[c, plus, upper], {"x": minus})
    sides.append(go(rows_v.at[c, plus], rows_v.at[c, plus], {"c": other}))
    next_plus.wait()
    next_minus.wait()
    sides.append(go(rows_v.at[c, far], rows_v.at[c, far], {"c": other}))
    own_rows.wait()
    for item in second_w:
        item.wait()
    weights = w_v[...].astype(F32).reshape(D, 384)
    w_out_ref[...] = weights.astype(BF16)
    gain = weights[:, 256:384].T[0:1, :]
    gain_ref[...] = jnp.broadcast_to(gain, (8, D))
    low_lanes = lane_index((256, 128)) < 64

    def project(block):
        longest = jnp.zeros((256, 1), F32)
        for i in range(2):
            rows = pl.ds(pl.multiple_of(block * 512 + i * 256, 256), 256)
            tok = rows_v[block, pl.ds(2 * i, 2)].astype(F32).reshape(256, D)
            scale = lax.rsqrt(jnp.mean(tok * tok, axis=-1, keepdims=True) + EPSILON)
            normed = (tok * scale * gain).astype(BF16)
            normed_v[rows, :] = normed
            pre = mm(normed, w_out_ref[:, 0:256])
            cos, sin = cos_ref[rows, :], sin_ref[rows, :]
            q_pre, kv_pre = pre[:, :128], pre[:, 128:]
            query = (q_pre * cos + turned(q_pre) * sin).astype(BF16).astype(F32) * 0.125
            q_ref[0, rows, :] = jnp.where(low_lanes, query, 0.0).astype(BF16)
            q_ref[1, rows, :] = jnp.where(low_lanes, pltpu.roll(query, 64, axis=1), 0.0).astype(BF16)
            key = kv_pre * cos + turned(kv_pre) * sin
            kv = jnp.where(low_lanes, key, kv_pre).astype(BF16)
            kv_own_ref[rows, :] = kv
            kv_v[block, pl.ds(i * 256, 256), :] = kv
            rounded = kv.astype(F32)
            square = jnp.sum(jnp.where(low_lanes, rounded * rounded, 0.0), axis=1, keepdims=True)
            longest = jnp.maximum(longest, square)
        return jnp.max(longest, axis=0, keepdims=True)

    longest = project(c)
    for item in sides:
        item.wait()
    longest = jnp.maximum(longest, project(other))
    long_v[chip] = jnp.broadcast_to(longest, (8, 128))
    longs = [go(long_v.at[chip], long_v.at[chip], moved(me, by)) for by in PLANE_OFFSETS]
    stores = []
    for item in (q_ref, kv_own_ref, cos_ref, sin_ref, w_out_ref, normed_v):
        item.store()

    def routing():
        routes = jnp.concatenate([routes_ref[...].astype(F32), jnp.full((120, 128), -1.0, F32)], axis=0).T
        member = jnp.zeros((ROWS, 128), F32)
        for choice in range(8):
            member += jnp.where(routes[:, choice : choice + 1].astype(jnp.int32) == lane, 1.0, 0.0)
        below = lax.broadcasted_iota(jnp.int32, (ROWS, ROWS), 0) > lane_index((ROWS, ROWS))
        earlier = mm(jnp.where(below, 1.0, 0.0).astype(BF16), member.astype(BF16))
        slot = jnp.where(member > 0.5, earlier, -1.0).astype(BF16)
        member_ref[...] = member
        take = jnp.where(mm(slot, expand_ref[...]) == row_ref[...], 1.0, 0.0)
        take_ref[...] = take.astype(BF16)
        put = jnp.where(mm(expand_t_ref[...], slot, NT) == col_ref[...].astype(F32), 1.0, 0.0)
        put = put.astype(BF16)
        put_ref[...] = put
        for item in (put_ref, take_ref):
            item.store()

    def segments():
        sub = lax.broadcasted_iota(jnp.int32, (8, 128), 0)
        begin = jnp.zeros((8, 128), jnp.int32)
        end = jnp.full((8, 128), TOKENS, jnp.int32)
        for i in range(NSEQ):
            begin = jnp.where(sub == 3 + i, ends[i] - lengths_ref[i], begin)
            end = jnp.where(sub == 3 + i, ends[i], end)
        spot = jnp.where(sub == lane_index((8, 128)), 1.0, 0.0).astype(BF16)

        def block(step, carry):
            rows = order_ref[pl.ds(pl.multiple_of(step * 8, 8), 8), :]
            for i in range(8):
                order = jnp.broadcast_to(rows[i : i + 1, :], (8, 128))
                within = jnp.where((order >= begin) & (order < end), 1.0, 0.0).astype(BF16)
                here = pl.ds(pl.multiple_of(step * 1024 + i * 128, 128), 128)
                aux_v[here, :] = mm(within, spot, TN).astype(BF16)
            return carry

        lax.fori_loop(0, 16, block, 0)
        aux_v.store()
        own_aux_ref[...] = aux_v[pl.ds(pl.multiple_of(chip * CHIP_ROWS, CHIP_ROWS), CHIP_ROWS), :]
        own_aux_ref.store()

    def late():
        for item in second_late:
            item.wait()
        stores.append(go(late_hbm.at[:, :, :, c], late_hbm.at[:, :, :, c], {"c": other}))

    for item in first_late:
        item.wait()
    second_late = [
        go(late_hbm.at[x, :, :, c], late_hbm.at[x, :, :, c], {"x": to}) for to in (far, plus, minus)
    ]

    last = gather_plane(kv_v, kv_hbm, go, me, local.at[3], (routing, segments, late))
    for item in longs:
        item.wait()
    longest = long_v[0]
    for i in range(1, 16):
        longest = jnp.maximum(longest, long_v[i])
    key_norm_ref[...] = jnp.sqrt(longest)
    for item in last + stores:
        item.wait()


def front(inputs, cid):
    count = 7 + 3 + 3 + 15 + 15 + 2 + 3 + 40 + 1 + 15
    return remote_call(
        front_kernel,
        inputs,
        ("s", "h") + ("v",) * 9 + ("l",) * 6,
        [
            shape((2, CHIP_ROWS, 128), BF16),
            shape((CHIP_ROWS, 128), BF16),
            shape((8, D), F32),
            shape((CHIP_ROWS, 128), F32),
            shape((CHIP_ROWS, 128), F32),
            shape((D, 384), BF16),
            shape((ROWS, 128), F32),
            shape((SLOTS, ROWS), BF16),
            shape((ROWS, SLOTS), BF16),
            shape((CHIP_ROWS, 128), BF16),
            shape((8, 128), F32),
            shape((8, 128), F32),
            shape((32, 128), jnp.int32),
            shape((4, 4, 2, 512, 128), BF16),
            shape((4, 4, 4, 2, 8, 1152), BF16),
            shape((CHIP_ROWS, D), BF16),
            shape((TOKENS, 128), BF16),
        ],
        ("e", "e", "v", "e", "e", "e", "v", "e", "e", "e", "v", "v", "v", "h", "h", "e", "e"),
        [
            pltpu.VMEM((2, 4, ROWS, D), BF16),
            pltpu.VMEM((4, 4, 4, 2, 8, 384), BF16),
            pltpu.VMEM((2, 512, 128), BF16),
            pltpu.VMEM((16, 8, 128), F32),
            pltpu.VMEM((8, 128), F32),
            pltpu.VMEM((8, 8, 384), BF16),
            pltpu.VMEM((8, 1152), BF16),
            pltpu.SemaphoreType.DMA((count,)),
            pltpu.SemaphoreType.DMA((count,)),
            pltpu.SemaphoreType.DMA((4,)),
        ],
        cid,
    )


def turn_tables(step):
    frequency = (np.float32(ROPE_BASE) ** (-np.arange(32, dtype=np.float32) / np.float32(32))).astype(np.float64)
    angles = (np.arange(128) * step)[:, None] * np.tile(frequency, 4)[None, :]
    rest = np.concatenate([np.cos(angles), np.sin(angles)], axis=1)
    parts = []
    for _ in range(3):
        part = rest.astype(np.float32).astype(ml_dtypes.bfloat16)
        parts.append(part)
        rest = rest - part.astype(np.float64)
    return jnp.asarray(np.stack(parts))


def order_pair(order_ref, index):
    row = jnp.concatenate([order_ref[pl.ds(2 * index, 1), :], order_ref[pl.ds(2 * index + 1, 1), :]], axis=1)
    row = jnp.broadcast_to(row, (RUN, RUN))
    return row, row.T


WIDE = 6
WIDE_BACK = 3


def run_lists(order_ref, base, first_ref):
    def note(block, carry):
        run = lax.shift_right_logical(order_ref[block, 0], 8)
        first_ref[run] = block * 512
        first_ref[63 - run] = block * 512 + RUN
        return carry

    lax.fori_loop(0, 32, note, 0)

    def count(part):
        run = lax.shift_right_logical(order_ref[lax.div(base, 512) + lax.div(part, 2), 0], 8)
        return jnp.where(lax.rem(part, 2) == 0, run, 31 - run)

    return count


def group_places(first_ref, number, half, step, wide):
    places = []
    for i in range(wide):
        index = step * wide + i
        at = jnp.where(index < number, half + index, 32 - half)
        places.append(pl.ds(pl.multiple_of(first_ref[at], RUN), RUN))
    return places


def attend_kernel(
    order_smem, base_ref, kv_hbm, aux_hbm, own_kv_ref, own_aux_ref, q_ref, order_ref, key_norm_ref,
    att_ref, norm_ref, sent_ref, qx_ref, kv_ref, aux_ref, acc_ref, first_ref, loads,
):
    copies = [
        pltpu.make_async_copy(kv_hbm, kv_ref, loads.at[0]),
        pltpu.make_async_copy(aux_hbm, aux_ref, loads.at[1]),
    ]
    for item in copies:
        item.start()
    count = run_lists(order_smem, base_ref[0], first_ref)
    key_norm = key_norm_ref[0:1, 0:1]
    lane = lane_index((RUN, 128))

    def right(keys):
        turned_keys = keys.T
        row = lax.broadcasted_iota(jnp.int32, turned_keys.shape, 0)
        return jnp.where(row < 64, jnp.ones_like(turned_keys), turned_keys)[56:]

    def prepare(part, carry):
        rows = pl.ds(pl.multiple_of(part * RUN, RUN), RUN)
        own_aux = own_aux_ref[rows, :]
        spread = jnp.where(lane < 3 + NSEQ, (own_aux.astype(F32) - 1.0) * FAR, 0.0)
        for head in range(2):
            query = q_ref[head, rows, :]
            wide = query.astype(F32)
            shift = jnp.ceil(jnp.sqrt(jnp.sum(wide * wide, axis=1, keepdims=True)) * key_norm)
            top = shift.astype(BF16).astype(F32)
            middle = (shift - top).astype(BF16).astype(F32)
            rest = shift - top - middle
            ext = jnp.where(lane == 0, -top, spread)
            ext = jnp.where(lane == 1, -middle, ext)
            ext = jnp.where(lane == 2, -rest, ext)
            here = pl.ds(head * RUN, RUN)
            qx_ref[part, here, 0:128] = query
            qx_ref[part, here, 128:256] = ext.astype(BF16)
        order_key, order_query = order_pair(order_ref, part)
        allowed = order_query <= order_key
        keys = own_kv_ref[rows, :]
        e = jnp.exp(mm(jnp.concatenate([keys, own_aux], axis=1), qx_ref[part], NT))
        e = jnp.where(jnp.concatenate([allowed, allowed], axis=1), e, 0.0)
        acc_ref[part] = mm(right(keys), e.astype(BF16))
        return carry

    lax.fori_loop(0, 4, prepare, 0)
    for item in copies:
        item.wait()

    def part_step(part, carry):
        number = count(part)
        half = lax.rem(part, 2) * 32

        def group(step, carry):
            places = group_places(first_ref, number, half, step, WIDE)
            keys = jnp.concatenate([kv_ref[here, :] for here in places], axis=0)
            aux = jnp.concatenate([aux_ref[here, :] for here in places], axis=0)
            e = jnp.exp(mm(jnp.concatenate([keys, aux], axis=1), qx_ref[part], NT))
            acc_ref[part] += mm(right(keys), e.astype(BF16))
            return carry

        lax.fori_loop(0, lax.div(number + WIDE - 1, WIDE), group, 0)
        rows = pl.ds(pl.multiple_of(part * RUN, RUN), RUN)
        total = acc_ref[part]
        value = total[8:72] / total[0:1]
        att = jnp.concatenate([value[:, :RUN], value[:, RUN:]], axis=0).T
        norm = jnp.broadcast_to(total[0:1], (64, 2 * RUN))
        norm = jnp.concatenate([norm[:, :RUN], norm[:, RUN:]], axis=0).T
        att_ref[rows, :] = att
        norm_ref[rows, :] = norm
        sent_ref[rows, :] = att.astype(BF16)
        return carry

    lax.fori_loop(0, 4, part_step, 0)


def attend(order, base, kv, aux, own_kv, own_aux, query, order_rows, key_norm):
    smem = pl.BlockSpec(memory_space=pltpu.SMEM)
    vmem = pl.BlockSpec(memory_space=pltpu.VMEM)
    hbm = pl.BlockSpec(memory_space=pl.ANY)
    return local_call(
        attend_kernel,
        (
            shape((CHIP_ROWS, 128), F32),
            shape((CHIP_ROWS, 128), F32),
            shape((CHIP_ROWS, 128), BF16),
            shape((4, 2 * RUN, 256), BF16),
        ),
        scratch=[
            pltpu.VMEM((TOKENS, 128), BF16),
            pltpu.VMEM((TOKENS, 128), BF16),
            pltpu.VMEM((4, 72, 2 * RUN), F32),
            pltpu.SMEM((64,), jnp.int32),
            pltpu.SemaphoreType.DMA((2,)),
        ],
        in_specs=[smem] * 2 + [hbm] * 2 + [vmem] * 5,
    )(order, base, kv, aux, own_kv, own_aux, query, order_rows, key_norm)


def attend_back_kernel(
    order_smem, base_ref, kv_hbm, aux_hbm, own_kv_ref, own_aux_ref, qx_ref, order_ref,
    gsent_ref, att_ref, norm_ref, dq_ref, dkv_hbm,
    kv_ref, aux_ref, acc_ref, dq_acc, gx_ref, rhs_ref, out_ref, first_ref, loads, stores,
):
    copies = [
        pltpu.make_async_copy(kv_hbm, kv_ref, loads.at[0]),
        pltpu.make_async_copy(aux_hbm, aux_ref, loads.at[1]),
    ]
    for item in copies:
        item.start()
    own_base = base_ref[0]
    count = run_lists(order_smem, own_base, first_ref)

    def clear(step, carry):
        acc_ref[pl.ds(pl.multiple_of(step * 512, 512), 512), :] = jnp.zeros((512, 128), F32)
        return carry

    lax.fori_loop(0, TOKENS // 512, clear, 0)
    lane = lane_index((RUN, 128))
    low_lanes = lane < 64

    def apply(part, here, e, prob):
        ds = (e * prob).astype(BF16)
        left = jnp.concatenate([ds, e.astype(BF16)], axis=1)
        acc_ref[here, :] += mm(left, rhs_ref[part])
        return ds

    def scores(part, keys, aux):
        both = jnp.concatenate([keys, aux], axis=1)
        return mm(both, qx_ref[part], NT), mm(both, gx_ref[part], NT)

    def prepare(part, carry):
        rows = pl.ds(pl.multiple_of(part * RUN, RUN), RUN)
        gsent = gsent_ref[rows, :].astype(F32)
        norm = norm_ref[rows, :]
        product = gsent * att_ref[rows, :] / norm
        scaled = (gsent / norm).astype(BF16).astype(F32)
        for head in range(2):
            mask = low_lanes if head == 0 else jnp.logical_not(low_lanes)
            delta = jnp.sum(jnp.where(mask, product, 0.0), axis=1, keepdims=True)
            top = delta.astype(BF16).astype(F32)
            middle = (delta - top).astype(BF16).astype(F32)
            rest = delta - top - middle
            ext = jnp.where(lane == 0, -top, 0.0)
            ext = jnp.where(lane == 1, -middle, ext)
            ext = jnp.where(lane == 2, -rest, ext)
            grad = pltpu.roll(scaled, 64, axis=1) if head == 0 else scaled
            grad = jnp.where(low_lanes, 0.0, grad).astype(BF16)
            here = pl.ds(head * RUN, RUN)
            gx_ref[part, here, 0:128] = grad
            gx_ref[part, here, 128:256] = ext.astype(BF16)
            rhs_ref[part, pl.ds(head * RUN, RUN), :] = qx_ref[part, here, 0:128]
            rhs_ref[part, pl.ds((2 + head) * RUN, RUN), :] = grad
        order_key, order_query = order_pair(order_ref, part)
        allowed = order_query <= order_key
        keys = own_kv_ref[rows, :]
        score, prob = scores(part, keys, own_aux_ref[rows, :])
        e = jnp.where(jnp.concatenate([allowed, allowed], axis=1), jnp.exp(score), 0.0)
        own = pl.ds(pl.multiple_of(own_base + part * RUN, RUN), RUN)
        dq_acc[part] = mm(keys.T[:64], apply(part, own, e, prob))
        return carry

    lax.fori_loop(0, 4, prepare, 0)
    for item in copies:
        item.wait()

    def part_step(part, carry):
        number = count(part)
        half = lax.rem(part, 2) * 32

        def group(step, carry):
            places = group_places(first_ref, number, half, step, WIDE_BACK)
            parts = [scores(part, kv_ref[here, :], aux_ref[here, :]) for here in places]
            ds = [
                apply(part, here, jnp.exp(score), prob)
                for here, (score, prob) in zip(places, parts)
            ]
            keys = jnp.concatenate([kv_ref[here, :] for here in places], axis=0)
            dq_acc[part] += mm(keys.T[:64], jnp.concatenate(ds, axis=0))
            return carry

        lax.fori_loop(0, lax.div(number + WIDE_BACK - 1, WIDE_BACK), group, 0)
        rows = pl.ds(pl.multiple_of(part * RUN, RUN), RUN)
        total = dq_acc[part] * 0.125
        dq_ref[rows, :] = jnp.concatenate([total[:, :RUN], total[:, RUN:]], axis=0).T
        return carry

    lax.fori_loop(0, 4, part_step, 0)

    def store(step):
        rows = pl.ds(pl.multiple_of(step * 2048, 2048), 2048)
        return pltpu.make_async_copy(out_ref.at[rows], dkv_hbm.at[rows], stores.at[step])

    def narrow(step, carry):
        rows = pl.ds(pl.multiple_of(step * 2048, 2048), 2048)
        out_ref[rows, :] = acc_ref[rows, :].astype(BF16)
        store(step).start()
        return carry

    def settle(step, carry):
        store(step).wait()
        return carry

    lax.fori_loop(0, 8, narrow, 0)
    lax.fori_loop(0, 8, settle, 0)


def attend_back(order, base, kv, aux, own_kv, own_aux, query_ext, order_rows, gsent, att, norm):
    smem = pl.BlockSpec(memory_space=pltpu.SMEM)
    vmem = pl.BlockSpec(memory_space=pltpu.VMEM)
    hbm = pl.BlockSpec(memory_space=pl.ANY)
    return local_call(
        attend_back_kernel,
        (shape((CHIP_ROWS, 128), F32), shape((TOKENS, 128), BF16)),
        scratch=[
            pltpu.VMEM((TOKENS, 128), BF16),
            pltpu.VMEM((TOKENS, 128), BF16),
            pltpu.VMEM((TOKENS, 128), F32),
            pltpu.VMEM((4, 64, 2 * RUN), F32),
            pltpu.VMEM((4, 2 * RUN, 256), BF16),
            pltpu.VMEM((4, 4 * RUN, 128), BF16),
            pltpu.VMEM((TOKENS, 128), BF16),
            pltpu.SMEM((64,), jnp.int32),
            pltpu.SemaphoreType.DMA((2,)),
            pltpu.SemaphoreType.DMA((8,)),
        ],
        in_specs=[smem] * 2 + [hbm] * 2 + [vmem] * 7,
        out_specs=[vmem, hbm],
    )(order, base, kv, aux, own_kv, own_aux, query_ext, order_rows, gsent, att, norm)


SLOT_EXPERT = np.arange(SLOTS) // SLOT
SLOT_PLACE = np.arange(SLOTS) % SLOT


def constant(array):
    return jnp.asarray(np.asarray(array).astype(ml_dtypes.bfloat16))


def expand_matrix():
    return constant(np.arange(128)[:, None] == SLOT_EXPERT[None, :])


def place_matrix():
    return constant(SLOT_PLACE[:, None] == np.arange(128)[None, :])


def origin_matrix():
    return constant((np.arange(8 * SLOT) // SLOT)[:, None] == np.arange(128)[None, :])


def place_column():
    used = np.where(SLOT_PLACE < CAP, SLOT_PLACE, -5)
    return constant(np.broadcast_to(used[:, None], (SLOTS, 128)))


def place_row():
    used = np.where(SLOT_PLACE < CAP, SLOT_PLACE, -5)
    return jnp.asarray(used[None, :].astype(np.float32))


BLOCK = 8 * SLOT


def packed_pairs(values):
    total = sum(int(value) << (2 * i) for i, value in enumerate(values))
    return np.uint32(total).astype(np.int32)


STEP_Y = packed_pairs([dy for dy, _ in PLANE_ORDER])
STEP_Z = packed_pairs([dz for _, dz in PLANE_ORDER])


def moe_kernel(
    sent_ref, tok_ref, w_out_ref, router_ref, member_ref, put_ref, take_ref, expand_ref,
    expand_t_ref, place_ref, place_t_ref, origin_ref, block_place_ref, cot_ref, cots_hbm, gate_hbm, up_hbm, down_hbm,
    residual_ref, weigh_high_ref, weigh_low_ref, gmid_ref, branch_ref, gsent_in, side_in,
    y_hbm, grads_hbm,
    sent_in, x_out, x_in, y_v, back_out, back_in, gate_v, up_v, down_v,
    sum_gate, sum_up, sum_down, grads_v, mixed_v, gate_probs, gsent_out, side_out, cots_v,
    note_out, note_in, answer_out, answer_in,
    x_send, x_recv, back_send, back_recv, note_send, note_recv, answer_send, answer_recv,
    line_send, line_recv, local,
):
    me = position(AXES)
    x_at, y_at, z_at, c_at = (me[axis] for axis in AXES)
    expert = (y_at * 4 + z_at) * 2 + c_at

    def offset(k):
        pair = lax.div(k, 2)
        dy = lax.shift_right_logical(jnp.int32(STEP_Y), 2 * pair) & 3
        dz = lax.shift_right_logical(jnp.int32(STEP_Z), 2 * pair) & 3
        return dy, dz, lax.rem(k + pair, 2)

    def toward(k):
        dy, dz, dc = offset(k)
        return {"y": lax.rem(y_at + dy, 4), "z": lax.rem(z_at + dz, 4), "c": lax.rem(c_at + dc, 2)}

    def source(k):
        dy, dz, dc = offset(k)
        return {
            "y": lax.rem(y_at + 4 - dy, 4),
            "z": lax.rem(z_at + 4 - dz, 4),
            "c": lax.rem(c_at + dc, 2),
        }

    def number(at):
        return (at["y"] * 4 + at["z"]) * 2 + at["c"]

    loads = [
        pltpu.make_async_copy(src, dst, local.at[i])
        for i, (src, dst) in enumerate(
            ((cots_hbm, cots_v), (gate_hbm, gate_v), (up_hbm, up_v), (down_hbm, down_v))
        )
    ]
    barrier = pltpu.get_barrier_semaphore()
    for by in LINE_OFFSETS:
        pl.semaphore_signal(barrier, inc=1, device_id=moved(me, by), device_id_type=MESH)

    def hello(k, carry):
        pl.semaphore_signal(barrier, inc=1, device_id=toward(k), device_id_type=MESH)
        return carry

    lax.fori_loop(0, 31, hello, 0)
    sum_gate[...] = jnp.zeros_like(sum_gate)
    sum_up[...] = jnp.zeros_like(sum_up)
    sum_down[...] = jnp.zeros_like(sum_down)
    pl.semaphore_wait(barrier, 31 + len(LINE_OFFSETS))

    here_line = x_at * 2 + c_at
    moves = []
    for i, by in enumerate(LINE_OFFSETS):
        to = moved(me, by)
        moves.append(
            remote(sent_ref.at[to["c"] * 4 + to["x"]], sent_in.at[here_line], line_send, line_recv, i, to)
        )
        moves[-1].start()
    kept = pltpu.make_async_copy(sent_ref.at[c_at * 4 + x_at], sent_in.at[here_line], local.at[4])
    kept.start()
    for item in loads:
        item.start()
    for item in moves + [kept]:
        item.wait()
    sent = jnp.concatenate([sent_in[i] for i in range(8)], axis=1)
    residual = tok_ref[...].astype(F32) + mm(sent, w_out_ref[...])
    residual_ref[...] = residual
    residual_ref.store()
    gain = router_ref[...].astype(F32).T[EXPERTS : EXPERTS + 1, :]
    scale = lax.rsqrt(jnp.mean(residual * residual, axis=-1, keepdims=True) + EPSILON)
    mixed = (residual * scale * gain).astype(BF16)
    mixed_v[...] = mixed
    put = put_ref[...]

    def tiles(value):
        return value.reshape(8, SLOT, 8, 128).astype(BF16)

    def rows_of(value):
        return value.astype(F32).reshape(value.shape[0] * SLOT, D).astype(BF16)

    for i in range(4):
        x_out[i * 8 : (i + 1) * 8] = tiles(mm(put[i * BLOCK : (i + 1) * BLOCK], mixed))

    def x_copy(k):
        to = toward(k)
        return remote(x_out.at[number(to)], x_in.at[k], x_send, x_recv, k, to)

    def note_copy(k):
        to = toward(k)
        return remote(note_out.at[number(to)], note_in.at[k], note_send, note_recv, k, to)

    def x_start(k, carry):
        x_copy(k).start()
        return carry

    lax.fori_loop(0, 8, x_start, 0)
    kept = pltpu.make_async_copy(x_out.at[expert], x_in.at[31], local.at[4])
    kept.start()
    logits = mm(mixed, router_ref[...])
    member = member_ref[...]
    masked = jnp.where(member > 0.5, logits, -FAR)
    top = jnp.max(masked, axis=1, keepdims=True)
    power = jnp.where(member > 0.5, jnp.exp(masked - top), 0.0)
    gate = power / jnp.sum(power, axis=1, keepdims=True)
    gate_probs[...] = gate
    gate_high, gate_low = halves(gate)
    spread = mm(gate_high, expand_ref[...]) + mm(gate_low, expand_ref[...])
    weigh = take_ref[...].astype(F32) * spread
    weigh_high, weigh_low = halves(weigh)
    weigh_high_ref[...] = weigh_high
    weigh_low_ref[...] = weigh_low
    weigh_high_ref.store()
    weigh_low_ref.store()
    wide_expand = expand_ref[...].astype(F32)
    rows_high, rows_low = halves(wide_expand * jnp.sum(weigh, axis=0, keepdims=True))
    gates = mm(rows_high, place_ref[...]) + mm(rows_low, place_ref[...])
    token = lax.broadcasted_iota(jnp.int32, (ROWS, SLOTS), 0).astype(F32)
    token = jnp.sum(take_ref[...].astype(F32) * token, axis=0, keepdims=True)
    token = mm((wide_expand * token).astype(BF16), place_ref[...])
    top_row = lax.broadcasted_iota(jnp.int32, (8, 128), 0) == 0
    for i in range(EXPERTS):
        note_out[i] = jnp.where(
            top_row,
            jnp.broadcast_to(gates[i : i + 1], (8, 128)),
            jnp.broadcast_to(token[i : i + 1], (8, 128)),
        )

    def note_start(k, carry):
        note_copy(k).start()
        return carry

    lax.fori_loop(0, 31, note_start, 0)
    lax.fori_loop(8, 31, x_start, 0)
    note_in[31] = note_out[expert]
    kept.wait()
    for item in loads:
        item.wait()

    def cot_of(at):
        return cots_v[number(at)]

    block_row = lax.broadcasted_iota(jnp.int32, (BLOCK, 1), 0)
    block_start = jnp.zeros((BLOCK, 1), F32)
    for i in range(1, 8):
        block_start += jnp.where(block_row >= i * SLOT, 128.0, 0.0)
    origin_ref.get()
    block_place_ref.get()

    def answer_copy(k):
        return remote(answer_out.at[k], answer_in.at[expert], answer_send, answer_recv, k, source(k))

    def back_copy(k):
        to = source(k)
        return remote(back_out.at[k], back_in.at[expert], back_send, back_recv, k, to)

    def back_kept():
        return pltpu.make_async_copy(back_out.at[31], back_in.at[expert], local.at[4])

    def group(step, carry):
        first = step * 8
        for i in range(8):
            k = first + i

            @pl.when(k < 31)
            def _():
                x_copy(k).wait_recv()
                note_copy(k).wait_recv()

        x = rows_of(x_in[pl.ds(first, 8)])
        origin, place = origin_ref[...], block_place_ref[...].astype(F32)
        blank = jnp.zeros((120, 128), F32)
        gates = [note_in[first + i][0:1] for i in range(8)]
        gates_high, gates_low = halves(jnp.concatenate(gates + [blank], axis=0))
        share = mm(origin, gates_high) + mm(origin, gates_low)
        share = jnp.sum(share * place, axis=1, keepdims=True)
        tokens = [note_in[first + i][1:2] for i in range(8)]
        row = mm(origin, jnp.concatenate(tokens + [blank], axis=0).astype(BF16))
        row = jnp.sum(row * place, axis=1, keepdims=True) + block_start
        chosen = jnp.where(lane_index((BLOCK, D)).astype(F32) == row, 1.0, 0.0).astype(BF16)
        g = mm(chosen, jnp.concatenate([cot_of(source(first + i)) for i in range(8)], axis=0))
        a = mm(x, gate_v[...])
        b = mm(x, up_v[...])
        s = 1.0 / (1.0 + jnp.exp(-a))
        silu = a * s
        hidden = (silu * b).astype(BF16)
        y = mm(hidden, down_v[...]).astype(BF16).astype(F32)
        dgate = jnp.sum(y * g, axis=1, keepdims=True)
        dgate_high, dgate_low = halves(dgate * place)
        answers = mm(origin, dgate_high, TN) + mm(origin, dgate_low, TN)
        for i in range(8):
            k = first + i
            answer_out[k] = jnp.broadcast_to(answers[i : i + 1], (8, 128))

            @pl.when(k < 31)
            def _():
                answer_copy(k).start()

        y = tiles(y)
        for i in range(8):
            y_v[number(source(first + i))] = y[i]
        gy = (g * share).astype(BF16)
        dhidden = mm(gy, down_v[...], NT)
        da = (dhidden * b * (s * (1.0 + a * (1.0 - s)))).astype(BF16)
        db = (dhidden * silu).astype(BF16)
        back = mm(da, gate_v[...], NT) + mm(db, up_v[...], NT)
        back_out[pl.ds(first, 8)] = tiles(back)
        for i in range(8):
            k = first + i

            @pl.when(k < 31)
            def _():
                back_copy(k).start()

            @pl.when(k == 31)
            def _():
                back_kept().start()

        sum_gate[...] += mm(x, da, TN)
        sum_up[...] += mm(x, db, TN)
        sum_down[...] += mm(hidden, gy, TN)
        return carry

    lax.fori_loop(0, 4, group, 0)
    answer_in[expert] = answer_out[31]
    for i in range(4):
        grads_v[i * 768 : i * 768 + 256] = sum_gate[i * 256 : (i + 1) * 256].astype(BF16)
        grads_v[i * 768 + 256 : i * 768 + 512] = sum_up[i * 256 : (i + 1) * 256].astype(BF16)
        down = sum_down[i * 128 : (i + 1) * 128].astype(BF16)
        grads_v[i * 768 + 512 : i * 768 + 640] = down[:, 0:FF]
        grads_v[i * 768 + 640 : i * 768 + 768] = down[:, FF:D]
    stores = [
        pltpu.make_async_copy(src, dst, local.at[i])
        for i, (src, dst) in enumerate(((y_v, y_hbm), (grads_v, grads_hbm)))
    ]
    for item in stores:
        item.start()

    def answers(k, carry):
        answer_copy(k).wait()
        return carry

    lax.fori_loop(0, 31, answers, 0)
    take = take_ref[...]
    rows_high, rows_low = halves(
        jnp.concatenate([answer_in[i][0:1] for i in range(EXPERTS)] + [jnp.zeros((96, 128), F32)], axis=0)
    )
    spread = mm(rows_high, place_t_ref[...]) + mm(rows_low, place_t_ref[...])
    along = jnp.sum(spread * expand_ref[...].astype(F32), axis=0, keepdims=True)
    found_high, found_low = halves(take.astype(F32) * along)
    dgate = mm(found_high, expand_t_ref[...]) + mm(found_low, expand_t_ref[...])
    gate = gate_probs[...]
    dlogits = gate * (dgate - jnp.sum(gate * dgate, axis=1, keepdims=True))
    dlogits = dlogits.astype(BF16)
    dmixed = mm(dlogits, router_ref[...], NT)

    def settle(k, carry):
        x_copy(k).wait_send()
        note_copy(k).wait_send()
        back_copy(k).wait()
        return carry

    lax.fori_loop(0, 31, settle, 0)
    back_kept().wait()

    dmixed += mm(take, rows_of(back_in[...]))
    residual = residual_ref[...]
    scale = lax.rsqrt(jnp.mean(residual * residual, axis=-1, keepdims=True) + EPSILON)
    gain = router_ref[...].astype(F32).T[EXPERTS : EXPERTS + 1, :]
    weighted = dmixed * gain
    inner = jnp.mean(weighted * residual, axis=-1, keepdims=True)
    gmid = cot_ref[...].astype(F32) + scale * weighted - residual * (scale * scale * scale) * inner
    gmid_ref[...] = gmid
    gmid_ref.store()
    branch = gmid.astype(BF16)
    branch_ref[...] = branch
    branch_ref.store()
    gsent = mm(branch, w_out_ref[...], NT).astype(BF16)
    for i in range(8):
        gsent_out[i] = gsent[:, i * 128 : (i + 1) * 128]
    back_line = c_at * 4 + x_at
    moves = []
    for i, by in enumerate(LINE_OFFSETS):
        to = moved(me, by)
        moves.append(
            remote(
                gsent_out.at[to["x"] * 2 + to["c"]], gsent_in.at[back_line], line_send, line_recv, 7 + i, to
            )
        )
        moves[-1].start()
    kept = pltpu.make_async_copy(gsent_out.at[here_line], gsent_in.at[back_line], local.at[4])
    kept.start()
    moves.append(kept)
    gain_grad = jnp.sum(dmixed * residual * scale, axis=0, keepdims=True)
    grads = mm(dlogits, mixed_v[...], TN)
    row = lax.broadcasted_iota(jnp.int32, (128, D), 0)
    grads = jnp.where(row == EXPERTS, gain_grad, grads).T.reshape(4, 16, 2, 8, 128)
    for i in range(8):
        side_out[i] = grads[i // 2, :, i % 2].reshape(ROWS, 128).astype(BF16)
    for i, by in enumerate(LINE_OFFSETS):
        to = moved(me, by)
        moves.append(
            remote(
                side_out.at[to["x"] * 2 + to["c"]], side_in.at[back_line], line_send, line_recv, 14 + i, to
            )
        )
        moves[-1].start()
    kept = pltpu.make_async_copy(side_out.at[here_line], side_in.at[back_line], local.at[5])
    kept.start()
    for item in moves + [kept] + stores:
        item.wait()


def moe(inputs, cid):
    slots = (EXPERTS, SLOT, 8, 128)
    up, down = (D, FF), (FF, D)
    dma = pltpu.SemaphoreType.DMA
    return remote_call(
        moe_kernel,
        inputs,
        ("h", "l", (0, D), (D, D + 128)) + ("l",) * 10 + ("h",) * 4,
        [
            shape((ROWS, D), F32),
            shape((ROWS, SLOTS), BF16),
            shape((ROWS, SLOTS), BF16),
            shape((ROWS, D), F32),
            shape((ROWS, D), BF16),
            shape((8, ROWS, 128), BF16),
            shape((8, ROWS, 128), BF16),
            shape(slots, BF16),
            shape((3 * D, FF), BF16),
        ],
        ("e", "e", "e", "e", "e", "v", "v", "h", "h"),
        [
            pltpu.VMEM((8, ROWS, 128), BF16),
            pltpu.VMEM(slots, BF16),
            pltpu.VMEM(slots, BF16),
            pltpu.VMEM(slots, BF16),
            pltpu.VMEM(slots, BF16),
            pltpu.VMEM(slots, BF16),
            pltpu.VMEM(up, BF16),
            pltpu.VMEM(up, BF16),
            pltpu.VMEM(down, BF16),
            pltpu.VMEM(up, F32),
            pltpu.VMEM(up, F32),
            pltpu.VMEM(down, F32),
            pltpu.VMEM((3 * D, FF), BF16),
            pltpu.VMEM((ROWS, D), BF16),
            pltpu.VMEM((ROWS, 128), F32),
            pltpu.VMEM((8, ROWS, 128), BF16),
            pltpu.VMEM((8, ROWS, 128), BF16),
            pltpu.VMEM((EXPERTS, ROWS, D), BF16),
            pltpu.VMEM((EXPERTS, 8, 128), F32),
            pltpu.VMEM((EXPERTS, 8, 128), F32),
            pltpu.VMEM((EXPERTS, 8, 128), F32),
            pltpu.VMEM((EXPERTS, 8, 128), F32),
        ]
        + [dma((31,))] * 8
        + [
            dma((21,)),
            dma((21,)),
            dma((6,)),
        ],
        cid,
    )


def tail_kernel(
    partial_ref, sent_ref, branch_ref, side_rows_ref, dq_ref, cos_ref, sin_ref, normed_ref, w_ref,
    y_ref, weigh_high_ref, weigh_low_ref, residual_ref,
    dnormed_out, mixed_out, grads_out, early_out,
    dqkv, part_out, part_in, part_own, line_out, line_in, share_out, share_in, total,
    out_in, side_in, dkv_ref, out_ref, side_ref, far_a, near_a, out_a, sum_a, far_b, near_b, out_b,
    plane_send, plane_recv, send, recv, local, out_recv,
):
    me = position(AXES)
    x, y, z, c = (me[axis] for axis in AXES)
    mine = y * 4 + z
    alone = jnp.where(c == lax.div(y, 2), 1, 0)
    barrier = pltpu.get_barrier_semaphore()

    def owner(k):
        at = lax.rem(lax.rem(y, 2) * 8 + z * 2 + c + k, 16)
        to = {"y": 2 * c + lax.div(at, 8), "z": lax.rem(lax.div(at, 2), 4), "c": lax.rem(at, 2)}
        return at, to

    def origin(k):
        at = lax.rem(mine + k, 16)
        return at, {"y": lax.div(at, 4), "z": lax.rem(at, 4), "c": lax.div(y, 2)}

    for k in range(1, 16):
        pl.semaphore_signal(barrier, inc=1, device_id=origin(k)[1], device_id_type=MESH)

    @pl.when(alone == 0)
    def _():
        pl.semaphore_signal(barrier, inc=1, device_id=origin(0)[1], device_id_type=MESH)

    offsets = LINE_OFFSETS + PLANE_OFFSETS
    for offset in offsets:
        pl.semaphore_signal(barrier, inc=1, device_id=moved(me, offset), device_id_type=MESH)
    grad_out = mm(sent_ref[...], branch_ref[...], TN)
    for j in range(16):
        out_ref[j] = grad_out[j * 8 : (j + 1) * 8]
    side = side_rows_ref[0].astype(F32)
    for i in range(1, 8):
        side += side_rows_ref[i].astype(F32)
    side_ref[...] = side.reshape(16, 8, 128)
    pl.semaphore_wait(barrier, len(offsets) + 16 - alone)
    def begun():
        for item in (
            dq_ref, cos_ref, sin_ref, w_ref, normed_ref, weigh_high_ref, weigh_low_ref, residual_ref
        ):
            item.begin()

    scatter_plane(
        me, begun, partial_ref, dkv_ref, far_a, near_a, out_a, sum_a, far_b, near_b, out_b, plane_send, plane_recv
    )
    used = [0]

    def go(src, dst, to):
        item = remote(src, dst, send, recv, used[0], to)
        used[0] += 1
        item.start()
        return item

    other = 1 - c
    low_lanes = lane_index((256, 128)) < 64

    def out_copy(k):
        at, to = owner(k)
        return pltpu.make_async_remote_copy(
            src_ref=out_ref.at[at], dst_ref=out_in.at[mine], send_sem=send.at[used[0] + k],
            recv_sem=out_recv.at[mine], device_id=to, device_id_type=MESH,
        )

    def out_kept():
        return pltpu.make_async_copy(out_ref.at[owner(0)[0]], out_in.at[mine], local.at[1])

    out_copies = [out_copy(k) for k in range(16)]
    used[0] += 16
    out_arrivals = []
    for k in range(16):
        at, to = origin(k)
        out_arrivals.append(
            pltpu.make_async_remote_copy(
                src_ref=out_ref.at[0], dst_ref=out_in.at[at], send_sem=send.at[0],
                recv_sem=out_recv.at[at], device_id=to, device_id_type=MESH,
            )
        )

    @pl.when(alone == 0)
    def _():
        out_copies[0].start()

    @pl.when(alone == 1)
    def _():
        out_kept().start()

    for item in out_copies[1:]:
        item.start()
    early = []
    for offset in PLANE_OFFSETS:
        to = moved(me, offset)
        early.append(go(side_ref.at[to["y"] * 4 + to["z"]], side_in.at[mine], to))
    side_kept = pltpu.make_async_copy(side_ref.at[mine], side_in.at[mine], local.at[2])
    side_kept.start()
    early.append(side_kept)

    def turn_back(first):
        rows = pl.ds(pl.multiple_of(first, 256), 256)
        cos, sin = cos_ref[rows, :], sin_ref[rows, :]
        dq, dkv = dq_ref[rows, :], dkv_ref[lax.div(first, 512), pl.ds(lax.rem(first, 512), 256), :]
        dq = (dq * cos - turned(dq) * sin).astype(BF16)
        dkv = jnp.where(low_lanes, dkv * cos - turned(dkv) * sin, dkv).astype(BF16)
        both = jnp.concatenate([dq, dkv], axis=1)
        dqkv[rows, :] = both
        return mm(both, w_ref[...], NT)

    crossing = []
    for i in range(2):
        value = turn_back(other * 512 + i * 256).astype(BF16)
        part_out[2 * i] = value[:ROWS]
        part_out[2 * i + 1] = value[ROWS:]
        span = pl.ds(2 * i, 2)
        crossing.append(go(part_out.at[span], part_in.at[span], {"c": other}))
    for i in range(2):
        value = turn_back(c * 512 + i * 256)
        part_own[2 * i] = value[:ROWS]
        part_own[2 * i + 1] = value[ROWS:]
    for item in crossing:
        item.wait()
    along = []
    for i, by in enumerate((2, 1, 3)):
        to = lax.rem(x + by, 4)
        line_out[i] = (part_own[to] + part_in[to].astype(F32)).astype(BF16)
        along.append(go(line_out.at[i], line_in.at[i], {"x": to}))
    for i in range(4):
        columns = pl.ds(i * 256, 256)
        grad = mm(normed_ref[:, columns], dqkv[...], TN).astype(BF16)
        share_out[i] = grad.reshape(16, 16, 256)
    spread = []
    for offset in PLANE_OFFSETS:
        to = moved(me, offset)
        spread.append(go(share_out.at[:, to["y"] * 4 + to["z"]], share_in.at[mine], to))
    kept = pltpu.make_async_copy(share_out.at[:, mine], share_in.at[mine], local.at[0])
    kept.start()
    outs = y_ref[...].astype(F32).reshape(SLOTS, D).astype(BF16)
    mixed = mm(weigh_high_ref[...], outs) + mm(weigh_low_ref[...], outs)
    mixed_out[...] = (residual_ref[...] + mixed).astype(BF16)
    mixed_out.store()
    for item in spread + [kept]:
        item.wait()
    for i in range(4):
        value = share_in[0, i].astype(F32)
        for j in range(1, 16):
            value += share_in[j, i].astype(F32)
        total[i] = value.reshape(2, 8, 256)
    ends = []
    here = x * 2 + c
    for offset in LINE_OFFSETS:
        to = moved(me, offset)
        ends.append(go(total.at[to["x"], to["c"]], grads_out.at[here], to))
    kept = pltpu.make_async_copy(total.at[x, c], grads_out.at[here], local.at[0])
    kept.start()
    for item in out_copies[1:]:
        item.wait_send()
    for item in out_arrivals[1:]:
        item.wait_recv()

    @pl.when(alone == 0)
    def _():
        out_copies[0].wait_send()
        out_arrivals[0].wait_recv()

    @pl.when(alone == 1)
    def _():
        out_kept().wait()

    for item in early:
        item.wait()
    out_total, side_total = out_in[0], side_in[0]
    for j in range(1, 16):
        out_total += out_in[j]
        side_total += side_in[j]
    early_out[:, 0:D] = out_total
    early_out[:, D : D + 128] = side_total
    for item in along:
        item.wait()
    dnormed = part_own[x] + part_in[x].astype(F32)
    for i in range(3):
        dnormed += line_in[i].astype(F32)
    dnormed_out[...] = dnormed
    for item in ends + [kept]:
        item.wait()


def tail(inputs, cid):
    count = 2 + 3 + 15 + 7 + 16 + 15
    return remote_call(
        tail_kernel,
        inputs,
        ("l",) * 4 + ("d",) * 4 + (DEFERRED_COLUMNS, "v", "d", "d", "d"),
        [
            shape((ROWS, D), F32),
            shape((ROWS, D), BF16),
            shape((8, 8, 256), F32),
            shape((8, D + 128), F32),
        ],
        ("v", "e", "v", "v"),
        [
            pltpu.VMEM((CHIP_ROWS, 256), BF16),
            pltpu.VMEM((4, ROWS, D), BF16),
            pltpu.VMEM((4, ROWS, D), BF16),
            pltpu.VMEM((4, ROWS, D), F32),
            pltpu.VMEM((3, ROWS, D), BF16),
            pltpu.VMEM((3, ROWS, D), BF16),
            pltpu.VMEM((4, 16, 16, 256), BF16),
            pltpu.VMEM((16, 4, 16, 256), BF16),
            pltpu.VMEM((4, 2, 8, 256), F32),
            pltpu.VMEM((16, 8, D), F32),
            pltpu.VMEM((16, 8, 128), F32),
            pltpu.VMEM((2, 512, 128), F32),
            pltpu.VMEM((16, 8, D), F32),
            pltpu.VMEM((16, 8, 128), F32),
            pltpu.VMEM((2, 4, 2, 256, 128), BF16),
            pltpu.VMEM((2, 4, 2, 512, 128), BF16),
            pltpu.VMEM((2, 4, 2, 512, 128), BF16),
            pltpu.VMEM((2, 2, 512, 128), F32),
            pltpu.VMEM((2, 2, 256, 128), BF16),
            pltpu.VMEM((2, 2, 512, 128), BF16),
            pltpu.VMEM((2, 3, 512, 128), BF16),
            pltpu.SemaphoreType.DMA((40,)),
            pltpu.SemaphoreType.DMA((40,)),
            pltpu.SemaphoreType.DMA((count,)),
            pltpu.SemaphoreType.DMA((count,)),
            pltpu.SemaphoreType.DMA((3,)),
            pltpu.SemaphoreType.DMA((16,)),
        ],
        cid,
        room=VMEM_BYTES,
    )


def last_kernel(
    dnormed_ref, tok_ref, gain_ref, gmid_ref, mixed_ref, rows_ref, wq_ref, wk_ref, wv_ref, own_gain_ref, early_ref,
    grads_ref,
    tokens_out, mixed_out, query_out, key_out, value_out, gains_out, grad_out, router_out,
    gate_out, up_out, down_out,
):
    tok = tok_ref[...].astype(F32)
    scale = lax.rsqrt(jnp.mean(tok * tok, axis=-1, keepdims=True) + EPSILON)
    weighted = dnormed_ref[...] * gain_ref[0:1, :]
    inner = jnp.mean(weighted * tok, axis=-1, keepdims=True)
    tokens_out[...] = gmid_ref[...] + scale * weighted - tok * (scale * scale * scale) * inner
    mixed_out[...] = mixed_ref[...]
    for i in range(8):
        query_out[:, i * 128 : (i + 1) * 128] = rows_ref[i][:, :128]
    lanes = lane_index((8, 128)) < 64
    for i in range(4):
        first, second = rows_ref[2 * i][:, 128:], rows_ref[2 * i + 1][:, 128:]
        key_out[:, i * 128 : (i + 1) * 128] = jnp.where(lanes, first, pltpu.roll(second, 64, axis=1))
        value_out[:, i * 128 : (i + 1) * 128] = jnp.where(lanes, pltpu.roll(first, 64, axis=1), second)
    total = (
        jnp.sum(query_out[...] * wq_ref[...].astype(F32), axis=1, keepdims=True)
        + jnp.sum(key_out[...] * wk_ref[...].astype(F32), axis=1, keepdims=True)
        + jnp.sum(value_out[...] * wv_ref[...].astype(F32), axis=1, keepdims=True)
    )
    row = jnp.broadcast_to(own_gain_ref[...].astype(F32), (8, 8))
    diagonal = lax.broadcasted_iota(jnp.int32, (8, 8), 0) == lane_index((8, 8))
    total = total / jnp.sum(jnp.where(diagonal, row, 0.0), axis=1, keepdims=True)
    side = early_ref[:, D : D + 128]
    wide = jnp.broadcast_to(total, (8, 128))
    blank = jnp.zeros((120, 128), F32)
    gain_one = jnp.concatenate([wide, blank], axis=0).T[0:1, :]
    gain_two = jnp.concatenate([side, blank], axis=0).T[EXPERTS : EXPERTS + 1, :]
    top_row = lax.broadcasted_iota(jnp.int32, (8, 128), 0) == 0
    gains_out[...] = jnp.where(top_row, jnp.broadcast_to(gain_one, (8, 128)), jnp.broadcast_to(gain_two, (8, 128)))
    grad_out[...] = early_ref[:, 0:D]
    router_out[...] = side[:, 0:EXPERTS]
    gate_out[...] = grads_ref[0:256].astype(F32)
    up_out[...] = grads_ref[256:512].astype(F32)
    down_out[:, 0:FF] = grads_ref[512:640].astype(F32)
    down_out[:, FF:D] = grads_ref[640:768].astype(F32)


def body(
    tokens,
    gain_one,
    w_query,
    w_key,
    w_value,
    w_out,
    gain_two,
    w_router,
    w_gate,
    w_up,
    w_down,
    dealt_order,
    lengths,
    routes,
    cotangent,
):
    y_at, z_at = lax.axis_index("y"), lax.axis_index("z")
    first_row = (y_at * 4 + z_at) * CHIP_ROWS

    cot_rows = lax.all_gather(cotangent, ("y", "z", "c"), axis=0, tiled=True)

    expand, expand_t = expand_matrix(), expand_matrix().T
    place, place_t = place_matrix(), place_matrix().T
    (
        query, kv, gain_first, cos, sin, w_mine, member, put, take, own_aux, order_rows, key_norm, heads,
        kv_all, w_late, normed, aux,
    ) = front(
        (
            lengths, tokens, w_query, w_key, w_value, w_out, w_router, gain_one.reshape(1, 8),
            gain_two.reshape(1, 8), dealt_order.reshape(128, 128), routes.T,
            expand, expand_t, place_column(), place_row(), turn_tables(128), turn_tables(1),
        ),
        1,
    )
    kv_all = kv_all.reshape(TOKENS, 128)
    w_late = w_late.reshape(D, 1152)
    plane = ("y", "z", "c")

    base = first_row.reshape(1).astype(jnp.int32)
    att, norm, sent, query_ext = attend(
        heads, base, kv_all, aux, kv, own_aux, query, order_rows, key_norm
    )

    (
        residual, weigh_high, weigh_low, gmid, branch, gsent_own, side_rows, y_out, expert_grads,
    ) = moe(
        (
            sent.reshape(8, ROWS, 128), tokens, w_late, w_late, member, put, take, expand, expand_t,
            place, place_t, origin_matrix(), place[:BLOCK], cotangent,
            cot_rows.reshape(EXPERTS, ROWS, D), w_gate[0], w_up[0], w_down[0],
        ),
        3,
    )
    y_in = lax.all_to_all(y_out, plane, split_axis=0, concat_axis=0, tiled=True)
    expert_grads = lax.psum_scatter(expert_grads, "x", scatter_dimension=0, tiled=True)

    gsent_own = gsent_own.reshape(CHIP_ROWS, 128)
    branch_rows = lax.all_gather(branch, ("c", "x"), axis=0, tiled=True)

    dq, dkv = attend_back(
        heads, base, kv_all, aux, kv, own_aux, query_ext, order_rows, gsent_own, att, norm
    )

    dnormed, mixed, qkv_rows, early = tail(
        (
            dkv.reshape(4, 4, 2, 512, 128), sent, branch_rows, side_rows, dq, cos, sin, normed, w_mine,
            y_in, weigh_high, weigh_low, residual,
        ),
        7,
    )
    (
        grad_tokens, mixed, grad_query, grad_key, grad_value, gains, grad_out_rows, grad_router,
        grad_gate, grad_up, grad_down,
    ) = local_call(
        last_kernel,
        (
            shape((ROWS, D), F32),
            shape((ROWS, D), BF16),
            shape((8, D), F32),
            shape((8, 512), F32),
            shape((8, 512), F32),
            shape((8, 128), F32),
            shape((8, D), F32),
            shape((8, EXPERTS), F32),
            shape((256, FF), F32),
            shape((256, FF), F32),
            shape((128, D), F32),
        ),
    )(
        dnormed, tokens, gain_first, gmid, mixed, qkv_rows, w_query, w_key, w_value,
        gain_one.reshape(1, 8), early, expert_grads,
    )
    grad_gain_one, grad_gain_two = gains[0, :8], gains[1, :8]
    grad_gate, grad_up, grad_down = grad_gate[None], grad_up[None], grad_down[None]
    return (
        mixed,
        grad_tokens,
        grad_gain_one,
        grad_query,
        grad_key,
        grad_value,
        grad_out_rows,
        grad_gain_two,
        grad_router,
        grad_gate,
        grad_up,
        grad_down,
    )


def solution(mesh):
    grid = Mesh(mesh.devices.reshape(4, 4, 4, 2), AXES)
    rows = P(("y", "z", "c", "x"), None)
    vector = P(AXES)
    matrix = P(AXES, None)
    expert = P(("y", "z", "c"), None, None)
    in_specs = (
        rows, vector, matrix, matrix, matrix, matrix, vector, matrix, expert, expert, expert,
        P(), P(), rows, rows,
    )
    grads = P(("y", "z", "c"), "x", None)
    out_specs = (
        rows, rows, vector, matrix, matrix, matrix, matrix, vector, matrix, grads, grads, grads,
    )
    return jax.shard_map(body, mesh=grid, in_specs=in_specs, out_specs=out_specs, check_vma=False)
```

```python
import functools
import math

import jax
import jax.numpy as jnp
import ml_dtypes
import numpy as np
from jax import lax
from jax.experimental import pallas as pl
from jax.experimental.pallas import tpu as pltpu
from jax.sharding import Mesh
from jax.sharding import PartitionSpec as P

D = 1024
HEADS = 16
KV_HEADS = 8
HEAD_DIM = 64
EXPERTS = 32
FF = 512
CAP = 36
SLOT = CAP
SLOTS = EXPERTS * SLOT
ROWS = 128
CHIP_ROWS = 1024
RUN = 256
TOKENS = 16384
NSEQ = 5
EPSILON = 1e-06
ROPE_BASE = 10000.0
FAR = float(2.0**100)
SIZE = {"x": 4, "y": 4, "z": 4, "c": 2}
AXES = ("x", "y", "z", "c")
MESH = pl.DeviceIdType.MESH
BF16 = jnp.bfloat16
F32 = jnp.float32
NN = (((1,), (0,)), ((), ()))
NT = (((1,), (1,)), ((), ()))
TN = (((0,), (0,)), ((), ()))
VMEM_BYTES = 56 * 1024 * 1024


def mm(a, b, dims=NN):
    return lax.dot_general(a, b, dims, preferred_element_type=F32)


def shape(dims, dtype):
    return jax.ShapeDtypeStruct(dims, dtype)


def halves(value):
    high = value.astype(BF16)
    return high, (value - high.astype(F32)).astype(BF16)


def local_call(kernel, outs, scratch=(), grid=None, in_specs=None, out_specs=None):
    extra = {}
    if grid is not None:
        extra = {"grid": grid, "in_specs": in_specs, "out_specs": out_specs}
    elif in_specs is not None:
        extra = {"in_specs": in_specs}
        if out_specs is not None:
            extra["out_specs"] = out_specs
    return pl.pallas_call(
        kernel,
        out_shape=outs,
        scratch_shapes=list(scratch),
        compiler_params=pltpu.CompilerParams(vmem_limit_bytes=VMEM_BYTES),
        **extra,
    )


class Late:
    def __init__(self, hbm, vmem, sem, columns, wait):
        self.hbm, self.vmem = hbm, vmem
        source = hbm if columns is None else hbm.at[:, columns[0] : columns[1]]
        self.copy, self.ready = pltpu.make_async_copy(source, vmem, sem), False
        if not wait:
            self.copy.start()

    def begin(self):
        self.copy.start()

    def get(self):
        if not self.ready:
            self.copy.wait()
            self.ready = True
        return self.vmem

    def __getitem__(self, index):
        return self.get()[index]


class Early:
    def __init__(self, hbm, vmem, sem):
        self.vmem, self.copy = vmem, pltpu.make_async_copy(vmem, hbm, sem)

    def __getitem__(self, index):
        return self.vmem[index]

    def __setitem__(self, index, value):
        self.vmem[index] = value

    def store(self):
        self.copy.start()


DEFERRED_COLUMNS = (0, 256)


def remote_call(kernel, inputs, kinds, outs, out_kinds, scratch, cid, room=VMEM_BYTES):
    spaces = {"s": pltpu.SMEM, "v": pltpu.VMEM}
    late = [(i, kind) for i, kind in enumerate(kinds) if kind not in ("s", "v", "h")]
    early = [i for i, kind in enumerate(out_kinds) if kind == "e"]

    def late_shape(i, kind):
        dims = inputs[i].shape if kind in ("l", "d") else (inputs[i].shape[0], kind[1] - kind[0])
        return pltpu.VMEM(dims, inputs[i].dtype)

    def wrapped(*refs):
        ins, rest = list(refs[: len(inputs)]), list(refs[len(inputs) :])
        results, rest = rest[: len(outs)], rest[len(outs) :]
        own, rest = rest[: len(scratch)], rest[len(scratch) :]
        late_v, rest = rest[: len(late)], rest[len(late) :]
        early_v, (late_sem, early_sem) = rest[: len(early)], rest[len(early) :]
        for n, (i, kind) in enumerate(late):
            columns = None if kind in ("l", "d") else kind
            ins[i] = Late(ins[i], late_v[n], late_sem.at[n], columns, kind == "d" or kind == DEFERRED_COLUMNS)
        for n, i in enumerate(early):
            results[i] = Early(results[i], early_v[n], early_sem.at[n])
        kernel(*ins, *results, *own)
        for i, _ in late:
            ins[i].get()
        for i in early:
            results[i].copy.wait()

    return pl.pallas_call(
        wrapped,
        out_shape=list(outs),
        in_specs=[pl.BlockSpec(memory_space=spaces.get(kind, pl.ANY)) for kind in kinds],
        out_specs=[pl.BlockSpec(memory_space=spaces.get(kind, pl.ANY)) for kind in out_kinds],
        scratch_shapes=list(scratch)
        + [late_shape(i, kind) for i, kind in late]
        + [pltpu.VMEM(outs[i].shape, outs[i].dtype) for i in early]
        + [pltpu.SemaphoreType.DMA((max(1, len(late)),)), pltpu.SemaphoreType.DMA((max(1, len(early)),))],
        compiler_params=pltpu.CompilerParams(
            collective_id=cid, has_side_effects=True, vmem_limit_bytes=room
        ),
    )(*inputs)


def flat_index(coords, order):
    index = 0
    for axis in order:
        index = index * SIZE[axis] + coords[axis]
    return index


PLANE_ORDER = (
    (2, 2), (2, 3), (2, 1), (3, 2), (1, 2), (0, 2), (2, 0), (3, 1), (1, 3),
    (3, 3), (1, 1), (0, 3), (0, 1), (3, 0), (1, 0), (0, 0),
)
PLANE_OFFSETS = tuple({"y": dy, "z": dz} for dy, dz in PLANE_ORDER[:-1])
SPREAD_OFFSETS = tuple(
    {"y": dy, "z": dz, "c": (dc + i + 1) % 2}
    for i, (dy, dz) in enumerate(PLANE_ORDER)
    for dc in range(2)
    if (dy, dz, (dc + i + 1) % 2) != (0, 0, 0)
)
LINE_OFFSETS = tuple(
    {"x": dx, "c": dc} for dx, dc in ((2, 0), (2, 1), (1, 0), (3, 0), (1, 1), (3, 1), (0, 1))
)
OFFSETS = {("y", "z"): PLANE_OFFSETS, ("y", "z", "c"): SPREAD_OFFSETS, ("x", "c"): LINE_OFFSETS}


def position(axes):
    return {axis: lax.axis_index(axis) for axis in axes}


def moved(me, offset):
    return {axis: lax.rem(me[axis] + by, SIZE[axis]) if by else me[axis] for axis, by in offset.items()}


def greet(me, offsets):
    barrier = pltpu.get_barrier_semaphore()
    for offset in offsets:
        pl.semaphore_signal(barrier, inc=1, device_id=moved(me, offset), device_id_type=MESH)
    return lambda: pl.semaphore_wait(barrier, len(offsets))


def remote(src, dst, send, recv, slot, to):
    return pltpu.make_async_remote_copy(
        src_ref=src,
        dst_ref=dst,
        send_sem=send.at[slot],
        recv_sem=recv.at[slot],
        device_id=to,
        device_id_type=MESH,
    )


def scatter_plane(me, begun, p_ref, o_ref, far_a, near_a, out_a, sum_a, far_b, near_b, out_b, send, recv):
    half = p_ref.vmem.shape[3] // 2
    lower, upper = pl.ds(0, half), pl.ds(half, half)
    axis = (("y", "z"), ("z", "y"))
    used = [0]

    def go(src, dst, t, which, by):
        to = {axis[t][which]: lax.rem(me[axis[t][which]] + by, 4)}
        item = remote(src, dst, send, recv, used[0], to)
        used[0] += 1
        item.start()
        return item

    def part(t, first, second, hbm=False):
        a = lax.rem(me[axis[t][0]] + first, 4)
        b = lax.rem(me[axis[t][1]] + second, 4)
        ref = p_ref.hbm if hbm else p_ref.get()
        return ref.at[a, b, 0] if t == 0 else ref.at[b, a, 1]

    turns = (2, 1, 3, 0)
    both = (0, 1)
    far, near = {}, {}
    for k, by in enumerate(turns):
        for t in both:
            far[k, t] = (
                go(part(t, 2, by, True).at[lower], far_a.at[t, k, 0], t, 0, 1),
                go(part(t, 2, by, True).at[upper], far_a.at[t, k, 1], t, 0, 3),
            )
    begun()
    for k, by in enumerate(turns):
        for t in both:
            ahead, behind = part(t, 1, by), part(t, 3, by)
            far[k, t][0].wait()
            out_a[t, k, 0, 0:half] = (ahead[0:half].astype(F32) + far_a[t, k, 0].astype(F32)).astype(BF16)
            out_a[t, k, 0, half : 2 * half] = ahead[half : 2 * half]
            first = go(out_a.at[t, k, 0], near_a.at[t, k, 0], t, 0, 1)
            far[k, t][1].wait()
            out_a[t, k, 1, 0:half] = behind[0:half]
            out_a[t, k, 1, half : 2 * half] = (
                behind[half : 2 * half].astype(F32) + far_a[t, k, 1].astype(F32)
            ).astype(BF16)
            near[k, t] = (first, go(out_a.at[t, k, 1], near_a.at[t, k, 1], t, 0, 3))

    def summed(k, t):
        near[k, t][0].wait()
        near[k, t][1].wait()
        return (
            part(t, 0, turns[k])[...].astype(F32)
            + near_a[t, k, 0].astype(F32)
            + near_a[t, k, 1].astype(F32)
        )

    far_two, near_two = {}, {}
    for t in both:
        value = summed(0, t).astype(BF16)
        out_b[t, 0] = value
        far_two[t] = (
            go(out_b.at[t, 0, lower], far_b.at[t, 0], t, 1, 1),
            go(out_b.at[t, 0, upper], far_b.at[t, 1], t, 1, 3),
        )
    for k in (1, 2):
        for t in both:
            sum_a[t, k - 1] = summed(k, t)
    for t in both:
        far_two[t][0].wait()
        out_b[t, 1, 0:half] = (sum_a[t, 0, 0:half] + far_b[t, 0].astype(F32)).astype(BF16)
        out_b[t, 1, half : 2 * half] = sum_a[t, 0, half : 2 * half].astype(BF16)
        first = go(out_b.at[t, 1], near_b.at[t, 0], t, 1, 1)
        far_two[t][1].wait()
        out_b[t, 2, 0:half] = sum_a[t, 1, 0:half].astype(BF16)
        out_b[t, 2, half : 2 * half] = (
            sum_a[t, 1, half : 2 * half] + far_b[t, 1].astype(F32)
        ).astype(BF16)
        near_two[t] = (first, go(out_b.at[t, 2], near_b.at[t, 1], t, 1, 3))
    for t in both:
        value = summed(3, t)
        near_two[t][0].wait()
        near_two[t][1].wait()
        o_ref[t] = value + near_b[t, 0].astype(F32) + near_b[t, 1].astype(F32)


def lane_index(shape):
    return lax.broadcasted_iota(jnp.int32, shape, 1)


def turned(values):
    lane = lane_index(values.shape)
    up = pltpu.roll(values, 32, axis=1)
    down = pltpu.roll(values, 96, axis=1)
    return jnp.where(lane % 64 < 32, -down, up)


def gather_plane(kv_v, kv_hbm, go, me, own_sem, fillers):
    own = pltpu.make_async_copy(kv_v, kv_hbm.at[me["y"], me["z"]], own_sem)
    own.start()
    half = kv_v.shape[1] // 2
    lower, upper = pl.ds(0, half), pl.ds(half, half)
    axis = (("y", "z"), ("z", "y"))
    here = tuple((me[a], me[b]) for a, b in axis)
    step = {"plus": 1, "minus": 3, "far": 2, "own": 0}

    def place(t, a, b):
        return kv_hbm.at[a, b, 0] if t == 0 else kv_hbm.at[b, a, 1]

    def at(t, which, name):
        return lax.rem(here[t][which] + step[name], 4)

    def send_second(t, src, name):
        dst = place(t, at(t, 0, name), here[t][1])
        src = dst if src is None else src
        return (
            go(src, dst, {axis[t][1]: at(t, 1, "plus")}),
            go(src, dst, {axis[t][1]: at(t, 1, "minus")}),
        )

    def pass_on(t, which, a_name, b_name, part, direction):
        ref = place(t, at(t, 0, a_name), at(t, 1, b_name)).at[part]
        return go(ref, ref, {axis[t][which]: at(t, which, direction)})

    def forward_second(t, name, pair):
        pair[0].wait()
        a = pass_on(t, 1, name, "minus", lower, "plus")
        pair[1].wait()
        b = pass_on(t, 1, name, "plus", upper, "minus")
        return [a, b]

    first, second, last = {}, {}, []
    for t in (0, 1):
        dst = place(t, *here[t])
        first[t] = (
            go(kv_v.at[t], dst, {axis[t][0]: at(t, 0, "plus")}),
            go(kv_v.at[t], dst, {axis[t][0]: at(t, 0, "minus")}),
        )
    for t in (0, 1):
        second[t, "own"] = send_second(t, kv_v.at[t], "own")
    fillers[0]()
    far = {}
    for t in (0, 1):
        first[t][0].wait()
        a = pass_on(t, 0, "minus", "own", lower, "plus")
        second[t, "minus"] = send_second(t, None, "minus")
        first[t][1].wait()
        b = pass_on(t, 0, "plus", "own", upper, "minus")
        second[t, "plus"] = send_second(t, None, "plus")
        far[t] = (a, b)
    fillers[1]()
    for t in (0, 1):
        last += forward_second(t, "own", second[t, "own"])
    for t in (0, 1):
        far[t][0].wait()
        far[t][1].wait()
        second[t, "far"] = send_second(t, None, "far")
    fillers[2]()
    for name in ("minus", "plus", "far"):
        for t in (0, 1):
            last += forward_second(t, name, second[t, name])
    return last + [own]


def front_kernel(
    lengths_ref, tok_ref, wq_ref, wk_ref, wv_ref, wo_ref, router_ref, gain_one_ref, gain_two_ref,
    order_ref, routes_ref, expand_ref, expand_t_ref, col_ref, row_ref, turn_high_ref, turn_low_ref,
    q_ref, kv_own_ref, gain_ref, cos_ref, sin_ref, w_out_ref, member_ref, put_ref, take_ref,
    own_aux_ref, order_rows_ref, key_norm_ref, heads_ref, kv_hbm, late_hbm, normed_v, aux_v,
    rows_v, w_v, kv_v, long_v, side_v, w_ref, late_ref, send, recv, local,
):
    me = position(AXES)
    x, y, z, c = (me[axis] for axis in AXES)
    arrived = greet(me, LINE_OFFSETS + PLANE_OFFSETS)
    small = lane_index((8, 128))
    diagonal = lax.broadcasted_iota(jnp.int32, (8, 8), 0) == lane_index((8, 8))

    def column(ref):
        row = jnp.broadcast_to(ref[...].astype(F32), (8, 8))
        return jnp.sum(jnp.where(diagonal, row, 0.0), axis=1, keepdims=True)

    gain_lane = jnp.where(small == 0, column(gain_one_ref), 0.0).astype(BF16)
    for i in range(8):
        span = slice((i // 2) * 128, (i // 2 + 1) * 128)
        key, value = wk_ref[:, span].astype(F32), wv_ref[:, span].astype(F32)
        if i % 2 == 0:
            pair = jnp.where(small < 64, key, pltpu.roll(value, 64, axis=1))
        else:
            pair = jnp.where(small < 64, pltpu.roll(key, 64, axis=1), value)
        w_ref[i, :, 0:128] = wq_ref[:, i * 128 : (i + 1) * 128]
        w_ref[i, :, 128:256] = pair.astype(BF16)
        w_ref[i, :, 256:384] = gain_lane
    side_v[...] = jnp.zeros_like(side_v)
    side_v[:, 0:EXPERTS] = router_ref[...].astype(F32)
    late_ref[:, 0:D] = wo_ref[...]
    late_ref[:, D : D + 128] = jnp.where(small == EXPERTS, column(gain_two_ref), side_v[...]).astype(BF16)
    arrived()
    plus, minus, far = lax.rem(x + 1, 4), lax.rem(x + 3, 4), lax.rem(x + 2, 4)
    other = 1 - c
    lower, upper = pl.ds(0, 64), pl.ds(64, 64)
    used = [0]

    def go(src, dst, to):
        item = remote(src, dst, send, recv, used[0], to)
        used[0] += 1
        item.start()
        return item

    def keep(src, dst, slot):
        item = pltpu.make_async_copy(src, dst, local.at[slot])
        item.start()
        return item

    own = [
        keep(w_ref.at[x * 2 + c], w_v.at[x, y, z, c], 0),
        keep(late_ref, late_hbm.at[x, y, z, c], 1),
    ]
    own_rows = keep(tok_ref, rows_v.at[c, x], 2)
    first_w = []
    for offset in LINE_OFFSETS:
        to = moved(me, offset)
        first_w.append(go(w_ref.at[to["x"] * 2 + to["c"]], w_v.at[x, y, z, c], to))
    to_plus = go(tok_ref, rows_v.at[c, x], {"x": plus})
    to_minus = go(tok_ref, rows_v.at[c, x], {"x": minus})
    sides = [go(tok_ref, rows_v.at[c, x], {"c": other})]

    for item in own + first_w:
        item.wait()
    second_w = [go(w_v.at[:, y, z], w_v.at[:, y, z], moved(me, by)) for by in PLANE_OFFSETS]
    first_late = [go(late_ref, late_hbm.at[x, y, z, c], moved(me, by)) for by in PLANE_OFFSETS]

    chip = y * 4 + z
    mine = order_ref[pl.ds(pl.multiple_of(chip * 8, 8), 8), :]
    ends, total = [], jnp.int32(0)
    for i in range(NSEQ):
        total = total + lengths_ref[i]
        ends.append(total)
    place = mine
    for i in range(NSEQ):
        place = place - jnp.where(mine >= ends[i], lengths_ref[i], 0)
    lane = lane_index((ROWS, 128))

    def table(ref, picked):
        return mm(picked, ref[0]) + mm(picked, ref[1]) + mm(picked, ref[2])

    for i in range(8):
        wide = jnp.broadcast_to(place[i : i + 1, :].astype(F32), (ROWS, 128)).T.astype(jnp.int32)
        high = table(turn_high_ref, jnp.where(lane == lax.shift_right_logical(wide, 7), 1.0, 0.0).astype(BF16))
        low = table(turn_low_ref, jnp.where(lane == (wide & 127), 1.0, 0.0).astype(BF16))
        cos_ref[pl.ds(i * 128, 128), :] = high[:, :128] * low[:, :128] - high[:, 128:] * low[:, 128:]
        sin_ref[pl.ds(i * 128, 128), :] = high[:, 128:] * low[:, :128] + high[:, :128] * low[:, 128:]
    heads_ref[...] = order_ref[pl.ds(0, 32, stride=4), :]
    order_rows_ref[...] = mine.astype(F32)

    to_plus.wait()
    next_plus = go(rows_v.at[c, minus, lower], rows_v.at[c, minus, lower], {"x": plus})
    sides.append(go(rows_v.at[c, minus], rows_v.at[c, minus], {"c": other}))
    to_minus.wait()
    next_minus = go(rows_v.at[c, plus, upper], rows_v.at[c, plus, upper], {"x": minus})
    sides.append(go(rows_v.at[c, plus], rows_v.at[c, plus], {"c": other}))
    next_plus.wait()
    next_minus.wait()
    sides.append(go(rows_v.at[c, far], rows_v.at[c, far], {"c": other}))
    own_rows.wait()
    for item in second_w:
        item.wait()
    weights = w_v[...].astype(F32).reshape(D, 384)
    w_out_ref[...] = weights.astype(BF16)
    gain = weights[:, 256:384].T[0:1, :]
    gain_ref[...] = jnp.broadcast_to(gain, (8, D))
    low_lanes = lane_index((256, 128)) < 64

    def project(block):
        longest = jnp.zeros((256, 1), F32)
        for i in range(2):
            rows = pl.ds(pl.multiple_of(block * 512 + i * 256, 256), 256)
            tok = rows_v[block, pl.ds(2 * i, 2)].astype(F32).reshape(256, D)
            scale = lax.rsqrt(jnp.mean(tok * tok, axis=-1, keepdims=True) + EPSILON)
            normed = (tok * scale * gain).astype(BF16)
            normed_v[rows, :] = normed
            pre = mm(normed, w_out_ref[:, 0:256])
            cos, sin = cos_ref[rows, :], sin_ref[rows, :]
            q_pre, kv_pre = pre[:, :128], pre[:, 128:]
            query = (q_pre * cos + turned(q_pre) * sin).astype(BF16).astype(F32) * 0.125
            q_ref[0, rows, :] = jnp.where(low_lanes, query, 0.0).astype(BF16)
            q_ref[1, rows, :] = jnp.where(low_lanes, pltpu.roll(query, 64, axis=1), 0.0).astype(BF16)
            key = kv_pre * cos + turned(kv_pre) * sin
            kv = jnp.where(low_lanes, key, kv_pre).astype(BF16)
            kv_own_ref[rows, :] = kv
            kv_v[block, pl.ds(i * 256, 256), :] = kv
            rounded = kv.astype(F32)
            square = jnp.sum(jnp.where(low_lanes, rounded * rounded, 0.0), axis=1, keepdims=True)
            longest = jnp.maximum(longest, square)
        return jnp.max(longest, axis=0, keepdims=True)

    longest = project(c)
    for item in sides:
        item.wait()
    longest = jnp.maximum(longest, project(other))
    long_v[chip] = jnp.broadcast_to(longest, (8, 128))
    longs = [go(long_v.at[chip], long_v.at[chip], moved(me, by)) for by in PLANE_OFFSETS]
    stores = []
    for item in (q_ref, kv_own_ref, cos_ref, sin_ref, w_out_ref, normed_v):
        item.store()

    def routing():
        routes = jnp.concatenate([routes_ref[...].astype(F32), jnp.full((120, 128), -1.0, F32)], axis=0).T
        member = jnp.zeros((ROWS, 128), F32)
        for choice in range(8):
            member += jnp.where(routes[:, choice : choice + 1].astype(jnp.int32) == lane, 1.0, 0.0)
        below = lax.broadcasted_iota(jnp.int32, (ROWS, ROWS), 0) > lane_index((ROWS, ROWS))
        earlier = mm(jnp.where(below, 1.0, 0.0).astype(BF16), member.astype(BF16))
        slot = jnp.where(member > 0.5, earlier, -1.0).astype(BF16)
        member_ref[...] = member
        take = jnp.where(mm(slot, expand_ref[...]) == row_ref[...], 1.0, 0.0)
        take_ref[...] = take.astype(BF16)
        put = jnp.where(mm(expand_t_ref[...], slot, NT) == col_ref[...].astype(F32), 1.0, 0.0)
        put = put.astype(BF16)
        put_ref[...] = put
        for item in (put_ref, take_ref):
            item.store()

    def segments():
        sub = lax.broadcasted_iota(jnp.int32, (8, 128), 0)
        begin = jnp.zeros((8, 128), jnp.int32)
        end = jnp.full((8, 128), TOKENS, jnp.int32)
        for i in range(NSEQ):
            begin = jnp.where(sub == 3 + i, ends[i] - lengths_ref[i], begin)
            end = jnp.where(sub == 3 + i, ends[i], end)
        spot = jnp.where(sub == lane_index((8, 128)), 1.0, 0.0).astype(BF16)

        def block(step, carry):
            rows = order_ref[pl.ds(pl.multiple_of(step * 8, 8), 8), :]
            for i in range(8):
                order = jnp.broadcast_to(rows[i : i + 1, :], (8, 128))
                within = jnp.where((order >= begin) & (order < end), 1.0, 0.0).astype(BF16)
                here = pl.ds(pl.multiple_of(step * 1024 + i * 128, 128), 128)
                aux_v[here, :] = mm(within, spot, TN).astype(BF16)
            return carry

        lax.fori_loop(0, 16, block, 0)
        aux_v.store()
        own_aux_ref[...] = aux_v[pl.ds(pl.multiple_of(chip * CHIP_ROWS, CHIP_ROWS), CHIP_ROWS), :]
        own_aux_ref.store()

    def late():
        for item in second_late:
            item.wait()
        stores.append(go(late_hbm.at[:, :, :, c], late_hbm.at[:, :, :, c], {"c": other}))

    for item in first_late:
        item.wait()
    second_late = [
        go(late_hbm.at[x, :, :, c], late_hbm.at[x, :, :, c], {"x": to}) for to in (far, plus, minus)
    ]

    last = gather_plane(kv_v, kv_hbm, go, me, local.at[3], (routing, segments, late))
    for item in longs:
        item.wait()
    longest = long_v[0]
    for i in range(1, 16):
        longest = jnp.maximum(longest, long_v[i])
    key_norm_ref[...] = jnp.sqrt(longest)
    for item in last + stores:
        item.wait()


def front(inputs, cid):
    count = 7 + 3 + 3 + 15 + 15 + 2 + 3 + 40 + 1 + 15
    return remote_call(
        front_kernel,
        inputs,
        ("s", "h") + ("v",) * 9 + ("l",) * 6,
        [
            shape((2, CHIP_ROWS, 128), BF16),
            shape((CHIP_ROWS, 128), BF16),
            shape((8, D), F32),
            shape((CHIP_ROWS, 128), F32),
            shape((CHIP_ROWS, 128), F32),
            shape((D, 384), BF16),
            shape((ROWS, 128), F32),
            shape((SLOTS, ROWS), BF16),
            shape((ROWS, SLOTS), BF16),
            shape((CHIP_ROWS, 128), BF16),
            shape((8, 128), F32),
            shape((8, 128), F32),
            shape((32, 128), jnp.int32),
            shape((4, 4, 2, 512, 128), BF16),
            shape((4, 4, 4, 2, 8, 1152), BF16),
            shape((CHIP_ROWS, D), BF16),
            shape((TOKENS, 128), BF16),
        ],
        ("e", "e", "v", "e", "e", "e", "v", "e", "e", "e", "v", "v", "v", "h", "h", "e", "e"),
        [
            pltpu.VMEM((2, 4, ROWS, D), BF16),
            pltpu.VMEM((4, 4, 4, 2, 8, 384), BF16),
            pltpu.VMEM((2, 512, 128), BF16),
            pltpu.VMEM((16, 8, 128), F32),
            pltpu.VMEM((8, 128), F32),
            pltpu.VMEM((8, 8, 384), BF16),
            pltpu.VMEM((8, 1152), BF16),
            pltpu.SemaphoreType.DMA((count,)),
            pltpu.SemaphoreType.DMA((count,)),
            pltpu.SemaphoreType.DMA((4,)),
        ],
        cid,
    )


def turn_tables(step):
    frequency = (np.float32(ROPE_BASE) ** (-np.arange(32, dtype=np.float32) / np.float32(32))).astype(np.float64)
    angles = (np.arange(128) * step)[:, None] * np.tile(frequency, 4)[None, :]
    rest = np.concatenate([np.cos(angles), np.sin(angles)], axis=1)
    parts = []
    for _ in range(3):
        part = rest.astype(np.float32).astype(ml_dtypes.bfloat16)
        parts.append(part)
        rest = rest - part.astype(np.float64)
    return jnp.asarray(np.stack(parts))


def order_pair(order_ref, index):
    row = jnp.concatenate([order_ref[pl.ds(2 * index, 1), :], order_ref[pl.ds(2 * index + 1, 1), :]], axis=1)
    row = jnp.broadcast_to(row, (RUN, RUN))
    return row, row.T


WIDE = 6
WIDE_BACK = 3


def run_lists(order_ref, base, first_ref):
    def note(block, carry):
        run = lax.shift_right_logical(order_ref[block, 0], 8)
        first_ref[run] = block * 512
        first_ref[63 - run] = block * 512 + RUN
        return carry

    lax.fori_loop(0, 32, note, 0)

    def count(part):
        run = lax.shift_right_logical(order_ref[lax.div(base, 512) + lax.div(part, 2), 0], 8)
        return jnp.where(lax.rem(part, 2) == 0, run, 31 - run)

    return count


def group_places(first_ref, number, half, step, wide):
    places = []
    for i in range(wide):
        index = step * wide + i
        at = jnp.where(index < number, half + index, 32 - half)
        places.append(pl.ds(pl.multiple_of(first_ref[at], RUN), RUN))
    return places


def attend_kernel(
    order_smem, base_ref, kv_hbm, aux_hbm, own_kv_ref, own_aux_ref, q_ref, order_ref, key_norm_ref,
    att_ref, norm_ref, sent_ref, qx_ref, kv_ref, aux_ref, acc_ref, first_ref, loads,
):
    copies = [
        pltpu.make_async_copy(kv_hbm, kv_ref, loads.at[0]),
        pltpu.make_async_copy(aux_hbm, aux_ref, loads.at[1]),
    ]
    for item in copies:
        item.start()
    count = run_lists(order_smem, base_ref[0], first_ref)
    key_norm = key_norm_ref[0:1, 0:1]
    lane = lane_index((RUN, 128))

    def right(keys):
        turned_keys = keys.T
        row = lax.broadcasted_iota(jnp.int32, turned_keys.shape, 0)
        return jnp.where(row < 64, jnp.ones_like(turned_keys), turned_keys)[56:]

    def prepare(part, carry):
        rows = pl.ds(pl.multiple_of(part * RUN, RUN), RUN)
        own_aux = own_aux_ref[rows, :]
        spread = jnp.where(lane < 3 + NSEQ, (own_aux.astype(F32) - 1.0) * FAR, 0.0)
        for head in range(2):
            query = q_ref[head, rows, :]
            wide = query.astype(F32)
            shift = jnp.ceil(jnp.sqrt(jnp.sum(wide * wide, axis=1, keepdims=True)) * key_norm)
            top = shift.astype(BF16).astype(F32)
            middle = (shift - top).astype(BF16).astype(F32)
            rest = shift - top - middle
            ext = jnp.where(lane == 0, -top, spread)
            ext = jnp.where(lane == 1, -middle, ext)
            ext = jnp.where(lane == 2, -rest, ext)
            here = pl.ds(head * RUN, RUN)
            qx_ref[part, here, 0:128] = query
            qx_ref[part, here, 128:256] = ext.astype(BF16)
        order_key, order_query = order_pair(order_ref, part)
        allowed = order_query <= order_key
        keys = own_kv_ref[rows, :]
        e = jnp.exp(mm(jnp.concatenate([keys, own_aux], axis=1), qx_ref[part], NT))
        e = jnp.where(jnp.concatenate([allowed, allowed], axis=1), e, 0.0)
        acc_ref[part] = mm(right(keys), e.astype(BF16))
        return carry

    lax.fori_loop(0, 4, prepare, 0)
    for item in copies:
        item.wait()

    def part_step(part, carry):
        number = count(part)
        half = lax.rem(part, 2) * 32

        def group(step, carry):
            places = group_places(first_ref, number, half, step, WIDE)
            keys = jnp.concatenate([kv_ref[here, :] for here in places], axis=0)
            aux = jnp.concatenate([aux_ref[here, :] for here in places], axis=0)
            e = jnp.exp(mm(jnp.concatenate([keys, aux], axis=1), qx_ref[part], NT))
            acc_ref[part] += mm(right(keys), e.astype(BF16))
            return carry

        lax.fori_loop(0, lax.div(number + WIDE - 1, WIDE), group, 0)
        rows = pl.ds(pl.multiple_of(part * RUN, RUN), RUN)
        total = acc_ref[part]
        value = total[8:72] / total[0:1]
        att = jnp.concatenate([value[:, :RUN], value[:, RUN:]], axis=0).T
        norm = jnp.broadcast_to(total[0:1], (64, 2 * RUN))
        norm = jnp.concatenate([norm[:, :RUN], norm[:, RUN:]], axis=0).T
        att_ref[rows, :] = att
        norm_ref[rows, :] = norm
        sent_ref[rows, :] = att.astype(BF16)
        return carry

    lax.fori_loop(0, 4, part_step, 0)


def attend(order, base, kv, aux, own_kv, own_aux, query, order_rows, key_norm):
    smem = pl.BlockSpec(memory_space=pltpu.SMEM)
    vmem = pl.BlockSpec(memory_space=pltpu.VMEM)
    hbm = pl.BlockSpec(memory_space=pl.ANY)
    return local_call(
        attend_kernel,
        (
            shape((CHIP_ROWS, 128), F32),
            shape((CHIP_ROWS, 128), F32),
            shape((CHIP_ROWS, 128), BF16),
            shape((4, 2 * RUN, 256), BF16),
        ),
        scratch=[
            pltpu.VMEM((TOKENS, 128), BF16),
            pltpu.VMEM((TOKENS, 128), BF16),
            pltpu.VMEM((4, 72, 2 * RUN), F32),
            pltpu.SMEM((64,), jnp.int32),
            pltpu.SemaphoreType.DMA((2,)),
        ],
        in_specs=[smem] * 2 + [hbm] * 2 + [vmem] * 5,
    )(order, base, kv, aux, own_kv, own_aux, query, order_rows, key_norm)


def attend_back_kernel(
    order_smem, base_ref, kv_hbm, aux_hbm, own_kv_ref, own_aux_ref, qx_ref, order_ref,
    gsent_ref, att_ref, norm_ref, dq_ref, dkv_hbm,
    kv_ref, aux_ref, acc_ref, dq_acc, gx_ref, rhs_ref, out_ref, first_ref, loads, stores,
):
    copies = [
        pltpu.make_async_copy(kv_hbm, kv_ref, loads.at[0]),
        pltpu.make_async_copy(aux_hbm, aux_ref, loads.at[1]),
    ]
    for item in copies:
        item.start()
    own_base = base_ref[0]
    count = run_lists(order_smem, own_base, first_ref)

    def clear(step, carry):
        acc_ref[pl.ds(pl.multiple_of(step * 512, 512), 512), :] = jnp.zeros((512, 128), F32)
        return carry

    lax.fori_loop(0, TOKENS // 512, clear, 0)
    lane = lane_index((RUN, 128))
    low_lanes = lane < 64

    def apply(part, here, e, prob):
        ds = (e * prob).astype(BF16)
        left = jnp.concatenate([ds, e.astype(BF16)], axis=1)
        acc_ref[here, :] += mm(left, rhs_ref[part])
        return ds

    def scores(part, keys, aux):
        both = jnp.concatenate([keys, aux], axis=1)
        return mm(both, qx_ref[part], NT), mm(both, gx_ref[part], NT)

    def prepare(part, carry):
        rows = pl.ds(pl.multiple_of(part * RUN, RUN), RUN)
        gsent = gsent_ref[rows, :].astype(F32)
        norm = norm_ref[rows, :]
        product = gsent * att_ref[rows, :] / norm
        scaled = (gsent / norm).astype(BF16).astype(F32)
        for head in range(2):
            mask = low_lanes if head == 0 else jnp.logical_not(low_lanes)
            delta = jnp.sum(jnp.where(mask, product, 0.0), axis=1, keepdims=True)
            top = delta.astype(BF16).astype(F32)
            middle = (delta - top).astype(BF16).astype(F32)
            rest = delta - top - middle
            ext = jnp.where(lane == 0, -top, 0.0)
            ext = jnp.where(lane == 1, -middle, ext)
            ext = jnp.where(lane == 2, -rest, ext)
            grad = pltpu.roll(scaled, 64, axis=1) if head == 0 else scaled
            grad = jnp.where(low_lanes, 0.0, grad).astype(BF16)
            here = pl.ds(head * RUN, RUN)
            gx_ref[part, here, 0:128] = grad
            gx_ref[part, here, 128:256] = ext.astype(BF16)
            rhs_ref[part, pl.ds(head * RUN, RUN), :] = qx_ref[part, here, 0:128]
            rhs_ref[part, pl.ds((2 + head) * RUN, RUN), :] = grad
        order_key, order_query = order_pair(order_ref, part)
        allowed = order_query <= order_key
        keys = own_kv_ref[rows, :]
        score, prob = scores(part, keys, own_aux_ref[rows, :])
        e = jnp.where(jnp.concatenate([allowed, allowed], axis=1), jnp.exp(score), 0.0)
        own = pl.ds(pl.multiple_of(own_base + part * RUN, RUN), RUN)
        dq_acc[part] = mm(keys.T[:64], apply(part, own, e, prob))
        return carry

    lax.fori_loop(0, 4, prepare, 0)
    for item in copies:
        item.wait()

    def part_step(part, carry):
        number = count(part)
        half = lax.rem(part, 2) * 32

        def group(step, carry):
            places = group_places(first_ref, number, half, step, WIDE_BACK)
            parts = [scores(part, kv_ref[here, :], aux_ref[here, :]) for here in places]
            ds = [
                apply(part, here, jnp.exp(score), prob)
                for here, (score, prob) in zip(places, parts)
            ]
            keys = jnp.concatenate([kv_ref[here, :] for here in places], axis=0)
            dq_acc[part] += mm(keys.T[:64], jnp.concatenate(ds, axis=0))
            return carry

        lax.fori_loop(0, lax.div(number + WIDE_BACK - 1, WIDE_BACK), group, 0)
        rows = pl.ds(pl.multiple_of(part * RUN, RUN), RUN)
        total = dq_acc[part] * 0.125
        dq_ref[rows, :] = jnp.concatenate([total[:, :RUN], total[:, RUN:]], axis=0).T
        return carry

    lax.fori_loop(0, 4, part_step, 0)

    def store(step):
        rows = pl.ds(pl.multiple_of(step * 2048, 2048), 2048)
        return pltpu.make_async_copy(out_ref.at[rows], dkv_hbm.at[rows], stores.at[step])

    def narrow(step, carry):
        rows = pl.ds(pl.multiple_of(step * 2048, 2048), 2048)
        out_ref[rows, :] = acc_ref[rows, :].astype(BF16)
        store(step).start()
        return carry

    def settle(step, carry):
        store(step).wait()
        return carry

    lax.fori_loop(0, 8, narrow, 0)
    lax.fori_loop(0, 8, settle, 0)


def attend_back(order, base, kv, aux, own_kv, own_aux, query_ext, order_rows, gsent, att, norm):
    smem = pl.BlockSpec(memory_space=pltpu.SMEM)
    vmem = pl.BlockSpec(memory_space=pltpu.VMEM)
    hbm = pl.BlockSpec(memory_space=pl.ANY)
    return local_call(
        attend_back_kernel,
        (shape((CHIP_ROWS, 128), F32), shape((TOKENS, 128), BF16)),
        scratch=[
            pltpu.VMEM((TOKENS, 128), BF16),
            pltpu.VMEM((TOKENS, 128), BF16),
            pltpu.VMEM((TOKENS, 128), F32),
            pltpu.VMEM((4, 64, 2 * RUN), F32),
            pltpu.VMEM((4, 2 * RUN, 256), BF16),
            pltpu.VMEM((4, 4 * RUN, 128), BF16),
            pltpu.VMEM((TOKENS, 128), BF16),
            pltpu.SMEM((64,), jnp.int32),
            pltpu.SemaphoreType.DMA((2,)),
            pltpu.SemaphoreType.DMA((8,)),
        ],
        in_specs=[smem] * 2 + [hbm] * 2 + [vmem] * 7,
        out_specs=[vmem, hbm],
    )(order, base, kv, aux, own_kv, own_aux, query_ext, order_rows, gsent, att, norm)


SLOT_EXPERT = np.arange(SLOTS) // SLOT
SLOT_PLACE = np.arange(SLOTS) % SLOT


def constant(array):
    return jnp.asarray(np.asarray(array).astype(ml_dtypes.bfloat16))


def expand_matrix():
    return constant(np.arange(128)[:, None] == SLOT_EXPERT[None, :])


def place_matrix():
    return constant(SLOT_PLACE[:, None] == np.arange(128)[None, :])


def origin_matrix():
    return constant((np.arange(8 * SLOT) // SLOT)[:, None] == np.arange(128)[None, :])


def place_column():
    used = np.where(SLOT_PLACE < CAP, SLOT_PLACE, -5)
    return constant(np.broadcast_to(used[:, None], (SLOTS, 128)))


def place_row():
    used = np.where(SLOT_PLACE < CAP, SLOT_PLACE, -5)
    return jnp.asarray(used[None, :].astype(np.float32))


BLOCK = 8 * SLOT


def packed_pairs(values):
    total = sum(int(value) << (2 * i) for i, value in enumerate(values))
    return np.uint32(total).astype(np.int32)


STEP_Y = packed_pairs([dy for dy, _ in PLANE_ORDER])
STEP_Z = packed_pairs([dz for _, dz in PLANE_ORDER])


def moe_kernel(
    sent_ref, tok_ref, w_out_ref, router_ref, member_ref, put_ref, take_ref, expand_ref,
    expand_t_ref, place_ref, place_t_ref, origin_ref, block_place_ref, cot_ref, cots_hbm, gate_hbm, up_hbm, down_hbm,
    residual_ref, weigh_high_ref, weigh_low_ref, gmid_ref, branch_ref, gsent_in, side_in,
    y_hbm, grads_hbm,
    sent_in, x_out, x_in, y_v, back_out, back_in, gate_v, up_v, down_v,
    sum_gate, sum_up, sum_down, grads_v, mixed_v, gate_probs, gsent_out, side_out, cots_v,
    note_out, note_in, answer_out, answer_in,
    x_send, x_recv, back_send, back_recv, note_send, note_recv, answer_send, answer_recv,
    line_send, line_recv, local,
):
    me = position(AXES)
    x_at, y_at, z_at, c_at = (me[axis] for axis in AXES)
    expert = (y_at * 4 + z_at) * 2 + c_at

    def offset(k):
        pair = lax.div(k, 2)
        dy = lax.shift_right_logical(jnp.int32(STEP_Y), 2 * pair) & 3
        dz = lax.shift_right_logical(jnp.int32(STEP_Z), 2 * pair) & 3
        return dy, dz, lax.rem(k + pair, 2)

    def toward(k):
        dy, dz, dc = offset(k)
        return {"y": lax.rem(y_at + dy, 4), "z": lax.rem(z_at + dz, 4), "c": lax.rem(c_at + dc, 2)}

    def source(k):
        dy, dz, dc = offset(k)
        return {
            "y": lax.rem(y_at + 4 - dy, 4),
            "z": lax.rem(z_at + 4 - dz, 4),
            "c": lax.rem(c_at + dc, 2),
        }

    def number(at):
        return (at["y"] * 4 + at["z"]) * 2 + at["c"]

    loads = [
        pltpu.make_async_copy(src, dst, local.at[i])
        for i, (src, dst) in enumerate(
            ((cots_hbm, cots_v), (gate_hbm, gate_v), (up_hbm, up_v), (down_hbm, down_v))
        )
    ]
    barrier = pltpu.get_barrier_semaphore()
    for by in LINE_OFFSETS:
        pl.semaphore_signal(barrier, inc=1, device_id=moved(me, by), device_id_type=MESH)

    def hello(k, carry):
        pl.semaphore_signal(barrier, inc=1, device_id=toward(k), device_id_type=MESH)
        return carry

    lax.fori_loop(0, 31, hello, 0)
    sum_gate[...] = jnp.zeros_like(sum_gate)
    sum_up[...] = jnp.zeros_like(sum_up)
    sum_down[...] = jnp.zeros_like(sum_down)
    pl.semaphore_wait(barrier, 31 + len(LINE_OFFSETS))

    here_line = x_at * 2 + c_at
    moves = []
    for i, by in enumerate(LINE_OFFSETS):
        to = moved(me, by)
        moves.append(
            remote(sent_ref.at[to["c"] * 4 + to["x"]], sent_in.at[here_line], line_send, line_recv, i, to)
        )
        moves[-1].start()
    kept = pltpu.make_async_copy(sent_ref.at[c_at * 4 + x_at], sent_in.at[here_line], local.at[4])
    kept.start()
    for item in loads:
        item.start()
    for item in moves + [kept]:
        item.wait()
    sent = jnp.concatenate([sent_in[i] for i in range(8)], axis=1)
    residual = tok_ref[...].astype(F32) + mm(sent, w_out_ref[...])
    residual_ref[...] = residual
    residual_ref.store()
    gain = router_ref[...].astype(F32).T[EXPERTS : EXPERTS + 1, :]
    scale = lax.rsqrt(jnp.mean(residual * residual, axis=-1, keepdims=True) + EPSILON)
    mixed = (residual * scale * gain).astype(BF16)
    mixed_v[...] = mixed
    def tiles(value):
        return value.reshape(8, SLOT, 8, 128).astype(BF16)

    def rows_of(value):
        return value.astype(F32).reshape(value.shape[0] * SLOT, D).astype(BF16)

    def plane_of(by):
        plane = lax.rem(y_at + by, 4)
        return pl.ds(plane * 8, 8), pl.ds(pl.multiple_of(plane * BLOCK, 32), BLOCK)

    def build(by):
        experts, rows = plane_of(by)
        x_out[experts] = tiles(mm(put_ref[rows, :], mixed))

    build(2)

    def x_copy(k):
        to = toward(k)
        return remote(x_out.at[number(to)], x_in.at[k], x_send, x_recv, k, to)

    def note_copy(k):
        to = toward(k)
        return remote(note_out.at[number(to)], note_in.at[k], note_send, note_recv, k, to)

    def x_start(k, carry):
        x_copy(k).start()
        return carry

    lax.fori_loop(0, 6, x_start, 0)
    for by in (3, 1, 0):
        build(by)
    lax.fori_loop(6, 8, x_start, 0)
    kept = pltpu.make_async_copy(x_out.at[expert], x_in.at[31], local.at[4])
    kept.start()
    logits = mm(mixed, router_ref[...])
    member = member_ref[...]
    masked = jnp.where(member > 0.5, logits, -FAR)
    top = jnp.max(masked, axis=1, keepdims=True)
    power = jnp.where(member > 0.5, jnp.exp(masked - top), 0.0)
    gate = power / jnp.sum(power, axis=1, keepdims=True)
    gate_probs[...] = gate
    gate_high, gate_low = halves(gate)
    spread = mm(gate_high, expand_ref[...]) + mm(gate_low, expand_ref[...])
    weigh = take_ref[...].astype(F32) * spread
    weigh_high, weigh_low = halves(weigh)
    weigh_high_ref[...] = weigh_high
    weigh_low_ref[...] = weigh_low
    weigh_high_ref.store()
    weigh_low_ref.store()
    wide_expand = expand_ref[...].astype(F32)
    rows_high, rows_low = halves(wide_expand * jnp.sum(weigh, axis=0, keepdims=True))
    gates = mm(rows_high, place_ref[...]) + mm(rows_low, place_ref[...])
    token = lax.broadcasted_iota(jnp.int32, (ROWS, SLOTS), 0).astype(F32)
    token = jnp.sum(take_ref[...].astype(F32) * token, axis=0, keepdims=True)
    token = mm((wide_expand * token).astype(BF16), place_ref[...])
    top_row = lax.broadcasted_iota(jnp.int32, (8, 128), 0) == 0
    for i in range(EXPERTS):
        note_out[i] = jnp.where(
            top_row,
            jnp.broadcast_to(gates[i : i + 1], (8, 128)),
            jnp.broadcast_to(token[i : i + 1], (8, 128)),
        )

    def note_start(k, carry):
        note_copy(k).start()
        return carry

    lax.fori_loop(0, 31, note_start, 0)
    lax.fori_loop(8, 31, x_start, 0)
    note_in[31] = note_out[expert]
    kept.wait()
    for item in loads:
        item.wait()

    def cot_of(at):
        return cots_v[number(at)]

    block_row = lax.broadcasted_iota(jnp.int32, (BLOCK, 1), 0)
    block_start = jnp.zeros((BLOCK, 1), F32)
    for i in range(1, 8):
        block_start += jnp.where(block_row >= i * SLOT, 128.0, 0.0)
    origin_ref.get()
    block_place_ref.get()

    def answer_copy(k):
        return remote(answer_out.at[k], answer_in.at[expert], answer_send, answer_recv, k, source(k))

    def back_copy(k):
        to = source(k)
        return remote(back_out.at[k], back_in.at[expert], back_send, back_recv, k, to)

    def back_kept():
        return pltpu.make_async_copy(back_out.at[31], back_in.at[expert], local.at[4])

    def group(step, carry):
        first = step * 8
        for i in range(8):
            k = first + i

            @pl.when(k < 31)
            def _():
                x_copy(k).wait_recv()
                note_copy(k).wait_recv()

        x = rows_of(x_in[pl.ds(first, 8)])
        origin, place = origin_ref[...], block_place_ref[...].astype(F32)
        blank = jnp.zeros((120, 128), F32)
        gates = [note_in[first + i][0:1] for i in range(8)]
        gates_high, gates_low = halves(jnp.concatenate(gates + [blank], axis=0))
        share = mm(origin, gates_high) + mm(origin, gates_low)
        share = jnp.sum(share * place, axis=1, keepdims=True)
        tokens = [note_in[first + i][1:2] for i in range(8)]
        row = mm(origin, jnp.concatenate(tokens + [blank], axis=0).astype(BF16))
        row = jnp.sum(row * place, axis=1, keepdims=True) + block_start
        chosen = jnp.where(lane_index((BLOCK, D)).astype(F32) == row, 1.0, 0.0).astype(BF16)
        g = mm(chosen, jnp.concatenate([cot_of(source(first + i)) for i in range(8)], axis=0))
        a = mm(x, gate_v[...])
        b = mm(x, up_v[...])
        s = 1.0 / (1.0 + jnp.exp(-a))
        silu = a * s
        hidden = (silu * b).astype(BF16)
        y = mm(hidden, down_v[...]).astype(BF16).astype(F32)
        dgate = jnp.sum(y * g, axis=1, keepdims=True)
        dgate_high, dgate_low = halves(dgate * place)
        answers = mm(origin, dgate_high, TN) + mm(origin, dgate_low, TN)
        for i in range(8):
            k = first + i
            answer_out[k] = jnp.broadcast_to(answers[i : i + 1], (8, 128))

            @pl.when(k < 31)
            def _():
                answer_copy(k).start()

        y = tiles(y)
        for i in range(8):
            y_v[number(source(first + i))] = y[i]
        gy = (g * share).astype(BF16)
        dhidden = mm(gy, down_v[...], NT)
        da = (dhidden * b * (s * (1.0 + a * (1.0 - s)))).astype(BF16)
        db = (dhidden * silu).astype(BF16)
        back = mm(da, gate_v[...], NT) + mm(db, up_v[...], NT)
        back_out[pl.ds(first, 8)] = tiles(back)
        for i in range(8):
            k = first + i

            @pl.when(k < 31)
            def _():
                back_copy(k).start()

            @pl.when(k == 31)
            def _():
                back_kept().start()

        sum_gate[...] += mm(x, da, TN)
        sum_up[...] += mm(x, db, TN)
        sum_down[...] += mm(hidden, gy, TN)
        return carry

    lax.fori_loop(0, 4, group, 0)
    answer_in[expert] = answer_out[31]
    for i in range(4):
        grads_v[i * 768 : i * 768 + 256] = sum_gate[i * 256 : (i + 1) * 256].astype(BF16)
        grads_v[i * 768 + 256 : i * 768 + 512] = sum_up[i * 256 : (i + 1) * 256].astype(BF16)
        down = sum_down[i * 128 : (i + 1) * 128].astype(BF16)
        grads_v[i * 768 + 512 : i * 768 + 640] = down[:, 0:FF]
        grads_v[i * 768 + 640 : i * 768 + 768] = down[:, FF:D]
    stores = [
        pltpu.make_async_copy(src, dst, local.at[i])
        for i, (src, dst) in enumerate(((y_v, y_hbm), (grads_v, grads_hbm)))
    ]
    for item in stores:
        item.start()

    def answers(k, carry):
        answer_copy(k).wait()
        return carry

    lax.fori_loop(0, 31, answers, 0)
    take = take_ref[...]
    rows_high, rows_low = halves(
        jnp.concatenate([answer_in[i][0:1] for i in range(EXPERTS)] + [jnp.zeros((96, 128), F32)], axis=0)
    )
    spread = mm(rows_high, place_t_ref[...]) + mm(rows_low, place_t_ref[...])
    along = jnp.sum(spread * expand_ref[...].astype(F32), axis=0, keepdims=True)
    found_high, found_low = halves(take.astype(F32) * along)
    dgate = mm(found_high, expand_t_ref[...]) + mm(found_low, expand_t_ref[...])
    gate = gate_probs[...]
    dlogits = gate * (dgate - jnp.sum(gate * dgate, axis=1, keepdims=True))
    dlogits = dlogits.astype(BF16)
    dmixed = mm(dlogits, router_ref[...], NT)

    def settle(k, carry):
        x_copy(k).wait_send()
        note_copy(k).wait_send()
        back_copy(k).wait()
        return carry

    def add(by):
        experts, rows = plane_of(by)
        return mm(put_ref[rows, :], rows_of(back_in[experts]), TN)

    lax.fori_loop(0, 6, settle, 0)
    lax.fori_loop(12, 14, settle, 0)
    dmixed += add(2)
    lax.fori_loop(6, 12, settle, 0)
    lax.fori_loop(14, 31, settle, 0)
    back_kept().wait()
    for by in (3, 1, 0):
        dmixed += add(by)

    residual = residual_ref[...]
    scale = lax.rsqrt(jnp.mean(residual * residual, axis=-1, keepdims=True) + EPSILON)
    gain = router_ref[...].astype(F32).T[EXPERTS : EXPERTS + 1, :]
    weighted = dmixed * gain
    inner = jnp.mean(weighted * residual, axis=-1, keepdims=True)
    gmid = cot_ref[...].astype(F32) + scale * weighted - residual * (scale * scale * scale) * inner
    gmid_ref[...] = gmid
    gmid_ref.store()
    branch = gmid.astype(BF16)
    branch_ref[...] = branch
    branch_ref.store()
    gsent = mm(branch, w_out_ref[...], NT).astype(BF16)
    for i in range(8):
        gsent_out[i] = gsent[:, i * 128 : (i + 1) * 128]
    back_line = c_at * 4 + x_at
    moves = []
    for i, by in enumerate(LINE_OFFSETS):
        to = moved(me, by)
        moves.append(
            remote(
                gsent_out.at[to["x"] * 2 + to["c"]], gsent_in.at[back_line], line_send, line_recv, 7 + i, to
            )
        )
        moves[-1].start()
    kept = pltpu.make_async_copy(gsent_out.at[here_line], gsent_in.at[back_line], local.at[4])
    kept.start()
    moves.append(kept)
    gain_grad = jnp.sum(dmixed * residual * scale, axis=0, keepdims=True)
    grads = mm(dlogits, mixed_v[...], TN)
    row = lax.broadcasted_iota(jnp.int32, (128, D), 0)
    grads = jnp.where(row == EXPERTS, gain_grad, grads).T.reshape(4, 16, 2, 8, 128)
    for i in range(8):
        side_out[i] = grads[i // 2, :, i % 2].reshape(ROWS, 128).astype(BF16)
    for i, by in enumerate(LINE_OFFSETS):
        to = moved(me, by)
        moves.append(
            remote(
                side_out.at[to["x"] * 2 + to["c"]], side_in.at[back_line], line_send, line_recv, 14 + i, to
            )
        )
        moves[-1].start()
    kept = pltpu.make_async_copy(side_out.at[here_line], side_in.at[back_line], local.at[5])
    kept.start()
    for item in moves + [kept] + stores:
        item.wait()


def moe(inputs, cid):
    slots = (EXPERTS, SLOT, 8, 128)
    up, down = (D, FF), (FF, D)
    dma = pltpu.SemaphoreType.DMA
    return remote_call(
        moe_kernel,
        inputs,
        ("h", "l", (0, D), (D, D + 128)) + ("l",) * 10 + ("h",) * 4,
        [
            shape((ROWS, D), F32),
            shape((ROWS, SLOTS), BF16),
            shape((ROWS, SLOTS), BF16),
            shape((ROWS, D), F32),
            shape((ROWS, D), BF16),
            shape((8, ROWS, 128), BF16),
            shape((8, ROWS, 128), BF16),
            shape(slots, BF16),
            shape((3 * D, FF), BF16),
        ],
        ("e", "e", "e", "e", "e", "v", "v", "h", "h"),
        [
            pltpu.VMEM((8, ROWS, 128), BF16),
            pltpu.VMEM(slots, BF16),
            pltpu.VMEM(slots, BF16),
            pltpu.VMEM(slots, BF16),
            pltpu.VMEM(slots, BF16),
            pltpu.VMEM(slots, BF16),
            pltpu.VMEM(up, BF16),
            pltpu.VMEM(up, BF16),
            pltpu.VMEM(down, BF16),
            pltpu.VMEM(up, F32),
            pltpu.VMEM(up, F32),
            pltpu.VMEM(down, F32),
            pltpu.VMEM((3 * D, FF), BF16),
            pltpu.VMEM((ROWS, D), BF16),
            pltpu.VMEM((ROWS, 128), F32),
            pltpu.VMEM((8, ROWS, 128), BF16),
            pltpu.VMEM((8, ROWS, 128), BF16),
            pltpu.VMEM((EXPERTS, ROWS, D), BF16),
            pltpu.VMEM((EXPERTS, 8, 128), F32),
            pltpu.VMEM((EXPERTS, 8, 128), F32),
            pltpu.VMEM((EXPERTS, 8, 128), F32),
            pltpu.VMEM((EXPERTS, 8, 128), F32),
        ]
        + [dma((31,))] * 8
        + [
            dma((21,)),
            dma((21,)),
            dma((6,)),
        ],
        cid,
    )


def tail_kernel(
    partial_ref, sent_ref, branch_ref, side_rows_ref, dq_ref, cos_ref, sin_ref, normed_ref, w_ref,
    y_ref, weigh_high_ref, weigh_low_ref, residual_ref,
    dnormed_out, mixed_out, grads_out, early_out,
    dqkv, part_out, part_in, part_own, line_out, line_in, share_out, share_in, total,
    out_in, side_in, dkv_ref, out_ref, side_ref, far_a, near_a, out_a, sum_a, far_b, near_b, out_b,
    plane_send, plane_recv, send, recv, local, out_recv,
):
    me = position(AXES)
    x, y, z, c = (me[axis] for axis in AXES)
    mine = y * 4 + z
    alone = jnp.where(c == lax.div(y, 2), 1, 0)
    barrier = pltpu.get_barrier_semaphore()

    def owner(k):
        at = lax.rem(lax.rem(y, 2) * 8 + z * 2 + c + k, 16)
        to = {"y": 2 * c + lax.div(at, 8), "z": lax.rem(lax.div(at, 2), 4), "c": lax.rem(at, 2)}
        return at, to

    def origin(k):
        at = lax.rem(mine + k, 16)
        return at, {"y": lax.div(at, 4), "z": lax.rem(at, 4), "c": lax.div(y, 2)}

    for k in range(1, 16):
        pl.semaphore_signal(barrier, inc=1, device_id=origin(k)[1], device_id_type=MESH)

    @pl.when(alone == 0)
    def _():
        pl.semaphore_signal(barrier, inc=1, device_id=origin(0)[1], device_id_type=MESH)

    offsets = LINE_OFFSETS + PLANE_OFFSETS
    for offset in offsets:
        pl.semaphore_signal(barrier, inc=1, device_id=moved(me, offset), device_id_type=MESH)
    grad_out = mm(sent_ref[...], branch_ref[...], TN)
    for j in range(16):
        out_ref[j] = grad_out[j * 8 : (j + 1) * 8]
    side = side_rows_ref[0].astype(F32)
    for i in range(1, 8):
        side += side_rows_ref[i].astype(F32)
    side_ref[...] = side.reshape(16, 8, 128)
    pl.semaphore_wait(barrier, len(offsets) + 16 - alone)
    def begun():
        for item in (
            dq_ref, cos_ref, sin_ref, w_ref, normed_ref, weigh_high_ref, weigh_low_ref, residual_ref
        ):
            item.begin()

    scatter_plane(
        me, begun, partial_ref, dkv_ref, far_a, near_a, out_a, sum_a, far_b, near_b, out_b, plane_send, plane_recv
    )
    used = [0]

    def go(src, dst, to):
        item = remote(src, dst, send, recv, used[0], to)
        used[0] += 1
        item.start()
        return item

    other = 1 - c
    low_lanes = lane_index((256, 128)) < 64

    def out_copy(k):
        at, to = owner(k)
        return pltpu.make_async_remote_copy(
            src_ref=out_ref.at[at], dst_ref=out_in.at[mine], send_sem=send.at[used[0] + k],
            recv_sem=out_recv.at[mine], device_id=to, device_id_type=MESH,
        )

    def out_kept():
        return pltpu.make_async_copy(out_ref.at[owner(0)[0]], out_in.at[mine], local.at[1])

    out_copies = [out_copy(k) for k in range(16)]
    used[0] += 16
    out_arrivals = []
    for k in range(16):
        at, to = origin(k)
        out_arrivals.append(
            pltpu.make_async_remote_copy(
                src_ref=out_ref.at[0], dst_ref=out_in.at[at], send_sem=send.at[0],
                recv_sem=out_recv.at[at], device_id=to, device_id_type=MESH,
            )
        )

    @pl.when(alone == 0)
    def _():
        out_copies[0].start()

    @pl.when(alone == 1)
    def _():
        out_kept().start()

    for item in out_copies[1:]:
        item.start()
    early = []
    for offset in PLANE_OFFSETS:
        to = moved(me, offset)
        early.append(go(side_ref.at[to["y"] * 4 + to["z"]], side_in.at[mine], to))
    side_kept = pltpu.make_async_copy(side_ref.at[mine], side_in.at[mine], local.at[2])
    side_kept.start()
    early.append(side_kept)

    def turn_back(first):
        rows = pl.ds(pl.multiple_of(first, 256), 256)
        cos, sin = cos_ref[rows, :], sin_ref[rows, :]
        dq, dkv = dq_ref[rows, :], dkv_ref[lax.div(first, 512), pl.ds(lax.rem(first, 512), 256), :]
        dq = (dq * cos - turned(dq) * sin).astype(BF16)
        dkv = jnp.where(low_lanes, dkv * cos - turned(dkv) * sin, dkv).astype(BF16)
        both = jnp.concatenate([dq, dkv], axis=1)
        dqkv[rows, :] = both
        return mm(both, w_ref[...], NT)

    crossing = []
    for i in range(2):
        value = turn_back(other * 512 + i * 256).astype(BF16)
        part_out[2 * i] = value[:ROWS]
        part_out[2 * i + 1] = value[ROWS:]
        span = pl.ds(2 * i, 2)
        crossing.append(go(part_out.at[span], part_in.at[span], {"c": other}))
    for i in range(2):
        value = turn_back(c * 512 + i * 256)
        part_own[2 * i] = value[:ROWS]
        part_own[2 * i + 1] = value[ROWS:]
    for item in crossing:
        item.wait()
    along = []
    for i, by in enumerate((2, 1, 3)):
        to = lax.rem(x + by, 4)
        line_out[i] = (part_own[to] + part_in[to].astype(F32)).astype(BF16)
        along.append(go(line_out.at[i], line_in.at[i], {"x": to}))
    for i in range(4):
        columns = pl.ds(i * 256, 256)
        grad = mm(normed_ref[:, columns], dqkv[...], TN).astype(BF16)
        share_out[i] = grad.reshape(16, 16, 256)
    spread = []
    for offset in PLANE_OFFSETS:
        to = moved(me, offset)
        spread.append(go(share_out.at[:, to["y"] * 4 + to["z"]], share_in.at[mine], to))
    kept = pltpu.make_async_copy(share_out.at[:, mine], share_in.at[mine], local.at[0])
    kept.start()
    outs = y_ref[...].astype(F32).reshape(SLOTS, D).astype(BF16)
    mixed = mm(weigh_high_ref[...], outs) + mm(weigh_low_ref[...], outs)
    mixed_out[...] = (residual_ref[...] + mixed).astype(BF16)
    mixed_out.store()
    for item in spread + [kept]:
        item.wait()
    for i in range(4):
        value = share_in[0, i].astype(F32)
        for j in range(1, 16):
            value += share_in[j, i].astype(F32)
        total[i] = value.reshape(2, 8, 256)
    ends = []
    here = x * 2 + c
    for offset in LINE_OFFSETS:
        to = moved(me, offset)
        ends.append(go(total.at[to["x"], to["c"]], grads_out.at[here], to))
    kept = pltpu.make_async_copy(total.at[x, c], grads_out.at[here], local.at[0])
    kept.start()
    for item in out_copies[1:]:
        item.wait_send()
    for item in out_arrivals[1:]:
        item.wait_recv()

    @pl.when(alone == 0)
    def _():
        out_copies[0].wait_send()
        out_arrivals[0].wait_recv()

    @pl.when(alone == 1)
    def _():
        out_kept().wait()

    for item in early:
        item.wait()
    out_total, side_total = out_in[0], side_in[0]
    for j in range(1, 16):
        out_total += out_in[j]
        side_total += side_in[j]
    early_out[:, 0:D] = out_total
    early_out[:, D : D + 128] = side_total
    for item in along:
        item.wait()
    dnormed = part_own[x] + part_in[x].astype(F32)
    for i in range(3):
        dnormed += line_in[i].astype(F32)
    dnormed_out[...] = dnormed
    for item in ends + [kept]:
        item.wait()


def tail(inputs, cid):
    count = 2 + 3 + 15 + 7 + 16 + 15
    return remote_call(
        tail_kernel,
        inputs,
        ("l",) * 4 + ("d",) * 4 + (DEFERRED_COLUMNS, "v", "d", "d", "d"),
        [
            shape((ROWS, D), F32),
            shape((ROWS, D), BF16),
            shape((8, 8, 256), F32),
            shape((8, D + 128), F32),
        ],
        ("v", "e", "v", "v"),
        [
            pltpu.VMEM((CHIP_ROWS, 256), BF16),
            pltpu.VMEM((4, ROWS, D), BF16),
            pltpu.VMEM((4, ROWS, D), BF16),
            pltpu.VMEM((4, ROWS, D), F32),
            pltpu.VMEM((3, ROWS, D), BF16),
            pltpu.VMEM((3, ROWS, D), BF16),
            pltpu.VMEM((4, 16, 16, 256), BF16),
            pltpu.VMEM((16, 4, 16, 256), BF16),
            pltpu.VMEM((4, 2, 8, 256), F32),
            pltpu.VMEM((16, 8, D), F32),
            pltpu.VMEM((16, 8, 128), F32),
            pltpu.VMEM((2, 512, 128), F32),
            pltpu.VMEM((16, 8, D), F32),
            pltpu.VMEM((16, 8, 128), F32),
            pltpu.VMEM((2, 4, 2, 256, 128), BF16),
            pltpu.VMEM((2, 4, 2, 512, 128), BF16),
            pltpu.VMEM((2, 4, 2, 512, 128), BF16),
            pltpu.VMEM((2, 2, 512, 128), F32),
            pltpu.VMEM((2, 2, 256, 128), BF16),
            pltpu.VMEM((2, 2, 512, 128), BF16),
            pltpu.VMEM((2, 3, 512, 128), BF16),
            pltpu.SemaphoreType.DMA((40,)),
            pltpu.SemaphoreType.DMA((40,)),
            pltpu.SemaphoreType.DMA((count,)),
            pltpu.SemaphoreType.DMA((count,)),
            pltpu.SemaphoreType.DMA((3,)),
            pltpu.SemaphoreType.DMA((16,)),
        ],
        cid,
        room=VMEM_BYTES,
    )


def last_kernel(
    dnormed_ref, tok_ref, gain_ref, gmid_ref, mixed_ref, rows_ref, wq_ref, wk_ref, wv_ref, own_gain_ref, early_ref,
    grads_ref,
    tokens_out, mixed_out, query_out, key_out, value_out, gains_out, grad_out, router_out,
    gate_out, up_out, down_out,
):
    tok = tok_ref[...].astype(F32)
    scale = lax.rsqrt(jnp.mean(tok * tok, axis=-1, keepdims=True) + EPSILON)
    weighted = dnormed_ref[...] * gain_ref[0:1, :]
    inner = jnp.mean(weighted * tok, axis=-1, keepdims=True)
    tokens_out[...] = gmid_ref[...] + scale * weighted - tok * (scale * scale * scale) * inner
    mixed_out[...] = mixed_ref[...]
    for i in range(8):
        query_out[:, i * 128 : (i + 1) * 128] = rows_ref[i][:, :128]
    lanes = lane_index((8, 128)) < 64
    for i in range(4):
        first, second = rows_ref[2 * i][:, 128:], rows_ref[2 * i + 1][:, 128:]
        key_out[:, i * 128 : (i + 1) * 128] = jnp.where(lanes, first, pltpu.roll(second, 64, axis=1))
        value_out[:, i * 128 : (i + 1) * 128] = jnp.where(lanes, pltpu.roll(first, 64, axis=1), second)
    total = (
        jnp.sum(query_out[...] * wq_ref[...].astype(F32), axis=1, keepdims=True)
        + jnp.sum(key_out[...] * wk_ref[...].astype(F32), axis=1, keepdims=True)
        + jnp.sum(value_out[...] * wv_ref[...].astype(F32), axis=1, keepdims=True)
    )
    row = jnp.broadcast_to(own_gain_ref[...].astype(F32), (8, 8))
    diagonal = lax.broadcasted_iota(jnp.int32, (8, 8), 0) == lane_index((8, 8))
    total = total / jnp.sum(jnp.where(diagonal, row, 0.0), axis=1, keepdims=True)
    side = early_ref[:, D : D + 128]
    wide = jnp.broadcast_to(total, (8, 128))
    blank = jnp.zeros((120, 128), F32)
    gain_one = jnp.concatenate([wide, blank], axis=0).T[0:1, :]
    gain_two = jnp.concatenate([side, blank], axis=0).T[EXPERTS : EXPERTS + 1, :]
    top_row = lax.broadcasted_iota(jnp.int32, (8, 128), 0) == 0
    gains_out[...] = jnp.where(top_row, jnp.broadcast_to(gain_one, (8, 128)), jnp.broadcast_to(gain_two, (8, 128)))
    grad_out[...] = early_ref[:, 0:D]
    router_out[...] = side[:, 0:EXPERTS]
    gate_out[...] = grads_ref[0:256].astype(F32)
    up_out[...] = grads_ref[256:512].astype(F32)
    down_out[:, 0:FF] = grads_ref[512:640].astype(F32)
    down_out[:, FF:D] = grads_ref[640:768].astype(F32)


def body(
    tokens,
    gain_one,
    w_query,
    w_key,
    w_value,
    w_out,
    gain_two,
    w_router,
    w_gate,
    w_up,
    w_down,
    dealt_order,
    lengths,
    routes,
    cotangent,
):
    y_at, z_at = lax.axis_index("y"), lax.axis_index("z")
    first_row = (y_at * 4 + z_at) * CHIP_ROWS

    cot_rows = lax.all_gather(cotangent, ("y", "z", "c"), axis=0, tiled=True)

    expand, expand_t = expand_matrix(), expand_matrix().T
    place, place_t = place_matrix(), place_matrix().T
    (
        query, kv, gain_first, cos, sin, w_mine, member, put, take, own_aux, order_rows, key_norm, heads,
        kv_all, w_late, normed, aux,
    ) = front(
        (
            lengths, tokens, w_query, w_key, w_value, w_out, w_router, gain_one.reshape(1, 8),
            gain_two.reshape(1, 8), dealt_order.reshape(128, 128), routes.T,
            expand, expand_t, place_column(), place_row(), turn_tables(128), turn_tables(1),
        ),
        1,
    )
    kv_all = kv_all.reshape(TOKENS, 128)
    w_late = w_late.reshape(D, 1152)
    plane = ("y", "z", "c")

    base = first_row.reshape(1).astype(jnp.int32)
    att, norm, sent, query_ext = attend(
        heads, base, kv_all, aux, kv, own_aux, query, order_rows, key_norm
    )

    (
        residual, weigh_high, weigh_low, gmid, branch, gsent_own, side_rows, y_out, expert_grads,
    ) = moe(
        (
            sent.reshape(8, ROWS, 128), tokens, w_late, w_late, member, put, take, expand, expand_t,
            place, place_t, origin_matrix(), place[:BLOCK], cotangent,
            cot_rows.reshape(EXPERTS, ROWS, D), w_gate[0], w_up[0], w_down[0],
        ),
        3,
    )
    y_in = lax.all_to_all(y_out, plane, split_axis=0, concat_axis=0, tiled=True)
    expert_grads = lax.psum_scatter(expert_grads, "x", scatter_dimension=0, tiled=True)

    gsent_own = gsent_own.reshape(CHIP_ROWS, 128)
    branch_rows = lax.all_gather(branch, ("c", "x"), axis=0, tiled=True)

    dq, dkv = attend_back(
        heads, base, kv_all, aux, kv, own_aux, query_ext, order_rows, gsent_own, att, norm
    )

    dnormed, mixed, qkv_rows, early = tail(
        (
            dkv.reshape(4, 4, 2, 512, 128), sent, branch_rows, side_rows, dq, cos, sin, normed, w_mine,
            y_in, weigh_high, weigh_low, residual,
        ),
        7,
    )
    (
        grad_tokens, mixed, grad_query, grad_key, grad_value, gains, grad_out_rows, grad_router,
        grad_gate, grad_up, grad_down,
    ) = local_call(
        last_kernel,
        (
            shape((ROWS, D), F32),
            shape((ROWS, D), BF16),
            shape((8, D), F32),
            shape((8, 512), F32),
            shape((8, 512), F32),
            shape((8, 128), F32),
            shape((8, D), F32),
            shape((8, EXPERTS), F32),
            shape((256, FF), F32),
            shape((256, FF), F32),
            shape((128, D), F32),
        ),
    )(
        dnormed, tokens, gain_first, gmid, mixed, qkv_rows, w_query, w_key, w_value,
        gain_one.reshape(1, 8), early, expert_grads,
    )
    grad_gain_one, grad_gain_two = gains[0, :8], gains[1, :8]
    grad_gate, grad_up, grad_down = grad_gate[None], grad_up[None], grad_down[None]
    return (
        mixed,
        grad_tokens,
        grad_gain_one,
        grad_query,
        grad_key,
        grad_value,
        grad_out_rows,
        grad_gain_two,
        grad_router,
        grad_gate,
        grad_up,
        grad_down,
    )


def solution(mesh):
    grid = Mesh(mesh.devices.reshape(4, 4, 4, 2), AXES)
    rows = P(("y", "z", "c", "x"), None)
    vector = P(AXES)
    matrix = P(AXES, None)
    expert = P(("y", "z", "c"), None, None)
    in_specs = (
        rows, vector, matrix, matrix, matrix, matrix, vector, matrix, expert, expert, expert,
        P(), P(), rows, rows,
    )
    grads = P(("y", "z", "c"), "x", None)
    out_specs = (
        rows, rows, vector, matrix, matrix, matrix, matrix, vector, matrix, grads, grads, grads,
    )
    return jax.shard_map(body, mesh=grid, in_specs=in_specs, out_specs=out_specs, check_vma=False)
```
